32 devices in a mesh: groups: 2 (over y), seg: 4 (over z), ctx: 2 (over x), head: 2 (over core).
Axes of the slice: x: 2, y: 2, z: 4, core: 2. Of those that a mesh axis runs over, the one named last changes fastest.
Arguments:
- queries: bfloat16 [1024, 1024], P(('groups', 'ctx'), 'head'), parts along dimension 0, may hold values from -40 to 40
- cached_keys: bfloat16 [4096, 128], P(('groups', 'seg', 'ctx')), parts along dimension 0, may hold values from -20 to 20
- cached_values: bfloat16 [4096, 128], P(('groups', 'seg', 'ctx')), parts along dimension 0, may hold values from -6 to 6
- key_offsets: int32 [16], P('groups'), parts along dimension 0, may hold values from 0 to 1792, as said below
- vertical_blocks: int32 [16, 16], P('groups'), parts along dimension 0, may hold values from 0 to 31
- slash_offsets: int32 [16, 32], P('groups'), parts along dimension 0, may hold values from 0 to 24, as said below
Outputs:
- attended: bfloat16 [1024, 1024], P(('groups', 'ctx'), 'head'), parts along dimension 0
The draws below stay inside these ranges and needn't reach their ends.
There are 2 independent parts, one for each index of `groups`. The reference program is written for one: setup_inputs(seed, part) draws one part's arguments, and reference() takes and returns one part's arrays. A program takes and returns all parts, laid end to end along the dimension named above; each array names one. Nothing has to cross between parts.
Inputs may be any that keep to these rules, and one draw needn't show every extreme that they name: `key_offsets`: holds k * 256 for every k below the number of key shards, each once. `slash_offsets`: column 0 is 0 in every row.
All inputs are finite; a program needn't handle non-finite values.
Results may differ from the reference program's by a relative error of at most 0.028.
Values may be sent and summed in bfloat16 or wider, within the bound.
No kernel may reach another device: no remote copies, remote signals or barrier semaphores. Data moves between devices by JAX's collectives and lax.ppermute only.
A program may use at most 64 MiB of HBM per device.

```python
import math
import jax
import jax.numpy as jnp
from jax import lax

HEAD_DIM = 128
QUERY_HEADS = 8
BLOCK = 64
VERTICAL = 16
SLASHES = 32
QUERY_ROWS = 256
KEY_ROWS = 256
KEY_TOTAL = 2048
PREFIX = 1536
QUERY_BLOCKS = 8
KEY_BLOCKS = 32
N_SEG = 4
N_CTX = 2


def slow_columns(columns):
    within = jnp.arange(columns, dtype=jnp.int32) % HEAD_DIM
    half_width = HEAD_DIM // 2
    return within % half_width >= half_width - HEAD_DIM // 8


def changed_column(columns):
    within = jnp.arange(columns, dtype=jnp.int32) % HEAD_DIM
    return within == HEAD_DIM // 2 - 1


def strong_rows(key):
    total_rows = QUERY_ROWS * N_CTX
    pick_key, sign_key, query_key, cache_key, tie_key = jax.random.split(jax.random.fold_in(key, 17), 5)
    index = jnp.arange(total_rows, dtype=jnp.int32)
    forced_high = index == 1
    forced_low = index == total_rows - 1
    picked = (jax.random.randint(pick_key, (total_rows,), 0, 32, dtype=jnp.int32) == 0) | forced_high | forced_low
    picked = picked & (index % 2 == 1)
    signs = jnp.where(jax.random.bernoulli(sign_key, 0.5, (total_rows, HEAD_DIM)), 1.0, -1.0).astype(jnp.float32)
    query_size = jax.random.uniform(query_key, (total_rows,), jnp.float32, 8.0, 38.0)
    cache_size = jax.random.uniform(cache_key, (total_rows,), jnp.float32, 4.0, 19.0)
    query_size = jnp.where(forced_high | forced_low, 30.0, query_size)
    cache_size = jnp.where(forced_high, 18.0, jnp.where(forced_low, 4.0, cache_size))
    tie_gap = jax.random.uniform(tie_key, (total_rows,), jnp.float32, 1.5, 2.5)
    return (picked, signs, query_size, cache_size, tie_gap)


def draw_queries(key, part):
    first_key = jax.random.fold_in(jax.random.fold_in(key, 11), 0)
    total_rows = QUERY_ROWS * N_CTX
    columns = QUERY_HEADS * HEAD_DIM
    drawn = jnp.clip(jax.random.normal(first_key, (total_rows, columns), jnp.float32), -6.0, 6.0)
    picked, signs, query_size, cache_size, tie_gap = strong_rows(key)
    strong_entries = jnp.tile(signs, (1, QUERY_HEADS)) * query_size[:, None]
    strong_entries = jnp.where(slow_columns(columns)[None, :], strong_entries, 0.0)
    values = jnp.where(picked[:, None], strong_entries, drawn)
    return values.astype(jnp.bfloat16)


def draw_cached_keys(key, part):
    first_key = jax.random.fold_in(jax.random.fold_in(key, 13), 0)
    total_rows = KEY_ROWS * N_SEG * N_CTX
    query_total = QUERY_ROWS * N_CTX
    drawn = jnp.clip(jax.random.normal(first_key, (total_rows, HEAD_DIM), jnp.float32), -6.0, 6.0)
    picked, signs, query_size, cache_size, tie_gap = strong_rows(key)
    offsets = draw_key_offsets(key, part)
    rows = jnp.arange(total_rows, dtype=jnp.int32)
    positions = offsets[rows // KEY_ROWS] + rows % KEY_ROWS
    query_index = (positions - PREFIX).astype(jnp.int32)
    next_index = (query_index + 1).astype(jnp.int32)
    own_clipped = jnp.clip(query_index, 0, query_total - 1).astype(jnp.int32)
    next_clipped = jnp.clip(next_index, 0, query_total - 1).astype(jnp.int32)
    self_hit = (query_index >= 0) & picked[own_clipped]
    prev_hit = (next_index >= 0) & (next_index < query_total) & picked[next_clipped]
    source = jnp.where(self_hit, own_clipped, next_clipped).astype(jnp.int32)
    change = tie_gap[source] * math.sqrt(HEAD_DIM) / query_size[source]
    lowered = jnp.where(prev_hit[:, None] & changed_column(HEAD_DIM)[None, :], change[:, None], 0.0)
    strong_entries = signs[source] * (cache_size[source][:, None] - lowered)
    use_strong = (self_hit | prev_hit)[:, None] & slow_columns(HEAD_DIM)[None, :]
    values = jnp.where(use_strong, strong_entries, drawn)
    return values.astype(jnp.bfloat16)


def draw_key_offsets(key, part):
    return (jax.random.permutation(key, N_SEG * N_CTX) * KEY_ROWS).astype(jnp.int32)


def draw_slash_offsets(key, part):
    drawn_offsets = jax.random.randint(key, (QUERY_BLOCKS, SLASHES), 1, PREFIX // BLOCK + 1, dtype=jnp.int32)
    column = jnp.arange(SLASHES, dtype=jnp.int32)[None, :]
    row_index = jnp.arange(QUERY_BLOCKS, dtype=jnp.int32)[:, None]
    drawn_offsets = jnp.where(column == 0, 0, drawn_offsets)
    drawn_offsets = jnp.where((row_index == 0) & (column == 1), PREFIX // BLOCK, drawn_offsets)
    return drawn_offsets.astype(jnp.int32)


def set_ends(entries, rng, least, largest):
    spot = [jax.random.randint(jax.random.fold_in(rng, axis), (), 0, length) for axis, length in enumerate(entries.shape)]
    longest = entries.shape.index(max(entries.shape))
    beside = spot[:longest] + [(spot[longest] + 1) % entries.shape[longest]] + spot[longest + 1:]
    return entries.at[tuple(spot)].set(least).at[tuple(beside)].set(largest)


def level_of(rng, shape, shards, least, high):
    def one(position, blocks):
        heights = jax.random.uniform(jax.random.fold_in(jax.random.fold_in(rng, 6), position), (blocks,), jnp.float32, least / len(shards), high / len(shards))
        return jnp.repeat(jnp.exp(heights), shape[position] // blocks).reshape((-1,) + (1,) * (len(shape) - position - 1))

    loudness = one(*shards[0])
    for cut in shards[1:]:
        loudness = loudness * one(*cut)
    return loudness


def noise(stream_key, dims, width, most, shards=(), held_as=jnp.bfloat16):
    entries = width * jax.random.normal(stream_key, dims, jnp.float32)
    if shards:
        entries = entries * level_of(stream_key, dims, shards, -0.22, 0.18)
    return jnp.clip(entries, -most, most).astype(held_as)


def setup_inputs(seed: int = 0, part: int = 0) -> dict:
    key_of = jax.random.split(jax.random.key(seed), 7)
    part_keys = jax.random.split(jax.random.fold_in(key_of[6], part), 7)
    return {
        "queries": draw_queries(jax.random.fold_in(jax.random.fold_in(key_of[6], part), 71), part),
        "cached_keys": draw_cached_keys(jax.random.fold_in(jax.random.fold_in(key_of[6], part), 71), part),
        "cached_values": noise(part_keys[2], (KEY_TOTAL, HEAD_DIM), 1.0, 6.0, ((0, 8),)),
        "key_offsets": draw_key_offsets(jax.random.fold_in(jax.random.fold_in(key_of[6], part), 71), part),
        "vertical_blocks": set_ends(jax.random.randint(part_keys[4], (QUERY_BLOCKS, VERTICAL), 0, KEY_BLOCKS), jax.random.fold_in(part_keys[4], 1), 0, KEY_BLOCKS - 1).astype(jnp.int32),
        "slash_offsets": draw_slash_offsets(jax.random.fold_in(jax.random.fold_in(key_of[6], part), 71), part),
    }


ROPE_THETA = 500000.0
ROPE_FACTOR = 8.0
LOW_FACTOR = 1.0
HIGH_FACTOR = 4.0
TRAINED_CONTEXT = 8192.0
MASKED_SCORE = -1.0e30


def inverse_frequencies(vector_width):
    exponent = jnp.arange(0, vector_width, 2, dtype=jnp.float32) / vector_width
    base_frequency = 1.0 / (ROPE_THETA ** exponent)
    wavelength = 2.0 * math.pi / base_frequency
    smooth = (TRAINED_CONTEXT / wavelength - LOW_FACTOR) / (HIGH_FACTOR - LOW_FACTOR)
    blended = (1.0 - smooth) * base_frequency / ROPE_FACTOR + smooth * base_frequency
    return jnp.where(wavelength < TRAINED_CONTEXT / HIGH_FACTOR, base_frequency,
                     jnp.where(wavelength > TRAINED_CONTEXT / LOW_FACTOR, base_frequency / ROPE_FACTOR, blended))


def rotate(vectors, positions):
    vector_width = vectors.shape[-1]
    half_width = vector_width // 2
    angles = positions.astype(jnp.float32)[:, None] * inverse_frequencies(vector_width)[None, :]
    cosine = jnp.concatenate([jnp.cos(angles), jnp.cos(angles)], axis=-1)[:, None, :]
    sine_table = jnp.concatenate([jnp.sin(angles), jnp.sin(angles)], axis=-1)[:, None, :]
    widened = vectors.astype(jnp.float32)
    turned = jnp.concatenate([-widened[..., half_width:], widened[..., :half_width]], axis=-1)
    return (widened * cosine + turned * sine_table).astype(jnp.bfloat16)


def widen(rounded):
    return lax.optimization_barrier(rounded).astype(jnp.float32)


def reference(queries, cached_keys, cached_values, key_offsets, vertical_blocks, slash_offsets):
    total_queries = queries.shape[0]
    total_keys = cached_keys.shape[0]
    prefix = total_keys - total_queries
    query_positions = (prefix + jnp.arange(total_queries, dtype=jnp.int32)).astype(jnp.int32)
    key_positions = (key_offsets[:, None] + jnp.arange(KEY_ROWS, dtype=jnp.int32)[None, :]).reshape(-1)
    rotated_queries = rotate(queries.reshape(total_queries, QUERY_HEADS, HEAD_DIM), query_positions)
    rotated_keys = widen(rotate(cached_keys.reshape(total_keys, 1, HEAD_DIM), key_positions).reshape(total_keys, HEAD_DIM))
    value_rows = cached_values.astype(jnp.float32)
    block_ids = jnp.arange(total_keys // BLOCK, dtype=jnp.int32)
    key_block = key_positions // BLOCK
    row_tile = math.gcd(total_queries, 128)
    score_scale = HEAD_DIM ** -0.5

    def attend_rows(tile_number):
        first_row = (tile_number * row_tile).astype(jnp.int32)
        query_tile = widen(lax.dynamic_slice_in_dim(rotated_queries, first_row, row_tile, 0))
        positions = lax.dynamic_slice_in_dim(query_positions, first_row, row_tile, 0)
        list_rows = (positions - prefix) // BLOCK
        vertical_hit = jnp.any(vertical_blocks[list_rows][:, :, None] == block_ids[None, None, :], axis=1)
        distance = positions[:, None] // BLOCK - block_ids[None, :]
        slash_hit = jnp.any(slash_offsets[list_rows][:, :, None] == distance[:, None, :], axis=1)
        allowed = (vertical_hit | slash_hit)[:, key_block] & (key_positions[None, :] <= positions[:, None])
        scores = jnp.einsum("thd,kd->thk", query_tile, rotated_keys, precision=lax.Precision.HIGHEST) * score_scale
        scores = jnp.where(allowed[:, None, :], scores, MASKED_SCORE)
        row_peak = jnp.max(scores, axis=-1, keepdims=True)
        weights = jnp.where(allowed[:, None, :], jnp.exp(scores - row_peak), 0.0)
        denominator = jnp.sum(weights, axis=-1)
        rounded_weights = widen(weights.astype(jnp.bfloat16))
        numerator = jnp.einsum("thk,kd->thd", rounded_weights, value_rows, precision=lax.Precision.HIGHEST)
        return (numerator / denominator[..., None]).astype(jnp.bfloat16).reshape(row_tile, QUERY_HEADS * HEAD_DIM)

    attended = lax.map(attend_rows, jnp.arange(total_queries // row_tile, dtype=jnp.int32))
    return attended.reshape(total_queries, QUERY_HEADS * HEAD_DIM)
```

```python
import functools
import math

import jax
import jax.numpy as jnp
import numpy as np
from jax import lax
from jax.experimental import pallas as pl
from jax.experimental.pallas import tpu as pltpu
from jax.sharding import PartitionSpec as P

HEAD_DIM = 128
BLOCK = 64
ROPE_THETA = 500000.0
ROPE_FACTOR = 8.0
LOW_FACTOR = 1.0
HIGH_FACTOR = 4.0
TRAINED_CONTEXT = 8192.0
MASKED_SCORE = -1e30
SCORE_SCALE = HEAD_DIM**-0.5 * math.log2(math.e)
VMEM_LIMIT = 56 * 1024 * 1024
DIRECT_SHARDS = 8


def frequency_row():
    exponent = np.arange(0, HEAD_DIM, 2, dtype=np.float64) / HEAD_DIM
    base = ROPE_THETA**-exponent
    wavelength = 2.0 * np.pi / base
    smooth = (TRAINED_CONTEXT / wavelength - LOW_FACTOR) / (HIGH_FACTOR - LOW_FACTOR)
    blended = (1.0 - smooth) * base / ROPE_FACTOR + smooth * base
    frequencies = np.where(
        wavelength < TRAINED_CONTEXT / HIGH_FACTOR,
        base,
        np.where(wavelength > TRAINED_CONTEXT / LOW_FACTOR, base / ROPE_FACTOR, blended),
    )
    return np.tile(frequencies, 2)[None, :].astype(np.float32)


def turned_sine(sine):
    lane = lax.broadcasted_iota(jnp.int32, sine.shape, 1)
    return jnp.where(lane < HEAD_DIM // 2, -sine, sine)


def rotate(vectors, cosine, signed_sine):
    wide = vectors.astype(jnp.float32)
    return (wide * cosine + pltpu.roll(wide, HEAD_DIM // 2, 1) * signed_sine).astype(jnp.bfloat16)


def shifted_table(cos_rows, sin_rows, cos_base, sin_base):
    return (
        cos_rows * cos_base - sin_rows * sin_base,
        sin_rows * cos_base + cos_rows * sin_base,
    )


def prepare_kernel(
    query_start_of, offsets, vertical, slash, queries, freq, rotated, cos_rows, sin_rows,
    cos_base, sin_base, bias, key_block,
):
    shards, rows = bias.shape[1:]
    query_rows = queries.shape[0]
    blocks = bias.shape[0]
    query_start, first_list = query_start_of()
    frequencies = freq[...]
    row = lax.broadcasted_iota(jnp.int32, (rows, HEAD_DIM), 0).astype(jnp.float32)
    angles = row * frequencies
    cos_r, sin_r = jnp.cos(angles), jnp.sin(angles)
    cos_rows[...] = cos_r
    sin_rows[...] = sin_r
    start_angle = query_start.astype(jnp.float32) * frequencies
    cosine, sine = shifted_table(cos_r, sin_r, jnp.cos(start_angle), jnp.sin(start_angle))
    sine = turned_sine(sine)
    for head in range(queries.shape[1] // HEAD_DIM):
        columns = pl.ds(head * HEAD_DIM, HEAD_DIM)
        rotated[:, columns] = rotate(queries[:, columns], cosine, sine)

    in_shard = lax.broadcasted_iota(jnp.int32, (1, rows), 1)

    @pl.loop(0, shards)
    def _(shard):
        offset = offsets[shard]
        angle = offset.astype(jnp.float32) * frequencies
        cos_base[pl.ds(shard, 1), :] = jnp.cos(angle)
        sin_base[pl.ds(shard, 1), :] = jnp.sin(angle)
        key_block[pl.ds(shard, 1), :] = (offset + in_shard) // BLOCK

    held = key_block[...]
    for block in range(blocks):
        line = first_list + block
        query_block = query_start // BLOCK + block
        hit = held == vertical[line, 0]
        for entry in range(1, vertical.shape[1]):
            hit = hit | (held == vertical[line, entry])
        for entry in range(slash.shape[1]):
            hit = hit | (held == query_block - slash[line, entry])
        bias[block] = jnp.where(hit, 0.0, MASKED_SCORE)


def attend_kernel(
    where_am_i, counts, offsets, rotated, cos_rows, sin_rows, cos_base, sin_base, bias, *refs
):
    pieces = refs[: 2 * len(counts)]
    out, peak, total, summed = refs[2 * len(counts) :]
    rows = cos_rows.shape[0]
    query_rows = rotated.shape[0]
    heads = rotated.shape[1] // HEAD_DIM
    query_start, head_core, shard_of = where_am_i()
    keys_mine = head_core == 0
    ahead = lax.broadcasted_iota(jnp.int32, (query_rows, rows), 0) - lax.broadcasted_iota(
        jnp.int32, (query_rows, rows), 1
    )
    cos_r, sin_r = cos_rows[...], sin_rows[...]

    def load(mine, other, shard):
        keys = jnp.where(keys_mine, mine, other)
        values = jnp.where(keys_mine, other, mine)
        cosine, sine = shifted_table(
            cos_r, sin_r, cos_base[pl.ds(shard, 1), :], sin_base[pl.ds(shard, 1), :]
        )
        keys = rotate(keys, cosine, turned_sine(sine))
        lines = [
            jnp.broadcast_to(bias[block, pl.ds(shard, 1), :], (BLOCK, rows))
            for block in range(bias.shape[0])
        ]
        mask = jnp.where(
            ahead >= offsets[shard] - query_start, jnp.concatenate(lines, axis=0), MASKED_SCORE
        )
        return keys, values, mask

    def update(loaded, first):
        for head in range(heads):
            columns = pl.ds(head * HEAD_DIM, HEAD_DIM)
            query = rotated[:, columns]
            scores = [
                lax.dot_general(
                    query, keys, (((1,), (1,)), ((), ())), preferred_element_type=jnp.float32
                )
                * SCORE_SCALE
                + mask
                for keys, _, mask in loaded
            ]
            fresh = functools.reduce(jnp.maximum, scores).max(axis=1, keepdims=True)
            if not first:
                old = peak[head][:, :1]
                fresh = jnp.maximum(old, fresh)
            weights = [jnp.exp2(score - fresh) for score in scores]
            part = functools.reduce(jnp.add, weights).sum(axis=1, keepdims=True)
            product = functools.reduce(
                jnp.add,
                [
                    jnp.dot(weight.astype(jnp.bfloat16), values, preferred_element_type=jnp.float32)
                    for weight, (_, values, _) in zip(weights, loaded)
                ],
            )
            if not first:
                scale = jnp.exp2(old - fresh)
                part = part + total[head][:, :1] * scale
                product = product + summed[head] * scale
            peak[head] = jnp.broadcast_to(fresh, peak.shape[1:])
            total[head] = jnp.broadcast_to(part, total.shape[1:])
            summed[head] = product

    if all(count == 1 for count in counts):
        update(
            [
                load(pieces[2 * i][...], pieces[2 * i + 1][...], shard_of(i))
                for i in range(len(counts))
            ],
            True,
        )
    else:
        peak[...] = jnp.full(peak.shape, MASKED_SCORE, jnp.float32)
        total[...] = jnp.zeros(total.shape, jnp.float32)
        summed[...] = jnp.zeros(summed.shape, jnp.float32)
        mine, other = pieces

        @pl.loop(0, counts[0])
        def _(shard):
            span = pl.ds(pl.multiple_of(shard * rows, rows), rows)
            update([load(mine[span, :], other[span, :], shard)], False)

    for head in range(heads):
        columns = pl.ds(head * HEAD_DIM, HEAD_DIM)
        out[:, columns] = (summed[head] / total[head]).astype(out.dtype)


def local(queries, cached_keys, cached_values, key_offsets, vertical_blocks, slash_offsets):
    query_rows = queries.shape[0]
    heads_here = queries.shape[1] // HEAD_DIM
    rows = cached_keys.shape[0]
    n_seg, n_ctx = lax.axis_size("seg"), lax.axis_size("ctx")
    shards = n_seg * n_ctx
    prefix = rows * shards - query_rows * n_ctx
    blocks = query_rows // BLOCK

    def query_start_of():
        ctx = lax.axis_index("ctx")
        return prefix + ctx * query_rows, ctx * blocks

    direct = shards <= DIRECT_SHARDS and n_seg & (n_seg - 1) == 0 and n_ctx == 2
    steps = [(s, c) for c in range(n_ctx) for s in range(n_seg)] if direct else []

    def where_am_i():
        seg, ctx = lax.axis_index("seg"), lax.axis_index("ctx")

        def shard_of(piece):
            s, c = steps[piece]
            return (seg ^ s) * n_ctx + (ctx ^ c)

        return prefix + ctx * query_rows, lax.axis_index("head"), shard_of

    def flip(a, axis, by):
        return lax.ppermute(a, axis, [(i, i ^ by) for i in range(lax.axis_size(axis))])

    on_first = lax.axis_index("head") == 0
    mine = jnp.where(on_first, cached_keys, cached_values)
    spare = jnp.where(on_first, cached_values, cached_keys)
    if direct:
        held = {(0, 0): mine}
        for s in range(1, n_seg):
            held[s, 0] = flip(mine, "seg", s)
        for s in range(n_seg):
            held[s, 1] = flip(held[s, 0], "ctx", 1)
        pieces = []
        for step in steps:
            pieces += [held[step], spare if step == (0, 0) else flip(held[step], "head", 1)]
        counts = (1,) * len(steps)
    else:
        gathered = lax.all_gather(mine, ("seg", "ctx"), axis=0, tiled=True)
        pieces = [gathered, flip(gathered, "head", 1)]
        counts = (shards,)

    vmem = pl.BlockSpec(memory_space=pltpu.VMEM)
    smem = pl.BlockSpec(memory_space=pltpu.SMEM)
    f32 = jnp.float32
    prepared = pl.pallas_call(
        functools.partial(prepare_kernel, query_start_of),
        out_shape=(
            jax.ShapeDtypeStruct(queries.shape, jnp.bfloat16),
            jax.ShapeDtypeStruct((rows, HEAD_DIM), f32),
            jax.ShapeDtypeStruct((rows, HEAD_DIM), f32),
            jax.ShapeDtypeStruct((shards, HEAD_DIM), f32),
            jax.ShapeDtypeStruct((shards, HEAD_DIM), f32),
            jax.ShapeDtypeStruct((blocks, shards, rows), f32),
        ),
        in_specs=[smem, smem, smem, vmem, vmem],
        out_specs=[vmem] * 6,
        scratch_shapes=[pltpu.VMEM((shards, rows), jnp.int32)],
        compiler_params=pltpu.CompilerParams(vmem_limit_bytes=VMEM_LIMIT),
        name="prepare",
    )(key_offsets, vertical_blocks, slash_offsets, queries, jnp.asarray(frequency_row()))
    return pl.pallas_call(
        functools.partial(attend_kernel, where_am_i, counts),
        out_shape=jax.ShapeDtypeStruct(queries.shape, jnp.bfloat16),
        in_specs=[smem] + [vmem] * (6 + len(pieces)),
        out_specs=vmem,
        scratch_shapes=[
            pltpu.VMEM((heads_here, query_rows, HEAD_DIM), f32),
            pltpu.VMEM((heads_here, query_rows, HEAD_DIM), f32),
            pltpu.VMEM((heads_here, query_rows, HEAD_DIM), f32),
        ],
        compiler_params=pltpu.CompilerParams(vmem_limit_bytes=VMEM_LIMIT),
        name="attend",
    )(key_offsets, *prepared, *pieces)


def solution(mesh):
    return jax.shard_map(
        local,
        mesh=mesh,
        in_specs=(
            P(("groups", "ctx"), "head"),
            P(("groups", "seg", "ctx"), None),
            P(("groups", "seg", "ctx"), None),
            P("groups"),
            P("groups", None),
            P("groups", None),
        ),
        out_specs=P(("groups", "ctx"), "head"),
        check_vma=False,
    )
```

```python
import functools
import math

import jax
import jax.numpy as jnp
import numpy as np
from jax import lax
from jax.experimental import pallas as pl
from jax.experimental.pallas import tpu as pltpu
from jax.sharding import PartitionSpec as P

HEAD_DIM = 128
BLOCK = 64
ROPE_THETA = 500000.0
ROPE_FACTOR = 8.0
LOW_FACTOR = 1.0
HIGH_FACTOR = 4.0
TRAINED_CONTEXT = 8192.0
MASKED_SCORE = -1e30
SCORE_SCALE = HEAD_DIM**-0.5 * math.log2(math.e)
TILE = 128
FINE = 16
DIRECT_SHARDS = (4, 2)
AXES = ("seg", "ctx", "head")


def frequency_row():
    exponent = np.arange(0, HEAD_DIM, 2, dtype=np.float64) / HEAD_DIM
    base = ROPE_THETA**-exponent
    wavelength = 2.0 * np.pi / base
    smooth = (TRAINED_CONTEXT / wavelength - LOW_FACTOR) / (HIGH_FACTOR - LOW_FACTOR)
    blended = (1.0 - smooth) * base / ROPE_FACTOR + smooth * base
    frequencies = np.where(
        wavelength < TRAINED_CONTEXT / HIGH_FACTOR,
        base,
        np.where(wavelength > TRAINED_CONTEXT / LOW_FACTOR, base / ROPE_FACTOR, blended),
    )
    return np.tile(frequencies, 2)[None, :].astype(np.float32)


def turned_sine(sine):
    lane = lax.broadcasted_iota(jnp.int32, sine.shape, 1)
    return jnp.where(lane < HEAD_DIM // 2, -sine, sine)


def rotate(vectors, cosine, signed_sine):
    wide = vectors.astype(jnp.float32)
    return (wide * cosine + pltpu.roll(wide, HEAD_DIM // 2, 1) * signed_sine).astype(jnp.bfloat16)


def angle_sum(cos_a, sin_a, cos_b, sin_b):
    return cos_a * cos_b - sin_a * sin_b, sin_a * cos_b + cos_a * sin_b


def prepare_kernel(
    query_start_of, offsets, vertical, slash, queries, freq, rotated, cos_rows, sin_rows,
    cos_base, sin_base, bias, starts,
):
    shards = cos_base.shape[0]
    rows = cos_rows.shape[0]
    query_rows = queries.shape[0]
    heads = queries.shape[1] // HEAD_DIM
    query_start, first_list = query_start_of()
    frequencies = freq[...]

    fine = lax.broadcasted_iota(jnp.int32, (FINE, HEAD_DIM), 0).astype(jnp.float32) * frequencies
    cos_f, sin_f = jnp.cos(fine), jnp.sin(fine)
    coarse_rows = lax.broadcasted_iota(jnp.int32, (rows // FINE, HEAD_DIM), 0) * FINE
    coarse = coarse_rows.astype(jnp.float32) * frequencies
    cos_c, sin_c = jnp.cos(coarse), jnp.sin(coarse)
    for part in range(rows // FINE):
        cosine, sine = angle_sum(cos_f, sin_f, cos_c[part : part + 1], sin_c[part : part + 1])
        cos_rows[pl.ds(part * FINE, FINE), :] = cosine
        sin_rows[pl.ds(part * FINE, FINE), :] = sine

    for shard in range(shards):
        starts[pl.ds(shard, 1), :] = jnp.full((1, HEAD_DIM), offsets[shard], jnp.int32)
    angle = starts[...].astype(jnp.float32) * frequencies
    cos_base[...] = jnp.cos(angle)
    sin_base[...] = jnp.sin(angle)

    start_angle = query_start.astype(jnp.float32) * frequencies
    cosine, sine = angle_sum(
        cos_rows[...], sin_rows[...], jnp.cos(start_angle), jnp.sin(start_angle)
    )
    sine = turned_sine(sine)
    unit = (
        lax.broadcasted_iota(jnp.int32, (TILE, TILE), 0)
        == lax.broadcasted_iota(jnp.int32, (TILE, TILE), 1)
    ).astype(jnp.bfloat16)
    for head in range(heads):
        turned = rotate(queries[:, pl.ds(head * HEAD_DIM, HEAD_DIM)], cosine, sine)
        for tile in range(query_rows // TILE):
            lines = pl.ds((tile * heads + head) * TILE, TILE)
            rotated[lines, :HEAD_DIM] = turned[tile * TILE : (tile + 1) * TILE]
            rotated[lines, HEAD_DIM:] = unit

    key_block = lax.broadcasted_iota(jnp.int32, bias.shape, 0)
    lane_block = lax.broadcasted_iota(jnp.int32, (1, query_rows), 1) // BLOCK
    hit = jnp.zeros(bias.shape, jnp.bool_)
    for entries, distance in ((vertical, False), (slash, True)):
        for entry in range(entries.shape[1]):
            wanted = jnp.zeros((1, query_rows), jnp.int32)
            for block in range(query_rows // BLOCK):
                value = entries[first_list + block, entry]
                if distance:
                    value = query_start // BLOCK + block - value
                wanted = jnp.where(lane_block == block, value, wanted)
            hit = hit | (key_block == wanted)
    bias[...] = jnp.where(hit, 0.0, MASKED_SCORE)


def attend_kernel(where_am_i, shard_numbers, first, last, *refs):
    offsets, rotated, cos_rows, sin_rows, cos_base, sin_base, bias = refs[:7]
    refs = refs[7:]
    if not first:
        old_peak, old_sums = refs[:2]
        refs = refs[2:]
    if last:
        pieces, out = refs[:-1], refs[-1]
    else:
        pieces, new_peak, new_sums = refs[:-2], refs[-2], refs[-1]
    rows = cos_rows.shape[0]
    query_rows = bias.shape[1]
    tiles = query_rows // TILE
    height = rotated.shape[0] // tiles
    query_start, place = where_am_i()
    ahead = lax.broadcasted_iota(jnp.int32, (rows, query_rows), 1) - lax.broadcasted_iota(
        jnp.int32, (rows, query_rows), 0
    )
    ones = jnp.ones((rows, HEAD_DIM), jnp.bfloat16)

    def load(keys, values, shard):
        cosine, sine = angle_sum(
            cos_rows[...], sin_rows[...], cos_base[pl.ds(shard, 1), :], sin_base[pl.ds(shard, 1), :]
        )
        keys = rotate(keys, cosine, turned_sine(sine))
        offset = offsets[shard]
        lines = [
            jnp.broadcast_to(bias[pl.ds(offset // BLOCK + block, 1), :], (BLOCK, query_rows))
            for block in range(rows // BLOCK)
        ]
        mask = jnp.where(
            ahead >= offset - query_start, jnp.concatenate(lines, axis=0), MASKED_SCORE
        ).astype(jnp.bfloat16)
        return (
            [
                jnp.concatenate([keys, mask[:, tile * TILE : (tile + 1) * TILE]], axis=1)
                for tile in range(tiles)
            ],
            jnp.concatenate([values, ones], axis=1),
        )

    def update(loaded, tile, before):
        query = rotated[pl.ds(tile * height, height), :]
        scores = [
            lax.dot_general(
                query, keys[tile], (((1,), (1,)), ((), ())), preferred_element_type=jnp.float32
            )
            for keys, _ in loaded
        ]
        peak = functools.reduce(jnp.maximum, scores).max(axis=1, keepdims=True)
        if before is not None:
            peak = jnp.maximum(before[0], peak)
        sums = functools.reduce(
            jnp.add,
            [
                jnp.dot(
                    jnp.exp2((score - peak) * SCORE_SCALE).astype(jnp.bfloat16),
                    values,
                    preferred_element_type=jnp.float32,
                )
                for score, (_, values) in zip(scores, loaded)
            ],
        )
        if before is not None:
            sums = sums + before[1] * jnp.exp2((before[0] - peak) * SCORE_SCALE)
        return peak, sums

    def finish(tile, peak, sums):
        if not last:
            span = pl.ds(tile * height, height)
            new_peak[span, :] = jnp.broadcast_to(peak, (height, HEAD_DIM))
            new_sums[span, :] = sums
            return
        for head in range(height // TILE):
            part = sums[head * TILE : (head + 1) * TILE]
            out[pl.ds(tile * TILE, TILE), pl.ds(head * HEAD_DIM, HEAD_DIM)] = (
                part[:, :HEAD_DIM] / part[:, HEAD_DIM:]
            ).astype(out.dtype)

    if shard_numbers is not None:
        loaded = [
            load(piece[:rows, :], piece[rows:, :], shard)
            for piece, shard in zip(pieces, shard_numbers(*place))
        ]
        for tile in range(tiles):
            before = None
            if not first:
                span = pl.ds(tile * height, height)
                before = (old_peak[span, :1], old_sums[span, :])
            finish(tile, *update(loaded, tile, before))
    else:
        (whole,) = pieces
        for tile in range(tiles):

            def step(shard, before, tile=tile):
                start = pl.multiple_of(shard * (2 * rows), 2 * rows)
                piece = load(whole[pl.ds(start, rows), :], whole[pl.ds(start + rows, rows), :], shard)
                return update([piece], tile, before)

            initial = (
                jnp.full((height, 1), MASKED_SCORE, jnp.float32),
                jnp.zeros((height, 2 * HEAD_DIM), jnp.float32),
            )
            finish(tile, *lax.fori_loop(0, whole.shape[0] // (2 * rows), step, initial))


def local(queries, cached_keys, cached_values, key_offsets, vertical_blocks, slash_offsets):
    query_rows = queries.shape[0]
    heads = queries.shape[1] // HEAD_DIM
    rows = cached_keys.shape[0]
    n_seg, n_ctx = lax.axis_size("seg"), lax.axis_size("ctx")
    shards = n_seg * n_ctx
    prefix = rows * shards - query_rows * n_ctx

    def query_start_of():
        ctx = lax.axis_index("ctx")
        return prefix + ctx * query_rows, ctx * (query_rows // BLOCK)

    def where_am_i():
        seg, ctx, head = (lax.axis_index(axis) for axis in AXES)
        return prefix + ctx * query_rows, (seg, ctx, head)

    def exchange(a, partner):
        pairs = []
        for seg in range(n_seg):
            for ctx in range(n_ctx):
                for head in range(2):
                    to_seg, to_ctx, to_head = partner(seg, ctx, head)
                    pairs.append(
                        ((seg * n_ctx + ctx) * 2 + head, (to_seg * n_ctx + to_ctx) * 2 + to_head)
                    )
        return lax.ppermute(a, AXES, pairs)

    def swap(a):
        return exchange(a, lambda s, c, h: (s, c, 1 - h))

    vmem = pl.BlockSpec(memory_space=pltpu.VMEM)
    smem = pl.BlockSpec(memory_space=pltpu.SMEM)
    f32 = jnp.float32
    direct = (n_seg, n_ctx) == DIRECT_SHARDS
    limit = (16 if direct else 56) * 1024 * 1024
    shape = jax.ShapeDtypeStruct
    prepared = pl.pallas_call(
        functools.partial(prepare_kernel, query_start_of),
        out_shape=(
            shape((query_rows * heads, HEAD_DIM + TILE), jnp.bfloat16),
            shape((rows, HEAD_DIM), f32),
            shape((rows, HEAD_DIM), f32),
            shape((shards, HEAD_DIM), f32),
            shape((shards, HEAD_DIM), f32),
            shape((shards * rows // BLOCK, query_rows), f32),
        ),
        in_specs=[smem, smem, smem, vmem, vmem],
        out_specs=[vmem] * 6,
        scratch_shapes=[pltpu.VMEM((shards, HEAD_DIM), jnp.int32)],
        compiler_params=pltpu.CompilerParams(vmem_limit_bytes=limit),
        cost_estimate=pl.CostEstimate(flops=10**9, bytes_accessed=10**6, transcendentals=10**5),
        name="prepare",
    )(key_offsets, vertical_blocks, slash_offsets, queries, jnp.asarray(frequency_row()))

    def attend(pieces, shard_numbers, state, last):
        count = len(pieces) if shard_numbers is not None else shards
        products = 2 * query_rows * heads * rows * 2 * HEAD_DIM * count
        state_shape = (
            shape((query_rows * heads, HEAD_DIM), f32),
            shape((query_rows * heads, 2 * HEAD_DIM), f32),
        )
        return pl.pallas_call(
            functools.partial(attend_kernel, where_am_i, shard_numbers, not state, last),
            out_shape=shape(queries.shape, jnp.bfloat16) if last else state_shape,
            in_specs=[smem] + [vmem] * (6 + len(state) + len(pieces)),
            out_specs=vmem if last else (vmem, vmem),
            compiler_params=pltpu.CompilerParams(vmem_limit_bytes=limit),
            cost_estimate=pl.CostEstimate(
                flops=2 * products,
                bytes_accessed=10**6,
                transcendentals=query_rows * heads * rows * count,
            ),
            name="attend",
        )(key_offsets, *prepared, *state, *pieces)

    own = jnp.concatenate([cached_keys, cached_values], axis=0)
    if not direct:
        gathered = lax.all_gather(own, ("seg", "ctx"), axis=0, tiled=True)
        return attend([gathered], None, (), True)

    far = exchange(own, lambda s, c, h: (s ^ (3 - h), c, h))
    near = exchange(own, lambda s, c, h: (s ^ (1 - h), c ^ h, h))
    diagonal = exchange(own, lambda s, c, h: (s ^ 1, c ^ 1, h))
    across = exchange(far, lambda s, c, h: (s, c ^ 1, h))

    def number(seg, ctx):
        return seg * n_ctx + ctx

    state = attend(
        [own, near, swap(near), diagonal],
        lambda s, c, h: [
            number(s, c),
            number(s ^ (1 - h), c ^ h),
            number(s ^ h, c ^ (1 - h)),
            number(s ^ 1, c ^ 1),
        ],
        (),
        False,
    )
    state = attend(
        [far, swap(far)], lambda s, c, h: [number(s ^ (3 - h), c), number(s ^ (2 + h), c)], state, False
    )
    return attend(
        [across, swap(across)],
        lambda s, c, h: [number(s ^ (3 - h), c ^ 1), number(s ^ (2 + h), c ^ 1)],
        state,
        True,
    )


def solution(mesh):
    return jax.shard_map(
        local,
        mesh=mesh,
        in_specs=(
            P(("groups", "ctx"), "head"),
            P(("groups", "seg", "ctx"), None),
            P(("groups", "seg", "ctx"), None),
            P("groups"),
            P("groups", None),
            P("groups", None),
        ),
        out_specs=P(("groups", "ctx"), "head"),
        check_vma=False,
    )
```

```python
import functools
import math

import jax
import jax.numpy as jnp
import numpy as np
from jax import lax
from jax.experimental import pallas as pl
from jax.experimental.pallas import tpu as pltpu
from jax.sharding import PartitionSpec as P

HEAD_DIM = 128
BLOCK = 64
ROPE_THETA = 500000.0
ROPE_FACTOR = 8.0
LOW_FACTOR = 1.0
HIGH_FACTOR = 4.0
TRAINED_CONTEXT = 8192.0
MASKED_SCORE = -1e30
SCORE_SCALE = HEAD_DIM**-0.5 * math.log2(math.e)
TILE = 128
FINE = 16
SUM_ROWS = 16
DIRECT_SHARDS = (4, 2)
AXES = ("seg", "ctx", "head")


def frequency_row():
    exponent = np.arange(0, HEAD_DIM, 2, dtype=np.float64) / HEAD_DIM
    base = ROPE_THETA**-exponent
    wavelength = 2.0 * np.pi / base
    smooth = (TRAINED_CONTEXT / wavelength - LOW_FACTOR) / (HIGH_FACTOR - LOW_FACTOR)
    blended = (1.0 - smooth) * base / ROPE_FACTOR + smooth * base
    frequencies = np.where(
        wavelength < TRAINED_CONTEXT / HIGH_FACTOR,
        base,
        np.where(wavelength > TRAINED_CONTEXT / LOW_FACTOR, base / ROPE_FACTOR, blended),
    )
    return np.tile(frequencies, 2)[None, :].astype(np.float32)


def turned_sine(sine):
    lane = lax.broadcasted_iota(jnp.int32, sine.shape, 1)
    return jnp.where(lane < HEAD_DIM // 2, -sine, sine)


def rotate(vectors, cosine, signed_sine):
    wide = vectors.astype(jnp.float32)
    return (wide * cosine + pltpu.roll(wide, HEAD_DIM // 2, 1) * signed_sine).astype(jnp.bfloat16)


def angle_sum(cos_a, sin_a, cos_b, sin_b):
    return cos_a * cos_b - sin_a * sin_b, sin_a * cos_b + cos_a * sin_b


def prepare_kernel(
    query_start_of, offsets, vertical, slash, queries, freq, rotated, cos_rows, sin_rows,
    cos_base, sin_base, bias, starts,
):
    shards = cos_base.shape[0]
    rows = cos_rows.shape[0]
    query_rows = queries.shape[0]
    heads = queries.shape[1] // HEAD_DIM
    query_start, first_list = query_start_of()
    frequencies = freq[...]

    fine = lax.broadcasted_iota(jnp.int32, (FINE, HEAD_DIM), 0).astype(jnp.float32) * frequencies
    cos_f, sin_f = jnp.cos(fine), jnp.sin(fine)
    coarse_rows = lax.broadcasted_iota(jnp.int32, (rows // FINE, HEAD_DIM), 0) * FINE
    coarse = coarse_rows.astype(jnp.float32) * frequencies
    cos_c, sin_c = jnp.cos(coarse), jnp.sin(coarse)
    for part in range(rows // FINE):
        cosine, sine = angle_sum(cos_f, sin_f, cos_c[part : part + 1], sin_c[part : part + 1])
        cos_rows[pl.ds(part * FINE, FINE), :] = cosine
        sin_rows[pl.ds(part * FINE, FINE), :] = sine

    for shard in range(shards):
        starts[pl.ds(shard, 1), :] = jnp.full((1, HEAD_DIM), offsets[shard], jnp.int32)
    angle = starts[...].astype(jnp.float32) * frequencies
    cos_base[...] = jnp.cos(angle)
    sin_base[...] = jnp.sin(angle)

    start_angle = query_start.astype(jnp.float32) * frequencies
    cosine, sine = angle_sum(
        cos_rows[...], sin_rows[...], jnp.cos(start_angle), jnp.sin(start_angle)
    )
    sine = turned_sine(sine)
    unit = (
        lax.broadcasted_iota(jnp.int32, (TILE, TILE), 0)
        == lax.broadcasted_iota(jnp.int32, (TILE, TILE), 1)
    ).astype(jnp.bfloat16)
    for head in range(heads):
        turned = rotate(queries[:, pl.ds(head * HEAD_DIM, HEAD_DIM)], cosine, sine).T
        for tile in range(query_rows // TILE):
            lines = pl.ds((tile * heads + head) * TILE, TILE)
            rotated[:HEAD_DIM, lines] = turned[:, tile * TILE : (tile + 1) * TILE]
            rotated[HEAD_DIM:, lines] = unit

    key_block = lax.broadcasted_iota(jnp.int32, bias.shape, 0)
    lane_block = lax.broadcasted_iota(jnp.int32, (1, query_rows), 1) // BLOCK
    hit = jnp.zeros(bias.shape, jnp.bool_)
    for entries, distance in ((vertical, False), (slash, True)):
        for entry in range(entries.shape[1]):
            wanted = jnp.zeros((1, query_rows), jnp.int32)
            for block in range(query_rows // BLOCK):
                value = entries[first_list + block, entry]
                if distance:
                    value = query_start // BLOCK + block - value
                wanted = jnp.where(lane_block == block, value, wanted)
            hit = hit | (key_block == wanted)
    bias[...] = jnp.where(hit, 0.0, MASKED_SCORE)


def attend_kernel(where_am_i, shard_numbers, first, last, *refs):
    offsets, rotated, cos_rows, sin_rows, cos_base, sin_base, bias = refs[:7]
    refs = refs[7:]
    if not first:
        old_peak, old_sums = refs[:2]
        refs = refs[2:]
    if last:
        pieces, out = refs[:-1], refs[-1]
    else:
        pieces, new_peak, new_sums = refs[:-2], refs[-2], refs[-1]
    rows = cos_rows.shape[0]
    query_rows = bias.shape[1]
    tiles = query_rows // TILE
    width = rotated.shape[1] // tiles
    query_start, place = where_am_i()
    ahead = lax.broadcasted_iota(jnp.int32, (rows, query_rows), 1) - lax.broadcasted_iota(
        jnp.int32, (rows, query_rows), 0
    )
    ones = jnp.ones((SUM_ROWS, rows), jnp.bfloat16)

    def load(keys, values, shard):
        cosine, sine = angle_sum(
            cos_rows[...], sin_rows[...], cos_base[pl.ds(shard, 1), :], sin_base[pl.ds(shard, 1), :]
        )
        keys = rotate(keys, cosine, turned_sine(sine))
        offset = offsets[shard]
        lines = [
            jnp.broadcast_to(bias[pl.ds(offset // BLOCK + block, 1), :], (BLOCK, query_rows))
            for block in range(rows // BLOCK)
        ]
        mask = jnp.where(
            ahead >= offset - query_start, jnp.concatenate(lines, axis=0), MASKED_SCORE
        ).astype(jnp.bfloat16)
        return keys, mask, jnp.concatenate([values.T, ones], axis=0)

    def update(loaded, tile, before):
        query = rotated[:, pl.ds(tile * width, width)]
        scores = [
            jnp.dot(
                jnp.concatenate([keys, mask[:, tile * TILE : (tile + 1) * TILE]], axis=1),
                query,
                preferred_element_type=jnp.float32,
            )
            for keys, mask, _ in loaded
        ]
        peak = functools.reduce(jnp.maximum, [score.max(axis=0, keepdims=True) for score in scores])
        if before is not None:
            peak = jnp.maximum(before[0], peak)
        sums = functools.reduce(
            jnp.add,
            [
                jnp.dot(
                    values,
                    jnp.exp2((score - peak) * SCORE_SCALE).astype(jnp.bfloat16),
                    preferred_element_type=jnp.float32,
                )
                for score, (_, _, values) in zip(scores, loaded)
            ],
        )
        if before is not None:
            sums = sums + before[1] * jnp.exp2((before[0] - peak) * SCORE_SCALE)
        return peak, sums

    def finish(tile, peak, sums):
        if not last:
            span = pl.ds(tile * width, width)
            new_peak[:, span] = jnp.broadcast_to(peak, (new_peak.shape[0], width))
            new_sums[:, span] = sums
            return
        part = sums[:HEAD_DIM] / sums[HEAD_DIM : HEAD_DIM + 1]
        for head in range(width // TILE):
            out[pl.ds(tile * TILE, TILE), pl.ds(head * HEAD_DIM, HEAD_DIM)] = part[
                :, head * TILE : (head + 1) * TILE
            ].T.astype(out.dtype)

    if shard_numbers is not None:
        loaded = [
            load(piece[:rows, :], piece[rows:, :], shard)
            for piece, shard in zip(pieces, shard_numbers(*place))
        ]
        for tile in range(tiles):
            before = None
            if not first:
                span = pl.ds(tile * width, width)
                before = (old_peak[:1, span], old_sums[:, span])
            finish(tile, *update(loaded, tile, before))
    else:
        (whole,) = pieces
        for tile in range(tiles):

            def step(shard, before, tile=tile):
                start = pl.multiple_of(shard * (2 * rows), 2 * rows)
                piece = load(whole[pl.ds(start, rows), :], whole[pl.ds(start + rows, rows), :], shard)
                return update([piece], tile, before)

            initial = (
                jnp.full((1, width), MASKED_SCORE, jnp.float32),
                jnp.zeros((HEAD_DIM + SUM_ROWS, width), jnp.float32),
            )
            finish(tile, *lax.fori_loop(0, whole.shape[0] // (2 * rows), step, initial))


def local(queries, cached_keys, cached_values, key_offsets, vertical_blocks, slash_offsets):
    query_rows = queries.shape[0]
    heads = queries.shape[1] // HEAD_DIM
    rows = cached_keys.shape[0]
    n_seg, n_ctx = lax.axis_size("seg"), lax.axis_size("ctx")
    shards = n_seg * n_ctx
    prefix = rows * shards - query_rows * n_ctx

    def query_start_of():
        ctx = lax.axis_index("ctx")
        return prefix + ctx * query_rows, ctx * (query_rows // BLOCK)

    def where_am_i():
        seg, ctx, head = (lax.axis_index(axis) for axis in AXES)
        return prefix + ctx * query_rows, (seg, ctx, head)

    def exchange(a, partner):
        pairs = []
        for seg in range(n_seg):
            for ctx in range(n_ctx):
                for head in range(2):
                    to_seg, to_ctx, to_head = partner(seg, ctx, head)
                    pairs.append(
                        ((seg * n_ctx + ctx) * 2 + head, (to_seg * n_ctx + to_ctx) * 2 + to_head)
                    )
        return lax.ppermute(a, AXES, pairs)

    def swap(a):
        return exchange(a, lambda s, c, h: (s, c, 1 - h))

    vmem = pl.BlockSpec(memory_space=pltpu.VMEM)
    smem = pl.BlockSpec(memory_space=pltpu.SMEM)
    f32 = jnp.float32
    direct = (n_seg, n_ctx) == DIRECT_SHARDS
    limit = (16 if direct else 56) * 1024 * 1024
    shape = jax.ShapeDtypeStruct
    prepared = pl.pallas_call(
        functools.partial(prepare_kernel, query_start_of),
        out_shape=(
            shape((HEAD_DIM + TILE, query_rows * heads), jnp.bfloat16),
            shape((rows, HEAD_DIM), f32),
            shape((rows, HEAD_DIM), f32),
            shape((shards, HEAD_DIM), f32),
            shape((shards, HEAD_DIM), f32),
            shape((shards * rows // BLOCK, query_rows), f32),
        ),
        in_specs=[smem, smem, smem, vmem, vmem],
        out_specs=[vmem] * 6,
        scratch_shapes=[pltpu.VMEM((shards, HEAD_DIM), jnp.int32)],
        compiler_params=pltpu.CompilerParams(vmem_limit_bytes=limit),
        cost_estimate=pl.CostEstimate(flops=4 * 10**9, bytes_accessed=10**6, transcendentals=10**5),
        name="prepare",
    )(key_offsets, vertical_blocks, slash_offsets, queries, jnp.asarray(frequency_row()))

    def attend(prepared, pieces, shard_numbers, state, last):
        count = len(pieces) if shard_numbers is not None else shards
        products = 2 * query_rows * heads * rows * 2 * HEAD_DIM * count
        state_shape = (
            shape((8, query_rows * heads), f32),
            shape((HEAD_DIM + SUM_ROWS, query_rows * heads), f32),
        )
        return pl.pallas_call(
            functools.partial(attend_kernel, where_am_i, shard_numbers, not state, last),
            out_shape=shape(queries.shape, jnp.bfloat16) if last else state_shape,
            in_specs=[smem] + [vmem] * (6 + len(state) + len(pieces)),
            out_specs=vmem if last else (vmem, vmem),
            compiler_params=pltpu.CompilerParams(vmem_limit_bytes=limit),
            cost_estimate=pl.CostEstimate(
                flops=4 * products,
                bytes_accessed=10**6,
                transcendentals=query_rows * heads * rows * count,
            ),
            name="attend",
        )(key_offsets, *prepared, *state, *pieces)

    own = jnp.concatenate([cached_keys, cached_values], axis=0)
    if not direct:
        gathered = lax.all_gather(own, ("seg", "ctx"), axis=0, tiled=True)
        return attend(prepared, [gathered], None, (), True)

    far = exchange(own, lambda s, c, h: (s ^ (3 - h), c, h))
    near = exchange(own, lambda s, c, h: (s ^ (1 - h), c ^ h, h))
    diagonal = exchange(own, lambda s, c, h: (s ^ 1, c ^ 1, h))
    near_swapped = swap(near)
    far, near_swapped, prepared = lax.optimization_barrier((far, near_swapped, prepared))
    across = exchange(far, lambda s, c, h: (s, c ^ 1, h))

    def number(seg, ctx):
        return seg * n_ctx + ctx

    state = attend(
        prepared,
        [own, near, near_swapped, diagonal, far, swap(far)],
        lambda s, c, h: [
            number(s, c),
            number(s ^ (1 - h), c ^ h),
            number(s ^ h, c ^ (1 - h)),
            number(s ^ 1, c ^ 1),
            number(s ^ (3 - h), c),
            number(s ^ (2 + h), c),
        ],
        (),
        False,
    )
    across, state = lax.optimization_barrier((across, state))
    return attend(
        prepared,
        [across, swap(across)],
        lambda s, c, h: [number(s ^ (3 - h), c ^ 1), number(s ^ (2 + h), c ^ 1)],
        state,
        True,
    )


def solution(mesh):
    return jax.shard_map(
        local,
        mesh=mesh,
        in_specs=(
            P(("groups", "ctx"), "head"),
            P(("groups", "seg", "ctx"), None),
            P(("groups", "seg", "ctx"), None),
            P("groups"),
            P("groups", None),
            P("groups", None),
        ),
        out_specs=P(("groups", "ctx"), "head"),
        check_vma=False,
    )
```

```python
import functools
import math

import jax
import jax.numpy as jnp
import numpy as np
from jax import lax
from jax.experimental import pallas as pl
from jax.experimental.pallas import tpu as pltpu
from jax.sharding import PartitionSpec as P

HEAD_DIM = 128
BLOCK = 64
ROPE_THETA = 500000.0
ROPE_FACTOR = 8.0
LOW_FACTOR = 1.0
HIGH_FACTOR = 4.0
TRAINED_CONTEXT = 8192.0
MASKED_SCORE = -1e30
SCORE_SCALE = HEAD_DIM**-0.5 * math.log2(math.e)
TILE = 128
FINE = 16
SUM_ROWS = 16
DIRECT_SHARDS = (4, 2)
AXES = ("seg", "ctx", "head")


def frequency_row():
    exponent = np.arange(0, HEAD_DIM, 2, dtype=np.float64) / HEAD_DIM
    base = ROPE_THETA**-exponent
    wavelength = 2.0 * np.pi / base
    smooth = (TRAINED_CONTEXT / wavelength - LOW_FACTOR) / (HIGH_FACTOR - LOW_FACTOR)
    blended = (1.0 - smooth) * base / ROPE_FACTOR + smooth * base
    frequencies = np.where(
        wavelength < TRAINED_CONTEXT / HIGH_FACTOR,
        base,
        np.where(wavelength > TRAINED_CONTEXT / LOW_FACTOR, base / ROPE_FACTOR, blended),
    )
    return np.tile(frequencies, 2)[None, :].astype(np.float32)


def turned_sine(sine):
    lane = lax.broadcasted_iota(jnp.int32, sine.shape, 1)
    return jnp.where(lane < HEAD_DIM // 2, -sine, sine)


def rotate(vectors, cosine, signed_sine):
    wide = vectors.astype(jnp.float32)
    return (wide * cosine + pltpu.roll(wide, HEAD_DIM // 2, 1) * signed_sine).astype(jnp.bfloat16)


def angle_sum(cos_a, sin_a, cos_b, sin_b):
    return cos_a * cos_b - sin_a * sin_b, sin_a * cos_b + cos_a * sin_b


def shard_tables(cosines, sines, line, rows):
    cos_f, sin_f = cosines[pl.ds(0, FINE), :], turned_sine(sines[pl.ds(0, FINE), :])
    cos_c, sin_c = angle_sum(
        cosines[pl.ds(FINE, FINE), :],
        sines[pl.ds(FINE, FINE), :],
        cosines[pl.ds(line, 1), :],
        sines[pl.ds(line, 1), :],
    )
    signed = turned_sine(sin_c)
    parts = [
        (
            cos_f * cos_c[i : i + 1] - sin_f * signed[i : i + 1],
            sin_f * cos_c[i : i + 1] + cos_f * signed[i : i + 1],
        )
        for i in range(rows // FINE)
    ]
    return tuple(jnp.concatenate(table, axis=0) for table in zip(*parts))


def prepare_kernel(
    query_start_of, offsets, vertical, slash, queries, freq, rotated, cosines, sines, bias,
    angles, held, arrival,
):
    query_rows, columns = held.shape
    heads = columns // HEAD_DIM
    fetch = pltpu.make_async_copy(queries, held, arrival)
    fetch.start()
    query_start, first_list = query_start_of()

    step = lax.broadcasted_iota(jnp.int32, (FINE, HEAD_DIM), 0)
    angles[pl.ds(0, FINE), :] = step
    angles[pl.ds(FINE, FINE), :] = step * FINE
    for shard in range(offsets.shape[0]):
        angles[pl.ds(2 * FINE + shard, 1), :] = jnp.full((1, HEAD_DIM), offsets[shard], jnp.int32)
    angles[pl.ds(angles.shape[0] - 8, 8), :] = jnp.full((8, HEAD_DIM), query_start, jnp.int32)
    angle = angles[...].astype(jnp.float32) * freq[...]
    cosines[...] = jnp.cos(angle)
    sines[...] = jnp.sin(angle)

    key_block = lax.broadcasted_iota(jnp.int32, bias.shape, 0)
    lane_block = lax.broadcasted_iota(jnp.int32, (1, query_rows), 1) // BLOCK
    hit = jnp.zeros(bias.shape, jnp.bool_)
    for entries, distance in ((vertical, False), (slash, True)):
        for entry in range(entries.shape[1]):
            wanted = jnp.zeros((1, query_rows), jnp.int32)
            for block in range(query_rows // BLOCK):
                value = entries[first_list + block, entry]
                if distance:
                    value = query_start // BLOCK + block - value
                wanted = jnp.where(lane_block == block, value, wanted)
            hit = hit | (key_block == wanted)
    bias[...] = jnp.where(hit, 0.0, MASKED_SCORE)

    cosine, sine = shard_tables(cosines, sines, angles.shape[0] - 8, query_rows)
    fetch.wait()
    for head in range(heads):
        turned = rotate(held[:, pl.ds(head * HEAD_DIM, HEAD_DIM)], cosine, sine).T
        for tile in range(query_rows // TILE):
            lines = pl.ds((tile * heads + head) * TILE, TILE)
            rotated[:, lines] = turned[:, tile * TILE : (tile + 1) * TILE]


def attend_kernel(where_am_i, shard_numbers, first, last, *refs):
    offsets, rotated, cosines, sines, bias = refs[:5]
    refs = refs[5:]
    if not first:
        old_peak, old_sums = refs[:2]
        refs = refs[2:]
    if last:
        pieces, out = refs[:-1], refs[-1]
    else:
        pieces, new_peak, new_sums = refs[:-2], refs[-2], refs[-1]
    query_rows = bias.shape[1]
    rows = bias.shape[0] * BLOCK // offsets.shape[0]
    tiles = query_rows // TILE
    width = rotated.shape[1] // tiles
    query_start, place = where_am_i()
    ahead = lax.broadcasted_iota(jnp.int32, (rows, query_rows), 1) - lax.broadcasted_iota(
        jnp.int32, (rows, query_rows), 0
    )
    ones = jnp.ones((SUM_ROWS, rows), jnp.bfloat16)
    unit = (
        lax.broadcasted_iota(jnp.int32, (TILE, width), 0)
        == lax.broadcasted_iota(jnp.int32, (TILE, width), 1) % TILE
    ).astype(jnp.bfloat16)

    def load(keys, values, shard):
        keys = rotate(keys, *shard_tables(cosines, sines, 2 * FINE + shard, rows))
        offset = offsets[shard]
        lines = [
            jnp.broadcast_to(bias[pl.ds(offset // BLOCK + block, 1), :], (BLOCK, query_rows))
            for block in range(rows // BLOCK)
        ]
        mask = jnp.where(
            ahead >= offset - query_start, jnp.concatenate(lines, axis=0), MASKED_SCORE
        ).astype(jnp.bfloat16)
        return keys, mask, jnp.concatenate([values.T, ones], axis=0)

    def update(loaded, tile, before):
        query = jnp.concatenate([rotated[:, pl.ds(tile * width, width)], unit], axis=0)
        scores = [
            jnp.dot(
                jnp.concatenate([keys, mask[:, tile * TILE : (tile + 1) * TILE]], axis=1),
                query,
                preferred_element_type=jnp.float32,
            )
            for keys, mask, _ in loaded
        ]
        peak = functools.reduce(jnp.maximum, [score.max(axis=0, keepdims=True) for score in scores])
        if before is not None:
            peak = jnp.maximum(before[0], peak)
        sums = functools.reduce(
            jnp.add,
            [
                jnp.dot(
                    values,
                    jnp.exp2((score - peak) * SCORE_SCALE).astype(jnp.bfloat16),
                    preferred_element_type=jnp.float32,
                )
                for score, (_, _, values) in zip(scores, loaded)
            ],
        )
        if before is not None:
            sums = sums + before[1] * jnp.exp2((before[0] - peak) * SCORE_SCALE)
        return peak, sums

    def finish(tile, peak, sums):
        if not last:
            span = pl.ds(tile * width, width)
            new_peak[:, span] = jnp.broadcast_to(peak, (new_peak.shape[0], width))
            new_sums[:, span] = sums
            return
        part = sums[:HEAD_DIM] * (1.0 / sums[HEAD_DIM : HEAD_DIM + 1])
        for head in range(width // TILE):
            out[pl.ds(tile * TILE, TILE), pl.ds(head * HEAD_DIM, HEAD_DIM)] = part[
                :, head * TILE : (head + 1) * TILE
            ].T.astype(out.dtype)

    if shard_numbers is not None:
        loaded = [
            load(piece[:rows, :], piece[rows:, :], shard)
            for piece, shard in zip(pieces, shard_numbers(*place))
        ]
        for tile in range(tiles):
            before = None
            if not first:
                span = pl.ds(tile * width, width)
                before = (old_peak[:1, span], old_sums[:, span])
            finish(tile, *update(loaded, tile, before))
    else:
        (whole,) = pieces
        for tile in range(tiles):

            def step(shard, before, tile=tile):
                start = pl.multiple_of(shard * (2 * rows), 2 * rows)
                piece = load(whole[pl.ds(start, rows), :], whole[pl.ds(start + rows, rows), :], shard)
                return update([piece], tile, before)

            initial = (
                jnp.full((1, width), MASKED_SCORE, jnp.float32),
                jnp.zeros((HEAD_DIM + SUM_ROWS, width), jnp.float32),
            )
            finish(tile, *lax.fori_loop(0, whole.shape[0] // (2 * rows), step, initial))


def local(queries, cached_keys, cached_values, key_offsets, vertical_blocks, slash_offsets):
    query_rows = queries.shape[0]
    heads = queries.shape[1] // HEAD_DIM
    rows = cached_keys.shape[0]
    n_seg, n_ctx = lax.axis_size("seg"), lax.axis_size("ctx")
    shards = n_seg * n_ctx
    prefix = rows * shards - query_rows * n_ctx

    def query_start_of():
        ctx = lax.axis_index("ctx")
        return prefix + ctx * query_rows, ctx * (query_rows // BLOCK)

    def where_am_i():
        seg, ctx, head = (lax.axis_index(axis) for axis in AXES)
        return prefix + ctx * query_rows, (seg, ctx, head)

    def exchange(a, partner):
        pairs = []
        for seg in range(n_seg):
            for ctx in range(n_ctx):
                for head in range(2):
                    to_seg, to_ctx, to_head = partner(seg, ctx, head)
                    pairs.append(
                        ((seg * n_ctx + ctx) * 2 + head, (to_seg * n_ctx + to_ctx) * 2 + to_head)
                    )
        return lax.ppermute(a, AXES, pairs)

    def swap(a):
        return exchange(a, lambda s, c, h: (s, c, 1 - h))

    vmem = pl.BlockSpec(memory_space=pltpu.VMEM)
    smem = pl.BlockSpec(memory_space=pltpu.SMEM)
    f32 = jnp.float32
    direct = (n_seg, n_ctx) == DIRECT_SHARDS
    limit = (16 if direct else 56) * 1024 * 1024
    shape = jax.ShapeDtypeStruct
    lines = 2 * FINE + shards + 8
    prepared = pl.pallas_call(
        functools.partial(prepare_kernel, query_start_of),
        out_shape=(
            shape((HEAD_DIM, query_rows * heads), jnp.bfloat16),
            shape((lines, HEAD_DIM), f32),
            shape((lines, HEAD_DIM), f32),
            shape((shards * rows // BLOCK, query_rows), f32),
        ),
        in_specs=[smem, smem, smem, pl.BlockSpec(memory_space=pltpu.HBM), vmem],
        out_specs=[vmem] * 4,
        scratch_shapes=[
            pltpu.VMEM((lines, HEAD_DIM), jnp.int32),
            pltpu.VMEM(queries.shape, queries.dtype),
            pltpu.SemaphoreType.DMA(()),
        ],
        compiler_params=pltpu.CompilerParams(vmem_limit_bytes=limit),
        cost_estimate=pl.CostEstimate(flops=4 * 10**9, bytes_accessed=10**6, transcendentals=10**5),
        name="prepare",
    )(key_offsets, vertical_blocks, slash_offsets, queries, jnp.asarray(frequency_row()))

    def attend(prepared, pieces, shard_numbers, state, last):
        count = len(pieces) if shard_numbers is not None else shards
        products = 2 * query_rows * heads * rows * 2 * HEAD_DIM * count
        state_shape = (
            shape((8, query_rows * heads), f32),
            shape((HEAD_DIM + SUM_ROWS, query_rows * heads), f32),
        )
        return pl.pallas_call(
            functools.partial(attend_kernel, where_am_i, shard_numbers, not state, last),
            out_shape=shape(queries.shape, jnp.bfloat16) if last else state_shape,
            in_specs=[smem] + [vmem] * (4 + len(state) + len(pieces)),
            out_specs=vmem if last else (vmem, vmem),
            compiler_params=pltpu.CompilerParams(vmem_limit_bytes=limit),
            cost_estimate=pl.CostEstimate(
                flops=4 * products,
                bytes_accessed=10**6,
                transcendentals=query_rows * heads * rows * count,
            ),
            name="attend",
        )(key_offsets, *prepared, *state, *pieces)

    own = jnp.concatenate([cached_keys, cached_values], axis=0)
    if not direct:
        gathered = lax.all_gather(own, ("seg", "ctx"), axis=0, tiled=True)
        return attend(prepared, [gathered], None, (), True)

    far = exchange(own, lambda s, c, h: (s ^ (3 - h), c, h))
    near = exchange(own, lambda s, c, h: (s ^ (1 - h), c ^ h, h))
    near, prepared = lax.optimization_barrier((near, prepared))
    near_swapped = swap(near)
    diagonal = exchange(near, lambda s, c, h: (s ^ h, c ^ (1 - h), h))
    far, near_swapped = lax.optimization_barrier((far, near_swapped))
    across = exchange(far, lambda s, c, h: (s, c ^ 1, h))

    def number(seg, ctx):
        return seg * n_ctx + ctx

    state = attend(
        prepared,
        [own, near, near_swapped, diagonal, far, swap(far)],
        lambda s, c, h: [
            number(s, c),
            number(s ^ (1 - h), c ^ h),
            number(s ^ h, c ^ (1 - h)),
            number(s ^ 1, c ^ 1),
            number(s ^ (3 - h), c),
            number(s ^ (2 + h), c),
        ],
        (),
        False,
    )
    across, state = lax.optimization_barrier((across, state))
    return attend(
        prepared,
        [across, swap(across)],
        lambda s, c, h: [number(s ^ (3 - h), c ^ 1), number(s ^ (2 + h), c ^ 1)],
        state,
        True,
    )


def solution(mesh):
    return jax.shard_map(
        local,
        mesh=mesh,
        in_specs=(
            P(("groups", "ctx"), "head"),
            P(("groups", "seg", "ctx"), None),
            P(("groups", "seg", "ctx"), None),
            P("groups"),
            P("groups", None),
            P("groups", None),
        ),
        out_specs=P(("groups", "ctx"), "head"),
        check_vma=False,
    )
```

```python
import functools
import math

import jax
import jax.numpy as jnp
import numpy as np
from jax import lax
from jax.experimental import pallas as pl
from jax.experimental.pallas import tpu as pltpu
from jax.sharding import PartitionSpec as P

HEAD_DIM = 128
BLOCK = 64
ROPE_THETA = 500000.0
ROPE_FACTOR = 8.0
LOW_FACTOR = 1.0
HIGH_FACTOR = 4.0
TRAINED_CONTEXT = 8192.0
MASKED_SCORE = -1e30
SCORE_SCALE = HEAD_DIM**-0.5 * math.log2(math.e)
TILE = 128
FINE = 16
SUM_ROWS = 16
DIRECT_SHARDS = (4, 2)
AXES = ("seg", "ctx", "head")


def frequency_row():
    exponent = np.arange(0, HEAD_DIM, 2, dtype=np.float64) / HEAD_DIM
    base = ROPE_THETA**-exponent
    wavelength = 2.0 * np.pi / base
    smooth = (TRAINED_CONTEXT / wavelength - LOW_FACTOR) / (HIGH_FACTOR - LOW_FACTOR)
    blended = (1.0 - smooth) * base / ROPE_FACTOR + smooth * base
    frequencies = np.where(
        wavelength < TRAINED_CONTEXT / HIGH_FACTOR,
        base,
        np.where(wavelength > TRAINED_CONTEXT / LOW_FACTOR, base / ROPE_FACTOR, blended),
    )
    return np.tile(frequencies, 2)[None, :].astype(np.float32)


def turned_sine(sine):
    lane = lax.broadcasted_iota(jnp.int32, sine.shape, 1)
    return jnp.where(lane < HEAD_DIM // 2, -sine, sine)


def rotate(vectors, cosine, signed_sine):
    wide = vectors.astype(jnp.float32)
    return (wide * cosine + pltpu.roll(wide, HEAD_DIM // 2, 1) * signed_sine).astype(jnp.bfloat16)


def angle_sum(cos_a, sin_a, cos_b, sin_b):
    return cos_a * cos_b - sin_a * sin_b, sin_a * cos_b + cos_a * sin_b


def shard_tables(cosines, sines, line, rows):
    cos_f, sin_f = cosines[pl.ds(0, FINE), :], turned_sine(sines[pl.ds(0, FINE), :])
    cos_c, sin_c = angle_sum(
        cosines[pl.ds(FINE, FINE), :],
        sines[pl.ds(FINE, FINE), :],
        cosines[pl.ds(line, 1), :],
        sines[pl.ds(line, 1), :],
    )
    signed = turned_sine(sin_c)
    parts = [
        (
            cos_f * cos_c[i : i + 1] - sin_f * signed[i : i + 1],
            sin_f * cos_c[i : i + 1] + cos_f * signed[i : i + 1],
        )
        for i in range(rows // FINE)
    ]
    return tuple(jnp.concatenate(table, axis=0) for table in zip(*parts))


def prepare_kernel(
    query_start_of, offsets, vertical, slash, queries, freq, rotated, cosines, sines, masks,
    angles, bias, held, arrival,
):
    query_rows, columns = held.shape
    heads = columns // HEAD_DIM
    fetch = pltpu.make_async_copy(queries, held, arrival)
    fetch.start()
    query_start, first_list = query_start_of()

    step = lax.broadcasted_iota(jnp.int32, (FINE, HEAD_DIM), 0)
    angles[pl.ds(0, FINE), :] = step
    angles[pl.ds(FINE, FINE), :] = step * FINE
    for shard in range(offsets.shape[0]):
        angles[pl.ds(2 * FINE + shard, 1), :] = jnp.full((1, HEAD_DIM), offsets[shard], jnp.int32)
    angles[pl.ds(angles.shape[0] - 8, 8), :] = jnp.full((8, HEAD_DIM), query_start, jnp.int32)
    angle = angles[...].astype(jnp.float32) * freq[...]
    cosines[...] = jnp.cos(angle)
    sines[...] = jnp.sin(angle)

    key_block = lax.broadcasted_iota(jnp.int32, bias.shape, 0)
    lane_block = lax.broadcasted_iota(jnp.int32, (1, query_rows), 1) // BLOCK
    hit = jnp.zeros(bias.shape, jnp.bool_)
    for entries, distance in ((vertical, False), (slash, True)):
        for entry in range(entries.shape[1]):
            wanted = jnp.zeros((1, query_rows), jnp.int32)
            for block in range(query_rows // BLOCK):
                value = entries[first_list + block, entry]
                if distance:
                    value = query_start // BLOCK + block - value
                wanted = jnp.where(lane_block == block, value, wanted)
            hit = hit | (key_block == wanted)
    bias[...] = jnp.where(hit, 0.0, MASKED_SCORE)

    rows = masks.shape[0] // offsets.shape[0]
    ahead = lax.broadcasted_iota(jnp.int32, (rows, query_rows), 1) - lax.broadcasted_iota(
        jnp.int32, (rows, query_rows), 0
    )

    @pl.loop(0, offsets.shape[0])
    def _(shard):
        offset = offsets[shard]
        lines = [
            jnp.broadcast_to(bias[pl.ds(offset // BLOCK + block, 1), :], (BLOCK, query_rows))
            for block in range(rows // BLOCK)
        ]
        masks[pl.ds(pl.multiple_of(shard * rows, rows), rows), :] = jnp.where(
            ahead >= offset - query_start, jnp.concatenate(lines, axis=0), MASKED_SCORE
        ).astype(masks.dtype)

    cosine, sine = shard_tables(cosines, sines, angles.shape[0] - 8, query_rows)
    fetch.wait()
    for head in range(heads):
        turned = rotate(held[:, pl.ds(head * HEAD_DIM, HEAD_DIM)], cosine, sine).T
        for tile in range(query_rows // TILE):
            lines = pl.ds((tile * heads + head) * TILE, TILE)
            rotated[:, lines] = turned[:, tile * TILE : (tile + 1) * TILE]


def attend_kernel(place_of, shards_of, first, last, *refs):
    rotated, cosines, sines, masks = refs[:4]
    refs = refs[4:]
    if not first:
        old_peak, old_sums = refs[:2]
        refs = refs[2:]
    if last:
        pieces, out = refs[:-1], refs[-1]
    else:
        pieces, new_peak, new_sums = refs[:-2], refs[-2], refs[-1]
    query_rows = masks.shape[1]
    tiles = query_rows // TILE
    width = rotated.shape[1] // tiles
    rows = masks.shape[0] // (cosines.shape[0] - 2 * FINE - 8)
    ones = jnp.ones((SUM_ROWS, rows), jnp.bfloat16)
    unit = (
        lax.broadcasted_iota(jnp.int32, (TILE, width), 0)
        == lax.broadcasted_iota(jnp.int32, (TILE, width), 1) % TILE
    ).astype(jnp.bfloat16)

    def load(keys, values, shard):
        keys = rotate(keys, *shard_tables(cosines, sines, 2 * FINE + shard, rows))
        mask = masks[pl.ds(pl.multiple_of(shard * rows, rows), rows), :]
        return keys, mask, jnp.concatenate([values.T, ones], axis=0)

    def update(loaded, tile, before):
        query = jnp.concatenate([rotated[:, pl.ds(tile * width, width)], unit], axis=0)
        scores = [
            jnp.dot(
                jnp.concatenate([keys, mask[:, tile * TILE : (tile + 1) * TILE]], axis=1),
                query,
                preferred_element_type=jnp.float32,
            )
            for keys, mask, _ in loaded
        ]
        peak = functools.reduce(jnp.maximum, [score.max(axis=0, keepdims=True) for score in scores])
        if before is not None:
            peak = jnp.maximum(before[0], peak)
        sums = functools.reduce(
            jnp.add,
            [
                jnp.dot(
                    values,
                    jnp.exp2((score - peak) * SCORE_SCALE).astype(jnp.bfloat16),
                    preferred_element_type=jnp.float32,
                )
                for score, (_, _, values) in zip(scores, loaded)
            ],
        )
        if before is not None:
            sums = sums + before[1] * jnp.exp2((before[0] - peak) * SCORE_SCALE)
        return peak, sums

    def finish(tile, peak, sums):
        if not last:
            span = pl.ds(tile * width, width)
            new_peak[:, span] = jnp.broadcast_to(peak, (new_peak.shape[0], width))
            new_sums[:, span] = sums
            return
        part = sums[:HEAD_DIM] * (1.0 / sums[HEAD_DIM : HEAD_DIM + 1])
        for head in range(width // TILE):
            out[pl.ds(tile * TILE, TILE), pl.ds(head * HEAD_DIM, HEAD_DIM)] = part[
                :, head * TILE : (head + 1) * TILE
            ].T.astype(out.dtype)

    if shards_of is not None:
        loaded = [
            load(keys, values, shard) for keys, values, shard in shards_of(pieces, *place_of())
        ]
        for tile in range(tiles):
            before = None
            if not first:
                span = pl.ds(tile * width, width)
                before = (old_peak[:1, span], old_sums[:, span])
            finish(tile, *update(loaded, tile, before))
    else:
        (whole,) = pieces
        for tile in range(tiles):

            def step(shard, before, tile=tile):
                start = pl.multiple_of(shard * (2 * rows), 2 * rows)
                piece = load(whole[pl.ds(start, rows), :], whole[pl.ds(start + rows, rows), :], shard)
                return update([piece], tile, before)

            initial = (
                jnp.full((1, width), MASKED_SCORE, jnp.float32),
                jnp.zeros((HEAD_DIM + SUM_ROWS, width), jnp.float32),
            )
            finish(tile, *lax.fori_loop(0, whole.shape[0] // (2 * rows), step, initial))


def local(queries, cached_keys, cached_values, key_offsets, vertical_blocks, slash_offsets):
    query_rows = queries.shape[0]
    heads = queries.shape[1] // HEAD_DIM
    rows = cached_keys.shape[0]
    n_seg, n_ctx = lax.axis_size("seg"), lax.axis_size("ctx")
    shards = n_seg * n_ctx
    prefix = rows * shards - query_rows * n_ctx

    def query_start_of():
        ctx = lax.axis_index("ctx")
        return prefix + ctx * query_rows, ctx * (query_rows // BLOCK)

    def place_of():
        return tuple(lax.axis_index(axis) for axis in AXES)

    def exchange(a, partner):
        pairs = []
        for seg in range(n_seg):
            for ctx in range(n_ctx):
                for head in range(2):
                    to_seg, to_ctx, to_head = partner(seg, ctx, head)
                    pairs.append(
                        ((seg * n_ctx + ctx) * 2 + head, (to_seg * n_ctx + to_ctx) * 2 + to_head)
                    )
        return lax.ppermute(a, AXES, pairs)

    def swap(a):
        return exchange(a, lambda s, c, h: (s, c, 1 - h))

    vmem = pl.BlockSpec(memory_space=pltpu.VMEM)
    smem = pl.BlockSpec(memory_space=pltpu.SMEM)
    f32 = jnp.float32
    direct = (n_seg, n_ctx) == DIRECT_SHARDS
    limit = (16 if direct else 56) * 1024 * 1024
    shape = jax.ShapeDtypeStruct
    lines = 2 * FINE + shards + 8
    prepared = pl.pallas_call(
        functools.partial(prepare_kernel, query_start_of),
        out_shape=(
            shape((HEAD_DIM, query_rows * heads), jnp.bfloat16),
            shape((lines, HEAD_DIM), f32),
            shape((lines, HEAD_DIM), f32),
            shape((shards * rows, query_rows), jnp.bfloat16),
        ),
        in_specs=[smem, smem, smem, pl.BlockSpec(memory_space=pltpu.HBM), vmem],
        out_specs=[vmem] * 4,
        scratch_shapes=[
            pltpu.VMEM((lines, HEAD_DIM), jnp.int32),
            pltpu.VMEM((shards * rows // BLOCK, query_rows), f32),
            pltpu.VMEM(queries.shape, queries.dtype),
            pltpu.SemaphoreType.DMA(()),
        ],
        compiler_params=pltpu.CompilerParams(vmem_limit_bytes=limit),
        cost_estimate=pl.CostEstimate(flops=4 * 10**9, bytes_accessed=10**6, transcendentals=10**5),
        name="prepare",
    )(key_offsets, vertical_blocks, slash_offsets, queries, jnp.asarray(frequency_row()))

    def attend(prepared, pieces, shards_of, state, last):
        count = len(pieces) if shards_of is not None else shards
        products = 2 * query_rows * heads * rows * 2 * HEAD_DIM * count
        state_shape = (
            shape((8, query_rows * heads), f32),
            shape((HEAD_DIM + SUM_ROWS, query_rows * heads), f32),
        )
        return pl.pallas_call(
            functools.partial(attend_kernel, place_of, shards_of, not state, last),
            out_shape=shape(queries.shape, queries.dtype) if last else state_shape,
            in_specs=[vmem] * (4 + len(state) + len(pieces)),
            out_specs=vmem if last else (vmem, vmem),
            compiler_params=pltpu.CompilerParams(vmem_limit_bytes=limit),
            cost_estimate=pl.CostEstimate(
                flops=4 * products,
                bytes_accessed=10**6,
                transcendentals=query_rows * heads * rows * count,
            ),
            name="attend",
        )(*prepared, *state, *pieces)

    own = jnp.concatenate([cached_keys, cached_values], axis=0)
    if not direct:
        gathered = lax.all_gather(own, ("seg", "ctx"), axis=0, tiled=True)
        return attend(prepared, [gathered], None, (), True)

    near = exchange(own, lambda s, c, h: (s ^ (1 - h), c ^ h, h))
    far = exchange(own, lambda s, c, h: (s ^ (3 - h), c, h))
    half = lax.dynamic_slice_in_dim(own, lax.axis_index("head") * rows, rows, 0)
    diagonal = exchange(half, lambda s, c, h: (s ^ 1, c ^ 1, h))
    near, diagonal, prepared = lax.optimization_barrier((near, diagonal, prepared))
    across = exchange(far, lambda s, c, h: (s, c ^ 1, h))
    beside = swap(jnp.concatenate([near, diagonal], axis=0))

    def number(seg, ctx):
        return seg * n_ctx + ctx

    def whole(ref):
        return ref[:rows, :], ref[rows : 2 * rows, :]

    def nearer(pieces, s, c, h):
        own, near, diagonal, beside, far, far_beside = pieces
        mine, other = diagonal[...], beside[2 * rows :, :]
        keys_mine = h == 0
        return [
            (*whole(own), number(s, c)),
            (*whole(near), number(s ^ (1 - h), c ^ h)),
            (*whole(beside), number(s ^ h, c ^ (1 - h))),
            (
                jnp.where(keys_mine, mine, other),
                jnp.where(keys_mine, other, mine),
                number(s ^ 1, c ^ 1),
            ),
            (*whole(far), number(s ^ (3 - h), c)),
            (*whole(far_beside), number(s ^ (2 + h), c)),
        ]

    def last_two(pieces, s, c, h):
        across, across_beside = pieces
        return [
            (*whole(across), number(s ^ (3 - h), c ^ 1)),
            (*whole(across_beside), number(s ^ (2 + h), c ^ 1)),
        ]

    state = attend(prepared, [own, near, diagonal, beside, far, swap(far)], nearer, (), False)
    across, state = lax.optimization_barrier((across, state))
    return attend(prepared, [across, swap(across)], last_two, state, True)


def solution(mesh):
    return jax.shard_map(
        local,
        mesh=mesh,
        in_specs=(
            P(("groups", "ctx"), "head"),
            P(("groups", "seg", "ctx"), None),
            P(("groups", "seg", "ctx"), None),
            P("groups"),
            P("groups", None),
            P("groups", None),
        ),
        out_specs=P(("groups", "ctx"), "head"),
        check_vma=False,
    )
```

```python
import functools
import math

import jax
import jax.numpy as jnp
import numpy as np
from jax import lax
from jax.experimental import pallas as pl
from jax.experimental.pallas import tpu as pltpu
from jax.sharding import PartitionSpec as P

HEAD_DIM = 128
BLOCK = 64
ROPE_THETA = 500000.0
ROPE_FACTOR = 8.0
LOW_FACTOR = 1.0
HIGH_FACTOR = 4.0
TRAINED_CONTEXT = 8192.0
MASKED_SCORE = -1e30
SCORE_SCALE = HEAD_DIM**-0.5 * math.log2(math.e)
TILE = 128
FINE = 16
SUM_ROWS = 16
DIRECT_SHARDS = (4, 2)
AXES = ("seg", "ctx", "head")


def frequency_row():
    exponent = np.arange(0, HEAD_DIM, 2, dtype=np.float64) / HEAD_DIM
    base = ROPE_THETA**-exponent
    wavelength = 2.0 * np.pi / base
    smooth = (TRAINED_CONTEXT / wavelength - LOW_FACTOR) / (HIGH_FACTOR - LOW_FACTOR)
    blended = (1.0 - smooth) * base / ROPE_FACTOR + smooth * base
    frequencies = np.where(
        wavelength < TRAINED_CONTEXT / HIGH_FACTOR,
        base,
        np.where(wavelength > TRAINED_CONTEXT / LOW_FACTOR, base / ROPE_FACTOR, blended),
    )
    return np.tile(frequencies, 2)[None, :].astype(np.float32)


def turned_sine(sine):
    lane = lax.broadcasted_iota(jnp.int32, sine.shape, 1)
    return jnp.where(lane < HEAD_DIM // 2, -sine, sine)


def rotate(vectors, cosine, signed_sine):
    wide = vectors.astype(jnp.float32)
    return (wide * cosine + pltpu.roll(wide, HEAD_DIM // 2, 1) * signed_sine).astype(jnp.bfloat16)


def angle_sum(cos_a, sin_a, cos_b, sin_b):
    return cos_a * cos_b - sin_a * sin_b, sin_a * cos_b + cos_a * sin_b


def shard_tables(cosines, sines, line, rows):
    cos_f, sin_f = cosines[pl.ds(0, FINE), :], turned_sine(sines[pl.ds(0, FINE), :])
    cos_c, sin_c = angle_sum(
        cosines[pl.ds(FINE, FINE), :],
        sines[pl.ds(FINE, FINE), :],
        cosines[pl.ds(line, 1), :],
        sines[pl.ds(line, 1), :],
    )
    signed = turned_sine(sin_c)
    parts = [
        (
            cos_f * cos_c[i : i + 1] - sin_f * signed[i : i + 1],
            sin_f * cos_c[i : i + 1] + cos_f * signed[i : i + 1],
        )
        for i in range(rows // FINE)
    ]
    return tuple(jnp.concatenate(table, axis=0) for table in zip(*parts))


def prepare_kernel(
    query_start_of, offsets, vertical, slash, queries, freq, rotated, cosines, sines, masks,
    angles, bias, held, arrival,
):
    query_rows, columns = held.shape
    heads = columns // HEAD_DIM
    fetch = pltpu.make_async_copy(queries, held, arrival)
    fetch.start()
    query_start, first_list = query_start_of()

    step = lax.broadcasted_iota(jnp.int32, (FINE, HEAD_DIM), 0)
    angles[pl.ds(0, FINE), :] = step
    angles[pl.ds(FINE, FINE), :] = step * FINE
    for shard in range(offsets.shape[0]):
        angles[pl.ds(2 * FINE + shard, 1), :] = jnp.full((1, HEAD_DIM), offsets[shard], jnp.int32)
    angles[pl.ds(angles.shape[0] - 8, 8), :] = jnp.full((8, HEAD_DIM), query_start, jnp.int32)
    angle = angles[...].astype(jnp.float32) * freq[...]
    cosines[...] = jnp.cos(angle)
    sines[...] = jnp.sin(angle)

    key_block = lax.broadcasted_iota(jnp.int32, bias.shape, 0)
    lane_block = lax.broadcasted_iota(jnp.int32, (1, query_rows), 1) // BLOCK
    hit = jnp.zeros(bias.shape, jnp.bool_)
    for entries, distance in ((vertical, False), (slash, True)):
        for entry in range(entries.shape[1]):
            wanted = jnp.zeros((1, query_rows), jnp.int32)
            for block in range(query_rows // BLOCK):
                value = entries[first_list + block, entry]
                if distance:
                    value = query_start // BLOCK + block - value
                wanted = jnp.where(lane_block == block, value, wanted)
            hit = hit | (key_block == wanted)
    bias[...] = jnp.where(hit, 0.0, MASKED_SCORE)

    rows = masks.shape[0] // offsets.shape[0]
    ahead = lax.broadcasted_iota(jnp.int32, (rows, query_rows), 1) - lax.broadcasted_iota(
        jnp.int32, (rows, query_rows), 0
    )

    @pl.loop(0, offsets.shape[0])
    def _(shard):
        offset = offsets[shard]
        lines = [
            jnp.broadcast_to(bias[pl.ds(offset // BLOCK + block, 1), :], (BLOCK, query_rows))
            for block in range(rows // BLOCK)
        ]
        masks[pl.ds(pl.multiple_of(shard * rows, rows), rows), :] = jnp.where(
            ahead >= offset - query_start, jnp.concatenate(lines, axis=0), MASKED_SCORE
        ).astype(masks.dtype)

    cosine, sine = shard_tables(cosines, sines, angles.shape[0] - 8, query_rows)
    fetch.wait()
    for head in range(heads):
        turned = rotate(held[:, pl.ds(head * HEAD_DIM, HEAD_DIM)], cosine, sine).T
        for tile in range(query_rows // TILE):
            lines = pl.ds((tile * heads + head) * TILE, TILE)
            rotated[:, lines] = turned[:, tile * TILE : (tile + 1) * TILE]


def attend_kernel(place_of, shards_of, first, last, *refs):
    rotated, cosines, sines, masks = refs[:4]
    refs = refs[4:]
    if not first:
        old_peak, old_sums = refs[:2]
        refs = refs[2:]
    if last:
        pieces, out = refs[:-1], refs[-1]
    else:
        pieces, new_peak, new_sums = refs[:-2], refs[-2], refs[-1]
    query_rows = masks.shape[1]
    tiles = query_rows // TILE
    width = rotated.shape[1] // tiles
    rows = masks.shape[0] // (cosines.shape[0] - 2 * FINE - 8)
    ones = jnp.ones((SUM_ROWS, rows), jnp.bfloat16)
    unit = (
        lax.broadcasted_iota(jnp.int32, (TILE, width), 0)
        == lax.broadcasted_iota(jnp.int32, (TILE, width), 1) % TILE
    ).astype(jnp.bfloat16)

    def load(keys, values, shard):
        keys = rotate(keys, *shard_tables(cosines, sines, 2 * FINE + shard, rows))
        mask = masks[pl.ds(pl.multiple_of(shard * rows, rows), rows), :]
        return keys, mask, jnp.concatenate([values.T, ones], axis=0)

    def update(loaded, tile, before):
        query = jnp.concatenate([rotated[:, pl.ds(tile * width, width)], unit], axis=0)
        scores = [
            jnp.dot(
                jnp.concatenate([keys, mask[:, tile * TILE : (tile + 1) * TILE]], axis=1),
                query,
                preferred_element_type=jnp.float32,
            )
            for keys, mask, _ in loaded
        ]
        peak = functools.reduce(jnp.maximum, [score.max(axis=0, keepdims=True) for score in scores])
        if before is not None:
            peak = jnp.maximum(before[0], peak)
        sums = functools.reduce(
            jnp.add,
            [
                jnp.dot(
                    values,
                    jnp.exp2((score - peak) * SCORE_SCALE).astype(jnp.bfloat16),
                    preferred_element_type=jnp.float32,
                )
                for score, (_, _, values) in zip(scores, loaded)
            ],
        )
        if before is not None:
            sums = sums + before[1] * jnp.exp2((before[0] - peak) * SCORE_SCALE)
        return peak, sums

    def finish(tile, peak, sums):
        if not last:
            span = pl.ds(tile * width, width)
            new_peak[:, span] = jnp.broadcast_to(peak, (new_peak.shape[0], width))
            new_sums[:, span] = sums
            return
        part = sums[:HEAD_DIM] * (1.0 / sums[HEAD_DIM : HEAD_DIM + 1])
        for head in range(width // TILE):
            out[pl.ds(tile * TILE, TILE), pl.ds(head * HEAD_DIM, HEAD_DIM)] = part[
                :, head * TILE : (head + 1) * TILE
            ].T.astype(out.dtype)

    if shards_of is not None:
        loaded = [
            load(keys, values, shard) for keys, values, shard in shards_of(pieces, *place_of())
        ]
        for tile in range(tiles):
            before = None
            if not first:
                span = pl.ds(tile * width, width)
                before = (old_peak[:1, span], old_sums[:, span])
            finish(tile, *update(loaded, tile, before))
    else:
        (whole,) = pieces
        for tile in range(tiles):

            def step(shard, before, tile=tile):
                start = pl.multiple_of(shard * (2 * rows), 2 * rows)
                piece = load(whole[pl.ds(start, rows), :], whole[pl.ds(start + rows, rows), :], shard)
                return update([piece], tile, before)

            initial = (
                jnp.full((1, width), MASKED_SCORE, jnp.float32),
                jnp.zeros((HEAD_DIM + SUM_ROWS, width), jnp.float32),
            )
            finish(tile, *lax.fori_loop(0, whole.shape[0] // (2 * rows), step, initial))


def local(queries, cached_keys, cached_values, key_offsets, vertical_blocks, slash_offsets):
    query_rows = queries.shape[0]
    heads = queries.shape[1] // HEAD_DIM
    rows = cached_keys.shape[0]
    n_seg, n_ctx = lax.axis_size("seg"), lax.axis_size("ctx")
    shards = n_seg * n_ctx
    prefix = rows * shards - query_rows * n_ctx

    def query_start_of():
        ctx = lax.axis_index("ctx")
        return prefix + ctx * query_rows, ctx * (query_rows // BLOCK)

    def place_of():
        return tuple(lax.axis_index(axis) for axis in AXES)

    def exchange(a, partner):
        pairs = []
        for seg in range(n_seg):
            for ctx in range(n_ctx):
                for head in range(2):
                    to_seg, to_ctx, to_head = partner(seg, ctx, head)
                    pairs.append(
                        ((seg * n_ctx + ctx) * 2 + head, (to_seg * n_ctx + to_ctx) * 2 + to_head)
                    )
        return lax.ppermute(a, AXES, pairs)

    def swap(a):
        return exchange(a, lambda s, c, h: (s, c, 1 - h))

    vmem = pl.BlockSpec(memory_space=pltpu.VMEM)
    smem = pl.BlockSpec(memory_space=pltpu.SMEM)
    f32 = jnp.float32
    direct = (n_seg, n_ctx) == DIRECT_SHARDS
    limit = (16 if direct else 56) * 1024 * 1024
    shape = jax.ShapeDtypeStruct
    lines = 2 * FINE + shards + 8
    prepared = pl.pallas_call(
        functools.partial(prepare_kernel, query_start_of),
        out_shape=(
            shape((HEAD_DIM, query_rows * heads), jnp.bfloat16),
            shape((lines, HEAD_DIM), f32),
            shape((lines, HEAD_DIM), f32),
            shape((shards * rows, query_rows), jnp.bfloat16),
        ),
        in_specs=[smem, smem, smem, pl.BlockSpec(memory_space=pltpu.HBM), vmem],
        out_specs=[vmem] * 4,
        scratch_shapes=[
            pltpu.VMEM((lines, HEAD_DIM), jnp.int32),
            pltpu.VMEM((shards * rows // BLOCK, query_rows), f32),
            pltpu.VMEM(queries.shape, queries.dtype),
            pltpu.SemaphoreType.DMA(()),
        ],
        compiler_params=pltpu.CompilerParams(vmem_limit_bytes=limit),
        cost_estimate=pl.CostEstimate(flops=4 * 10**9, bytes_accessed=10**6, transcendentals=10**5),
        name="prepare",
    )(key_offsets, vertical_blocks, slash_offsets, queries, jnp.asarray(frequency_row()))

    def attend(prepared, pieces, shards_of, state, last):
        count = len(pieces) if shards_of is not None else shards
        products = 2 * query_rows * heads * rows * 2 * HEAD_DIM * count
        state_shape = (
            shape((8, query_rows * heads), f32),
            shape((HEAD_DIM + SUM_ROWS, query_rows * heads), f32),
        )
        return pl.pallas_call(
            functools.partial(attend_kernel, place_of, shards_of, not state, last),
            out_shape=shape(queries.shape, queries.dtype) if last else state_shape,
            in_specs=[vmem] * (4 + len(state) + len(pieces)),
            out_specs=vmem if last else (vmem, vmem),
            compiler_params=pltpu.CompilerParams(vmem_limit_bytes=limit),
            cost_estimate=pl.CostEstimate(
                flops=4 * products,
                bytes_accessed=10**6,
                transcendentals=query_rows * heads * rows * count,
            ),
            name="attend",
        )(*prepared, *state, *pieces)

    own = jnp.concatenate([cached_keys, cached_values], axis=0)
    if not direct:
        gathered = lax.all_gather(own, ("seg", "ctx"), axis=0, tiled=True)
        return attend(prepared, [gathered], None, (), True)

    half = lax.dynamic_slice_in_dim(own, lax.axis_index("head") * rows, rows, 0)
    middle = exchange(half, lambda s, c, h: (s ^ 2, c, h))
    near = exchange(own, lambda s, c, h: (s ^ (1 - h), c ^ h, h))
    diagonal = exchange(half, lambda s, c, h: (s ^ 1, c ^ 1, h))
    middle, prepared = lax.optimization_barrier((middle, prepared))
    later = [
        exchange(middle, lambda s, c, h: (s ^ 1, c, h)),
        exchange(middle, lambda s, c, h: (s, c ^ 1, h)),
        exchange(middle, lambda s, c, h: (s ^ 1, c ^ 1, h)),
    ]
    beside = swap(jnp.concatenate([near, diagonal, middle], axis=0))

    def number(seg, ctx):
        return seg * n_ctx + ctx

    def whole(ref):
        return ref[:rows, :], ref[rows : 2 * rows, :]

    def halves(mine, other, index, head):
        mine, other = mine[...], other[pl.ds(index * rows, rows), :]
        return jnp.where(head == 0, mine, other), jnp.where(head == 0, other, mine)

    def nearer(pieces, s, c, h):
        own, near, diagonal, middle, beside = pieces
        return [
            (*whole(own), number(s, c)),
            (*whole(near), number(s ^ (1 - h), c ^ h)),
            (*whole(beside), number(s ^ h, c ^ (1 - h))),
            (*halves(diagonal, beside, 2, h), number(s ^ 1, c ^ 1)),
            (*halves(middle, beside, 3, h), number(s ^ 2, c)),
        ]

    def farther(pieces, s, c, h):
        along, across, corner, beside = pieces
        return [
            (*halves(along, beside, 0, h), number(s ^ 3, c)),
            (*halves(across, beside, 1, h), number(s ^ 2, c ^ 1)),
            (*halves(corner, beside, 2, h), number(s ^ 3, c ^ 1)),
        ]

    state = attend(prepared, [own, near, diagonal, middle, beside], nearer, (), False)
    later, state = lax.optimization_barrier((later, state))
    beside = swap(jnp.concatenate(later, axis=0))
    return attend(prepared, [*later, beside], farther, state, True)


def solution(mesh):
    return jax.shard_map(
        local,
        mesh=mesh,
        in_specs=(
            P(("groups", "ctx"), "head"),
            P(("groups", "seg", "ctx"), None),
            P(("groups", "seg", "ctx"), None),
            P("groups"),
            P("groups", None),
            P("groups", None),
        ),
        out_specs=P(("groups", "ctx"), "head"),
        check_vma=False,
    )
```

```python
import functools
import math

import jax
import jax.numpy as jnp
import numpy as np
from jax import lax
from jax.experimental import pallas as pl
from jax.experimental.pallas import tpu as pltpu
from jax.sharding import PartitionSpec as P

HEAD_DIM = 128
BLOCK = 64
ROPE_THETA = 500000.0
ROPE_FACTOR = 8.0
LOW_FACTOR = 1.0
HIGH_FACTOR = 4.0
TRAINED_CONTEXT = 8192.0
MASKED_SCORE = -1e30
SCORE_SCALE = HEAD_DIM**-0.5 * math.log2(math.e)
TILE = 128
FINE = 16
SUM_ROWS = 16
DIRECT_SHARDS = (4, 2)
AXES = ("seg", "ctx", "head")


def frequency_row():
    exponent = np.arange(0, HEAD_DIM, 2, dtype=np.float64) / HEAD_DIM
    base = ROPE_THETA**-exponent
    wavelength = 2.0 * np.pi / base
    smooth = (TRAINED_CONTEXT / wavelength - LOW_FACTOR) / (HIGH_FACTOR - LOW_FACTOR)
    blended = (1.0 - smooth) * base / ROPE_FACTOR + smooth * base
    frequencies = np.where(
        wavelength < TRAINED_CONTEXT / HIGH_FACTOR,
        base,
        np.where(wavelength > TRAINED_CONTEXT / LOW_FACTOR, base / ROPE_FACTOR, blended),
    )
    return np.tile(frequencies, 2)[None, :].astype(np.float32)


def turned_sine(sine):
    lane = lax.broadcasted_iota(jnp.int32, sine.shape, 1)
    return jnp.where(lane < HEAD_DIM // 2, -sine, sine)


def rotate(vectors, cosine, signed_sine):
    wide = vectors.astype(jnp.float32)
    return (wide * cosine + pltpu.roll(wide, HEAD_DIM // 2, 1) * signed_sine).astype(jnp.bfloat16)


def angle_sum(cos_a, sin_a, cos_b, sin_b):
    return cos_a * cos_b - sin_a * sin_b, sin_a * cos_b + cos_a * sin_b


def shard_tables(cosines, sines, line, rows):
    cos_f, sin_f = cosines[pl.ds(0, FINE), :], turned_sine(sines[pl.ds(0, FINE), :])
    cos_c, sin_c = angle_sum(
        cosines[pl.ds(FINE, FINE), :],
        sines[pl.ds(FINE, FINE), :],
        cosines[pl.ds(line, 1), :],
        sines[pl.ds(line, 1), :],
    )
    signed = turned_sine(sin_c)
    parts = [
        (
            cos_f * cos_c[i : i + 1] - sin_f * signed[i : i + 1],
            sin_f * cos_c[i : i + 1] + cos_f * signed[i : i + 1],
        )
        for i in range(rows // FINE)
    ]
    return tuple(jnp.concatenate(table, axis=0) for table in zip(*parts))


def prepare_kernel(
    query_start_of, offsets, vertical, slash, queries, freq, rotated, cosines, sines, masks,
    angles, bias, held, arrival,
):
    query_rows, columns = held.shape
    heads = columns // HEAD_DIM
    fetch = pltpu.make_async_copy(queries, held, arrival)
    fetch.start()
    query_start, first_list = query_start_of()

    step = lax.broadcasted_iota(jnp.int32, (FINE, HEAD_DIM), 0)
    angles[pl.ds(0, FINE), :] = step
    angles[pl.ds(FINE, FINE), :] = step * FINE
    for shard in range(offsets.shape[0]):
        angles[pl.ds(2 * FINE + shard, 1), :] = jnp.full((1, HEAD_DIM), offsets[shard], jnp.int32)
    angles[pl.ds(angles.shape[0] - 8, 8), :] = jnp.full((8, HEAD_DIM), query_start, jnp.int32)
    angle = angles[...].astype(jnp.float32) * freq[...]
    cosines[...] = jnp.cos(angle)
    sines[...] = jnp.sin(angle)

    key_block = lax.broadcasted_iota(jnp.int32, bias.shape, 0)
    lane_block = lax.broadcasted_iota(jnp.int32, (1, query_rows), 1) // BLOCK
    hit = jnp.zeros(bias.shape, jnp.bool_)
    for entries, distance in ((vertical, False), (slash, True)):
        for entry in range(entries.shape[1]):
            wanted = jnp.zeros((1, query_rows), jnp.int32)
            for block in range(query_rows // BLOCK):
                value = entries[first_list + block, entry]
                if distance:
                    value = query_start // BLOCK + block - value
                wanted = jnp.where(lane_block == block, value, wanted)
            hit = hit | (key_block == wanted)
    bias[...] = jnp.where(hit, 0.0, MASKED_SCORE)

    rows = masks.shape[0] // offsets.shape[0]
    ahead = lax.broadcasted_iota(jnp.int32, (rows, query_rows), 1) - lax.broadcasted_iota(
        jnp.int32, (rows, query_rows), 0
    )

    @pl.loop(0, offsets.shape[0])
    def _(shard):
        offset = offsets[shard]
        lines = [
            jnp.broadcast_to(bias[pl.ds(offset // BLOCK + block, 1), :], (BLOCK, query_rows))
            for block in range(rows // BLOCK)
        ]
        masks[pl.ds(pl.multiple_of(shard * rows, rows), rows), :] = jnp.where(
            ahead >= offset - query_start, jnp.concatenate(lines, axis=0), MASKED_SCORE
        ).astype(masks.dtype)

    cosine, sine = shard_tables(cosines, sines, angles.shape[0] - 8, query_rows)
    fetch.wait()
    for head in range(heads):
        turned = rotate(held[:, pl.ds(head * HEAD_DIM, HEAD_DIM)], cosine, sine).T
        for tile in range(query_rows // TILE):
            lines = pl.ds((tile * heads + head) * TILE, TILE)
            rotated[:, lines] = turned[:, tile * TILE : (tile + 1) * TILE]


def attend_kernel(place_of, shards_of, first, last, *refs):
    rotated, cosines, sines, masks = refs[:4]
    refs = refs[4:]
    if not first:
        old_peak, old_sums = refs[:2]
        refs = refs[2:]
    if last:
        pieces, out = refs[:-1], refs[-1]
    else:
        pieces, new_peak, new_sums = refs[:-2], refs[-2], refs[-1]
    query_rows = masks.shape[1]
    tiles = query_rows // TILE
    width = rotated.shape[1] // tiles
    rows = masks.shape[0] // (cosines.shape[0] - 2 * FINE - 8)
    ones = jnp.ones((SUM_ROWS, rows), jnp.bfloat16)
    unit = (
        lax.broadcasted_iota(jnp.int32, (TILE, width), 0)
        == lax.broadcasted_iota(jnp.int32, (TILE, width), 1) % TILE
    ).astype(jnp.bfloat16)

    def load(keys, values, shard):
        keys = rotate(keys, *shard_tables(cosines, sines, 2 * FINE + shard, rows))
        mask = masks[pl.ds(pl.multiple_of(shard * rows, rows), rows), :]
        return keys, mask, jnp.concatenate([values.T, ones], axis=0)

    def update(loaded, tile, before):
        query = jnp.concatenate([rotated[:, pl.ds(tile * width, width)], unit], axis=0)
        scores = [
            jnp.dot(
                jnp.concatenate([keys, mask[:, tile * TILE : (tile + 1) * TILE]], axis=1),
                query,
                preferred_element_type=jnp.float32,
            )
            for keys, mask, _ in loaded
        ]
        peak = functools.reduce(jnp.maximum, [score.max(axis=0, keepdims=True) for score in scores])
        if before is not None:
            peak = jnp.maximum(before[0], peak)
        sums = functools.reduce(
            jnp.add,
            [
                jnp.dot(
                    values,
                    jnp.exp2((score - peak) * SCORE_SCALE).astype(jnp.bfloat16),
                    preferred_element_type=jnp.float32,
                )
                for score, (_, _, values) in zip(scores, loaded)
            ],
        )
        if before is not None:
            sums = sums + before[1] * jnp.exp2((before[0] - peak) * SCORE_SCALE)
        return peak, sums

    def finish(tile, peak, sums):
        if not last:
            span = pl.ds(tile * width, width)
            new_peak[:, span] = jnp.broadcast_to(peak, (new_peak.shape[0], width))
            new_sums[:, span] = sums
            return
        part = sums[:HEAD_DIM] * (1.0 / sums[HEAD_DIM : HEAD_DIM + 1])
        for head in range(width // TILE):
            out[pl.ds(tile * TILE, TILE), pl.ds(head * HEAD_DIM, HEAD_DIM)] = part[
                :, head * TILE : (head + 1) * TILE
            ].T.astype(out.dtype)

    if shards_of is not None:
        loaded = [
            load(keys, values, shard) for keys, values, shard in shards_of(pieces, *place_of())
        ]
        for tile in range(tiles):
            before = None
            if not first:
                span = pl.ds(tile * width, width)
                before = (old_peak[:1, span], old_sums[:, span])
            finish(tile, *update(loaded, tile, before))
    else:
        (whole,) = pieces
        for tile in range(tiles):

            def step(shard, before, tile=tile):
                start = pl.multiple_of(shard * (2 * rows), 2 * rows)
                piece = load(whole[pl.ds(start, rows), :], whole[pl.ds(start + rows, rows), :], shard)
                return update([piece], tile, before)

            initial = (
                jnp.full((1, width), MASKED_SCORE, jnp.float32),
                jnp.zeros((HEAD_DIM + SUM_ROWS, width), jnp.float32),
            )
            finish(tile, *lax.fori_loop(0, whole.shape[0] // (2 * rows), step, initial))


def local(queries, cached_keys, cached_values, key_offsets, vertical_blocks, slash_offsets):
    query_rows = queries.shape[0]
    heads = queries.shape[1] // HEAD_DIM
    rows = cached_keys.shape[0]
    n_seg, n_ctx = lax.axis_size("seg"), lax.axis_size("ctx")
    shards = n_seg * n_ctx
    prefix = rows * shards - query_rows * n_ctx

    def query_start_of():
        ctx = lax.axis_index("ctx")
        return prefix + ctx * query_rows, ctx * (query_rows // BLOCK)

    def place_of():
        return tuple(lax.axis_index(axis) for axis in AXES)

    def exchange(a, partner):
        pairs = []
        for seg in range(n_seg):
            for ctx in range(n_ctx):
                for head in range(2):
                    to_seg, to_ctx, to_head = partner(seg, ctx, head)
                    pairs.append(
                        ((seg * n_ctx + ctx) * 2 + head, (to_seg * n_ctx + to_ctx) * 2 + to_head)
                    )
        return lax.ppermute(a, AXES, pairs)

    def swap(a):
        return exchange(a, lambda s, c, h: (s, c, 1 - h))

    vmem = pl.BlockSpec(memory_space=pltpu.VMEM)
    smem = pl.BlockSpec(memory_space=pltpu.SMEM)
    f32 = jnp.float32
    direct = (n_seg, n_ctx) == DIRECT_SHARDS
    limit = (16 if direct else 56) * 1024 * 1024
    shape = jax.ShapeDtypeStruct
    lines = 2 * FINE + shards + 8
    prepared = pl.pallas_call(
        functools.partial(prepare_kernel, query_start_of),
        out_shape=(
            shape((HEAD_DIM, query_rows * heads), jnp.bfloat16),
            shape((lines, HEAD_DIM), f32),
            shape((lines, HEAD_DIM), f32),
            shape((shards * rows, query_rows), jnp.bfloat16),
        ),
        in_specs=[smem, smem, smem, pl.BlockSpec(memory_space=pltpu.HBM), vmem],
        out_specs=[vmem] * 4,
        scratch_shapes=[
            pltpu.VMEM((lines, HEAD_DIM), jnp.int32),
            pltpu.VMEM((shards * rows // BLOCK, query_rows), f32),
            pltpu.VMEM(queries.shape, queries.dtype),
            pltpu.SemaphoreType.DMA(()),
        ],
        compiler_params=pltpu.CompilerParams(vmem_limit_bytes=limit),
        cost_estimate=pl.CostEstimate(flops=4 * 10**9, bytes_accessed=10**6, transcendentals=10**5),
        name="prepare",
    )(key_offsets, vertical_blocks, slash_offsets, queries, jnp.asarray(frequency_row()))

    def attend(prepared, pieces, shards_of, state, last):
        count = len(pieces) if shards_of is not None else shards
        products = 2 * query_rows * heads * rows * 2 * HEAD_DIM * count
        state_shape = (
            shape((8, query_rows * heads), f32),
            shape((HEAD_DIM + SUM_ROWS, query_rows * heads), f32),
        )
        return pl.pallas_call(
            functools.partial(attend_kernel, place_of, shards_of, not state, last),
            out_shape=shape(queries.shape, queries.dtype) if last else state_shape,
            in_specs=[vmem] * (4 + len(state) + len(pieces)),
            out_specs=vmem if last else (vmem, vmem),
            compiler_params=pltpu.CompilerParams(vmem_limit_bytes=limit),
            cost_estimate=pl.CostEstimate(
                flops=4 * products,
                bytes_accessed=10**6,
                transcendentals=query_rows * heads * rows * count,
            ),
            name="attend",
        )(*prepared, *state, *pieces)

    own = jnp.concatenate([cached_keys, cached_values], axis=0)
    if not direct:
        gathered = lax.all_gather(own, ("seg", "ctx"), axis=0, tiled=True)
        return attend(prepared, [gathered], None, (), True)

    far = exchange(own, lambda s, c, h: (s ^ (3 - h), c, h))
    near = exchange(own, lambda s, c, h: (s ^ (1 - h), c ^ h, h))
    near, prepared = lax.optimization_barrier((near, prepared))
    across = exchange(far, lambda s, c, h: (s, c ^ 1, h))
    beside = swap(near)
    far_after, beside = lax.optimization_barrier((far, beside))
    far_beside = swap(far_after)
    half = jnp.where(lax.axis_index("head") == 0, beside[:rows], near[rows:])
    diagonal = exchange(half, lambda s, c, h: (s ^ 1, c, h))

    def number(seg, ctx):
        return seg * n_ctx + ctx

    def whole(ref):
        return ref[:rows, :], ref[rows : 2 * rows, :]

    def nearer(pieces, s, c, h):
        own, near, beside, far, far_beside = pieces
        return [
            (*whole(own), number(s, c)),
            (*whole(near), number(s ^ (1 - h), c ^ h)),
            (*whole(beside), number(s ^ h, c ^ (1 - h))),
            (*whole(far), number(s ^ (3 - h), c)),
            (*whole(far_beside), number(s ^ (2 + h), c)),
        ]

    def farther(pieces, s, c, h):
        across, diagonal, beside = pieces
        mine, other = diagonal[...], beside[2 * rows :, :]
        return [
            (*whole(across), number(s ^ (3 - h), c ^ 1)),
            (*whole(beside), number(s ^ (2 + h), c ^ 1)),
            (
                jnp.where(h == 0, mine, other),
                jnp.where(h == 0, other, mine),
                number(s ^ 1, c ^ 1),
            ),
        ]

    state = attend(prepared, [own, near, beside, far, far_beside], nearer, (), False)
    across, diagonal, state = lax.optimization_barrier((across, diagonal, state))
    beside = swap(jnp.concatenate([across, diagonal], axis=0))
    return attend(prepared, [across, diagonal, beside], farther, state, True)


def solution(mesh):
    return jax.shard_map(
        local,
        mesh=mesh,
        in_specs=(
            P(("groups", "ctx"), "head"),
            P(("groups", "seg", "ctx"), None),
            P(("groups", "seg", "ctx"), None),
            P("groups"),
            P("groups", None),
            P("groups", None),
        ),
        out_specs=P(("groups", "ctx"), "head"),
        check_vma=False,
    )
```

```python
import functools
import math

import jax
import jax.numpy as jnp
import numpy as np
from jax import lax
from jax.experimental import pallas as pl
from jax.experimental.pallas import tpu as pltpu
from jax.sharding import PartitionSpec as P

HEAD_DIM = 128
BLOCK = 64
ROPE_THETA = 500000.0
ROPE_FACTOR = 8.0
LOW_FACTOR = 1.0
HIGH_FACTOR = 4.0
TRAINED_CONTEXT = 8192.0
MASKED_SCORE = -1e30
SCORE_SCALE = HEAD_DIM**-0.5 * math.log2(math.e)
TILE = 128
FINE = 16
SUM_ROWS = 16
DIRECT_SHARDS = (4, 2)
AXES = ("seg", "ctx", "head")


def frequency_row():
    exponent = np.arange(0, HEAD_DIM, 2, dtype=np.float64) / HEAD_DIM
    base = ROPE_THETA**-exponent
    wavelength = 2.0 * np.pi / base
    smooth = (TRAINED_CONTEXT / wavelength - LOW_FACTOR) / (HIGH_FACTOR - LOW_FACTOR)
    blended = (1.0 - smooth) * base / ROPE_FACTOR + smooth * base
    frequencies = np.where(
        wavelength < TRAINED_CONTEXT / HIGH_FACTOR,
        base,
        np.where(wavelength > TRAINED_CONTEXT / LOW_FACTOR, base / ROPE_FACTOR, blended),
    )
    return np.tile(frequencies, 2)[None, :].astype(np.float32)


def turned_sine(sine):
    lane = lax.broadcasted_iota(jnp.int32, sine.shape, 1)
    return jnp.where(lane < HEAD_DIM // 2, -sine, sine)


def rotate(vectors, cosine, signed_sine):
    wide = vectors.astype(jnp.float32)
    return (wide * cosine + pltpu.roll(wide, HEAD_DIM // 2, 1) * signed_sine).astype(jnp.bfloat16)


def angle_sum(cos_a, sin_a, cos_b, sin_b):
    return cos_a * cos_b - sin_a * sin_b, sin_a * cos_b + cos_a * sin_b


def shard_tables(cosines, sines, line, rows):
    cos_f, sin_f = cosines[pl.ds(0, FINE), :], turned_sine(sines[pl.ds(0, FINE), :])
    cos_c, sin_c = angle_sum(
        cosines[pl.ds(FINE, FINE), :],
        sines[pl.ds(FINE, FINE), :],
        cosines[pl.ds(line, 1), :],
        sines[pl.ds(line, 1), :],
    )
    signed = turned_sine(sin_c)
    parts = [
        (
            cos_f * cos_c[i : i + 1] - sin_f * signed[i : i + 1],
            sin_f * cos_c[i : i + 1] + cos_f * signed[i : i + 1],
        )
        for i in range(rows // FINE)
    ]
    return tuple(jnp.concatenate(table, axis=0) for table in zip(*parts))


def prepare_kernel(
    query_start_of, offsets, vertical, slash, queries, freq, rotated, cosines, sines, masks,
    angles, bias, held, arrival,
):
    query_rows, columns = held.shape
    heads = columns // HEAD_DIM
    fetch = pltpu.make_async_copy(queries, held, arrival)
    fetch.start()
    query_start, first_list = query_start_of()

    step = lax.broadcasted_iota(jnp.int32, (FINE, HEAD_DIM), 0)
    angles[pl.ds(0, FINE), :] = step
    angles[pl.ds(FINE, FINE), :] = step * FINE
    for shard in range(offsets.shape[0]):
        angles[pl.ds(2 * FINE + shard, 1), :] = jnp.full((1, HEAD_DIM), offsets[shard], jnp.int32)
    angles[pl.ds(angles.shape[0] - 8, 8), :] = jnp.full((8, HEAD_DIM), query_start, jnp.int32)
    angle = angles[...].astype(jnp.float32) * freq[...]
    cosines[...] = jnp.cos(angle)
    sines[...] = jnp.sin(angle)

    key_block = lax.broadcasted_iota(jnp.int32, bias.shape, 0)
    lane_block = lax.broadcasted_iota(jnp.int32, (1, query_rows), 1) // BLOCK
    hit = jnp.zeros(bias.shape, jnp.bool_)
    for entries, distance in ((vertical, False), (slash, True)):
        for entry in range(entries.shape[1]):
            wanted = jnp.zeros((1, query_rows), jnp.int32)
            for block in range(query_rows // BLOCK):
                value = entries[first_list + block, entry]
                if distance:
                    value = query_start // BLOCK + block - value
                wanted = jnp.where(lane_block == block, value, wanted)
            hit = hit | (key_block == wanted)
    bias[...] = jnp.where(hit, 0.0, MASKED_SCORE)

    rows = masks.shape[0] // offsets.shape[0]
    ahead = lax.broadcasted_iota(jnp.int32, (rows, query_rows), 1) - lax.broadcasted_iota(
        jnp.int32, (rows, query_rows), 0
    )

    @pl.loop(0, offsets.shape[0])
    def _(shard):
        offset = offsets[shard]
        lines = [
            jnp.broadcast_to(bias[pl.ds(offset // BLOCK + block, 1), :], (BLOCK, query_rows))
            for block in range(rows // BLOCK)
        ]
        masks[pl.ds(pl.multiple_of(shard * rows, rows), rows), :] = jnp.where(
            ahead >= offset - query_start, jnp.concatenate(lines, axis=0), MASKED_SCORE
        ).astype(masks.dtype)

    cosine, sine = shard_tables(cosines, sines, angles.shape[0] - 8, query_rows)
    fetch.wait()
    for head in range(heads):
        turned = rotate(held[:, pl.ds(head * HEAD_DIM, HEAD_DIM)], cosine, sine).T
        for tile in range(query_rows // TILE):
            lines = pl.ds((tile * heads + head) * TILE, TILE)
            rotated[:, lines] = turned[:, tile * TILE : (tile + 1) * TILE]


def attend_kernel(place_of, shards_of, first, last, *refs):
    rotated, cosines, sines, masks = refs[:4]
    refs = refs[4:]
    if not first:
        old_peak, old_sums = refs[:2]
        refs = refs[2:]
    if last:
        pieces, out = refs[:-1], refs[-1]
    else:
        pieces, new_peak, new_sums = refs[:-2], refs[-2], refs[-1]
    query_rows = masks.shape[1]
    tiles = query_rows // TILE
    width = rotated.shape[1] // tiles
    rows = masks.shape[0] // (cosines.shape[0] - 2 * FINE - 8)
    ones = jnp.ones((SUM_ROWS, rows), jnp.bfloat16)
    unit = (
        lax.broadcasted_iota(jnp.int32, (TILE, width), 0)
        == lax.broadcasted_iota(jnp.int32, (TILE, width), 1) % TILE
    ).astype(jnp.bfloat16)

    def load(keys, values, shard):
        keys = rotate(keys, *shard_tables(cosines, sines, 2 * FINE + shard, rows))
        mask = masks[pl.ds(pl.multiple_of(shard * rows, rows), rows), :]
        return keys, mask, jnp.concatenate([values.T, ones], axis=0)

    def update(loaded, tile, before):
        query = jnp.concatenate([rotated[:, pl.ds(tile * width, width)], unit], axis=0)
        scores = [
            jnp.dot(
                jnp.concatenate([keys, mask[:, tile * TILE : (tile + 1) * TILE]], axis=1),
                query,
                preferred_element_type=jnp.float32,
            )
            for keys, mask, _ in loaded
        ]
        peak = functools.reduce(jnp.maximum, [score.max(axis=0, keepdims=True) for score in scores])
        if before is not None:
            peak = jnp.maximum(before[0], peak)
        sums = functools.reduce(
            jnp.add,
            [
                jnp.dot(
                    values,
                    jnp.exp2((score - peak) * SCORE_SCALE).astype(jnp.bfloat16),
                    preferred_element_type=jnp.float32,
                )
                for score, (_, _, values) in zip(scores, loaded)
            ],
        )
        if before is not None:
            sums = sums + before[1] * jnp.exp2((before[0] - peak) * SCORE_SCALE)
        return peak, sums

    def finish(tile, peak, sums):
        if not last:
            span = pl.ds(tile * width, width)
            new_peak[:, span] = jnp.broadcast_to(peak, (new_peak.shape[0], width))
            new_sums[:, span] = sums
            return
        part = sums[:HEAD_DIM] * (1.0 / sums[HEAD_DIM : HEAD_DIM + 1])
        for head in range(width // TILE):
            out[pl.ds(tile * TILE, TILE), pl.ds(head * HEAD_DIM, HEAD_DIM)] = part[
                :, head * TILE : (head + 1) * TILE
            ].T.astype(out.dtype)

    if shards_of is not None:
        loaded = [
            load(keys, values, shard) for keys, values, shard in shards_of(pieces, *place_of())
        ]
        for tile in range(tiles):
            before = None
            if not first:
                span = pl.ds(tile * width, width)
                before = (old_peak[:1, span], old_sums[:, span])
            finish(tile, *update(loaded, tile, before))
    else:
        (whole,) = pieces
        for tile in range(tiles):

            def step(shard, before, tile=tile):
                start = pl.multiple_of(shard * (2 * rows), 2 * rows)
                piece = load(whole[pl.ds(start, rows), :], whole[pl.ds(start + rows, rows), :], shard)
                return update([piece], tile, before)

            initial = (
                jnp.full((1, width), MASKED_SCORE, jnp.float32),
                jnp.zeros((HEAD_DIM + SUM_ROWS, width), jnp.float32),
            )
            finish(tile, *lax.fori_loop(0, whole.shape[0] // (2 * rows), step, initial))


def local(queries, cached_keys, cached_values, key_offsets, vertical_blocks, slash_offsets):
    query_rows = queries.shape[0]
    heads = queries.shape[1] // HEAD_DIM
    rows = cached_keys.shape[0]
    n_seg, n_ctx = lax.axis_size("seg"), lax.axis_size("ctx")
    shards = n_seg * n_ctx
    prefix = rows * shards - query_rows * n_ctx

    def query_start_of():
        ctx = lax.axis_index("ctx")
        return prefix + ctx * query_rows, ctx * (query_rows // BLOCK)

    def place_of():
        return tuple(lax.axis_index(axis) for axis in AXES)

    def exchange(a, partner):
        pairs = []
        for seg in range(n_seg):
            for ctx in range(n_ctx):
                for head in range(2):
                    to_seg, to_ctx, to_head = partner(seg, ctx, head)
                    pairs.append(
                        ((seg * n_ctx + ctx) * 2 + head, (to_seg * n_ctx + to_ctx) * 2 + to_head)
                    )
        return lax.ppermute(a, AXES, pairs)

    def swap(a):
        return exchange(a, lambda s, c, h: (s, c, 1 - h))

    vmem = pl.BlockSpec(memory_space=pltpu.VMEM)
    smem = pl.BlockSpec(memory_space=pltpu.SMEM)
    f32 = jnp.float32
    direct = (n_seg, n_ctx) == DIRECT_SHARDS
    limit = (16 if direct else 56) * 1024 * 1024
    shape = jax.ShapeDtypeStruct
    lines = 2 * FINE + shards + 8
    prepared = pl.pallas_call(
        functools.partial(prepare_kernel, query_start_of),
        out_shape=(
            shape((HEAD_DIM, query_rows * heads), jnp.bfloat16),
            shape((lines, HEAD_DIM), f32),
            shape((lines, HEAD_DIM), f32),
            shape((shards * rows, query_rows), jnp.bfloat16),
        ),
        in_specs=[smem, smem, smem, pl.BlockSpec(memory_space=pltpu.HBM), vmem],
        out_specs=[vmem] * 4,
        scratch_shapes=[
            pltpu.VMEM((lines, HEAD_DIM), jnp.int32),
            pltpu.VMEM((shards * rows // BLOCK, query_rows), f32),
            pltpu.VMEM(queries.shape, queries.dtype),
            pltpu.SemaphoreType.DMA(()),
        ],
        compiler_params=pltpu.CompilerParams(vmem_limit_bytes=limit),
        cost_estimate=pl.CostEstimate(flops=4 * 10**9, bytes_accessed=10**6, transcendentals=10**5),
        name="prepare",
    )(key_offsets, vertical_blocks, slash_offsets, queries, jnp.asarray(frequency_row()))

    def attend(prepared, pieces, shards_of, state, last):
        count = len(pieces) if shards_of is not None else shards
        products = 2 * query_rows * heads * rows * 2 * HEAD_DIM * count
        state_shape = (
            shape((8, query_rows * heads), f32),
            shape((HEAD_DIM + SUM_ROWS, query_rows * heads), f32),
        )
        return pl.pallas_call(
            functools.partial(attend_kernel, place_of, shards_of, not state, last),
            out_shape=shape(queries.shape, queries.dtype) if last else state_shape,
            in_specs=[vmem] * (4 + len(state) + len(pieces)),
            out_specs=vmem if last else (vmem, vmem),
            compiler_params=pltpu.CompilerParams(vmem_limit_bytes=limit),
            cost_estimate=pl.CostEstimate(
                flops=4 * products,
                bytes_accessed=10**6,
                transcendentals=query_rows * heads * rows * count,
            ),
            name="attend",
        )(*prepared, *state, *pieces)

    own = jnp.concatenate([cached_keys, cached_values], axis=0)
    if not direct:
        gathered = lax.all_gather(own, ("seg", "ctx"), axis=0, tiled=True)
        return attend(prepared, [gathered], None, (), True)

    def number(seg, ctx):
        return seg * n_ctx + ctx

    def whole(ref):
        return ref[:rows, :], ref[rows : 2 * rows, :]

    far = exchange(own, lambda s, c, h: (s ^ (3 - h), c, h))
    near = exchange(own, lambda s, c, h: (s ^ (1 - h), c ^ h, h))
    near, prepared = lax.optimization_barrier((near, prepared))
    beside = swap(near)
    state = attend(
        prepared,
        [own, near, beside],
        lambda refs, s, c, h: [
            (*whole(refs[0]), number(s, c)),
            (*whole(refs[1]), number(s ^ (1 - h), c ^ h)),
            (*whole(refs[2]), number(s ^ h, c ^ (1 - h))),
        ],
        (),
        False,
    )
    across = exchange(far, lambda s, c, h: (s, c ^ 1, h))
    far_after, beside = lax.optimization_barrier((far, beside))
    far_beside = swap(far_after)
    half = jnp.where(lax.axis_index("head") == 0, beside[:rows], near[rows:])
    diagonal = exchange(half, lambda s, c, h: (s ^ 1, c, h))
    across_after, diagonal_after, state = lax.optimization_barrier((across, diagonal, state))
    state = attend(
        prepared,
        [far, far_beside],
        lambda refs, s, c, h: [
            (*whole(refs[0]), number(s ^ (3 - h), c)),
            (*whole(refs[1]), number(s ^ (2 + h), c)),
        ],
        state,
        False,
    )
    beside = swap(jnp.concatenate([across_after, diagonal_after], axis=0))

    def last_shards(refs, s, c, h):
        across, diagonal, beside = refs
        mine, other = diagonal[...], beside[2 * rows :, :]
        return [
            (*whole(across), number(s ^ (3 - h), c ^ 1)),
            (*whole(beside), number(s ^ (2 + h), c ^ 1)),
            (
                jnp.where(h == 0, mine, other),
                jnp.where(h == 0, other, mine),
                number(s ^ 1, c ^ 1),
            ),
        ]

    return attend(prepared, [across, diagonal, beside], last_shards, state, True)


def solution(mesh):
    return jax.shard_map(
        local,
        mesh=mesh,
        in_specs=(
            P(("groups", "ctx"), "head"),
            P(("groups", "seg", "ctx"), None),
            P(("groups", "seg", "ctx"), None),
            P("groups"),
            P("groups", None),
            P("groups", None),
        ),
        out_specs=P(("groups", "ctx"), "head"),
        check_vma=False,
    )
```

```python
import functools
import math

import jax
import jax.numpy as jnp
import numpy as np
from jax import lax
from jax.experimental import pallas as pl
from jax.experimental.pallas import tpu as pltpu
from jax.sharding import PartitionSpec as P

HEAD_DIM = 128
BLOCK = 64
ROPE_THETA = 500000.0
ROPE_FACTOR = 8.0
LOW_FACTOR = 1.0
HIGH_FACTOR = 4.0
TRAINED_CONTEXT = 8192.0
MASKED_SCORE = -1e30
SCORE_SCALE = HEAD_DIM**-0.5 * math.log2(math.e)
TILE = 128
FINE = 16
SUM_ROWS = 16
DIRECT_SHARDS = (4, 2)
AXES = ("seg", "ctx", "head")


def frequency_row():
    exponent = np.arange(0, HEAD_DIM, 2, dtype=np.float64) / HEAD_DIM
    base = ROPE_THETA**-exponent
    wavelength = 2.0 * np.pi / base
    smooth = (TRAINED_CONTEXT / wavelength - LOW_FACTOR) / (HIGH_FACTOR - LOW_FACTOR)
    blended = (1.0 - smooth) * base / ROPE_FACTOR + smooth * base
    frequencies = np.where(
        wavelength < TRAINED_CONTEXT / HIGH_FACTOR,
        base,
        np.where(wavelength > TRAINED_CONTEXT / LOW_FACTOR, base / ROPE_FACTOR, blended),
    )
    return np.tile(frequencies, 2)[None, :].astype(np.float32)


def turned_sine(sine):
    lane = lax.broadcasted_iota(jnp.int32, sine.shape, 1)
    return jnp.where(lane < HEAD_DIM // 2, -sine, sine)


def rotate(vectors, cosine, signed_sine):
    wide = vectors.astype(jnp.float32)
    return (wide * cosine + pltpu.roll(wide, HEAD_DIM // 2, 1) * signed_sine).astype(jnp.bfloat16)


def angle_sum(cos_a, sin_a, cos_b, sin_b):
    return cos_a * cos_b - sin_a * sin_b, sin_a * cos_b + cos_a * sin_b


def shard_tables(cosines, sines, line, rows):
    cos_f, sin_f = cosines[pl.ds(0, FINE), :], turned_sine(sines[pl.ds(0, FINE), :])
    cos_c, sin_c = angle_sum(
        cosines[pl.ds(FINE, FINE), :],
        sines[pl.ds(FINE, FINE), :],
        cosines[pl.ds(line, 1), :],
        sines[pl.ds(line, 1), :],
    )
    signed = turned_sine(sin_c)
    parts = [
        (
            cos_f * cos_c[i : i + 1] - sin_f * signed[i : i + 1],
            sin_f * cos_c[i : i + 1] + cos_f * signed[i : i + 1],
        )
        for i in range(rows // FINE)
    ]
    return tuple(jnp.concatenate(table, axis=0) for table in zip(*parts))


def prepare_kernel(
    query_start_of, offsets, vertical, slash, queries, freq, rotated, cosines, sines, masks,
    angles, bias, held, arrival,
):
    query_rows, columns = held.shape
    heads = columns // HEAD_DIM
    fetch = pltpu.make_async_copy(queries, held, arrival)
    fetch.start()
    query_start, first_list = query_start_of()

    step = lax.broadcasted_iota(jnp.int32, (FINE, HEAD_DIM), 0)
    angles[pl.ds(0, FINE), :] = step
    angles[pl.ds(FINE, FINE), :] = step * FINE
    for shard in range(offsets.shape[0]):
        angles[pl.ds(2 * FINE + shard, 1), :] = jnp.full((1, HEAD_DIM), offsets[shard], jnp.int32)
    angles[pl.ds(angles.shape[0] - 8, 8), :] = jnp.full((8, HEAD_DIM), query_start, jnp.int32)
    angle = angles[...].astype(jnp.float32) * freq[...]
    cosines[...] = jnp.cos(angle)
    sines[...] = jnp.sin(angle)

    key_block = lax.broadcasted_iota(jnp.int32, bias.shape, 0)
    lane_block = lax.broadcasted_iota(jnp.int32, (1, query_rows), 1) // BLOCK
    hit = jnp.zeros(bias.shape, jnp.bool_)
    for entries, distance in ((vertical, False), (slash, True)):
        for entry in range(entries.shape[1]):
            wanted = jnp.zeros((1, query_rows), jnp.int32)
            for block in range(query_rows // BLOCK):
                value = entries[first_list + block, entry]
                if distance:
                    value = query_start // BLOCK + block - value
                wanted = jnp.where(lane_block == block, value, wanted)
            hit = hit | (key_block == wanted)
    bias[...] = jnp.where(hit, 0.0, MASKED_SCORE)

    rows = masks.shape[0] // offsets.shape[0]
    ahead = lax.broadcasted_iota(jnp.int32, (rows, query_rows), 1) - lax.broadcasted_iota(
        jnp.int32, (rows, query_rows), 0
    )

    @pl.loop(0, offsets.shape[0])
    def _(shard):
        offset = offsets[shard]
        lines = [
            jnp.broadcast_to(bias[pl.ds(offset // BLOCK + block, 1), :], (BLOCK, query_rows))
            for block in range(rows // BLOCK)
        ]
        masks[pl.ds(pl.multiple_of(shard * rows, rows), rows), :] = jnp.where(
            ahead >= offset - query_start, jnp.concatenate(lines, axis=0), MASKED_SCORE
        ).astype(masks.dtype)

    cosine, sine = shard_tables(cosines, sines, angles.shape[0] - 8, query_rows)
    fetch.wait()
    for head in range(heads):
        turned = rotate(held[:, pl.ds(head * HEAD_DIM, HEAD_DIM)], cosine, sine).T
        for tile in range(query_rows // TILE):
            lines = pl.ds((tile * heads + head) * TILE, TILE)
            rotated[:, lines] = turned[:, tile * TILE : (tile + 1) * TILE]


def attend_kernel(place_of, shards_of, first, last, *refs):
    rotated, cosines, sines, masks = refs[:4]
    refs = refs[4:]
    if not first:
        old_peak, old_sums = refs[:2]
        refs = refs[2:]
    if last:
        pieces, out = refs[:-1], refs[-1]
    else:
        pieces, new_peak, new_sums = refs[:-2], refs[-2], refs[-1]
    query_rows = masks.shape[1]
    tiles = query_rows // TILE
    width = rotated.shape[1] // tiles
    rows = masks.shape[0] // (cosines.shape[0] - 2 * FINE - 8)
    ones = jnp.ones((SUM_ROWS, rows), jnp.bfloat16)
    unit = (
        lax.broadcasted_iota(jnp.int32, (TILE, width), 0)
        == lax.broadcasted_iota(jnp.int32, (TILE, width), 1) % TILE
    ).astype(jnp.bfloat16)

    def load(keys, values, shard):
        keys = rotate(keys, *shard_tables(cosines, sines, 2 * FINE + shard, rows))
        mask = masks[pl.ds(pl.multiple_of(shard * rows, rows), rows), :]
        return keys, mask, jnp.concatenate([values.T, ones], axis=0)

    def update(loaded, tile, before):
        query = jnp.concatenate([rotated[:, pl.ds(tile * width, width)], unit], axis=0)
        scores = [
            jnp.dot(
                jnp.concatenate([keys, mask[:, tile * TILE : (tile + 1) * TILE]], axis=1),
                query,
                preferred_element_type=jnp.float32,
            )
            for keys, mask, _ in loaded
        ]
        peak = functools.reduce(jnp.maximum, [score.max(axis=0, keepdims=True) for score in scores])
        if before is not None:
            peak = jnp.maximum(before[0], peak)
        sums = functools.reduce(
            jnp.add,
            [
                jnp.dot(
                    values,
                    jnp.exp2((score - peak) * SCORE_SCALE).astype(jnp.bfloat16),
                    preferred_element_type=jnp.float32,
                )
                for score, (_, _, values) in zip(scores, loaded)
            ],
        )
        if before is not None:
            sums = sums + before[1] * jnp.exp2((before[0] - peak) * SCORE_SCALE)
        return peak, sums

    def finish(tile, peak, sums):
        if not last:
            span = pl.ds(tile * width, width)
            new_peak[:, span] = jnp.broadcast_to(peak, (new_peak.shape[0], width))
            new_sums[:, span] = sums
            return
        part = sums[:HEAD_DIM] * (1.0 / sums[HEAD_DIM : HEAD_DIM + 1])
        for head in range(width // TILE):
            out[pl.ds(tile * TILE, TILE), pl.ds(head * HEAD_DIM, HEAD_DIM)] = part[
                :, head * TILE : (head + 1) * TILE
            ].T.astype(out.dtype)

    if shards_of is not None:
        loaded = [
            load(keys, values, shard) for keys, values, shard in shards_of(pieces, *place_of())
        ]
        for tile in range(tiles):
            before = None
            if not first:
                span = pl.ds(tile * width, width)
                before = (old_peak[:1, span], old_sums[:, span])
            finish(tile, *update(loaded, tile, before))
    else:
        (whole,) = pieces
        for tile in range(tiles):

            def step(shard, before, tile=tile):
                start = pl.multiple_of(shard * (2 * rows), 2 * rows)
                piece = load(whole[pl.ds(start, rows), :], whole[pl.ds(start + rows, rows), :], shard)
                return update([piece], tile, before)

            initial = (
                jnp.full((1, width), MASKED_SCORE, jnp.float32),
                jnp.zeros((HEAD_DIM + SUM_ROWS, width), jnp.float32),
            )
            finish(tile, *lax.fori_loop(0, whole.shape[0] // (2 * rows), step, initial))


def local(queries, cached_keys, cached_values, key_offsets, vertical_blocks, slash_offsets):
    query_rows = queries.shape[0]
    heads = queries.shape[1] // HEAD_DIM
    rows = cached_keys.shape[0]
    n_seg, n_ctx = lax.axis_size("seg"), lax.axis_size("ctx")
    shards = n_seg * n_ctx
    prefix = rows * shards - query_rows * n_ctx

    def query_start_of():
        ctx = lax.axis_index("ctx")
        return prefix + ctx * query_rows, ctx * (query_rows // BLOCK)

    def place_of():
        return tuple(lax.axis_index(axis) for axis in AXES)

    def exchange(a, partner):
        pairs = []
        for seg in range(n_seg):
            for ctx in range(n_ctx):
                for head in range(2):
                    to_seg, to_ctx, to_head = partner(seg, ctx, head)
                    pairs.append(
                        ((seg * n_ctx + ctx) * 2 + head, (to_seg * n_ctx + to_ctx) * 2 + to_head)
                    )
        return lax.ppermute(a, AXES, pairs)

    def swap(a):
        return exchange(a, lambda s, c, h: (s, c, 1 - h))

    vmem = pl.BlockSpec(memory_space=pltpu.VMEM)
    smem = pl.BlockSpec(memory_space=pltpu.SMEM)
    f32 = jnp.float32
    direct = (n_seg, n_ctx) == DIRECT_SHARDS
    limit = (16 if direct else 56) * 1024 * 1024
    shape = jax.ShapeDtypeStruct
    lines = 2 * FINE + shards + 8
    prepared = pl.pallas_call(
        functools.partial(prepare_kernel, query_start_of),
        out_shape=(
            shape((HEAD_DIM, query_rows * heads), jnp.bfloat16),
            shape((lines, HEAD_DIM), f32),
            shape((lines, HEAD_DIM), f32),
            shape((shards * rows, query_rows), jnp.bfloat16),
        ),
        in_specs=[smem, smem, smem, pl.BlockSpec(memory_space=pltpu.HBM), vmem],
        out_specs=[vmem] * 4,
        scratch_shapes=[
            pltpu.VMEM((lines, HEAD_DIM), jnp.int32),
            pltpu.VMEM((shards * rows // BLOCK, query_rows), f32),
            pltpu.VMEM(queries.shape, queries.dtype),
            pltpu.SemaphoreType.DMA(()),
        ],
        compiler_params=pltpu.CompilerParams(vmem_limit_bytes=limit),
        cost_estimate=pl.CostEstimate(flops=4 * 10**9, bytes_accessed=10**6, transcendentals=10**5),
        name="prepare",
    )(key_offsets, vertical_blocks, slash_offsets, queries, jnp.asarray(frequency_row()))

    def attend(prepared, pieces, shards_of, state, last):
        count = len(pieces) if shards_of is not None else shards
        products = 2 * query_rows * heads * rows * 2 * HEAD_DIM * count
        state_shape = (
            shape((8, query_rows * heads), f32),
            shape((HEAD_DIM + SUM_ROWS, query_rows * heads), f32),
        )
        return pl.pallas_call(
            functools.partial(attend_kernel, place_of, shards_of, not state, last),
            out_shape=shape(queries.shape, queries.dtype) if last else state_shape,
            in_specs=[vmem] * (4 + len(state) + len(pieces)),
            out_specs=vmem if last else (vmem, vmem),
            compiler_params=pltpu.CompilerParams(vmem_limit_bytes=limit),
            cost_estimate=pl.CostEstimate(
                flops=4 * products,
                bytes_accessed=10**6,
                transcendentals=query_rows * heads * rows * count,
            ),
            name="attend",
        )(*prepared, *state, *pieces)

    def number(seg, ctx):
        return seg * n_ctx + ctx

    def whole(ref):
        return ref[:rows, :], ref[rows : 2 * rows, :]

    if not direct:
        own = jnp.concatenate([cached_keys, cached_values], axis=0)
        gathered = lax.all_gather(own, ("seg", "ctx"), axis=0, tiled=True)
        return attend(prepared, [gathered], None, (), True)

    far_keys, far_values = [
        exchange(a, lambda s, c, h: (s ^ (3 - h), c, h)) for a in (cached_keys, cached_values)
    ]
    own = jnp.concatenate([cached_keys, cached_values], axis=0)
    near = exchange(own, lambda s, c, h: (s ^ (1 - h), c ^ h, h))
    beside = swap(near)
    beside, prepared = lax.optimization_barrier((beside, prepared))
    half = jnp.where(lax.axis_index("head") == 0, beside[:rows], near[rows:])
    diagonal = exchange(half, lambda s, c, h: (s ^ 1, c, h))
    across_keys, across_values = [
        exchange(a, lambda s, c, h: (s, c ^ 1, h)) for a in (far_keys, far_values)
    ]
    state = attend(
        prepared,
        [own, near, beside],
        lambda refs, s, c, h: [
            (*whole(refs[0]), number(s, c)),
            (*whole(refs[1]), number(s ^ (1 - h), c ^ h)),
            (*whole(refs[2]), number(s ^ h, c ^ (1 - h))),
        ],
        (),
        False,
    )
    far_beside = swap(jnp.concatenate([far_keys, far_values, diagonal], axis=0))
    across_keys, across_values, state = lax.optimization_barrier(
        (across_keys, across_values, state)
    )

    def middle_shards(refs, s, c, h):
        keys, values, diagonal, beside = refs
        mine, other = diagonal[...], beside[2 * rows :, :]
        return [
            (keys[...], values[...], number(s ^ (3 - h), c)),
            (*whole(beside), number(s ^ (2 + h), c)),
            (
                jnp.where(h == 0, mine, other),
                jnp.where(h == 0, other, mine),
                number(s ^ 1, c ^ 1),
            ),
        ]

    def last_shards(refs, s, c, h):
        keys, values, beside = refs
        return [
            (keys[...], values[...], number(s ^ (3 - h), c ^ 1)),
            (*whole(beside), number(s ^ (2 + h), c ^ 1)),
        ]

    across_beside = swap(jnp.concatenate([across_keys, across_values], axis=0))
    state = attend(
        prepared, [far_keys, far_values, diagonal, far_beside], middle_shards, state, False
    )
    return attend(prepared, [across_keys, across_values, across_beside], last_shards, state, True)


def solution(mesh):
    return jax.shard_map(
        local,
        mesh=mesh,
        in_specs=(
            P(("groups", "ctx"), "head"),
            P(("groups", "seg", "ctx"), None),
            P(("groups", "seg", "ctx"), None),
            P("groups"),
            P("groups", None),
            P("groups", None),
        ),
        out_specs=P(("groups", "ctx"), "head"),
        check_vma=False,
    )
```

```python
import functools
import math

import jax
import jax.numpy as jnp
import numpy as np
from jax import lax
from jax.experimental import pallas as pl
from jax.experimental.pallas import tpu as pltpu
from jax.sharding import PartitionSpec as P

HEAD_DIM = 128
BLOCK = 64
ROPE_THETA = 500000.0
ROPE_FACTOR = 8.0
LOW_FACTOR = 1.0
HIGH_FACTOR = 4.0
TRAINED_CONTEXT = 8192.0
MASKED_SCORE = -1e30
SCORE_SCALE = HEAD_DIM**-0.5 * math.log2(math.e)
TILE = 128
FINE = 16
SUM_ROWS = 16
DIRECT_SHARDS = (4, 2)
AXES = ("seg", "ctx", "head")


def frequency_row():
    exponent = np.arange(0, HEAD_DIM, 2, dtype=np.float64) / HEAD_DIM
    base = ROPE_THETA**-exponent
    wavelength = 2.0 * np.pi / base
    smooth = (TRAINED_CONTEXT / wavelength - LOW_FACTOR) / (HIGH_FACTOR - LOW_FACTOR)
    blended = (1.0 - smooth) * base / ROPE_FACTOR + smooth * base
    frequencies = np.where(
        wavelength < TRAINED_CONTEXT / HIGH_FACTOR,
        base,
        np.where(wavelength > TRAINED_CONTEXT / LOW_FACTOR, base / ROPE_FACTOR, blended),
    )
    return np.tile(frequencies, 2)[None, :].astype(np.float32)


def turned_sine(sine):
    lane = lax.broadcasted_iota(jnp.int32, sine.shape, 1)
    return jnp.where(lane < HEAD_DIM // 2, -sine, sine)


def rotate(vectors, cosine, signed_sine):
    wide = vectors.astype(jnp.float32)
    return (wide * cosine + pltpu.roll(wide, HEAD_DIM // 2, 1) * signed_sine).astype(jnp.bfloat16)


def angle_sum(cos_a, sin_a, cos_b, sin_b):
    return cos_a * cos_b - sin_a * sin_b, sin_a * cos_b + cos_a * sin_b


def shard_tables(cosines, sines, line, rows):
    cos_f, sin_f = cosines[pl.ds(0, FINE), :], turned_sine(sines[pl.ds(0, FINE), :])
    cos_c, sin_c = angle_sum(
        cosines[pl.ds(FINE, FINE), :],
        sines[pl.ds(FINE, FINE), :],
        cosines[pl.ds(line, 1), :],
        sines[pl.ds(line, 1), :],
    )
    signed = turned_sine(sin_c)
    parts = [
        (
            cos_f * cos_c[i : i + 1] - sin_f * signed[i : i + 1],
            sin_f * cos_c[i : i + 1] + cos_f * signed[i : i + 1],
        )
        for i in range(rows // FINE)
    ]
    return tuple(jnp.concatenate(table, axis=0) for table in zip(*parts))


def prepare_kernel(
    query_start_of, offsets, vertical, slash, queries, freq, rotated, cosines, sines, masks,
    angles, bias, held, arrival,
):
    query_rows, columns = held.shape
    heads = columns // HEAD_DIM
    fetch = pltpu.make_async_copy(queries, held, arrival)
    fetch.start()
    query_start, first_list = query_start_of()

    step = lax.broadcasted_iota(jnp.int32, (FINE, HEAD_DIM), 0)
    angles[pl.ds(0, FINE), :] = step
    angles[pl.ds(FINE, FINE), :] = step * FINE
    for shard in range(offsets.shape[0]):
        angles[pl.ds(2 * FINE + shard, 1), :] = jnp.full((1, HEAD_DIM), offsets[shard], jnp.int32)
    angles[pl.ds(angles.shape[0] - 8, 8), :] = jnp.full((8, HEAD_DIM), query_start, jnp.int32)
    angle = angles[...].astype(jnp.float32) * freq[...]
    cosines[...] = jnp.cos(angle)
    sines[...] = jnp.sin(angle)

    key_block = lax.broadcasted_iota(jnp.int32, bias.shape, 0)
    lane_block = lax.broadcasted_iota(jnp.int32, (1, query_rows), 1) // BLOCK
    hit = jnp.zeros(bias.shape, jnp.bool_)
    for entries, distance in ((vertical, False), (slash, True)):
        for entry in range(entries.shape[1]):
            wanted = jnp.zeros((1, query_rows), jnp.int32)
            for block in range(query_rows // BLOCK):
                value = entries[first_list + block, entry]
                if distance:
                    value = query_start // BLOCK + block - value
                wanted = jnp.where(lane_block == block, value, wanted)
            hit = hit | (key_block == wanted)
    bias[...] = jnp.where(hit, 0.0, MASKED_SCORE)

    rows = masks.shape[0] // offsets.shape[0]
    ahead = lax.broadcasted_iota(jnp.int32, (rows, query_rows), 1) - lax.broadcasted_iota(
        jnp.int32, (rows, query_rows), 0
    )

    @pl.loop(0, offsets.shape[0])
    def _(shard):
        offset = offsets[shard]
        lines = [
            jnp.broadcast_to(bias[pl.ds(offset // BLOCK + block, 1), :], (BLOCK, query_rows))
            for block in range(rows // BLOCK)
        ]
        masks[pl.ds(pl.multiple_of(shard * rows, rows), rows), :] = jnp.where(
            ahead >= offset - query_start, jnp.concatenate(lines, axis=0), MASKED_SCORE
        ).astype(masks.dtype)

    cosine, sine = shard_tables(cosines, sines, angles.shape[0] - 8, query_rows)
    fetch.wait()
    for head in range(heads):
        turned = rotate(held[:, pl.ds(head * HEAD_DIM, HEAD_DIM)], cosine, sine).T
        for tile in range(query_rows // TILE):
            lines = pl.ds((tile * heads + head) * TILE, TILE)
            rotated[:, lines] = turned[:, tile * TILE : (tile + 1) * TILE]


def attend_kernel(place_of, shards_of, first, last, *refs):
    rotated, cosines, sines, masks = refs[:4]
    refs = refs[4:]
    if not first:
        old_peak, old_sums = refs[:2]
        refs = refs[2:]
    if last:
        pieces, out = refs[:-1], refs[-1]
    else:
        pieces, new_peak, new_sums = refs[:-2], refs[-2], refs[-1]
    query_rows = masks.shape[1]
    tiles = query_rows // TILE
    width = rotated.shape[1] // tiles
    rows = masks.shape[0] // (cosines.shape[0] - 2 * FINE - 8)
    ones = jnp.ones((SUM_ROWS, rows), jnp.bfloat16)
    unit = (
        lax.broadcasted_iota(jnp.int32, (TILE, width), 0)
        == lax.broadcasted_iota(jnp.int32, (TILE, width), 1) % TILE
    ).astype(jnp.bfloat16)

    def load(keys, values, shard):
        keys = rotate(keys, *shard_tables(cosines, sines, 2 * FINE + shard, rows))
        mask = masks[pl.ds(pl.multiple_of(shard * rows, rows), rows), :]
        return keys, mask, jnp.concatenate([values.T, ones], axis=0)

    def update(loaded, tile, before):
        query = jnp.concatenate([rotated[:, pl.ds(tile * width, width)], unit], axis=0)
        scores = [
            jnp.dot(
                jnp.concatenate([keys, mask[:, tile * TILE : (tile + 1) * TILE]], axis=1),
                query,
                preferred_element_type=jnp.float32,
            )
            for keys, mask, _ in loaded
        ]
        peak = functools.reduce(jnp.maximum, [score.max(axis=0, keepdims=True) for score in scores])
        if before is not None:
            peak = jnp.maximum(before[0], peak)
        sums = functools.reduce(
            jnp.add,
            [
                jnp.dot(
                    values,
                    jnp.exp2((score - peak) * SCORE_SCALE).astype(jnp.bfloat16),
                    preferred_element_type=jnp.float32,
                )
                for score, (_, _, values) in zip(scores, loaded)
            ],
        )
        if before is not None:
            sums = sums + before[1] * jnp.exp2((before[0] - peak) * SCORE_SCALE)
        return peak, sums

    def finish(tile, peak, sums):
        if not last:
            span = pl.ds(tile * width, width)
            new_peak[:, span] = jnp.broadcast_to(peak, (new_peak.shape[0], width))
            new_sums[:, span] = sums
            return
        part = sums[:HEAD_DIM] * (1.0 / sums[HEAD_DIM : HEAD_DIM + 1])
        for head in range(width // TILE):
            out[pl.ds(tile * TILE, TILE), pl.ds(head * HEAD_DIM, HEAD_DIM)] = part[
                :, head * TILE : (head + 1) * TILE
            ].T.astype(out.dtype)

    if shards_of is not None:
        loaded = [
            load(keys, values, shard) for keys, values, shard in shards_of(pieces, *place_of())
        ]
        for tile in range(tiles):
            before = None
            if not first:
                span = pl.ds(tile * width, width)
                before = (old_peak[:1, span], old_sums[:, span])
            finish(tile, *update(loaded, tile, before))
    else:
        (whole,) = pieces
        for tile in range(tiles):

            def step(shard, before, tile=tile):
                start = pl.multiple_of(shard * (2 * rows), 2 * rows)
                piece = load(whole[pl.ds(start, rows), :], whole[pl.ds(start + rows, rows), :], shard)
                return update([piece], tile, before)

            initial = (
                jnp.full((1, width), MASKED_SCORE, jnp.float32),
                jnp.zeros((HEAD_DIM + SUM_ROWS, width), jnp.float32),
            )
            finish(tile, *lax.fori_loop(0, whole.shape[0] // (2 * rows), step, initial))


def local(queries, cached_keys, cached_values, key_offsets, vertical_blocks, slash_offsets):
    query_rows = queries.shape[0]
    heads = queries.shape[1] // HEAD_DIM
    rows = cached_keys.shape[0]
    n_seg, n_ctx = lax.axis_size("seg"), lax.axis_size("ctx")
    shards = n_seg * n_ctx
    prefix = rows * shards - query_rows * n_ctx

    def query_start_of():
        ctx = lax.axis_index("ctx")
        return prefix + ctx * query_rows, ctx * (query_rows // BLOCK)

    def place_of():
        return tuple(lax.axis_index(axis) for axis in AXES)

    def exchange(a, partner, cores=(0, 1)):
        pairs = []
        for seg in range(n_seg):
            for ctx in range(n_ctx):
                for head in cores:
                    to_seg, to_ctx, to_head = partner(seg, ctx, head)
                    pairs.append(
                        ((seg * n_ctx + ctx) * 2 + head, (to_seg * n_ctx + to_ctx) * 2 + to_head)
                    )
        return lax.ppermute(a, AXES, pairs)

    def swap(a):
        return exchange(a, lambda s, c, h: (s, c, 1 - h))

    vmem = pl.BlockSpec(memory_space=pltpu.VMEM)
    smem = pl.BlockSpec(memory_space=pltpu.SMEM)
    f32 = jnp.float32
    direct = (n_seg, n_ctx) == DIRECT_SHARDS
    limit = (16 if direct else 56) * 1024 * 1024
    shape = jax.ShapeDtypeStruct
    lines = 2 * FINE + shards + 8
    prepared = pl.pallas_call(
        functools.partial(prepare_kernel, query_start_of),
        out_shape=(
            shape((HEAD_DIM, query_rows * heads), jnp.bfloat16),
            shape((lines, HEAD_DIM), f32),
            shape((lines, HEAD_DIM), f32),
            shape((shards * rows, query_rows), jnp.bfloat16),
        ),
        in_specs=[smem, smem, smem, pl.BlockSpec(memory_space=pltpu.HBM), vmem],
        out_specs=[vmem] * 4,
        scratch_shapes=[
            pltpu.VMEM((lines, HEAD_DIM), jnp.int32),
            pltpu.VMEM((shards * rows // BLOCK, query_rows), f32),
            pltpu.VMEM(queries.shape, queries.dtype),
            pltpu.SemaphoreType.DMA(()),
        ],
        compiler_params=pltpu.CompilerParams(vmem_limit_bytes=limit),
        cost_estimate=pl.CostEstimate(flops=4 * 10**9, bytes_accessed=10**6, transcendentals=10**5),
        name="prepare",
    )(key_offsets, vertical_blocks, slash_offsets, queries, jnp.asarray(frequency_row()))

    def attend(prepared, pieces, shards_of, state, last):
        count = len(pieces) if shards_of is not None else shards
        products = 2 * query_rows * heads * rows * 2 * HEAD_DIM * count
        state_shape = (
            shape((8, query_rows * heads), f32),
            shape((HEAD_DIM + SUM_ROWS, query_rows * heads), f32),
        )
        return pl.pallas_call(
            functools.partial(attend_kernel, place_of, shards_of, not state, last),
            out_shape=shape(queries.shape, queries.dtype) if last else state_shape,
            in_specs=[vmem] * (4 + len(state) + len(pieces)),
            out_specs=vmem if last else (vmem, vmem),
            compiler_params=pltpu.CompilerParams(vmem_limit_bytes=limit),
            cost_estimate=pl.CostEstimate(
                flops=4 * products,
                bytes_accessed=10**6,
                transcendentals=query_rows * heads * rows * count,
            ),
            name="attend",
        )(*prepared, *state, *pieces)

    def number(seg, ctx):
        return seg * n_ctx + ctx

    def whole(ref):
        return ref[:rows, :], ref[rows : 2 * rows, :]

    if not direct:
        own = jnp.concatenate([cached_keys, cached_values], axis=0)
        gathered = lax.all_gather(own, ("seg", "ctx"), axis=0, tiled=True)
        return attend(prepared, [gathered], None, (), True)

    own = jnp.concatenate([cached_keys, cached_values], axis=0)
    far = exchange(own, lambda s, c, h: (s ^ (3 - h), c, h))
    near = exchange(own, lambda s, c, h: (s ^ (1 - h), c ^ h, h))
    near, prepared = lax.optimization_barrier((near, prepared))
    beside = swap(near)
    diagonal = exchange(near, lambda s, c, h: (s, c ^ 1, h), cores=(0,))
    across = exchange(far, lambda s, c, h: (s, c ^ 1, h))
    state = attend(
        prepared,
        [own, near, beside],
        lambda refs, s, c, h: [
            (*whole(refs[0]), number(s, c)),
            (*whole(refs[1]), number(s ^ (1 - h), c ^ h)),
            (*whole(refs[2]), number(s ^ h, c ^ (1 - h))),
        ],
        (),
        False,
    )
    far_after, beside = lax.optimization_barrier((far, beside))
    far_beside = swap(jnp.concatenate([far_after, diagonal], axis=0))
    across, state = lax.optimization_barrier((across, state))

    def middle_shards(refs, s, c, h):
        far, diagonal, beside = refs
        corner = jnp.where(h == 0, diagonal[...], beside[2 * rows :, :])
        return [
            (*whole(far), number(s ^ (3 - h), c)),
            (*whole(beside), number(s ^ (2 + h), c)),
            (corner[:rows], corner[rows:], number(s ^ 1, c ^ 1)),
        ]

    def last_shards(refs, s, c, h):
        across, beside = refs
        return [
            (*whole(across), number(s ^ (3 - h), c ^ 1)),
            (*whole(beside), number(s ^ (2 + h), c ^ 1)),
        ]

    across_beside = swap(across)
    state = attend(
        prepared, [far, diagonal, far_beside], middle_shards, state, False
    )
    return attend(prepared, [across, across_beside], last_shards, state, True)


def solution(mesh):
    return jax.shard_map(
        local,
        mesh=mesh,
        in_specs=(
            P(("groups", "ctx"), "head"),
            P(("groups", "seg", "ctx"), None),
            P(("groups", "seg", "ctx"), None),
            P("groups"),
            P("groups", None),
            P("groups", None),
        ),
        out_specs=P(("groups", "ctx"), "head"),
        check_vma=False,
    )
```

```python
import functools
import math

import jax
import jax.numpy as jnp
import numpy as np
from jax import lax
from jax.experimental import pallas as pl
from jax.experimental.pallas import tpu as pltpu
from jax.sharding import PartitionSpec as P

HEAD_DIM = 128
BLOCK = 64
ROPE_THETA = 500000.0
ROPE_FACTOR = 8.0
LOW_FACTOR = 1.0
HIGH_FACTOR = 4.0
TRAINED_CONTEXT = 8192.0
MASKED_SCORE = -1e30
SCORE_SCALE = HEAD_DIM**-0.5 * math.log2(math.e)
TILE = 128
FINE = 16
SUM_ROWS = 16
DIRECT_SHARDS = (4, 2)
AXES = ("seg", "ctx", "head")


def frequency_row():
    exponent = np.arange(0, HEAD_DIM, 2, dtype=np.float64) / HEAD_DIM
    base = ROPE_THETA**-exponent
    wavelength = 2.0 * np.pi / base
    smooth = (TRAINED_CONTEXT / wavelength - LOW_FACTOR) / (HIGH_FACTOR - LOW_FACTOR)
    blended = (1.0 - smooth) * base / ROPE_FACTOR + smooth * base
    frequencies = np.where(
        wavelength < TRAINED_CONTEXT / HIGH_FACTOR,
        base,
        np.where(wavelength > TRAINED_CONTEXT / LOW_FACTOR, base / ROPE_FACTOR, blended),
    )
    return np.tile(frequencies, 2)[None, :].astype(np.float32)


def turned_sine(sine):
    lane = lax.broadcasted_iota(jnp.int32, sine.shape, 1)
    return jnp.where(lane < HEAD_DIM // 2, -sine, sine)


def rotate(vectors, cosine, signed_sine):
    wide = vectors.astype(jnp.float32)
    return (wide * cosine + pltpu.roll(wide, HEAD_DIM // 2, 1) * signed_sine).astype(jnp.bfloat16)


def angle_sum(cos_a, sin_a, cos_b, sin_b):
    return cos_a * cos_b - sin_a * sin_b, sin_a * cos_b + cos_a * sin_b


def shard_tables(cosines, sines, line, rows):
    cos_f, sin_f = cosines[pl.ds(0, FINE), :], turned_sine(sines[pl.ds(0, FINE), :])
    cos_c, sin_c = angle_sum(
        cosines[pl.ds(FINE, FINE), :],
        sines[pl.ds(FINE, FINE), :],
        cosines[pl.ds(line, 1), :],
        sines[pl.ds(line, 1), :],
    )
    signed = turned_sine(sin_c)
    parts = [
        (
            cos_f * cos_c[i : i + 1] - sin_f * signed[i : i + 1],
            sin_f * cos_c[i : i + 1] + cos_f * signed[i : i + 1],
        )
        for i in range(rows // FINE)
    ]
    return tuple(jnp.concatenate(table, axis=0) for table in zip(*parts))


def prepare_kernel(
    query_start_of, offsets, vertical, slash, queries, freq, rotated, cosines, sines, masks,
    angles, bias, held, arrival,
):
    query_rows, columns = held.shape
    heads = columns // HEAD_DIM
    fetch = pltpu.make_async_copy(queries, held, arrival)
    fetch.start()
    query_start, first_list = query_start_of()

    step = lax.broadcasted_iota(jnp.int32, (FINE, HEAD_DIM), 0)
    angles[pl.ds(0, FINE), :] = step
    angles[pl.ds(FINE, FINE), :] = step * FINE
    for shard in range(offsets.shape[0]):
        angles[pl.ds(2 * FINE + shard, 1), :] = jnp.full((1, HEAD_DIM), offsets[shard], jnp.int32)
    angles[pl.ds(angles.shape[0] - 8, 8), :] = jnp.full((8, HEAD_DIM), query_start, jnp.int32)
    angle = angles[...].astype(jnp.float32) * freq[...]
    cosines[...] = jnp.cos(angle)
    sines[...] = jnp.sin(angle)

    key_block = lax.broadcasted_iota(jnp.int32, bias.shape, 0)
    lane_block = lax.broadcasted_iota(jnp.int32, (1, query_rows), 1) // BLOCK
    hit = jnp.zeros(bias.shape, jnp.bool_)
    for entries, distance in ((vertical, False), (slash, True)):
        for entry in range(entries.shape[1]):
            wanted = jnp.zeros((1, query_rows), jnp.int32)
            for block in range(query_rows // BLOCK):
                value = entries[first_list + block, entry]
                if distance:
                    value = query_start // BLOCK + block - value
                wanted = jnp.where(lane_block == block, value, wanted)
            hit = hit | (key_block == wanted)
    bias[...] = jnp.where(hit, 0.0, MASKED_SCORE)

    rows = masks.shape[0] // offsets.shape[0]
    ahead = lax.broadcasted_iota(jnp.int32, (rows, query_rows), 1) - lax.broadcasted_iota(
        jnp.int32, (rows, query_rows), 0
    )

    @pl.loop(0, offsets.shape[0])
    def _(shard):
        offset = offsets[shard]
        lines = [
            jnp.broadcast_to(bias[pl.ds(offset // BLOCK + block, 1), :], (BLOCK, query_rows))
            for block in range(rows // BLOCK)
        ]
        masks[pl.ds(pl.multiple_of(shard * rows, rows), rows), :] = jnp.where(
            ahead >= offset - query_start, jnp.concatenate(lines, axis=0), MASKED_SCORE
        ).astype(masks.dtype)

    cosine, sine = shard_tables(cosines, sines, angles.shape[0] - 8, query_rows)
    fetch.wait()
    for head in range(heads):
        turned = rotate(held[:, pl.ds(head * HEAD_DIM, HEAD_DIM)], cosine, sine).T
        for tile in range(query_rows // TILE):
            lines = pl.ds((tile * heads + head) * TILE, TILE)
            rotated[:, lines] = turned[:, tile * TILE : (tile + 1) * TILE]


def attend_kernel(place_of, shards_of, first, last, *refs):
    rotated, cosines, sines, masks = refs[:4]
    refs = refs[4:]
    if not first:
        old_peak, old_sums = refs[:2]
        refs = refs[2:]
    if last:
        pieces, out = refs[:-1], refs[-1]
    else:
        pieces, new_peak, new_sums = refs[:-2], refs[-2], refs[-1]
    query_rows = masks.shape[1]
    tiles = query_rows // TILE
    width = rotated.shape[1] // tiles
    rows = masks.shape[0] // (cosines.shape[0] - 2 * FINE - 8)
    ones = jnp.ones((SUM_ROWS, rows), jnp.bfloat16)
    unit = (
        lax.broadcasted_iota(jnp.int32, (TILE, width), 0)
        == lax.broadcasted_iota(jnp.int32, (TILE, width), 1) % TILE
    ).astype(jnp.bfloat16)

    def load(keys, values, shard):
        keys = rotate(keys, *shard_tables(cosines, sines, 2 * FINE + shard, rows))
        mask = masks[pl.ds(pl.multiple_of(shard * rows, rows), rows), :]
        return keys, mask, jnp.concatenate([values.T, ones], axis=0)

    def update(loaded, tile, before):
        query = jnp.concatenate([rotated[:, pl.ds(tile * width, width)], unit], axis=0)
        scores = [
            jnp.dot(
                jnp.concatenate([keys, mask[:, tile * TILE : (tile + 1) * TILE]], axis=1),
                query,
                preferred_element_type=jnp.float32,
            )
            for keys, mask, _ in loaded
        ]
        peak = functools.reduce(jnp.maximum, [score.max(axis=0, keepdims=True) for score in scores])
        if before is not None:
            peak = jnp.maximum(before[0], peak)
        sums = functools.reduce(
            jnp.add,
            [
                jnp.dot(
                    values,
                    jnp.exp2((score - peak) * SCORE_SCALE).astype(jnp.bfloat16),
                    preferred_element_type=jnp.float32,
                )
                for score, (_, _, values) in zip(scores, loaded)
            ],
        )
        if before is not None:
            sums = sums + before[1] * jnp.exp2((before[0] - peak) * SCORE_SCALE)
        return peak, sums

    def finish(tile, peak, sums):
        if not last:
            span = pl.ds(tile * width, width)
            new_peak[:, span] = jnp.broadcast_to(peak, (new_peak.shape[0], width))
            new_sums[:, span] = sums
            return
        part = sums[:HEAD_DIM] * (1.0 / sums[HEAD_DIM : HEAD_DIM + 1])
        for head in range(width // TILE):
            out[pl.ds(tile * TILE, TILE), pl.ds(head * HEAD_DIM, HEAD_DIM)] = part[
                :, head * TILE : (head + 1) * TILE
            ].T.astype(out.dtype)

    if shards_of is not None:
        loaded = [
            load(keys, values, shard) for keys, values, shard in shards_of(pieces, *place_of())
        ]
        for tile in range(tiles):
            before = None
            if not first:
                span = pl.ds(tile * width, width)
                before = (old_peak[:1, span], old_sums[:, span])
            finish(tile, *update(loaded, tile, before))
    else:
        (whole,) = pieces
        for tile in range(tiles):

            def step(shard, before, tile=tile):
                start = pl.multiple_of(shard * (2 * rows), 2 * rows)
                piece = load(whole[pl.ds(start, rows), :], whole[pl.ds(start + rows, rows), :], shard)
                return update([piece], tile, before)

            initial = (
                jnp.full((1, width), MASKED_SCORE, jnp.float32),
                jnp.zeros((HEAD_DIM + SUM_ROWS, width), jnp.float32),
            )
            finish(tile, *lax.fori_loop(0, whole.shape[0] // (2 * rows), step, initial))


def local(queries, cached_keys, cached_values, key_offsets, vertical_blocks, slash_offsets):
    query_rows = queries.shape[0]
    heads = queries.shape[1] // HEAD_DIM
    rows = cached_keys.shape[0]
    n_seg, n_ctx = lax.axis_size("seg"), lax.axis_size("ctx")
    shards = n_seg * n_ctx
    prefix = rows * shards - query_rows * n_ctx

    def query_start_of():
        ctx = lax.axis_index("ctx")
        return prefix + ctx * query_rows, ctx * (query_rows // BLOCK)

    def place_of():
        return tuple(lax.axis_index(axis) for axis in AXES)

    def exchange(a, partner):
        pairs = []
        for seg in range(n_seg):
            for ctx in range(n_ctx):
                for head in range(2):
                    to_seg, to_ctx, to_head = partner(seg, ctx, head)
                    pairs.append(
                        ((seg * n_ctx + ctx) * 2 + head, (to_seg * n_ctx + to_ctx) * 2 + to_head)
                    )
        return lax.ppermute(a, AXES, pairs)

    def swap(a):
        return exchange(a, lambda s, c, h: (s, c, 1 - h))

    vmem = pl.BlockSpec(memory_space=pltpu.VMEM)
    smem = pl.BlockSpec(memory_space=pltpu.SMEM)
    f32 = jnp.float32
    direct = (n_seg, n_ctx) == DIRECT_SHARDS
    limit = (16 if direct else 56) * 1024 * 1024
    shape = jax.ShapeDtypeStruct
    lines = 2 * FINE + shards + 8
    prepared = pl.pallas_call(
        functools.partial(prepare_kernel, query_start_of),
        out_shape=(
            shape((HEAD_DIM, query_rows * heads), jnp.bfloat16),
            shape((lines, HEAD_DIM), f32),
            shape((lines, HEAD_DIM), f32),
            shape((shards * rows, query_rows), jnp.bfloat16),
        ),
        in_specs=[smem, smem, smem, pl.BlockSpec(memory_space=pltpu.HBM), vmem],
        out_specs=[vmem] * 4,
        scratch_shapes=[
            pltpu.VMEM((lines, HEAD_DIM), jnp.int32),
            pltpu.VMEM((shards * rows // BLOCK, query_rows), f32),
            pltpu.VMEM(queries.shape, queries.dtype),
            pltpu.SemaphoreType.DMA(()),
        ],
        compiler_params=pltpu.CompilerParams(vmem_limit_bytes=limit),
        cost_estimate=pl.CostEstimate(flops=4 * 10**9, bytes_accessed=10**6, transcendentals=10**5),
        name="prepare",
    )(key_offsets, vertical_blocks, slash_offsets, queries, jnp.asarray(frequency_row()))

    def attend(prepared, pieces, shards_of, state, last):
        count = len(pieces) if shards_of is not None else shards
        products = 2 * query_rows * heads * rows * 2 * HEAD_DIM * count
        state_shape = (
            shape((8, query_rows * heads), f32),
            shape((HEAD_DIM + SUM_ROWS, query_rows * heads), f32),
        )
        return pl.pallas_call(
            functools.partial(attend_kernel, place_of, shards_of, not state, last),
            out_shape=shape(queries.shape, queries.dtype) if last else state_shape,
            in_specs=[vmem] * (4 + len(state) + len(pieces)),
            out_specs=vmem if last else (vmem, vmem),
            compiler_params=pltpu.CompilerParams(vmem_limit_bytes=limit),
            cost_estimate=pl.CostEstimate(
                flops=4 * products,
                bytes_accessed=10**6,
                transcendentals=query_rows * heads * rows * count,
            ),
            name="attend",
        )(*prepared, *state, *pieces)

    own = jnp.concatenate([cached_keys, cached_values], axis=0)
    if not direct:
        gathered = lax.all_gather(own, ("seg", "ctx"), axis=0, tiled=True)
        return attend(prepared, [gathered], None, (), True)

    def number(seg, ctx):
        return seg * n_ctx + ctx

    def whole(ref):
        return ref[:rows, :], ref[rows : 2 * rows, :]

    far = exchange(own, lambda s, c, h: (s ^ (3 - h), c, h))
    near = exchange(own, lambda s, c, h: (s ^ (1 - h), c ^ h, h))
    half = lax.dynamic_slice_in_dim(own, lax.axis_index("head") * rows, rows, 0)
    near, half, prepared = lax.optimization_barrier((near, half, prepared))
    diagonal = exchange(half, lambda s, c, h: (s ^ 1, c ^ 1, h))
    beside = swap(near)
    state = attend(
        prepared,
        [own, near, beside],
        lambda refs, s, c, h: [
            (*whole(refs[0]), number(s, c)),
            (*whole(refs[1]), number(s ^ (1 - h), c ^ h)),
            (*whole(refs[2]), number(s ^ h, c ^ (1 - h))),
        ],
        (),
        False,
    )
    across = exchange(far, lambda s, c, h: (s, c ^ 1, h))
    far_after, beside = lax.optimization_barrier((far, beside))
    far_beside = swap(far_after)
    across_after, diagonal_after, state = lax.optimization_barrier((across, diagonal, state))
    state = attend(
        prepared,
        [far, far_beside],
        lambda refs, s, c, h: [
            (*whole(refs[0]), number(s ^ (3 - h), c)),
            (*whole(refs[1]), number(s ^ (2 + h), c)),
        ],
        state,
        False,
    )
    beside = swap(jnp.concatenate([across_after, diagonal_after], axis=0))

    def last_shards(refs, s, c, h):
        across, diagonal, beside = refs
        mine, other = diagonal[...], beside[2 * rows :, :]
        return [
            (*whole(across), number(s ^ (3 - h), c ^ 1)),
            (*whole(beside), number(s ^ (2 + h), c ^ 1)),
            (
                jnp.where(h == 0, mine, other),
                jnp.where(h == 0, other, mine),
                number(s ^ 1, c ^ 1),
            ),
        ]

    return attend(prepared, [across, diagonal, beside], last_shards, state, True)


def solution(mesh):
    return jax.shard_map(
        local,
        mesh=mesh,
        in_specs=(
            P(("groups", "ctx"), "head"),
            P(("groups", "seg", "ctx"), None),
            P(("groups", "seg", "ctx"), None),
            P("groups"),
            P("groups", None),
            P("groups", None),
        ),
        out_specs=P(("groups", "ctx"), "head"),
        check_vma=False,
    )
```

```python
import functools
import math

import jax
import jax.numpy as jnp
import numpy as np
from jax import lax
from jax.experimental import pallas as pl
from jax.experimental.pallas import tpu as pltpu
from jax.sharding import PartitionSpec as P

HEAD_DIM = 128
BLOCK = 64
ROPE_THETA = 500000.0
ROPE_FACTOR = 8.0
LOW_FACTOR = 1.0
HIGH_FACTOR = 4.0
TRAINED_CONTEXT = 8192.0
MASKED_SCORE = -1e30
SCORE_SCALE = HEAD_DIM**-0.5 * math.log2(math.e)
TILE = 128
FINE = 16
SUM_ROWS = 16
DIRECT_SHARDS = (4, 2)
AXES = ("seg", "ctx", "head")


def frequency_row():
    exponent = np.arange(0, HEAD_DIM, 2, dtype=np.float64) / HEAD_DIM
    base = ROPE_THETA**-exponent
    wavelength = 2.0 * np.pi / base
    smooth = (TRAINED_CONTEXT / wavelength - LOW_FACTOR) / (HIGH_FACTOR - LOW_FACTOR)
    blended = (1.0 - smooth) * base / ROPE_FACTOR + smooth * base
    frequencies = np.where(
        wavelength < TRAINED_CONTEXT / HIGH_FACTOR,
        base,
        np.where(wavelength > TRAINED_CONTEXT / LOW_FACTOR, base / ROPE_FACTOR, blended),
    )
    return np.tile(frequencies, 2)[None, :].astype(np.float32)


def turned_sine(sine):
    lane = lax.broadcasted_iota(jnp.int32, sine.shape, 1)
    return jnp.where(lane < HEAD_DIM // 2, -sine, sine)


def rotate(vectors, cosine, signed_sine):
    wide = vectors.astype(jnp.float32)
    return (wide * cosine + pltpu.roll(wide, HEAD_DIM // 2, 1) * signed_sine).astype(jnp.bfloat16)


def angle_sum(cos_a, sin_a, cos_b, sin_b):
    return cos_a * cos_b - sin_a * sin_b, sin_a * cos_b + cos_a * sin_b


def shard_tables(cosines, sines, line, rows):
    cos_f, sin_f = cosines[pl.ds(0, FINE), :], turned_sine(sines[pl.ds(0, FINE), :])
    cos_c, sin_c = angle_sum(
        cosines[pl.ds(FINE, FINE), :],
        sines[pl.ds(FINE, FINE), :],
        cosines[pl.ds(line, 1), :],
        sines[pl.ds(line, 1), :],
    )
    signed = turned_sine(sin_c)
    parts = [
        (
            cos_f * cos_c[i : i + 1] - sin_f * signed[i : i + 1],
            sin_f * cos_c[i : i + 1] + cos_f * signed[i : i + 1],
        )
        for i in range(rows // FINE)
    ]
    return tuple(jnp.concatenate(table, axis=0) for table in zip(*parts))


def prepare_kernel(
    query_start_of, offsets, vertical, slash, queries, freq, rotated, cosines, sines, masks,
    angles, bias, held, arrival,
):
    query_rows, columns = held.shape
    heads = columns // HEAD_DIM
    fetch = pltpu.make_async_copy(queries, held, arrival)
    fetch.start()
    query_start, first_list = query_start_of()

    step = lax.broadcasted_iota(jnp.int32, (FINE, HEAD_DIM), 0)
    angles[pl.ds(0, FINE), :] = step
    angles[pl.ds(FINE, FINE), :] = step * FINE
    for shard in range(offsets.shape[0]):
        angles[pl.ds(2 * FINE + shard, 1), :] = jnp.full((1, HEAD_DIM), offsets[shard], jnp.int32)
    angles[pl.ds(angles.shape[0] - 8, 8), :] = jnp.full((8, HEAD_DIM), query_start, jnp.int32)
    angle = angles[...].astype(jnp.float32) * freq[...]
    cosines[...] = jnp.cos(angle)
    sines[...] = jnp.sin(angle)

    key_block = lax.broadcasted_iota(jnp.int32, bias.shape, 0)
    lane_block = lax.broadcasted_iota(jnp.int32, (1, query_rows), 1) // BLOCK
    hit = jnp.zeros(bias.shape, jnp.bool_)
    for entries, distance in ((vertical, False), (slash, True)):
        for entry in range(entries.shape[1]):
            wanted = jnp.zeros((1, query_rows), jnp.int32)
            for block in range(query_rows // BLOCK):
                value = entries[first_list + block, entry]
                if distance:
                    value = query_start // BLOCK + block - value
                wanted = jnp.where(lane_block == block, value, wanted)
            hit = hit | (key_block == wanted)
    bias[...] = jnp.where(hit, 0.0, MASKED_SCORE)

    rows = masks.shape[0] // offsets.shape[0]
    ahead = lax.broadcasted_iota(jnp.int32, (rows, query_rows), 1) - lax.broadcasted_iota(
        jnp.int32, (rows, query_rows), 0
    )

    @pl.loop(0, offsets.shape[0])
    def _(shard):
        offset = offsets[shard]
        lines = [
            jnp.broadcast_to(bias[pl.ds(offset // BLOCK + block, 1), :], (BLOCK, query_rows))
            for block in range(rows // BLOCK)
        ]
        masks[pl.ds(pl.multiple_of(shard * rows, rows), rows), :] = jnp.where(
            ahead >= offset - query_start, jnp.concatenate(lines, axis=0), MASKED_SCORE
        ).astype(masks.dtype)

    cosine, sine = shard_tables(cosines, sines, angles.shape[0] - 8, query_rows)
    fetch.wait()
    for head in range(heads):
        turned = rotate(held[:, pl.ds(head * HEAD_DIM, HEAD_DIM)], cosine, sine).T
        for tile in range(query_rows // TILE):
            lines = pl.ds((tile * heads + head) * TILE, TILE)
            rotated[:, lines] = turned[:, tile * TILE : (tile + 1) * TILE]


def attend_kernel(place_of, shards_of, first, last, *refs):
    rotated, cosines, sines, masks = refs[:4]
    refs = refs[4:]
    if not first:
        old_peak, old_sums = refs[:2]
        refs = refs[2:]
    if last:
        pieces, out = refs[:-1], refs[-1]
    else:
        pieces, new_peak, new_sums = refs[:-2], refs[-2], refs[-1]
    query_rows = masks.shape[1]
    tiles = query_rows // TILE
    width = rotated.shape[1] // tiles
    rows = masks.shape[0] // (cosines.shape[0] - 2 * FINE - 8)
    ones = jnp.ones((SUM_ROWS, rows), jnp.bfloat16)
    unit = (
        lax.broadcasted_iota(jnp.int32, (TILE, width), 0)
        == lax.broadcasted_iota(jnp.int32, (TILE, width), 1) % TILE
    ).astype(jnp.bfloat16)

    def load(keys, values, shard):
        keys = rotate(keys, *shard_tables(cosines, sines, 2 * FINE + shard, rows))
        mask = masks[pl.ds(pl.multiple_of(shard * rows, rows), rows), :]
        return keys, mask, jnp.concatenate([values.T, ones], axis=0)

    def update(loaded, tile, before):
        query = jnp.concatenate([rotated[:, pl.ds(tile * width, width)], unit], axis=0)
        scores = [
            jnp.dot(
                jnp.concatenate([keys, mask[:, tile * TILE : (tile + 1) * TILE]], axis=1),
                query,
                preferred_element_type=jnp.float32,
            )
            for keys, mask, _ in loaded
        ]
        peak = functools.reduce(jnp.maximum, [score.max(axis=0, keepdims=True) for score in scores])
        if before is not None:
            peak = jnp.maximum(before[0], peak)
        sums = functools.reduce(
            jnp.add,
            [
                jnp.dot(
                    values,
                    jnp.exp2((score - peak) * SCORE_SCALE).astype(jnp.bfloat16),
                    preferred_element_type=jnp.float32,
                )
                for score, (_, _, values) in zip(scores, loaded)
            ],
        )
        if before is not None:
            sums = sums + before[1] * jnp.exp2((before[0] - peak) * SCORE_SCALE)
        return peak, sums

    def finish(tile, peak, sums):
        if not last:
            span = pl.ds(tile * width, width)
            new_peak[:, span] = jnp.broadcast_to(peak, (new_peak.shape[0], width))
            new_sums[:, span] = sums
            return
        part = sums[:HEAD_DIM] * (1.0 / sums[HEAD_DIM : HEAD_DIM + 1])
        for head in range(width // TILE):
            out[pl.ds(tile * TILE, TILE), pl.ds(head * HEAD_DIM, HEAD_DIM)] = part[
                :, head * TILE : (head + 1) * TILE
            ].T.astype(out.dtype)

    if shards_of is not None:
        loaded = [
            load(keys, values, shard) for keys, values, shard in shards_of(pieces, *place_of())
        ]
        for tile in range(tiles):
            before = None
            if not first:
                span = pl.ds(tile * width, width)
                before = (old_peak[:1, span], old_sums[:, span])
            finish(tile, *update(loaded, tile, before))
    else:
        (whole,) = pieces
        for tile in range(tiles):

            def step(shard, before, tile=tile):
                start = pl.multiple_of(shard * (2 * rows), 2 * rows)
                piece = load(whole[pl.ds(start, rows), :], whole[pl.ds(start + rows, rows), :], shard)
                return update([piece], tile, before)

            initial = (
                jnp.full((1, width), MASKED_SCORE, jnp.float32),
                jnp.zeros((HEAD_DIM + SUM_ROWS, width), jnp.float32),
            )
            finish(tile, *lax.fori_loop(0, whole.shape[0] // (2 * rows), step, initial))


def local(queries, cached_keys, cached_values, key_offsets, vertical_blocks, slash_offsets):
    query_rows = queries.shape[0]
    heads = queries.shape[1] // HEAD_DIM
    rows = cached_keys.shape[0]
    n_seg, n_ctx = lax.axis_size("seg"), lax.axis_size("ctx")
    shards = n_seg * n_ctx
    prefix = rows * shards - query_rows * n_ctx

    def query_start_of():
        ctx = lax.axis_index("ctx")
        return prefix + ctx * query_rows, ctx * (query_rows // BLOCK)

    def place_of():
        return tuple(lax.axis_index(axis) for axis in AXES)

    def exchange(a, partner):
        pairs = []
        for seg in range(n_seg):
            for ctx in range(n_ctx):
                for head in range(2):
                    to_seg, to_ctx, to_head = partner(seg, ctx, head)
                    pairs.append(
                        ((seg * n_ctx + ctx) * 2 + head, (to_seg * n_ctx + to_ctx) * 2 + to_head)
                    )
        return lax.ppermute(a, AXES, pairs)

    def swap(a):
        return exchange(a, lambda s, c, h: (s, c, 1 - h))

    vmem = pl.BlockSpec(memory_space=pltpu.VMEM)
    smem = pl.BlockSpec(memory_space=pltpu.SMEM)
    f32 = jnp.float32
    direct = (n_seg, n_ctx) == DIRECT_SHARDS
    limit = (16 if direct else 56) * 1024 * 1024
    shape = jax.ShapeDtypeStruct
    lines = 2 * FINE + shards + 8
    prepared = pl.pallas_call(
        functools.partial(prepare_kernel, query_start_of),
        out_shape=(
            shape((HEAD_DIM, query_rows * heads), jnp.bfloat16),
            shape((lines, HEAD_DIM), f32),
            shape((lines, HEAD_DIM), f32),
            shape((shards * rows, query_rows), jnp.bfloat16),
        ),
        in_specs=[smem, smem, smem, pl.BlockSpec(memory_space=pltpu.HBM), vmem],
        out_specs=[vmem] * 4,
        scratch_shapes=[
            pltpu.VMEM((lines, HEAD_DIM), jnp.int32),
            pltpu.VMEM((shards * rows // BLOCK, query_rows), f32),
            pltpu.VMEM(queries.shape, queries.dtype),
            pltpu.SemaphoreType.DMA(()),
        ],
        compiler_params=pltpu.CompilerParams(vmem_limit_bytes=limit),
        name="prepare",
    )(key_offsets, vertical_blocks, slash_offsets, queries, jnp.asarray(frequency_row()))

    def attend(prepared, pieces, shards_of, state, last):
        state_shape = (
            shape((8, query_rows * heads), f32),
            shape((HEAD_DIM + SUM_ROWS, query_rows * heads), f32),
        )
        return pl.pallas_call(
            functools.partial(attend_kernel, place_of, shards_of, not state, last),
            out_shape=shape(queries.shape, queries.dtype) if last else state_shape,
            in_specs=[vmem] * (4 + len(state) + len(pieces)),
            out_specs=vmem if last else (vmem, vmem),
            compiler_params=pltpu.CompilerParams(vmem_limit_bytes=limit),
            name="attend",
        )(*prepared, *state, *pieces)

    own = jnp.concatenate([cached_keys, cached_values], axis=0)
    if not direct:
        gathered = lax.all_gather(own, ("seg", "ctx"), axis=0, tiled=True)
        return attend(prepared, [gathered], None, (), True)

    def number(seg, ctx):
        return seg * n_ctx + ctx

    def whole(ref):
        return ref[:rows, :], ref[rows : 2 * rows, :]

    on_first = lax.axis_index("head") == 0
    first = exchange(own, lambda s, c, h: (s ^ (2 - 2 * h), c ^ h, h))
    second = exchange(own, lambda s, c, h: (s ^ (1 + 2 * h), c, h))
    half = lax.dynamic_slice_in_dim(own, lax.axis_index("head") * rows, rows, 0)
    third = exchange(half, lambda s, c, h: (s ^ 1, c ^ 1, h))
    first, prepared = lax.optimization_barrier((first, prepared))
    fourth = exchange(
        jnp.where(on_first, first, own), lambda s, c, h: (s ^ (3 * h), c ^ 1, h)
    )
    first_beside = swap(first)
    state = attend(
        prepared,
        [own, first, first_beside],
        lambda refs, s, c, h: [
            (*whole(refs[0]), number(s, c)),
            (*whole(refs[1]), number(s ^ (2 - 2 * h), c ^ h)),
            (*whole(refs[2]), number(s ^ (2 * h), c ^ (1 - h))),
        ],
        (),
        False,
    )
    second, third, state = lax.optimization_barrier((second, third, state))
    second_beside = swap(jnp.concatenate([second, third], axis=0))
    fourth, state = lax.optimization_barrier((fourth, state))
    fourth_beside = swap(fourth)

    def middle_shards(refs, s, c, h):
        second, third, beside = refs
        mine, other = third[...], beside[2 * rows :, :]
        return [
            (*whole(second), number(s ^ (1 + 2 * h), c)),
            (*whole(beside), number(s ^ (3 - 2 * h), c)),
            (
                jnp.where(h == 0, mine, other),
                jnp.where(h == 0, other, mine),
                number(s ^ 1, c ^ 1),
            ),
        ]

    state = attend(prepared, [second, third, second_beside], middle_shards, state, False)
    return attend(
        prepared,
        [fourth, fourth_beside],
        lambda refs, s, c, h: [
            (*whole(refs[0]), number(s ^ (2 + h), c ^ 1)),
            (*whole(refs[1]), number(s ^ (3 - h), c ^ 1)),
        ],
        state,
        True,
    )


def solution(mesh):
    return jax.shard_map(
        local,
        mesh=mesh,
        in_specs=(
            P(("groups", "ctx"), "head"),
            P(("groups", "seg", "ctx"), None),
            P(("groups", "seg", "ctx"), None),
            P("groups"),
            P("groups", None),
            P("groups", None),
        ),
        out_specs=P(("groups", "ctx"), "head"),
        check_vma=False,
    )
```

```python
import functools
import math

import jax
import jax.numpy as jnp
import numpy as np
from jax import lax
from jax.experimental import pallas as pl
from jax.experimental.pallas import tpu as pltpu
from jax.sharding import PartitionSpec as P

HEAD_DIM = 128
BLOCK = 64
ROPE_THETA = 500000.0
ROPE_FACTOR = 8.0
LOW_FACTOR = 1.0
HIGH_FACTOR = 4.0
TRAINED_CONTEXT = 8192.0
MASKED_SCORE = -1e30
SCORE_SCALE = HEAD_DIM**-0.5 * math.log2(math.e)
TILE = 128
FINE = 16
SUM_ROWS = 16
DIRECT_SHARDS = (4, 2)
AXES = ("seg", "ctx", "head")


def frequency_row():
    exponent = np.arange(0, HEAD_DIM, 2, dtype=np.float64) / HEAD_DIM
    base = ROPE_THETA**-exponent
    wavelength = 2.0 * np.pi / base
    smooth = (TRAINED_CONTEXT / wavelength - LOW_FACTOR) / (HIGH_FACTOR - LOW_FACTOR)
    blended = (1.0 - smooth) * base / ROPE_FACTOR + smooth * base
    frequencies = np.where(
        wavelength < TRAINED_CONTEXT / HIGH_FACTOR,
        base,
        np.where(wavelength > TRAINED_CONTEXT / LOW_FACTOR, base / ROPE_FACTOR, blended),
    )
    return np.tile(frequencies, 2)[None, :].astype(np.float32)


def turned_sine(sine):
    lane = lax.broadcasted_iota(jnp.int32, sine.shape, 1)
    return jnp.where(lane < HEAD_DIM // 2, -sine, sine)


def rotate(vectors, cosine, signed_sine):
    wide = vectors.astype(jnp.float32)
    return (wide * cosine + pltpu.roll(wide, HEAD_DIM // 2, 1) * signed_sine).astype(jnp.bfloat16)


def angle_sum(cos_a, sin_a, cos_b, sin_b):
    return cos_a * cos_b - sin_a * sin_b, sin_a * cos_b + cos_a * sin_b


def shard_tables(cosines, sines, line, rows):
    cos_f, sin_f = cosines[pl.ds(0, FINE), :], turned_sine(sines[pl.ds(0, FINE), :])
    cos_c, sin_c = angle_sum(
        cosines[pl.ds(FINE, FINE), :],
        sines[pl.ds(FINE, FINE), :],
        cosines[pl.ds(line, 1), :],
        sines[pl.ds(line, 1), :],
    )
    signed = turned_sine(sin_c)
    parts = [
        (
            cos_f * cos_c[i : i + 1] - sin_f * signed[i : i + 1],
            sin_f * cos_c[i : i + 1] + cos_f * signed[i : i + 1],
        )
        for i in range(rows // FINE)
    ]
    return tuple(jnp.concatenate(table, axis=0) for table in zip(*parts))


def prepare_kernel(
    query_start_of, offsets, vertical, slash, queries, freq, rotated, cosines, sines, masks,
    angles, bias, held, arrival,
):
    query_rows, columns = held.shape
    heads = columns // HEAD_DIM
    fetch = pltpu.make_async_copy(queries, held, arrival)
    fetch.start()
    query_start, first_list = query_start_of()

    step = lax.broadcasted_iota(jnp.int32, (FINE, HEAD_DIM), 0)
    angles[pl.ds(0, FINE), :] = step
    angles[pl.ds(FINE, FINE), :] = step * FINE
    for shard in range(offsets.shape[0]):
        angles[pl.ds(2 * FINE + shard, 1), :] = jnp.full((1, HEAD_DIM), offsets[shard], jnp.int32)
    angles[pl.ds(angles.shape[0] - 8, 8), :] = jnp.full((8, HEAD_DIM), query_start, jnp.int32)
    angle = angles[...].astype(jnp.float32) * freq[...]
    cosines[...] = jnp.cos(angle)
    sines[...] = jnp.sin(angle)

    key_block = lax.broadcasted_iota(jnp.int32, bias.shape, 0)
    lane_block = lax.broadcasted_iota(jnp.int32, (1, query_rows), 1) // BLOCK
    hit = jnp.zeros(bias.shape, jnp.bool_)
    for entries, distance in ((vertical, False), (slash, True)):
        for entry in range(entries.shape[1]):
            wanted = jnp.zeros((1, query_rows), jnp.int32)
            for block in range(query_rows // BLOCK):
                value = entries[first_list + block, entry]
                if distance:
                    value = query_start // BLOCK + block - value
                wanted = jnp.where(lane_block == block, value, wanted)
            hit = hit | (key_block == wanted)
    bias[...] = jnp.where(hit, 0.0, MASKED_SCORE)

    rows = masks.shape[0] // offsets.shape[0]
    ahead = lax.broadcasted_iota(jnp.int32, (rows, query_rows), 1) - lax.broadcasted_iota(
        jnp.int32, (rows, query_rows), 0
    )

    @pl.loop(0, offsets.shape[0])
    def _(shard):
        offset = offsets[shard]
        lines = [
            jnp.broadcast_to(bias[pl.ds(offset // BLOCK + block, 1), :], (BLOCK, query_rows))
            for block in range(rows // BLOCK)
        ]
        masks[pl.ds(pl.multiple_of(shard * rows, rows), rows), :] = jnp.where(
            ahead >= offset - query_start, jnp.concatenate(lines, axis=0), MASKED_SCORE
        ).astype(masks.dtype)

    cosine, sine = shard_tables(cosines, sines, angles.shape[0] - 8, query_rows)
    fetch.wait()
    for head in range(heads):
        turned = rotate(held[:, pl.ds(head * HEAD_DIM, HEAD_DIM)], cosine, sine).T
        for tile in range(query_rows // TILE):
            lines = pl.ds((tile * heads + head) * TILE, TILE)
            rotated[:, lines] = turned[:, tile * TILE : (tile + 1) * TILE]


def attend_kernel(place_of, shards_of, first, last, *refs):
    rotated, cosines, sines, masks = refs[:4]
    refs = refs[4:]
    if not first:
        old_peak, old_sums = refs[:2]
        refs = refs[2:]
    if last:
        pieces, out = refs[:-1], refs[-1]
    else:
        pieces, new_peak, new_sums = refs[:-2], refs[-2], refs[-1]
    query_rows = masks.shape[1]
    tiles = query_rows // TILE
    width = rotated.shape[1] // tiles
    rows = masks.shape[0] // (cosines.shape[0] - 2 * FINE - 8)
    ones = jnp.ones((SUM_ROWS, rows), jnp.bfloat16)
    unit = (
        lax.broadcasted_iota(jnp.int32, (TILE, width), 0)
        == lax.broadcasted_iota(jnp.int32, (TILE, width), 1) % TILE
    ).astype(jnp.bfloat16)

    def load(keys, values, shard):
        keys = rotate(keys, *shard_tables(cosines, sines, 2 * FINE + shard, rows))
        mask = masks[pl.ds(pl.multiple_of(shard * rows, rows), rows), :]
        return keys, mask, jnp.concatenate([values.T, ones], axis=0)

    def update(loaded, tile, before):
        query = jnp.concatenate([rotated[:, pl.ds(tile * width, width)], unit], axis=0)
        scores = [
            jnp.dot(
                jnp.concatenate([keys, mask[:, tile * TILE : (tile + 1) * TILE]], axis=1),
                query,
                preferred_element_type=jnp.float32,
            )
            for keys, mask, _ in loaded
        ]
        peak = functools.reduce(jnp.maximum, [score.max(axis=0, keepdims=True) for score in scores])
        if before is not None:
            peak = jnp.maximum(before[0], peak)
        sums = functools.reduce(
            jnp.add,
            [
                jnp.dot(
                    values,
                    jnp.exp2((score - peak) * SCORE_SCALE).astype(jnp.bfloat16),
                    preferred_element_type=jnp.float32,
                )
                for score, (_, _, values) in zip(scores, loaded)
            ],
        )
        if before is not None:
            sums = sums + before[1] * jnp.exp2((before[0] - peak) * SCORE_SCALE)
        return peak, sums

    def finish(tile, peak, sums):
        if not last:
            span = pl.ds(tile * width, width)
            new_peak[:, span] = jnp.broadcast_to(peak, (new_peak.shape[0], width))
            new_sums[:, span] = sums
            return
        part = sums[:HEAD_DIM] * (1.0 / sums[HEAD_DIM : HEAD_DIM + 1])
        for head in range(width // TILE):
            out[pl.ds(tile * TILE, TILE), pl.ds(head * HEAD_DIM, HEAD_DIM)] = part[
                :, head * TILE : (head + 1) * TILE
            ].T.astype(out.dtype)

    if shards_of is not None:
        loaded = [
            load(keys, values, shard) for keys, values, shard in shards_of(pieces, *place_of())
        ]
        for tile in range(tiles):
            before = None
            if not first:
                span = pl.ds(tile * width, width)
                before = (old_peak[:1, span], old_sums[:, span])
            finish(tile, *update(loaded, tile, before))
    else:
        (whole,) = pieces
        for tile in range(tiles):

            def step(shard, before, tile=tile):
                start = pl.multiple_of(shard * (2 * rows), 2 * rows)
                piece = load(whole[pl.ds(start, rows), :], whole[pl.ds(start + rows, rows), :], shard)
                return update([piece], tile, before)

            initial = (
                jnp.full((1, width), MASKED_SCORE, jnp.float32),
                jnp.zeros((HEAD_DIM + SUM_ROWS, width), jnp.float32),
            )
            finish(tile, *lax.fori_loop(0, whole.shape[0] // (2 * rows), step, initial))


def local(queries, cached_keys, cached_values, key_offsets, vertical_blocks, slash_offsets):
    query_rows = queries.shape[0]
    heads = queries.shape[1] // HEAD_DIM
    rows = cached_keys.shape[0]
    n_seg, n_ctx = lax.axis_size("seg"), lax.axis_size("ctx")
    shards = n_seg * n_ctx
    prefix = rows * shards - query_rows * n_ctx

    def query_start_of():
        ctx = lax.axis_index("ctx")
        return prefix + ctx * query_rows, ctx * (query_rows // BLOCK)

    def place_of():
        return tuple(lax.axis_index(axis) for axis in AXES)

    def exchange(a, partner):
        pairs = []
        for seg in range(n_seg):
            for ctx in range(n_ctx):
                for head in range(2):
                    to_seg, to_ctx, to_head = partner(seg, ctx, head)
                    pairs.append(
                        ((seg * n_ctx + ctx) * 2 + head, (to_seg * n_ctx + to_ctx) * 2 + to_head)
                    )
        return lax.ppermute(a, AXES, pairs)

    def swap(a):
        return exchange(a, lambda s, c, h: (s, c, 1 - h))

    vmem = pl.BlockSpec(memory_space=pltpu.VMEM)
    smem = pl.BlockSpec(memory_space=pltpu.SMEM)
    f32 = jnp.float32
    direct = (n_seg, n_ctx) == DIRECT_SHARDS
    limit = (16 if direct else 56) * 1024 * 1024
    shape = jax.ShapeDtypeStruct
    lines = 2 * FINE + shards + 8
    prepared = pl.pallas_call(
        functools.partial(prepare_kernel, query_start_of),
        out_shape=(
            shape((HEAD_DIM, query_rows * heads), jnp.bfloat16),
            shape((lines, HEAD_DIM), f32),
            shape((lines, HEAD_DIM), f32),
            shape((shards * rows, query_rows), jnp.bfloat16),
        ),
        in_specs=[smem, smem, smem, pl.BlockSpec(memory_space=pltpu.HBM), vmem],
        out_specs=[vmem] * 4,
        scratch_shapes=[
            pltpu.VMEM((lines, HEAD_DIM), jnp.int32),
            pltpu.VMEM((shards * rows // BLOCK, query_rows), f32),
            pltpu.VMEM(queries.shape, queries.dtype),
            pltpu.SemaphoreType.DMA(()),
        ],
        compiler_params=pltpu.CompilerParams(vmem_limit_bytes=limit),
        name="prepare",
    )(key_offsets, vertical_blocks, slash_offsets, queries, jnp.asarray(frequency_row()))

    def attend(prepared, pieces, shards_of, state, last):
        state_shape = (
            shape((8, query_rows * heads), f32),
            shape((HEAD_DIM + SUM_ROWS, query_rows * heads), f32),
        )
        return pl.pallas_call(
            functools.partial(attend_kernel, place_of, shards_of, not state, last),
            out_shape=shape(queries.shape, queries.dtype) if last else state_shape,
            in_specs=[vmem] * (4 + len(state) + len(pieces)),
            out_specs=vmem if last else (vmem, vmem),
            compiler_params=pltpu.CompilerParams(vmem_limit_bytes=limit),
            name="attend",
        )(*prepared, *state, *pieces)

    own = jnp.concatenate([cached_keys, cached_values], axis=0)
    if not direct:
        gathered = lax.all_gather(own, ("seg", "ctx"), axis=0, tiled=True)
        return attend(prepared, [gathered], None, (), True)

    def number(seg, ctx):
        return seg * n_ctx + ctx

    def whole(ref):
        return ref[:rows, :], ref[rows : 2 * rows, :]

    on_first = lax.axis_index("head") == 0
    first = exchange(own, lambda s, c, h: (s ^ (2 - 2 * h), c ^ h, h))
    second = exchange(own, lambda s, c, h: (s ^ (1 + 2 * h), c, h))
    half = lax.dynamic_slice_in_dim(own, lax.axis_index("head") * rows, rows, 0)
    third = exchange(half, lambda s, c, h: (s ^ 1, c ^ 1, h))
    first, prepared = lax.optimization_barrier((first, prepared))
    fourth = exchange(jnp.where(on_first, first, second), lambda s, c, h: (s, c ^ 1, h))
    first_beside = swap(first)
    state = attend(
        prepared,
        [own, first, first_beside],
        lambda refs, s, c, h: [
            (*whole(refs[0]), number(s, c)),
            (*whole(refs[1]), number(s ^ (2 - 2 * h), c ^ h)),
            (*whole(refs[2]), number(s ^ (2 * h), c ^ (1 - h))),
        ],
        (),
        False,
    )
    second, third, state = lax.optimization_barrier((second, third, state))
    second_beside = swap(jnp.concatenate([second, third], axis=0))
    fourth, state = lax.optimization_barrier((fourth, state))
    fourth_beside = swap(fourth)

    def middle_shards(refs, s, c, h):
        second, third, beside = refs
        mine, other = third[...], beside[2 * rows :, :]
        return [
            (*whole(second), number(s ^ (1 + 2 * h), c)),
            (*whole(beside), number(s ^ (3 - 2 * h), c)),
            (
                jnp.where(h == 0, mine, other),
                jnp.where(h == 0, other, mine),
                number(s ^ 1, c ^ 1),
            ),
        ]

    state = attend(prepared, [second, third, second_beside], middle_shards, state, False)
    return attend(
        prepared,
        [fourth, fourth_beside],
        lambda refs, s, c, h: [
            (*whole(refs[0]), number(s ^ (2 + h), c ^ 1)),
            (*whole(refs[1]), number(s ^ (3 - h), c ^ 1)),
        ],
        state,
        True,
    )


def solution(mesh):
    return jax.shard_map(
        local,
        mesh=mesh,
        in_specs=(
            P(("groups", "ctx"), "head"),
            P(("groups", "seg", "ctx"), None),
            P(("groups", "seg", "ctx"), None),
            P("groups"),
            P("groups", None),
            P("groups", None),
        ),
        out_specs=P(("groups", "ctx"), "head"),
        check_vma=False,
    )
```

```python
import functools
import math

import jax
import jax.numpy as jnp
import numpy as np
from jax import lax
from jax.experimental import pallas as pl
from jax.experimental.pallas import tpu as pltpu
from jax.sharding import PartitionSpec as P

HEAD_DIM = 128
BLOCK = 64
ROPE_THETA = 500000.0
ROPE_FACTOR = 8.0
LOW_FACTOR = 1.0
HIGH_FACTOR = 4.0
TRAINED_CONTEXT = 8192.0
MASKED_SCORE = -1e30
SCORE_SCALE = HEAD_DIM**-0.5 * math.log2(math.e)
TILE = 128
FINE = 16
SUM_ROWS = 16
DIRECT_SHARDS = (4, 2)
AXES = ("seg", "ctx", "head")


def frequency_row():
    exponent = np.arange(0, HEAD_DIM, 2, dtype=np.float64) / HEAD_DIM
    base = ROPE_THETA**-exponent
    wavelength = 2.0 * np.pi / base
    smooth = (TRAINED_CONTEXT / wavelength - LOW_FACTOR) / (HIGH_FACTOR - LOW_FACTOR)
    blended = (1.0 - smooth) * base / ROPE_FACTOR + smooth * base
    frequencies = np.where(
        wavelength < TRAINED_CONTEXT / HIGH_FACTOR,
        base,
        np.where(wavelength > TRAINED_CONTEXT / LOW_FACTOR, base / ROPE_FACTOR, blended),
    )
    return np.tile(frequencies, 2)[None, :].astype(np.float32)


def turned_sine(sine):
    lane = lax.broadcasted_iota(jnp.int32, sine.shape, 1)
    return jnp.where(lane < HEAD_DIM // 2, -sine, sine)


def rotate(vectors, cosine, signed_sine):
    wide = vectors.astype(jnp.float32)
    return (wide * cosine + pltpu.roll(wide, HEAD_DIM // 2, 1) * signed_sine).astype(jnp.bfloat16)


def angle_sum(cos_a, sin_a, cos_b, sin_b):
    return cos_a * cos_b - sin_a * sin_b, sin_a * cos_b + cos_a * sin_b


def shard_tables(cosines, sines, line, rows):
    cos_f, sin_f = cosines[pl.ds(0, FINE), :], turned_sine(sines[pl.ds(0, FINE), :])
    cos_c, sin_c = angle_sum(
        cosines[pl.ds(FINE, FINE), :],
        sines[pl.ds(FINE, FINE), :],
        cosines[pl.ds(line, 1), :],
        sines[pl.ds(line, 1), :],
    )
    signed = turned_sine(sin_c)
    parts = [
        (
            cos_f * cos_c[i : i + 1] - sin_f * signed[i : i + 1],
            sin_f * cos_c[i : i + 1] + cos_f * signed[i : i + 1],
        )
        for i in range(rows // FINE)
    ]
    return tuple(jnp.concatenate(table, axis=0) for table in zip(*parts))


def prepare_kernel(
    query_start_of, offsets, vertical, slash, queries, freq, rotated, cosines, sines, masks,
    angles, bias, held, arrival,
):
    query_rows, columns = held.shape
    heads = columns // HEAD_DIM
    fetch = pltpu.make_async_copy(queries, held, arrival)
    fetch.start()
    query_start, first_list = query_start_of()

    step = lax.broadcasted_iota(jnp.int32, (FINE, HEAD_DIM), 0)
    angles[pl.ds(0, FINE), :] = step
    angles[pl.ds(FINE, FINE), :] = step * FINE
    for shard in range(offsets.shape[0]):
        angles[pl.ds(2 * FINE + shard, 1), :] = jnp.full((1, HEAD_DIM), offsets[shard], jnp.int32)
    angles[pl.ds(angles.shape[0] - 8, 8), :] = jnp.full((8, HEAD_DIM), query_start, jnp.int32)
    angle = angles[...].astype(jnp.float32) * freq[...]
    cosines[...] = jnp.cos(angle)
    sines[...] = jnp.sin(angle)

    key_block = lax.broadcasted_iota(jnp.int32, bias.shape, 0)
    lane_block = lax.broadcasted_iota(jnp.int32, (1, query_rows), 1) // BLOCK
    hit = jnp.zeros(bias.shape, jnp.bool_)
    for entries, distance in ((vertical, False), (slash, True)):
        for entry in range(entries.shape[1]):
            wanted = jnp.zeros((1, query_rows), jnp.int32)
            for block in range(query_rows // BLOCK):
                value = entries[first_list + block, entry]
                if distance:
                    value = query_start // BLOCK + block - value
                wanted = jnp.where(lane_block == block, value, wanted)
            hit = hit | (key_block == wanted)
    bias[...] = jnp.where(hit, 0.0, MASKED_SCORE)

    rows = masks.shape[0] // offsets.shape[0]
    ahead = lax.broadcasted_iota(jnp.int32, (rows, query_rows), 1) - lax.broadcasted_iota(
        jnp.int32, (rows, query_rows), 0
    )

    @pl.loop(0, offsets.shape[0])
    def _(shard):
        offset = offsets[shard]
        lines = [
            jnp.broadcast_to(bias[pl.ds(offset // BLOCK + block, 1), :], (BLOCK, query_rows))
            for block in range(rows // BLOCK)
        ]
        masks[pl.ds(pl.multiple_of(shard * rows, rows), rows), :] = jnp.where(
            ahead >= offset - query_start, jnp.concatenate(lines, axis=0), MASKED_SCORE
        ).astype(masks.dtype)

    cosine, sine = shard_tables(cosines, sines, angles.shape[0] - 8, query_rows)
    fetch.wait()
    for head in range(heads):
        turned = rotate(held[:, pl.ds(head * HEAD_DIM, HEAD_DIM)], cosine, sine).T
        for tile in range(query_rows // TILE):
            lines = pl.ds((tile * heads + head) * TILE, TILE)
            rotated[:, lines] = turned[:, tile * TILE : (tile + 1) * TILE]


def attend_kernel(place_of, shards_of, first, last, *refs):
    rotated, cosines, sines, masks = refs[:4]
    refs = refs[4:]
    if not first:
        old_peak, old_sums = refs[:2]
        refs = refs[2:]
    if last:
        pieces, out = refs[:-1], refs[-1]
    else:
        pieces, new_peak, new_sums = refs[:-2], refs[-2], refs[-1]
    query_rows = masks.shape[1]
    tiles = query_rows // TILE
    width = rotated.shape[1] // tiles
    rows = masks.shape[0] // (cosines.shape[0] - 2 * FINE - 8)
    ones = jnp.ones((SUM_ROWS, rows), jnp.bfloat16)
    unit = (
        lax.broadcasted_iota(jnp.int32, (TILE, width), 0)
        == lax.broadcasted_iota(jnp.int32, (TILE, width), 1) % TILE
    ).astype(jnp.bfloat16)

    def load(keys, values, shard):
        keys = rotate(keys, *shard_tables(cosines, sines, 2 * FINE + shard, rows))
        mask = masks[pl.ds(pl.multiple_of(shard * rows, rows), rows), :]
        return keys, mask, jnp.concatenate([values.T, ones], axis=0)

    def update(loaded, tile, before):
        query = jnp.concatenate([rotated[:, pl.ds(tile * width, width)], unit], axis=0)
        scores = [
            jnp.dot(
                jnp.concatenate([keys, mask[:, tile * TILE : (tile + 1) * TILE]], axis=1),
                query,
                preferred_element_type=jnp.float32,
            )
            for keys, mask, _ in loaded
        ]
        peak = functools.reduce(jnp.maximum, [score.max(axis=0, keepdims=True) for score in scores])
        if before is not None:
            peak = jnp.maximum(before[0], peak)
        sums = functools.reduce(
            jnp.add,
            [
                jnp.dot(
                    values,
                    jnp.exp2((score - peak) * SCORE_SCALE).astype(jnp.bfloat16),
                    preferred_element_type=jnp.float32,
                )
                for score, (_, _, values) in zip(scores, loaded)
            ],
        )
        if before is not None:
            sums = sums + before[1] * jnp.exp2((before[0] - peak) * SCORE_SCALE)
        return peak, sums

    def finish(tile, peak, sums):
        if not last:
            span = pl.ds(tile * width, width)
            new_peak[:, span] = jnp.broadcast_to(peak, (new_peak.shape[0], width))
            new_sums[:, span] = sums
            return
        part = sums[:HEAD_DIM] * (1.0 / sums[HEAD_DIM : HEAD_DIM + 1])
        for head in range(width // TILE):
            out[pl.ds(tile * TILE, TILE), pl.ds(head * HEAD_DIM, HEAD_DIM)] = part[
                :, head * TILE : (head + 1) * TILE
            ].T.astype(out.dtype)

    if shards_of is not None:
        loaded = [
            load(keys, values, shard) for keys, values, shard in shards_of(pieces, *place_of())
        ]
        for tile in range(tiles):
            before = None
            if not first:
                span = pl.ds(tile * width, width)
                before = (old_peak[:1, span], old_sums[:, span])
            finish(tile, *update(loaded, tile, before))
    else:
        (whole,) = pieces
        for tile in range(tiles):

            def step(shard, before, tile=tile):
                start = pl.multiple_of(shard * (2 * rows), 2 * rows)
                piece = load(whole[pl.ds(start, rows), :], whole[pl.ds(start + rows, rows), :], shard)
                return update([piece], tile, before)

            initial = (
                jnp.full((1, width), MASKED_SCORE, jnp.float32),
                jnp.zeros((HEAD_DIM + SUM_ROWS, width), jnp.float32),
            )
            finish(tile, *lax.fori_loop(0, whole.shape[0] // (2 * rows), step, initial))


def local(queries, cached_keys, cached_values, key_offsets, vertical_blocks, slash_offsets):
    query_rows = queries.shape[0]
    heads = queries.shape[1] // HEAD_DIM
    rows = cached_keys.shape[0]
    n_seg, n_ctx = lax.axis_size("seg"), lax.axis_size("ctx")
    shards = n_seg * n_ctx
    prefix = rows * shards - query_rows * n_ctx

    def query_start_of():
        ctx = lax.axis_index("ctx")
        return prefix + ctx * query_rows, ctx * (query_rows // BLOCK)

    def place_of():
        return tuple(lax.axis_index(axis) for axis in AXES)

    def exchange(a, partner):
        pairs = []
        for seg in range(n_seg):
            for ctx in range(n_ctx):
                for head in range(2):
                    to_seg, to_ctx, to_head = partner(seg, ctx, head)
                    pairs.append(
                        ((seg * n_ctx + ctx) * 2 + head, (to_seg * n_ctx + to_ctx) * 2 + to_head)
                    )
        return lax.ppermute(a, AXES, pairs)

    def swap(a):
        return exchange(a, lambda s, c, h: (s, c, 1 - h))

    vmem = pl.BlockSpec(memory_space=pltpu.VMEM)
    smem = pl.BlockSpec(memory_space=pltpu.SMEM)
    f32 = jnp.float32
    direct = (n_seg, n_ctx) == DIRECT_SHARDS
    limit = (16 if direct else 56) * 1024 * 1024
    shape = jax.ShapeDtypeStruct
    lines = 2 * FINE + shards + 8
    prepared = pl.pallas_call(
        functools.partial(prepare_kernel, query_start_of),
        out_shape=(
            shape((HEAD_DIM, query_rows * heads), jnp.bfloat16),
            shape((lines, HEAD_DIM), f32),
            shape((lines, HEAD_DIM), f32),
            shape((shards * rows, query_rows), jnp.bfloat16),
        ),
        in_specs=[smem, smem, smem, pl.BlockSpec(memory_space=pltpu.HBM), vmem],
        out_specs=[vmem] * 4,
        scratch_shapes=[
            pltpu.VMEM((lines, HEAD_DIM), jnp.int32),
            pltpu.VMEM((shards * rows // BLOCK, query_rows), f32),
            pltpu.VMEM(queries.shape, queries.dtype),
            pltpu.SemaphoreType.DMA(()),
        ],
        compiler_params=pltpu.CompilerParams(vmem_limit_bytes=limit),
        name="prepare",
    )(key_offsets, vertical_blocks, slash_offsets, queries, jnp.asarray(frequency_row()))

    def attend(prepared, pieces, shards_of, state, last):
        state_shape = (
            shape((8, query_rows * heads), f32),
            shape((HEAD_DIM + SUM_ROWS, query_rows * heads), f32),
        )
        return pl.pallas_call(
            functools.partial(attend_kernel, place_of, shards_of, not state, last),
            out_shape=shape(queries.shape, queries.dtype) if last else state_shape,
            in_specs=[vmem] * (4 + len(state) + len(pieces)),
            out_specs=vmem if last else (vmem, vmem),
            compiler_params=pltpu.CompilerParams(vmem_limit_bytes=limit),
            name="attend",
        )(*prepared, *state, *pieces)

    own = jnp.concatenate([cached_keys, cached_values], axis=0)
    if not direct:
        gathered = lax.all_gather(own, ("seg", "ctx"), axis=0, tiled=True)
        return attend(prepared, [gathered], None, (), True)

    def number(seg, ctx):
        return seg * n_ctx + ctx

    def whole(ref):
        return ref[:rows, :], ref[rows : 2 * rows, :]

    on_first = lax.axis_index("head") == 0
    first = exchange(own, lambda s, c, h: (s ^ (2 - 2 * h), c ^ h, h))
    second = exchange(own, lambda s, c, h: (s ^ (1 + 2 * h), c, h))
    half = lax.dynamic_slice_in_dim(own, lax.axis_index("head") * rows, rows, 0)
    third = exchange(half, lambda s, c, h: (s ^ 1, c ^ 1, h))
    first, prepared = lax.optimization_barrier((first, prepared))
    fourth = exchange(jnp.where(on_first, first, second), lambda s, c, h: (s, c ^ 1, h))
    first_beside = swap(first)
    state = attend(
        prepared,
        [own, first, first_beside],
        lambda refs, s, c, h: [
            (*whole(refs[0]), number(s, c)),
            (*whole(refs[1]), number(s ^ (2 - 2 * h), c ^ h)),
            (*whole(refs[2]), number(s ^ (2 * h), c ^ (1 - h))),
        ],
        (),
        False,
    )
    second, third, state = lax.optimization_barrier((second, third, state))
    second_beside = swap(jnp.concatenate([second, third], axis=0))
    def middle_shards(refs, s, c, h):
        second, third, beside = refs
        mine, other = third[...], beside[2 * rows :, :]
        return [
            (*whole(second), number(s ^ (1 + 2 * h), c)),
            (*whole(beside), number(s ^ (3 - 2 * h), c)),
            (
                jnp.where(h == 0, mine, other),
                jnp.where(h == 0, other, mine),
                number(s ^ 1, c ^ 1),
            ),
        ]

    state = attend(prepared, [second, third, second_beside], middle_shards, state, False)
    fourth, state = lax.optimization_barrier((fourth, state))
    fourth_beside = swap(fourth)
    state = attend(
        prepared,
        [fourth],
        lambda refs, s, c, h: [(*whole(refs[0]), number(s ^ (2 + h), c ^ 1))],
        state,
        False,
    )
    return attend(
        prepared,
        [fourth_beside],
        lambda refs, s, c, h: [(*whole(refs[0]), number(s ^ (3 - h), c ^ 1))],
        state,
        True,
    )


def solution(mesh):
    return jax.shard_map(
        local,
        mesh=mesh,
        in_specs=(
            P(("groups", "ctx"), "head"),
            P(("groups", "seg", "ctx"), None),
            P(("groups", "seg", "ctx"), None),
            P("groups"),
            P("groups", None),
            P("groups", None),
        ),
        out_specs=P(("groups", "ctx"), "head"),
        check_vma=False,
    )
```

```python
import functools
import math

import jax
import jax.numpy as jnp
import numpy as np
from jax import lax
from jax.experimental import pallas as pl
from jax.experimental.pallas import tpu as pltpu
from jax.sharding import PartitionSpec as P

HEAD_DIM = 128
BLOCK = 64
ROPE_THETA = 500000.0
ROPE_FACTOR = 8.0
LOW_FACTOR = 1.0
HIGH_FACTOR = 4.0
TRAINED_CONTEXT = 8192.0
MASKED_SCORE = -1e30
SCORE_SCALE = HEAD_DIM**-0.5 * math.log2(math.e)
TILE = 128
FINE = 16
SUM_ROWS = 16
DIRECT_SHARDS = (4, 2)
AXES = ("seg", "ctx", "head")


def frequency_row():
    exponent = np.arange(0, HEAD_DIM, 2, dtype=np.float64) / HEAD_DIM
    base = ROPE_THETA**-exponent
    wavelength = 2.0 * np.pi / base
    smooth = (TRAINED_CONTEXT / wavelength - LOW_FACTOR) / (HIGH_FACTOR - LOW_FACTOR)
    blended = (1.0 - smooth) * base / ROPE_FACTOR + smooth * base
    frequencies = np.where(
        wavelength < TRAINED_CONTEXT / HIGH_FACTOR,
        base,
        np.where(wavelength > TRAINED_CONTEXT / LOW_FACTOR, base / ROPE_FACTOR, blended),
    )
    return np.tile(frequencies, 2)[None, :].astype(np.float32)


def turned_sine(sine):
    lane = lax.broadcasted_iota(jnp.int32, sine.shape, 1)
    return jnp.where(lane < HEAD_DIM // 2, -sine, sine)


def rotate(vectors, cosine, signed_sine):
    wide = vectors.astype(jnp.float32)
    return (wide * cosine + pltpu.roll(wide, HEAD_DIM // 2, 1) * signed_sine).astype(jnp.bfloat16)


def angle_sum(cos_a, sin_a, cos_b, sin_b):
    return cos_a * cos_b - sin_a * sin_b, sin_a * cos_b + cos_a * sin_b


def shard_tables(cosines, sines, line, rows):
    cos_f, sin_f = cosines[pl.ds(0, FINE), :], turned_sine(sines[pl.ds(0, FINE), :])
    cos_c, sin_c = angle_sum(
        cosines[pl.ds(FINE, FINE), :],
        sines[pl.ds(FINE, FINE), :],
        cosines[pl.ds(line, 1), :],
        sines[pl.ds(line, 1), :],
    )
    signed = turned_sine(sin_c)
    parts = [
        (
            cos_f * cos_c[i : i + 1] - sin_f * signed[i : i + 1],
            sin_f * cos_c[i : i + 1] + cos_f * signed[i : i + 1],
        )
        for i in range(rows // FINE)
    ]
    return tuple(jnp.concatenate(table, axis=0) for table in zip(*parts))


def prepare_kernel(
    query_start_of, offsets, vertical, slash, queries, freq, rotated, cosines, sines, masks,
    angles, bias, held, arrival,
):
    query_rows, columns = held.shape
    heads = columns // HEAD_DIM
    fetch = pltpu.make_async_copy(queries, held, arrival)
    fetch.start()
    query_start, first_list = query_start_of()

    step = lax.broadcasted_iota(jnp.int32, (FINE, HEAD_DIM), 0)
    angles[pl.ds(0, FINE), :] = step
    angles[pl.ds(FINE, FINE), :] = step * FINE
    for shard in range(offsets.shape[0]):
        angles[pl.ds(2 * FINE + shard, 1), :] = jnp.full((1, HEAD_DIM), offsets[shard], jnp.int32)
    angles[pl.ds(angles.shape[0] - 8, 8), :] = jnp.full((8, HEAD_DIM), query_start, jnp.int32)
    angle = angles[...].astype(jnp.float32) * freq[...]
    cosines[...] = jnp.cos(angle)
    sines[...] = jnp.sin(angle)

    key_block = lax.broadcasted_iota(jnp.int32, bias.shape, 0)
    lane_block = lax.broadcasted_iota(jnp.int32, (1, query_rows), 1) // BLOCK
    hit = jnp.zeros(bias.shape, jnp.bool_)
    for entries, distance in ((vertical, False), (slash, True)):
        for entry in range(entries.shape[1]):
            wanted = jnp.zeros((1, query_rows), jnp.int32)
            for block in range(query_rows // BLOCK):
                value = entries[first_list + block, entry]
                if distance:
                    value = query_start // BLOCK + block - value
                wanted = jnp.where(lane_block == block, value, wanted)
            hit = hit | (key_block == wanted)
    bias[...] = jnp.where(hit, 0.0, MASKED_SCORE)

    rows = masks.shape[0] // offsets.shape[0]
    ahead = lax.broadcasted_iota(jnp.int32, (rows, query_rows), 1) - lax.broadcasted_iota(
        jnp.int32, (rows, query_rows), 0
    )

    @pl.loop(0, offsets.shape[0])
    def _(shard):
        offset = offsets[shard]
        lines = [
            jnp.broadcast_to(bias[pl.ds(offset // BLOCK + block, 1), :], (BLOCK, query_rows))
            for block in range(rows // BLOCK)
        ]
        masks[pl.ds(pl.multiple_of(shard * rows, rows), rows), :] = jnp.where(
            ahead >= offset - query_start, jnp.concatenate(lines, axis=0), MASKED_SCORE
        ).astype(masks.dtype)

    cosine, sine = shard_tables(cosines, sines, angles.shape[0] - 8, query_rows)
    fetch.wait()
    for head in range(heads):
        turned = rotate(held[:, pl.ds(head * HEAD_DIM, HEAD_DIM)], cosine, sine).T
        for tile in range(query_rows // TILE):
            lines = pl.ds((tile * heads + head) * TILE, TILE)
            rotated[:, lines] = turned[:, tile * TILE : (tile + 1) * TILE]


def attend_kernel(place_of, shards_of, first, last, *refs):
    rotated, cosines, sines, masks = refs[:4]
    refs = refs[4:]
    if not first:
        old_peak, old_sums = refs[:2]
        refs = refs[2:]
    if last:
        pieces, out = refs[:-1], refs[-1]
    else:
        pieces, new_peak, new_sums = refs[:-2], refs[-2], refs[-1]
    query_rows = masks.shape[1]
    tiles = query_rows // TILE
    width = rotated.shape[1] // tiles
    rows = masks.shape[0] // (cosines.shape[0] - 2 * FINE - 8)
    ones = jnp.ones((SUM_ROWS, rows), jnp.bfloat16)
    unit = (
        lax.broadcasted_iota(jnp.int32, (TILE, width), 0)
        == lax.broadcasted_iota(jnp.int32, (TILE, width), 1) % TILE
    ).astype(jnp.bfloat16)

    def load(keys, values, shard):
        keys = rotate(keys, *shard_tables(cosines, sines, 2 * FINE + shard, rows))
        mask = masks[pl.ds(pl.multiple_of(shard * rows, rows), rows), :]
        return keys, mask, jnp.concatenate([values.T, ones], axis=0)

    def update(loaded, tile, before):
        query = jnp.concatenate([rotated[:, pl.ds(tile * width, width)], unit], axis=0)
        scores = [
            jnp.dot(
                jnp.concatenate([keys, mask[:, tile * TILE : (tile + 1) * TILE]], axis=1),
                query,
                preferred_element_type=jnp.float32,
            )
            for keys, mask, _ in loaded
        ]
        peak = functools.reduce(jnp.maximum, [score.max(axis=0, keepdims=True) for score in scores])
        if before is not None:
            peak = jnp.maximum(before[0], peak)
        sums = functools.reduce(
            jnp.add,
            [
                jnp.dot(
                    values,
                    jnp.exp2((score - peak) * SCORE_SCALE).astype(jnp.bfloat16),
                    preferred_element_type=jnp.float32,
                )
                for score, (_, _, values) in zip(scores, loaded)
            ],
        )
        if before is not None:
            sums = sums + before[1] * jnp.exp2((before[0] - peak) * SCORE_SCALE)
        return peak, sums

    def finish(tile, peak, sums):
        if not last:
            span = pl.ds(tile * width, width)
            new_peak[:, span] = jnp.broadcast_to(peak, (new_peak.shape[0], width))
            new_sums[:, span] = sums
            return
        part = sums[:HEAD_DIM] * (1.0 / sums[HEAD_DIM : HEAD_DIM + 1])
        part = part.astype(out.dtype)
        for head in range(width // TILE):
            out[pl.ds(tile * TILE, TILE), pl.ds(head * HEAD_DIM, HEAD_DIM)] = part[
                :, head * TILE : (head + 1) * TILE
            ].T

    if shards_of is not None:
        loaded = [
            load(keys, values, shard) for keys, values, shard in shards_of(pieces, *place_of())
        ]
        for tile in range(tiles):
            before = None
            if not first:
                span = pl.ds(tile * width, width)
                before = (old_peak[:1, span], old_sums[:, span])
            finish(tile, *update(loaded, tile, before))
    else:
        (whole,) = pieces
        for tile in range(tiles):

            def step(shard, before, tile=tile):
                start = pl.multiple_of(shard * (2 * rows), 2 * rows)
                piece = load(whole[pl.ds(start, rows), :], whole[pl.ds(start + rows, rows), :], shard)
                return update([piece], tile, before)

            initial = (
                jnp.full((1, width), MASKED_SCORE, jnp.float32),
                jnp.zeros((HEAD_DIM + SUM_ROWS, width), jnp.float32),
            )
            finish(tile, *lax.fori_loop(0, whole.shape[0] // (2 * rows), step, initial))


def local(queries, cached_keys, cached_values, key_offsets, vertical_blocks, slash_offsets):
    query_rows = queries.shape[0]
    heads = queries.shape[1] // HEAD_DIM
    rows = cached_keys.shape[0]
    n_seg, n_ctx = lax.axis_size("seg"), lax.axis_size("ctx")
    shards = n_seg * n_ctx
    prefix = rows * shards - query_rows * n_ctx

    def query_start_of():
        ctx = lax.axis_index("ctx")
        return prefix + ctx * query_rows, ctx * (query_rows // BLOCK)

    def place_of():
        return tuple(lax.axis_index(axis) for axis in AXES)

    def exchange(a, partner):
        pairs = []
        for seg in range(n_seg):
            for ctx in range(n_ctx):
                for head in range(2):
                    to_seg, to_ctx, to_head = partner(seg, ctx, head)
                    pairs.append(
                        ((seg * n_ctx + ctx) * 2 + head, (to_seg * n_ctx + to_ctx) * 2 + to_head)
                    )
        return lax.ppermute(a, AXES, pairs)

    def swap(a):
        return exchange(a, lambda s, c, h: (s, c, 1 - h))

    vmem = pl.BlockSpec(memory_space=pltpu.VMEM)
    smem = pl.BlockSpec(memory_space=pltpu.SMEM)
    f32 = jnp.float32
    direct = (n_seg, n_ctx) == DIRECT_SHARDS
    limit = (16 if direct else 56) * 1024 * 1024
    shape = jax.ShapeDtypeStruct
    lines = 2 * FINE + shards + 8
    prepared = pl.pallas_call(
        functools.partial(prepare_kernel, query_start_of),
        out_shape=(
            shape((HEAD_DIM, query_rows * heads), jnp.bfloat16),
            shape((lines, HEAD_DIM), f32),
            shape((lines, HEAD_DIM), f32),
            shape((shards * rows, query_rows), jnp.bfloat16),
        ),
        in_specs=[smem, smem, smem, pl.BlockSpec(memory_space=pltpu.HBM), vmem],
        out_specs=[vmem] * 4,
        scratch_shapes=[
            pltpu.VMEM((lines, HEAD_DIM), jnp.int32),
            pltpu.VMEM((shards * rows // BLOCK, query_rows), f32),
            pltpu.VMEM(queries.shape, queries.dtype),
            pltpu.SemaphoreType.DMA(()),
        ],
        compiler_params=pltpu.CompilerParams(vmem_limit_bytes=limit),
        name="prepare",
    )(key_offsets, vertical_blocks, slash_offsets, queries, jnp.asarray(frequency_row()))

    def attend(prepared, pieces, shards_of, state, last):
        state_shape = (
            shape((8, query_rows * heads), f32),
            shape((HEAD_DIM + SUM_ROWS, query_rows * heads), f32),
        )
        return pl.pallas_call(
            functools.partial(attend_kernel, place_of, shards_of, not state, last),
            out_shape=shape(queries.shape, queries.dtype) if last else state_shape,
            in_specs=[vmem] * (4 + len(state) + len(pieces)),
            out_specs=vmem if last else (vmem, vmem),
            compiler_params=pltpu.CompilerParams(vmem_limit_bytes=limit),
            name="attend",
        )(*prepared, *state, *pieces)

    own = jnp.concatenate([cached_keys, cached_values], axis=0)
    if not direct:
        gathered = lax.all_gather(own, ("seg", "ctx"), axis=0, tiled=True)
        return attend(prepared, [gathered], None, (), True)

    def number(seg, ctx):
        return seg * n_ctx + ctx

    def whole(ref):
        return ref[:rows, :], ref[rows : 2 * rows, :]

    on_first = lax.axis_index("head") == 0
    first = exchange(own, lambda s, c, h: (s ^ (2 - 2 * h), c ^ h, h))
    second = exchange(own, lambda s, c, h: (s ^ (1 + 2 * h), c, h))
    half = lax.dynamic_slice_in_dim(own, lax.axis_index("head") * rows, rows, 0)
    third = exchange(half, lambda s, c, h: (s ^ 1, c ^ 1, h))
    first, prepared = lax.optimization_barrier((first, prepared))
    fourth = exchange(jnp.where(on_first, first, second), lambda s, c, h: (s, c ^ 1, h))
    first_beside = swap(first)
    state = attend(
        prepared,
        [own, first, first_beside, second],
        lambda refs, s, c, h: [
            (*whole(refs[0]), number(s, c)),
            (*whole(refs[1]), number(s ^ (2 - 2 * h), c ^ h)),
            (*whole(refs[2]), number(s ^ (2 * h), c ^ (1 - h))),
            (*whole(refs[3]), number(s ^ (1 + 2 * h), c)),
        ],
        (),
        False,
    )
    second, third, state = lax.optimization_barrier((second, third, state))
    second_beside = swap(jnp.concatenate([second, third], axis=0))
    fourth, state = lax.optimization_barrier((fourth, state))
    fourth_beside = swap(fourth)

    def middle_shards(refs, s, c, h):
        third, beside = refs
        mine, other = third[...], beside[2 * rows :, :]
        return [
            (*whole(beside), number(s ^ (3 - 2 * h), c)),
            (
                jnp.where(h == 0, mine, other),
                jnp.where(h == 0, other, mine),
                number(s ^ 1, c ^ 1),
            ),
        ]

    state = attend(prepared, [third, second_beside], middle_shards, state, False)
    return attend(
        prepared,
        [fourth, fourth_beside],
        lambda refs, s, c, h: [
            (*whole(refs[0]), number(s ^ (2 + h), c ^ 1)),
            (*whole(refs[1]), number(s ^ (3 - h), c ^ 1)),
        ],
        state,
        True,
    )


def solution(mesh):
    return jax.shard_map(
        local,
        mesh=mesh,
        in_specs=(
            P(("groups", "ctx"), "head"),
            P(("groups", "seg", "ctx"), None),
            P(("groups", "seg", "ctx"), None),
            P("groups"),
            P("groups", None),
            P("groups", None),
        ),
        out_specs=P(("groups", "ctx"), "head"),
        check_vma=False,
    )
```

```python
import functools
import math

import jax
import jax.numpy as jnp
import numpy as np
from jax import lax
from jax.experimental import pallas as pl
from jax.experimental.pallas import tpu as pltpu
from jax.sharding import PartitionSpec as P

HEAD_DIM = 128
BLOCK = 64
ROPE_THETA = 500000.0
ROPE_FACTOR = 8.0
LOW_FACTOR = 1.0
HIGH_FACTOR = 4.0
TRAINED_CONTEXT = 8192.0
MASKED_SCORE = -1e30
SCORE_SCALE = HEAD_DIM**-0.5 * math.log2(math.e)
TILE = 128
FINE = 16
SUM_ROWS = 16
DIRECT_SHARDS = (4, 2)
AXES = ("seg", "ctx", "head")


def frequency_row():
    exponent = np.arange(0, HEAD_DIM, 2, dtype=np.float64) / HEAD_DIM
    base = ROPE_THETA**-exponent
    wavelength = 2.0 * np.pi / base
    smooth = (TRAINED_CONTEXT / wavelength - LOW_FACTOR) / (HIGH_FACTOR - LOW_FACTOR)
    blended = (1.0 - smooth) * base / ROPE_FACTOR + smooth * base
    frequencies = np.where(
        wavelength < TRAINED_CONTEXT / HIGH_FACTOR,
        base,
        np.where(wavelength > TRAINED_CONTEXT / LOW_FACTOR, base / ROPE_FACTOR, blended),
    )
    return np.tile(frequencies, 2)[None, :].astype(np.float32)


def turned_sine(sine):
    lane = lax.broadcasted_iota(jnp.int32, sine.shape, 1)
    return jnp.where(lane < HEAD_DIM // 2, -sine, sine)


def rotate(vectors, cosine, signed_sine):
    wide = vectors.astype(jnp.float32)
    return (wide * cosine + pltpu.roll(wide, HEAD_DIM // 2, 1) * signed_sine).astype(jnp.bfloat16)


def angle_sum(cos_a, sin_a, cos_b, sin_b):
    return cos_a * cos_b - sin_a * sin_b, sin_a * cos_b + cos_a * sin_b


def shard_tables(cosines, sines, line, rows):
    cos_f, sin_f = cosines[pl.ds(0, FINE), :], turned_sine(sines[pl.ds(0, FINE), :])
    cos_c, sin_c = angle_sum(
        cosines[pl.ds(FINE, FINE), :],
        sines[pl.ds(FINE, FINE), :],
        cosines[pl.ds(line, 1), :],
        sines[pl.ds(line, 1), :],
    )
    signed = turned_sine(sin_c)
    parts = [
        (
            cos_f * cos_c[i : i + 1] - sin_f * signed[i : i + 1],
            sin_f * cos_c[i : i + 1] + cos_f * signed[i : i + 1],
        )
        for i in range(rows // FINE)
    ]
    return tuple(jnp.concatenate(table, axis=0) for table in zip(*parts))


def prepare_kernel(
    query_start_of, offsets, vertical, slash, queries, freq, rotated, cosines, sines, masks,
    angles, bias, held, arrival,
):
    query_rows, columns = held.shape
    heads = columns // HEAD_DIM
    fetch = pltpu.make_async_copy(queries, held, arrival)
    fetch.start()
    query_start, first_list = query_start_of()

    step = lax.broadcasted_iota(jnp.int32, (FINE, HEAD_DIM), 0)
    angles[pl.ds(0, FINE), :] = step
    angles[pl.ds(FINE, FINE), :] = step * FINE
    for shard in range(offsets.shape[0]):
        angles[pl.ds(2 * FINE + shard, 1), :] = jnp.full((1, HEAD_DIM), offsets[shard], jnp.int32)
    angles[pl.ds(angles.shape[0] - 8, 8), :] = jnp.full((8, HEAD_DIM), query_start, jnp.int32)
    angle = angles[...].astype(jnp.float32) * freq[...]
    cosines[...] = jnp.cos(angle)
    sines[...] = jnp.sin(angle)

    key_block = lax.broadcasted_iota(jnp.int32, bias.shape, 0)
    lane_block = lax.broadcasted_iota(jnp.int32, (1, query_rows), 1) // BLOCK
    hit = jnp.zeros(bias.shape, jnp.bool_)
    for entries, distance in ((vertical, False), (slash, True)):
        for entry in range(entries.shape[1]):
            wanted = jnp.zeros((1, query_rows), jnp.int32)
            for block in range(query_rows // BLOCK):
                value = entries[first_list + block, entry]
                if distance:
                    value = query_start // BLOCK + block - value
                wanted = jnp.where(lane_block == block, value, wanted)
            hit = hit | (key_block == wanted)
    bias[...] = jnp.where(hit, 0.0, MASKED_SCORE)

    rows = masks.shape[0] // offsets.shape[0]
    ahead = lax.broadcasted_iota(jnp.int32, (rows, query_rows), 1) - lax.broadcasted_iota(
        jnp.int32, (rows, query_rows), 0
    )

    @pl.loop(0, offsets.shape[0])
    def _(shard):
        offset = offsets[shard]
        lines = [
            jnp.broadcast_to(bias[pl.ds(offset // BLOCK + block, 1), :], (BLOCK, query_rows))
            for block in range(rows // BLOCK)
        ]
        masks[pl.ds(pl.multiple_of(shard * rows, rows), rows), :] = jnp.where(
            ahead >= offset - query_start, jnp.concatenate(lines, axis=0), MASKED_SCORE
        ).astype(masks.dtype)

    cosine, sine = shard_tables(cosines, sines, angles.shape[0] - 8, query_rows)
    fetch.wait()
    for head in range(heads):
        turned = rotate(held[:, pl.ds(head * HEAD_DIM, HEAD_DIM)], cosine, sine).T
        for tile in range(query_rows // TILE):
            lines = pl.ds((tile * heads + head) * TILE, TILE)
            rotated[:, lines] = turned[:, tile * TILE : (tile + 1) * TILE]


def attend_kernel(place_of, shards_of, first, last, *refs):
    rotated, cosines, sines, masks = refs[:4]
    refs = refs[4:]
    if not first:
        old_peak, old_sums = refs[:2]
        refs = refs[2:]
    if last:
        pieces, out = refs[:-1], refs[-1]
    else:
        pieces, new_peak, new_sums = refs[:-2], refs[-2], refs[-1]
    query_rows = masks.shape[1]
    tiles = query_rows // TILE
    width = rotated.shape[1] // tiles
    rows = masks.shape[0] // (cosines.shape[0] - 2 * FINE - 8)
    ones = jnp.ones((SUM_ROWS, rows), jnp.bfloat16)
    unit = (
        lax.broadcasted_iota(jnp.int32, (TILE, width), 0)
        == lax.broadcasted_iota(jnp.int32, (TILE, width), 1) % TILE
    ).astype(jnp.bfloat16)

    def load(keys, values, shard):
        keys = rotate(keys, *shard_tables(cosines, sines, 2 * FINE + shard, rows))
        mask = masks[pl.ds(pl.multiple_of(shard * rows, rows), rows), :]
        return keys, mask, jnp.concatenate([values.T, ones], axis=0)

    def joined(loaded):
        keys, masks, values = zip(*loaded)
        return (
            jnp.concatenate(keys, axis=0),
            jnp.concatenate(masks, axis=0),
            jnp.concatenate(values, axis=1),
        )

    def update(keys, mask, values, tile, before):
        query = jnp.concatenate([rotated[:, pl.ds(tile * width, width)], unit], axis=0)
        scores = jnp.dot(
            jnp.concatenate([keys, mask[:, tile * TILE : (tile + 1) * TILE]], axis=1),
            query,
            preferred_element_type=jnp.float32,
        )
        peak = scores.max(axis=0, keepdims=True)
        if before is not None:
            peak = jnp.maximum(before[0], peak)
        weights = jnp.exp2((scores - peak) * SCORE_SCALE).astype(jnp.bfloat16)
        sums = jnp.dot(values, weights, preferred_element_type=jnp.float32)
        if before is not None:
            sums = sums + before[1] * jnp.exp2((before[0] - peak) * SCORE_SCALE)
        return peak, sums

    def finish(tile, peak, sums):
        if not last:
            span = pl.ds(tile * width, width)
            new_peak[:, span] = jnp.broadcast_to(peak, (new_peak.shape[0], width))
            new_sums[:, span] = sums
            return
        part = sums[:HEAD_DIM] * (1.0 / sums[HEAD_DIM : HEAD_DIM + 1])
        part = part.astype(out.dtype)
        for head in range(width // TILE):
            out[pl.ds(tile * TILE, TILE), pl.ds(head * HEAD_DIM, HEAD_DIM)] = part[
                :, head * TILE : (head + 1) * TILE
            ].T

    if shards_of is not None:
        loaded = joined(
            [load(keys, values, shard) for keys, values, shard in shards_of(pieces, *place_of())]
        )
        for tile in range(tiles):
            before = None
            if not first:
                span = pl.ds(tile * width, width)
                before = (old_peak[:1, span], old_sums[:, span])
            finish(tile, *update(*loaded, tile, before))
    else:
        (whole,) = pieces
        for tile in range(tiles):

            def step(shard, before, tile=tile):
                start = pl.multiple_of(shard * (2 * rows), 2 * rows)
                piece = load(whole[pl.ds(start, rows), :], whole[pl.ds(start + rows, rows), :], shard)
                return update(*piece, tile, before)

            initial = (
                jnp.full((1, width), MASKED_SCORE, jnp.float32),
                jnp.zeros((HEAD_DIM + SUM_ROWS, width), jnp.float32),
            )
            finish(tile, *lax.fori_loop(0, whole.shape[0] // (2 * rows), step, initial))


def local(queries, cached_keys, cached_values, key_offsets, vertical_blocks, slash_offsets):
    query_rows = queries.shape[0]
    heads = queries.shape[1] // HEAD_DIM
    rows = cached_keys.shape[0]
    n_seg, n_ctx = lax.axis_size("seg"), lax.axis_size("ctx")
    shards = n_seg * n_ctx
    prefix = rows * shards - query_rows * n_ctx

    def query_start_of():
        ctx = lax.axis_index("ctx")
        return prefix + ctx * query_rows, ctx * (query_rows // BLOCK)

    def place_of():
        return tuple(lax.axis_index(axis) for axis in AXES)

    def exchange(a, partner):
        pairs = []
        for seg in range(n_seg):
            for ctx in range(n_ctx):
                for head in range(2):
                    to_seg, to_ctx, to_head = partner(seg, ctx, head)
                    pairs.append(
                        ((seg * n_ctx + ctx) * 2 + head, (to_seg * n_ctx + to_ctx) * 2 + to_head)
                    )
        return lax.ppermute(a, AXES, pairs)

    def swap(a):
        return exchange(a, lambda s, c, h: (s, c, 1 - h))

    vmem = pl.BlockSpec(memory_space=pltpu.VMEM)
    smem = pl.BlockSpec(memory_space=pltpu.SMEM)
    f32 = jnp.float32
    direct = (n_seg, n_ctx) == DIRECT_SHARDS
    limit = (16 if direct else 56) * 1024 * 1024
    shape = jax.ShapeDtypeStruct
    lines = 2 * FINE + shards + 8
    prepared = pl.pallas_call(
        functools.partial(prepare_kernel, query_start_of),
        out_shape=(
            shape((HEAD_DIM, query_rows * heads), jnp.bfloat16),
            shape((lines, HEAD_DIM), f32),
            shape((lines, HEAD_DIM), f32),
            shape((shards * rows, query_rows), jnp.bfloat16),
        ),
        in_specs=[smem, smem, smem, pl.BlockSpec(memory_space=pltpu.HBM), vmem],
        out_specs=[vmem] * 4,
        scratch_shapes=[
            pltpu.VMEM((lines, HEAD_DIM), jnp.int32),
            pltpu.VMEM((shards * rows // BLOCK, query_rows), f32),
            pltpu.VMEM(queries.shape, queries.dtype),
            pltpu.SemaphoreType.DMA(()),
        ],
        compiler_params=pltpu.CompilerParams(vmem_limit_bytes=limit),
        name="prepare",
    )(key_offsets, vertical_blocks, slash_offsets, queries, jnp.asarray(frequency_row()))

    def attend(prepared, pieces, shards_of, state, last):
        state_shape = (
            shape((8, query_rows * heads), f32),
            shape((HEAD_DIM + SUM_ROWS, query_rows * heads), f32),
        )
        return pl.pallas_call(
            functools.partial(attend_kernel, place_of, shards_of, not state, last),
            out_shape=shape(queries.shape, queries.dtype) if last else state_shape,
            in_specs=[vmem] * (4 + len(state) + len(pieces)),
            out_specs=vmem if last else (vmem, vmem),
            compiler_params=pltpu.CompilerParams(vmem_limit_bytes=limit),
            name="attend",
        )(*prepared, *state, *pieces)

    own = jnp.concatenate([cached_keys, cached_values], axis=0)
    if not direct:
        gathered = lax.all_gather(own, ("seg", "ctx"), axis=0, tiled=True)
        return attend(prepared, [gathered], None, (), True)

    def number(seg, ctx):
        return seg * n_ctx + ctx

    def whole(ref):
        return ref[:rows, :], ref[rows : 2 * rows, :]

    on_first = lax.axis_index("head") == 0
    first = exchange(own, lambda s, c, h: (s ^ (2 - 2 * h), c ^ h, h))
    second = exchange(own, lambda s, c, h: (s ^ (1 + 2 * h), c, h))
    half = lax.dynamic_slice_in_dim(own, lax.axis_index("head") * rows, rows, 0)
    third = exchange(half, lambda s, c, h: (s ^ 1, c ^ 1, h))
    first, prepared = lax.optimization_barrier((first, prepared))
    fourth = exchange(jnp.where(on_first, first, second), lambda s, c, h: (s, c ^ 1, h))
    first_beside = swap(first)
    state = attend(
        prepared,
        [own, first, first_beside, second],
        lambda refs, s, c, h: [
            (*whole(refs[0]), number(s, c)),
            (*whole(refs[1]), number(s ^ (2 - 2 * h), c ^ h)),
            (*whole(refs[2]), number(s ^ (2 * h), c ^ (1 - h))),
            (*whole(refs[3]), number(s ^ (1 + 2 * h), c)),
        ],
        (),
        False,
    )
    second, third, state = lax.optimization_barrier((second, third, state))
    second_beside = swap(jnp.concatenate([second, third], axis=0))
    fourth, state = lax.optimization_barrier((fourth, state))
    fourth_beside = swap(fourth)

    def middle_shards(refs, s, c, h):
        third, beside = refs
        mine, other = third[...], beside[2 * rows :, :]
        return [
            (*whole(beside), number(s ^ (3 - 2 * h), c)),
            (
                jnp.where(h == 0, mine, other),
                jnp.where(h == 0, other, mine),
                number(s ^ 1, c ^ 1),
            ),
        ]

    state = attend(prepared, [third, second_beside], middle_shards, state, False)
    return attend(
        prepared,
        [fourth, fourth_beside],
        lambda refs, s, c, h: [
            (*whole(refs[0]), number(s ^ (2 + h), c ^ 1)),
            (*whole(refs[1]), number(s ^ (3 - h), c ^ 1)),
        ],
        state,
        True,
    )


def solution(mesh):
    return jax.shard_map(
        local,
        mesh=mesh,
        in_specs=(
            P(("groups", "ctx"), "head"),
            P(("groups", "seg", "ctx"), None),
            P(("groups", "seg", "ctx"), None),
            P("groups"),
            P("groups", None),
            P("groups", None),
        ),
        out_specs=P(("groups", "ctx"), "head"),
        check_vma=False,
    )
```

```python
import functools
import math

import jax
import jax.numpy as jnp
import numpy as np
from jax import lax
from jax.experimental import pallas as pl
from jax.experimental.pallas import tpu as pltpu
from jax.sharding import PartitionSpec as P

HEAD_DIM = 128
BLOCK = 64
ROPE_THETA = 500000.0
ROPE_FACTOR = 8.0
LOW_FACTOR = 1.0
HIGH_FACTOR = 4.0
TRAINED_CONTEXT = 8192.0
MASKED_SCORE = -1e30
SCORE_SCALE = HEAD_DIM**-0.5 * math.log2(math.e)
TILE = 128
FINE = 16
SUM_ROWS = 16
DIRECT_SHARDS = (4, 2)
AXES = ("seg", "ctx", "head")


def frequency_row():
    exponent = np.arange(0, HEAD_DIM, 2, dtype=np.float64) / HEAD_DIM
    base = ROPE_THETA**-exponent
    wavelength = 2.0 * np.pi / base
    smooth = (TRAINED_CONTEXT / wavelength - LOW_FACTOR) / (HIGH_FACTOR - LOW_FACTOR)
    blended = (1.0 - smooth) * base / ROPE_FACTOR + smooth * base
    frequencies = np.where(
        wavelength < TRAINED_CONTEXT / HIGH_FACTOR,
        base,
        np.where(wavelength > TRAINED_CONTEXT / LOW_FACTOR, base / ROPE_FACTOR, blended),
    )
    return np.tile(frequencies, 2)[None, :].astype(np.float32)


def turned_sine(sine):
    lane = lax.broadcasted_iota(jnp.int32, sine.shape, 1)
    return jnp.where(lane < HEAD_DIM // 2, -sine, sine)


def rotate(vectors, cosine, signed_sine):
    wide = vectors.astype(jnp.float32)
    return (wide * cosine + pltpu.roll(wide, HEAD_DIM // 2, 1) * signed_sine).astype(jnp.bfloat16)


def angle_sum(cos_a, sin_a, cos_b, sin_b):
    return cos_a * cos_b - sin_a * sin_b, sin_a * cos_b + cos_a * sin_b


def shard_tables(cosines, sines, line, rows):
    cos_f, sin_f = cosines[pl.ds(0, FINE), :], turned_sine(sines[pl.ds(0, FINE), :])
    cos_c, sin_c = angle_sum(
        cosines[pl.ds(FINE, FINE), :],
        sines[pl.ds(FINE, FINE), :],
        cosines[pl.ds(line, 1), :],
        sines[pl.ds(line, 1), :],
    )
    signed = turned_sine(sin_c)
    parts = [
        (
            cos_f * cos_c[i : i + 1] - sin_f * signed[i : i + 1],
            sin_f * cos_c[i : i + 1] + cos_f * signed[i : i + 1],
        )
        for i in range(rows // FINE)
    ]
    return tuple(jnp.concatenate(table, axis=0) for table in zip(*parts))


def prepare_kernel(
    query_start_of, offsets, vertical, slash, queries, freq, rotated, cosines, sines, masks,
    angles, bias, held, arrival,
):
    query_rows, columns = held.shape
    heads = columns // HEAD_DIM
    fetch = pltpu.make_async_copy(queries, held, arrival)
    fetch.start()
    query_start, first_list = query_start_of()

    step = lax.broadcasted_iota(jnp.int32, (FINE, HEAD_DIM), 0)
    angles[pl.ds(0, FINE), :] = step
    angles[pl.ds(FINE, FINE), :] = step * FINE
    for shard in range(offsets.shape[0]):
        angles[pl.ds(2 * FINE + shard, 1), :] = jnp.full((1, HEAD_DIM), offsets[shard], jnp.int32)
    angles[pl.ds(angles.shape[0] - 8, 8), :] = jnp.full((8, HEAD_DIM), query_start, jnp.int32)
    angle = angles[...].astype(jnp.float32) * freq[...]
    cosines[...] = jnp.cos(angle)
    sines[...] = jnp.sin(angle)

    key_block = lax.broadcasted_iota(jnp.int32, bias.shape, 0)
    lane_block = lax.broadcasted_iota(jnp.int32, (1, query_rows), 1) // BLOCK
    hit = jnp.zeros(bias.shape, jnp.bool_)
    for entries, distance in ((vertical, False), (slash, True)):
        for entry in range(entries.shape[1]):
            wanted = jnp.zeros((1, query_rows), jnp.int32)
            for block in range(query_rows // BLOCK):
                value = entries[first_list + block, entry]
                if distance:
                    value = query_start // BLOCK + block - value
                wanted = jnp.where(lane_block == block, value, wanted)
            hit = hit | (key_block == wanted)
    bias[...] = jnp.where(hit, 0.0, MASKED_SCORE)

    rows = masks.shape[0] // offsets.shape[0]
    ahead = lax.broadcasted_iota(jnp.int32, (rows, query_rows), 1) - lax.broadcasted_iota(
        jnp.int32, (rows, query_rows), 0
    )

    @pl.loop(0, offsets.shape[0])
    def _(shard):
        offset = offsets[shard]
        lines = [
            jnp.broadcast_to(bias[pl.ds(offset // BLOCK + block, 1), :], (BLOCK, query_rows))
            for block in range(rows // BLOCK)
        ]
        masks[pl.ds(pl.multiple_of(shard * rows, rows), rows), :] = jnp.where(
            ahead >= offset - query_start, jnp.concatenate(lines, axis=0), MASKED_SCORE
        ).astype(masks.dtype)

    cosine, sine = shard_tables(cosines, sines, angles.shape[0] - 8, query_rows)
    fetch.wait()
    for head in range(heads):
        turned = rotate(held[:, pl.ds(head * HEAD_DIM, HEAD_DIM)], cosine, sine).T
        for tile in range(query_rows // TILE):
            lines = pl.ds((tile * heads + head) * TILE, TILE)
            rotated[:, lines] = turned[:, tile * TILE : (tile + 1) * TILE]


def attend_kernel(place_of, shards_of, first, last, *refs):
    rotated, cosines, sines, masks = refs[:4]
    refs = refs[4:]
    if not first:
        old_peak, old_sums = refs[:2]
        refs = refs[2:]
    if last:
        pieces, out = refs[:-1], refs[-1]
    else:
        pieces, new_peak, new_sums = refs[:-2], refs[-2], refs[-1]
    query_rows = masks.shape[1]
    tiles = query_rows // TILE
    width = rotated.shape[1] // tiles
    rows = masks.shape[0] // (cosines.shape[0] - 2 * FINE - 8)
    ones = jnp.ones((SUM_ROWS, rows), jnp.bfloat16)
    unit = (
        lax.broadcasted_iota(jnp.int32, (TILE, width), 0)
        == lax.broadcasted_iota(jnp.int32, (TILE, width), 1) % TILE
    ).astype(jnp.bfloat16)

    def load(keys, values, shard):
        keys = rotate(keys, *shard_tables(cosines, sines, 2 * FINE + shard, rows))
        mask = masks[pl.ds(pl.multiple_of(shard * rows, rows), rows), :]
        return keys, mask, jnp.concatenate([values.T, ones], axis=0)

    def joined(loaded):
        keys, masks, values = zip(*loaded)
        return (
            jnp.concatenate(keys, axis=0),
            jnp.concatenate(masks, axis=0),
            jnp.concatenate(values, axis=1),
        )

    def update(keys, mask, values, tile, before):
        query = jnp.concatenate([rotated[:, pl.ds(tile * width, width)], unit], axis=0)
        scores = jnp.dot(
            jnp.concatenate([keys, mask[:, tile * TILE : (tile + 1) * TILE]], axis=1),
            query,
            preferred_element_type=jnp.float32,
        )
        peak = scores.max(axis=0, keepdims=True)
        if before is not None:
            peak = jnp.maximum(before[0], peak)
        weights = jnp.exp2((scores - peak) * SCORE_SCALE).astype(jnp.bfloat16)
        sums = jnp.dot(values, weights, preferred_element_type=jnp.float32)
        if before is not None:
            sums = sums + before[1] * jnp.exp2((before[0] - peak) * SCORE_SCALE)
        return peak, sums

    def finish(tile, peak, sums):
        if not last:
            span = pl.ds(tile * width, width)
            new_peak[:, span] = jnp.broadcast_to(peak, (new_peak.shape[0], width))
            new_sums[:, span] = sums
            return
        part = sums[:HEAD_DIM] * (1.0 / sums[HEAD_DIM : HEAD_DIM + 1])
        part = part.astype(out.dtype)
        for head in range(width // TILE):
            out[pl.ds(tile * TILE, TILE), pl.ds(head * HEAD_DIM, HEAD_DIM)] = part[
                :, head * TILE : (head + 1) * TILE
            ].T

    if shards_of is not None:
        loaded = joined(
            [load(keys, values, shard) for keys, values, shard in shards_of(pieces, *place_of())]
        )
        for tile in range(tiles):
            before = None
            if not first:
                span = pl.ds(tile * width, width)
                before = (old_peak[:1, span], old_sums[:, span])
            finish(tile, *update(*loaded, tile, before))
    else:
        (whole,) = pieces
        for tile in range(tiles):

            def step(shard, before, tile=tile):
                start = pl.multiple_of(shard * (2 * rows), 2 * rows)
                piece = load(whole[pl.ds(start, rows), :], whole[pl.ds(start + rows, rows), :], shard)
                return update(*piece, tile, before)

            initial = (
                jnp.full((1, width), MASKED_SCORE, jnp.float32),
                jnp.zeros((HEAD_DIM + SUM_ROWS, width), jnp.float32),
            )
            finish(tile, *lax.fori_loop(0, whole.shape[0] // (2 * rows), step, initial))


def local(queries, cached_keys, cached_values, key_offsets, vertical_blocks, slash_offsets):
    query_rows = queries.shape[0]
    heads = queries.shape[1] // HEAD_DIM
    rows = cached_keys.shape[0]
    n_seg, n_ctx = lax.axis_size("seg"), lax.axis_size("ctx")
    shards = n_seg * n_ctx
    prefix = rows * shards - query_rows * n_ctx

    def query_start_of():
        ctx = lax.axis_index("ctx")
        return prefix + ctx * query_rows, ctx * (query_rows // BLOCK)

    def place_of():
        return tuple(lax.axis_index(axis) for axis in AXES)

    def exchange(a, partner):
        pairs = []
        for seg in range(n_seg):
            for ctx in range(n_ctx):
                for head in range(2):
                    to_seg, to_ctx, to_head = partner(seg, ctx, head)
                    pairs.append(
                        ((seg * n_ctx + ctx) * 2 + head, (to_seg * n_ctx + to_ctx) * 2 + to_head)
                    )
        return lax.ppermute(a, AXES, pairs)

    def swap(a):
        return exchange(a, lambda s, c, h: (s, c, 1 - h))

    vmem = pl.BlockSpec(memory_space=pltpu.VMEM)
    smem = pl.BlockSpec(memory_space=pltpu.SMEM)
    f32 = jnp.float32
    direct = (n_seg, n_ctx) == DIRECT_SHARDS
    limit = (16 if direct else 56) * 1024 * 1024
    shape = jax.ShapeDtypeStruct
    lines = 2 * FINE + shards + 8
    prepared = pl.pallas_call(
        functools.partial(prepare_kernel, query_start_of),
        out_shape=(
            shape((HEAD_DIM, query_rows * heads), jnp.bfloat16),
            shape((lines, HEAD_DIM), f32),
            shape((lines, HEAD_DIM), f32),
            shape((shards * rows, query_rows), jnp.bfloat16),
        ),
        in_specs=[smem, smem, smem, pl.BlockSpec(memory_space=pltpu.HBM), vmem],
        out_specs=[vmem] * 4,
        scratch_shapes=[
            pltpu.VMEM((lines, HEAD_DIM), jnp.int32),
            pltpu.VMEM((shards * rows // BLOCK, query_rows), f32),
            pltpu.VMEM(queries.shape, queries.dtype),
            pltpu.SemaphoreType.DMA(()),
        ],
        compiler_params=pltpu.CompilerParams(vmem_limit_bytes=limit),
        name="prepare",
    )(key_offsets, vertical_blocks, slash_offsets, queries, jnp.asarray(frequency_row()))

    def attend(prepared, pieces, shards_of, state, last):
        state_shape = (
            shape((8, query_rows * heads), f32),
            shape((HEAD_DIM + SUM_ROWS, query_rows * heads), f32),
        )
        return pl.pallas_call(
            functools.partial(attend_kernel, place_of, shards_of, not state, last),
            out_shape=shape(queries.shape, queries.dtype) if last else state_shape,
            in_specs=[vmem] * (4 + len(state) + len(pieces)),
            out_specs=vmem if last else (vmem, vmem),
            compiler_params=pltpu.CompilerParams(vmem_limit_bytes=limit),
            name="attend",
        )(*prepared, *state, *pieces)

    own = jnp.concatenate([cached_keys, cached_values], axis=0)
    if not direct:
        gathered = lax.all_gather(own, ("seg", "ctx"), axis=0, tiled=True)
        return attend(prepared, [gathered], None, (), True)

    def number(seg, ctx):
        return seg * n_ctx + ctx

    def whole(ref):
        return ref[:rows, :], ref[rows : 2 * rows, :]

    on_first = lax.axis_index("head") == 0
    first_keys, first_values = [
        exchange(a, lambda s, c, h: (s ^ (2 - 2 * h), c ^ h, h))
        for a in (cached_keys, cached_values)
    ]
    second = exchange(own, lambda s, c, h: (s ^ (1 + 2 * h), c, h))
    half = lax.dynamic_slice_in_dim(own, lax.axis_index("head") * rows, rows, 0)
    third = exchange(half, lambda s, c, h: (s ^ 1, c ^ 1, h))
    first_keys, first_values, prepared = lax.optimization_barrier(
        (first_keys, first_values, prepared)
    )
    first = jnp.concatenate([first_keys, first_values], axis=0)
    fourth = exchange(jnp.where(on_first, first, second), lambda s, c, h: (s, c ^ 1, h))
    first_beside = swap(first)
    state = attend(
        prepared,
        [own, first, first_beside, second],
        lambda refs, s, c, h: [
            (*whole(refs[0]), number(s, c)),
            (*whole(refs[1]), number(s ^ (2 - 2 * h), c ^ h)),
            (*whole(refs[2]), number(s ^ (2 * h), c ^ (1 - h))),
            (*whole(refs[3]), number(s ^ (1 + 2 * h), c)),
        ],
        (),
        False,
    )
    second, first_beside = lax.optimization_barrier((second, first_beside))
    second_beside = swap(second)
    third, state = lax.optimization_barrier((third, state))
    third_beside = swap(third)
    def middle_shards(refs, s, c, h):
        third, third_beside, beside = refs
        mine, other = third[...], third_beside[...]
        return [
            (*whole(beside), number(s ^ (3 - 2 * h), c)),
            (
                jnp.where(h == 0, mine, other),
                jnp.where(h == 0, other, mine),
                number(s ^ 1, c ^ 1),
            ),
        ]

    state = attend(prepared, [third, third_beside, second_beside], middle_shards, state, False)
    fourth, state = lax.optimization_barrier((fourth, state))
    fourth_beside = swap(fourth)
    state = attend(
        prepared,
        [fourth],
        lambda refs, s, c, h: [(*whole(refs[0]), number(s ^ (2 + h), c ^ 1))],
        state,
        False,
    )
    return attend(
        prepared,
        [fourth_beside],
        lambda refs, s, c, h: [(*whole(refs[0]), number(s ^ (3 - h), c ^ 1))],
        state,
        True,
    )


def solution(mesh):
    return jax.shard_map(
        local,
        mesh=mesh,
        in_specs=(
            P(("groups", "ctx"), "head"),
            P(("groups", "seg", "ctx"), None),
            P(("groups", "seg", "ctx"), None),
            P("groups"),
            P("groups", None),
            P("groups", None),
        ),
        out_specs=P(("groups", "ctx"), "head"),
        check_vma=False,
    )
```

```python
import functools
import math

import jax
import jax.numpy as jnp
import numpy as np
from jax import lax
from jax.experimental import pallas as pl
from jax.experimental.pallas import tpu as pltpu
from jax.sharding import PartitionSpec as P

HEAD_DIM = 128
BLOCK = 64
ROPE_THETA = 500000.0
ROPE_FACTOR = 8.0
LOW_FACTOR = 1.0
HIGH_FACTOR = 4.0
TRAINED_CONTEXT = 8192.0
MASKED_SCORE = -1e30
SCORE_SCALE = HEAD_DIM**-0.5 * math.log2(math.e)
TILE = 128
FINE = 16
SUM_ROWS = 16
DIRECT_SHARDS = (4, 2)
AXES = ("seg", "ctx", "head")


def frequency_row():
    exponent = np.arange(0, HEAD_DIM, 2, dtype=np.float64) / HEAD_DIM
    base = ROPE_THETA**-exponent
    wavelength = 2.0 * np.pi / base
    smooth = (TRAINED_CONTEXT / wavelength - LOW_FACTOR) / (HIGH_FACTOR - LOW_FACTOR)
    blended = (1.0 - smooth) * base / ROPE_FACTOR + smooth * base
    frequencies = np.where(
        wavelength < TRAINED_CONTEXT / HIGH_FACTOR,
        base,
        np.where(wavelength > TRAINED_CONTEXT / LOW_FACTOR, base / ROPE_FACTOR, blended),
    )
    return np.tile(frequencies, 2)[None, :].astype(np.float32)


def turned_sine(sine):
    lane = lax.broadcasted_iota(jnp.int32, sine.shape, 1)
    return jnp.where(lane < HEAD_DIM // 2, -sine, sine)


def rotate(vectors, cosine, signed_sine):
    wide = vectors.astype(jnp.float32)
    return (wide * cosine + pltpu.roll(wide, HEAD_DIM // 2, 1) * signed_sine).astype(jnp.bfloat16)


def angle_sum(cos_a, sin_a, cos_b, sin_b):
    return cos_a * cos_b - sin_a * sin_b, sin_a * cos_b + cos_a * sin_b


def shard_tables(cosines, sines, line, rows):
    cos_f, sin_f = cosines[pl.ds(0, FINE), :], turned_sine(sines[pl.ds(0, FINE), :])
    cos_c, sin_c = angle_sum(
        cosines[pl.ds(FINE, FINE), :],
        sines[pl.ds(FINE, FINE), :],
        cosines[pl.ds(line, 1), :],
        sines[pl.ds(line, 1), :],
    )
    signed = turned_sine(sin_c)
    parts = [
        (
            cos_f * cos_c[i : i + 1] - sin_f * signed[i : i + 1],
            sin_f * cos_c[i : i + 1] + cos_f * signed[i : i + 1],
        )
        for i in range(rows // FINE)
    ]
    return tuple(jnp.concatenate(table, axis=0) for table in zip(*parts))


def prepare_kernel(
    query_start_of, offsets, vertical, slash, queries, freq, rotated, cosines, sines, masks,
    angles, bias, held, arrival,
):
    query_rows, columns = held.shape
    heads = columns // HEAD_DIM
    fetch = pltpu.make_async_copy(queries, held, arrival)
    fetch.start()
    query_start, first_list = query_start_of()

    step = lax.broadcasted_iota(jnp.int32, (FINE, HEAD_DIM), 0)
    angles[pl.ds(0, FINE), :] = step
    angles[pl.ds(FINE, FINE), :] = step * FINE
    for shard in range(offsets.shape[0]):
        angles[pl.ds(2 * FINE + shard, 1), :] = jnp.full((1, HEAD_DIM), offsets[shard], jnp.int32)
    angles[pl.ds(angles.shape[0] - 8, 8), :] = jnp.full((8, HEAD_DIM), query_start, jnp.int32)
    angle = angles[...].astype(jnp.float32) * freq[...]
    cosines[...] = jnp.cos(angle)
    sines[...] = jnp.sin(angle)

    key_block = lax.broadcasted_iota(jnp.int32, bias.shape, 0)
    lane_block = lax.broadcasted_iota(jnp.int32, (1, query_rows), 1) // BLOCK
    hit = jnp.zeros(bias.shape, jnp.bool_)
    for entries, distance in ((vertical, False), (slash, True)):
        for entry in range(entries.shape[1]):
            wanted = jnp.zeros((1, query_rows), jnp.int32)
            for block in range(query_rows // BLOCK):
                value = entries[first_list + block, entry]
                if distance:
                    value = query_start // BLOCK + block - value
                wanted = jnp.where(lane_block == block, value, wanted)
            hit = hit | (key_block == wanted)
    bias[...] = jnp.where(hit, 0.0, MASKED_SCORE)

    rows = masks.shape[0] // offsets.shape[0]
    ahead = lax.broadcasted_iota(jnp.int32, (rows, query_rows), 1) - lax.broadcasted_iota(
        jnp.int32, (rows, query_rows), 0
    )

    @pl.loop(0, offsets.shape[0])
    def _(shard):
        offset = offsets[shard]
        lines = [
            jnp.broadcast_to(bias[pl.ds(offset // BLOCK + block, 1), :], (BLOCK, query_rows))
            for block in range(rows // BLOCK)
        ]
        masks[pl.ds(pl.multiple_of(shard * rows, rows), rows), :] = jnp.where(
            ahead >= offset - query_start, jnp.concatenate(lines, axis=0), MASKED_SCORE
        ).astype(masks.dtype)

    cosine, sine = shard_tables(cosines, sines, angles.shape[0] - 8, query_rows)
    fetch.wait()
    for head in range(heads):
        turned = rotate(held[:, pl.ds(head * HEAD_DIM, HEAD_DIM)], cosine, sine).T
        for tile in range(query_rows // TILE):
            lines = pl.ds((tile * heads + head) * TILE, TILE)
            rotated[:, lines] = turned[:, tile * TILE : (tile + 1) * TILE]


def attend_kernel(place_of, shards_of, first, last, *refs):
    rotated, cosines, sines, masks = refs[:4]
    refs = refs[4:]
    if not first:
        old_peak, old_sums = refs[:2]
        refs = refs[2:]
    if last:
        pieces, out = refs[:-1], refs[-1]
    else:
        pieces, new_peak, new_sums = refs[:-2], refs[-2], refs[-1]
    query_rows = masks.shape[1]
    tiles = query_rows // TILE
    width = rotated.shape[1] // tiles
    rows = masks.shape[0] // (cosines.shape[0] - 2 * FINE - 8)
    ones = jnp.ones((SUM_ROWS, rows), jnp.bfloat16)
    unit = (
        lax.broadcasted_iota(jnp.int32, (TILE, width), 0)
        == lax.broadcasted_iota(jnp.int32, (TILE, width), 1) % TILE
    ).astype(jnp.bfloat16)

    def load(keys, values, shard):
        keys = rotate(keys, *shard_tables(cosines, sines, 2 * FINE + shard, rows))
        mask = masks[pl.ds(pl.multiple_of(shard * rows, rows), rows), :]
        return keys, mask, jnp.concatenate([values.T, ones], axis=0)

    def joined(loaded):
        keys, masks, values = zip(*loaded)
        return (
            jnp.concatenate(keys, axis=0),
            jnp.concatenate(masks, axis=0),
            jnp.concatenate(values, axis=1),
        )

    def update(keys, mask, values, tile, before):
        query = jnp.concatenate([rotated[:, pl.ds(tile * width, width)], unit], axis=0)
        scores = jnp.dot(
            jnp.concatenate([keys, mask[:, tile * TILE : (tile + 1) * TILE]], axis=1),
            query,
            preferred_element_type=jnp.float32,
        )
        peak = scores.max(axis=0, keepdims=True)
        if before is not None:
            peak = jnp.maximum(before[0], peak)
        weights = jnp.exp2((scores - peak) * SCORE_SCALE).astype(jnp.bfloat16)
        sums = jnp.dot(values, weights, preferred_element_type=jnp.float32)
        if before is not None:
            sums = sums + before[1] * jnp.exp2((before[0] - peak) * SCORE_SCALE)
        return peak, sums

    def finish(tile, peak, sums):
        if not last:
            span = pl.ds(tile * width, width)
            new_peak[:, span] = jnp.broadcast_to(peak, (new_peak.shape[0], width))
            new_sums[:, span] = sums
            return
        part = sums[:HEAD_DIM] * (1.0 / sums[HEAD_DIM : HEAD_DIM + 1])
        part = part.astype(out.dtype)
        for head in range(width // TILE):
            out[pl.ds(tile * TILE, TILE), pl.ds(head * HEAD_DIM, HEAD_DIM)] = part[
                :, head * TILE : (head + 1) * TILE
            ].T

    if shards_of is not None:
        loaded = joined(
            [load(keys, values, shard) for keys, values, shard in shards_of(pieces, *place_of())]
        )
        for tile in range(tiles):
            before = None
            if not first:
                span = pl.ds(tile * width, width)
                before = (old_peak[:1, span], old_sums[:, span])
            finish(tile, *update(*loaded, tile, before))
    else:
        (whole,) = pieces
        for tile in range(tiles):

            def step(shard, before, tile=tile):
                start = pl.multiple_of(shard * (2 * rows), 2 * rows)
                piece = load(whole[pl.ds(start, rows), :], whole[pl.ds(start + rows, rows), :], shard)
                return update(*piece, tile, before)

            initial = (
                jnp.full((1, width), MASKED_SCORE, jnp.float32),
                jnp.zeros((HEAD_DIM + SUM_ROWS, width), jnp.float32),
            )
            finish(tile, *lax.fori_loop(0, whole.shape[0] // (2 * rows), step, initial))


def local(queries, cached_keys, cached_values, key_offsets, vertical_blocks, slash_offsets):
    query_rows = queries.shape[0]
    heads = queries.shape[1] // HEAD_DIM
    rows = cached_keys.shape[0]
    n_seg, n_ctx = lax.axis_size("seg"), lax.axis_size("ctx")
    shards = n_seg * n_ctx
    prefix = rows * shards - query_rows * n_ctx

    def query_start_of():
        ctx = lax.axis_index("ctx")
        return prefix + ctx * query_rows, ctx * (query_rows // BLOCK)

    def place_of():
        return tuple(lax.axis_index(axis) for axis in AXES)

    def exchange(a, partner):
        pairs = []
        for seg in range(n_seg):
            for ctx in range(n_ctx):
                for head in range(2):
                    to_seg, to_ctx, to_head = partner(seg, ctx, head)
                    pairs.append(
                        ((seg * n_ctx + ctx) * 2 + head, (to_seg * n_ctx + to_ctx) * 2 + to_head)
                    )
        return lax.ppermute(a, AXES, pairs)

    def swap(a):
        return exchange(a, lambda s, c, h: (s, c, 1 - h))

    vmem = pl.BlockSpec(memory_space=pltpu.VMEM)
    smem = pl.BlockSpec(memory_space=pltpu.SMEM)
    f32 = jnp.float32
    direct = (n_seg, n_ctx) == DIRECT_SHARDS
    limit = (16 if direct else 56) * 1024 * 1024
    shape = jax.ShapeDtypeStruct
    lines = 2 * FINE + shards + 8
    prepared = pl.pallas_call(
        functools.partial(prepare_kernel, query_start_of),
        out_shape=(
            shape((HEAD_DIM, query_rows * heads), jnp.bfloat16),
            shape((lines, HEAD_DIM), f32),
            shape((lines, HEAD_DIM), f32),
            shape((shards * rows, query_rows), jnp.bfloat16),
        ),
        in_specs=[smem, smem, smem, pl.BlockSpec(memory_space=pltpu.HBM), vmem],
        out_specs=[vmem] * 4,
        scratch_shapes=[
            pltpu.VMEM((lines, HEAD_DIM), jnp.int32),
            pltpu.VMEM((shards * rows // BLOCK, query_rows), f32),
            pltpu.VMEM(queries.shape, queries.dtype),
            pltpu.SemaphoreType.DMA(()),
        ],
        compiler_params=pltpu.CompilerParams(vmem_limit_bytes=limit),
        cost_estimate=pl.CostEstimate(flops=4 * 10**9, bytes_accessed=10**6, transcendentals=10**5),
        name="prepare",
    )(key_offsets, vertical_blocks, slash_offsets, queries, jnp.asarray(frequency_row()))

    def attend(prepared, pieces, shards_of, state, last):
        state_shape = (
            shape((8, query_rows * heads), f32),
            shape((HEAD_DIM + SUM_ROWS, query_rows * heads), f32),
        )
        return pl.pallas_call(
            functools.partial(attend_kernel, place_of, shards_of, not state, last),
            out_shape=shape(queries.shape, queries.dtype) if last else state_shape,
            in_specs=[vmem] * (4 + len(state) + len(pieces)),
            out_specs=vmem if last else (vmem, vmem),
            compiler_params=pltpu.CompilerParams(vmem_limit_bytes=limit),
            cost_estimate=pl.CostEstimate(
                flops=4 * 10**9, bytes_accessed=10**6, transcendentals=10**6
            ),
            name="attend",
        )(*prepared, *state, *pieces)

    own = jnp.concatenate([cached_keys, cached_values], axis=0)
    if not direct:
        gathered = lax.all_gather(own, ("seg", "ctx"), axis=0, tiled=True)
        return attend(prepared, [gathered], None, (), True)

    def number(seg, ctx):
        return seg * n_ctx + ctx

    def whole(ref):
        return ref[:rows, :], ref[rows : 2 * rows, :]

    far = exchange(own, lambda s, c, h: (s ^ (3 - h), c, h))
    near = exchange(own, lambda s, c, h: (s ^ (1 - h), c ^ h, h))
    near, prepared = lax.optimization_barrier((near, prepared))
    beside = swap(near)
    across = exchange(far, lambda s, c, h: (s, c ^ 1, h))
    state = attend(
        prepared,
        [own, near, beside, far],
        lambda refs, s, c, h: [
            (*whole(refs[0]), number(s, c)),
            (*whole(refs[1]), number(s ^ (1 - h), c ^ h)),
            (*whole(refs[2]), number(s ^ h, c ^ (1 - h))),
            (*whole(refs[3]), number(s ^ (3 - h), c)),
        ],
        (),
        False,
    )
    far_after, beside = lax.optimization_barrier((far, beside))
    far_beside = swap(far_after)
    half = jnp.where(lax.axis_index("head") == 0, beside[:rows], near[rows:])
    diagonal = exchange(half, lambda s, c, h: (s ^ 1, c, h))
    across, diagonal, state = lax.optimization_barrier((across, diagonal, state))
    last_beside = swap(jnp.concatenate([across, diagonal], axis=0))
    state = attend(
        prepared,
        [far_beside, across],
        lambda refs, s, c, h: [
            (*whole(refs[0]), number(s ^ (2 + h), c)),
            (*whole(refs[1]), number(s ^ (3 - h), c ^ 1)),
        ],
        state,
        False,
    )

    def last_shards(refs, s, c, h):
        diagonal, beside = refs
        mine, other = diagonal[...], beside[2 * rows :, :]
        return [
            (*whole(beside), number(s ^ (2 + h), c ^ 1)),
            (
                jnp.where(h == 0, mine, other),
                jnp.where(h == 0, other, mine),
                number(s ^ 1, c ^ 1),
            ),
        ]

    return attend(prepared, [diagonal, last_beside], last_shards, state, True)


def solution(mesh):
    return jax.shard_map(
        local,
        mesh=mesh,
        in_specs=(
            P(("groups", "ctx"), "head"),
            P(("groups", "seg", "ctx"), None),
            P(("groups", "seg", "ctx"), None),
            P("groups"),
            P("groups", None),
            P("groups", None),
        ),
        out_specs=P(("groups", "ctx"), "head"),
        check_vma=False,
    )
```

```python
import functools
import math

import jax
import jax.numpy as jnp
import numpy as np
from jax import lax
from jax.experimental import pallas as pl
from jax.experimental.pallas import tpu as pltpu
from jax.sharding import PartitionSpec as P

HEAD_DIM = 128
BLOCK = 64
ROPE_THETA = 500000.0
ROPE_FACTOR = 8.0
LOW_FACTOR = 1.0
HIGH_FACTOR = 4.0
TRAINED_CONTEXT = 8192.0
MASKED_SCORE = -1e30
SCORE_SCALE = HEAD_DIM**-0.5 * math.log2(math.e)
TILE = 128
FINE = 16
SUM_ROWS = 16
DIRECT_SHARDS = (4, 2)
AXES = ("seg", "ctx", "head")


def frequency_row():
    exponent = np.arange(0, HEAD_DIM, 2, dtype=np.float64) / HEAD_DIM
    base = ROPE_THETA**-exponent
    wavelength = 2.0 * np.pi / base
    smooth = (TRAINED_CONTEXT / wavelength - LOW_FACTOR) / (HIGH_FACTOR - LOW_FACTOR)
    blended = (1.0 - smooth) * base / ROPE_FACTOR + smooth * base
    frequencies = np.where(
        wavelength < TRAINED_CONTEXT / HIGH_FACTOR,
        base,
        np.where(wavelength > TRAINED_CONTEXT / LOW_FACTOR, base / ROPE_FACTOR, blended),
    )
    return np.tile(frequencies, 2)[None, :].astype(np.float32)


def turned_sine(sine):
    lane = lax.broadcasted_iota(jnp.int32, sine.shape, 1)
    return jnp.where(lane < HEAD_DIM // 2, -sine, sine)


def rotate(vectors, cosine, signed_sine):
    wide = vectors.astype(jnp.float32)
    return (wide * cosine + pltpu.roll(wide, HEAD_DIM // 2, 1) * signed_sine).astype(jnp.bfloat16)


def angle_sum(cos_a, sin_a, cos_b, sin_b):
    return cos_a * cos_b - sin_a * sin_b, sin_a * cos_b + cos_a * sin_b


def shard_tables(cosines, sines, line, rows):
    cos_f, sin_f = cosines[pl.ds(0, FINE), :], turned_sine(sines[pl.ds(0, FINE), :])
    cos_c, sin_c = angle_sum(
        cosines[pl.ds(FINE, FINE), :],
        sines[pl.ds(FINE, FINE), :],
        cosines[pl.ds(line, 1), :],
        sines[pl.ds(line, 1), :],
    )
    signed = turned_sine(sin_c)
    parts = [
        (
            cos_f * cos_c[i : i + 1] - sin_f * signed[i : i + 1],
            sin_f * cos_c[i : i + 1] + cos_f * signed[i : i + 1],
        )
        for i in range(rows // FINE)
    ]
    return tuple(jnp.concatenate(table, axis=0) for table in zip(*parts))


def prepare_kernel(
    query_start_of, offsets, vertical, slash, queries, freq, rotated, cosines, sines, masks,
    angles, bias, held, arrival,
):
    query_rows, columns = held.shape
    heads = columns // HEAD_DIM
    fetch = pltpu.make_async_copy(queries, held, arrival)
    fetch.start()
    query_start, first_list = query_start_of()

    step = lax.broadcasted_iota(jnp.int32, (FINE, HEAD_DIM), 0)
    angles[pl.ds(0, FINE), :] = step
    angles[pl.ds(FINE, FINE), :] = step * FINE
    for shard in range(offsets.shape[0]):
        angles[pl.ds(2 * FINE + shard, 1), :] = jnp.full((1, HEAD_DIM), offsets[shard], jnp.int32)
    angles[pl.ds(angles.shape[0] - 8, 8), :] = jnp.full((8, HEAD_DIM), query_start, jnp.int32)
    angle = angles[...].astype(jnp.float32) * freq[...]
    cosines[...] = jnp.cos(angle)
    sines[...] = jnp.sin(angle)

    key_block = lax.broadcasted_iota(jnp.int32, bias.shape, 0)
    lane_block = lax.broadcasted_iota(jnp.int32, (1, query_rows), 1) // BLOCK
    hit = jnp.zeros(bias.shape, jnp.bool_)
    for entries, distance in ((vertical, False), (slash, True)):
        for entry in range(entries.shape[1]):
            wanted = jnp.zeros((1, query_rows), jnp.int32)
            for block in range(query_rows // BLOCK):
                value = entries[first_list + block, entry]
                if distance:
                    value = query_start // BLOCK + block - value
                wanted = jnp.where(lane_block == block, value, wanted)
            hit = hit | (key_block == wanted)
    bias[...] = jnp.where(hit, 0.0, MASKED_SCORE)

    rows = masks.shape[0] // offsets.shape[0]
    ahead = lax.broadcasted_iota(jnp.int32, (rows, query_rows), 1) - lax.broadcasted_iota(
        jnp.int32, (rows, query_rows), 0
    )

    @pl.loop(0, offsets.shape[0])
    def _(shard):
        offset = offsets[shard]
        lines = [
            jnp.broadcast_to(bias[pl.ds(offset // BLOCK + block, 1), :], (BLOCK, query_rows))
            for block in range(rows // BLOCK)
        ]
        masks[pl.ds(pl.multiple_of(shard * rows, rows), rows), :] = jnp.where(
            ahead >= offset - query_start, jnp.concatenate(lines, axis=0), MASKED_SCORE
        ).astype(masks.dtype)

    cosine, sine = shard_tables(cosines, sines, angles.shape[0] - 8, query_rows)
    fetch.wait()
    for head in range(heads):
        turned = rotate(held[:, pl.ds(head * HEAD_DIM, HEAD_DIM)], cosine, sine).T
        for tile in range(query_rows // TILE):
            lines = pl.ds((tile * heads + head) * TILE, TILE)
            rotated[:, lines] = turned[:, tile * TILE : (tile + 1) * TILE]


def attend_kernel(place_of, shards_of, first, last, *refs):
    rotated, cosines, sines, masks = refs[:4]
    refs = refs[4:]
    if not first:
        old_peak, old_sums = refs[:2]
        refs = refs[2:]
    if last:
        pieces, out = refs[:-1], refs[-1]
    else:
        pieces, new_peak, new_sums = refs[:-2], refs[-2], refs[-1]
    query_rows = masks.shape[1]
    tiles = query_rows // TILE
    width = rotated.shape[1] // tiles
    rows = masks.shape[0] // (cosines.shape[0] - 2 * FINE - 8)
    ones = jnp.ones((SUM_ROWS, rows), jnp.bfloat16)
    unit = (
        lax.broadcasted_iota(jnp.int32, (TILE, width), 0)
        == lax.broadcasted_iota(jnp.int32, (TILE, width), 1) % TILE
    ).astype(jnp.bfloat16)

    def load(keys, values, shard):
        keys = rotate(keys, *shard_tables(cosines, sines, 2 * FINE + shard, rows))
        mask = masks[pl.ds(pl.multiple_of(shard * rows, rows), rows), :]
        return keys, mask, jnp.concatenate([values.T, ones], axis=0)

    def joined(loaded):
        keys, masks, values = zip(*loaded)
        return (
            jnp.concatenate(keys, axis=0),
            jnp.concatenate(masks, axis=0),
            jnp.concatenate(values, axis=1),
        )

    def score(keys, mask, tile):
        query = jnp.concatenate([rotated[:, pl.ds(tile * width, width)], unit], axis=0)
        return jnp.dot(
            jnp.concatenate([keys, mask[:, tile * TILE : (tile + 1) * TILE]], axis=1),
            query,
            preferred_element_type=jnp.float32,
        )

    def update(scores, values, before):
        peak = scores.max(axis=0, keepdims=True)
        if before is not None:
            peak = jnp.maximum(before[0], peak)
        weights = jnp.exp2((scores - peak) * SCORE_SCALE).astype(jnp.bfloat16)
        sums = jnp.dot(values, weights, preferred_element_type=jnp.float32)
        if before is not None:
            sums = sums + before[1] * jnp.exp2((before[0] - peak) * SCORE_SCALE)
        return peak, sums

    def finish(tile, peak, sums):
        if not last:
            span = pl.ds(tile * width, width)
            new_peak[:, span] = jnp.broadcast_to(peak, (new_peak.shape[0], width))
            new_sums[:, span] = sums
            return
        part = sums[:HEAD_DIM] * (1.0 / sums[HEAD_DIM : HEAD_DIM + 1])
        part = part.astype(out.dtype)
        for head in range(width // TILE):
            out[pl.ds(tile * TILE, TILE), pl.ds(head * HEAD_DIM, HEAD_DIM)] = part[
                :, head * TILE : (head + 1) * TILE
            ].T

    if shards_of is not None:
        keys, mask, values = joined(
            [load(keys, values, shard) for keys, values, shard in shards_of(pieces, *place_of())]
        )
        scores = [score(keys, mask, tile) for tile in range(tiles)]
        states = []
        for tile in range(tiles):
            before = None
            if not first:
                span = pl.ds(tile * width, width)
                before = (old_peak[:1, span], old_sums[:, span])
            states.append(update(scores[tile], values, before))
        for tile in range(tiles):
            finish(tile, *states[tile])
    else:
        (whole,) = pieces
        for tile in range(tiles):

            def step(shard, before, tile=tile):
                start = pl.multiple_of(shard * (2 * rows), 2 * rows)
                piece = load(whole[pl.ds(start, rows), :], whole[pl.ds(start + rows, rows), :], shard)
                keys, mask, values = piece
                return update(score(keys, mask, tile), values, before)

            initial = (
                jnp.full((1, width), MASKED_SCORE, jnp.float32),
                jnp.zeros((HEAD_DIM + SUM_ROWS, width), jnp.float32),
            )
            finish(tile, *lax.fori_loop(0, whole.shape[0] // (2 * rows), step, initial))


def local(queries, cached_keys, cached_values, key_offsets, vertical_blocks, slash_offsets):
    query_rows = queries.shape[0]
    heads = queries.shape[1] // HEAD_DIM
    rows = cached_keys.shape[0]
    n_seg, n_ctx = lax.axis_size("seg"), lax.axis_size("ctx")
    shards = n_seg * n_ctx
    prefix = rows * shards - query_rows * n_ctx

    def query_start_of():
        ctx = lax.axis_index("ctx")
        return prefix + ctx * query_rows, ctx * (query_rows // BLOCK)

    def place_of():
        return tuple(lax.axis_index(axis) for axis in AXES)

    def exchange(a, partner):
        pairs = []
        for seg in range(n_seg):
            for ctx in range(n_ctx):
                for head in range(2):
                    to_seg, to_ctx, to_head = partner(seg, ctx, head)
                    pairs.append(
                        ((seg * n_ctx + ctx) * 2 + head, (to_seg * n_ctx + to_ctx) * 2 + to_head)
                    )
        return lax.ppermute(a, AXES, pairs)

    def swap(a):
        return exchange(a, lambda s, c, h: (s, c, 1 - h))

    vmem = pl.BlockSpec(memory_space=pltpu.VMEM)
    smem = pl.BlockSpec(memory_space=pltpu.SMEM)
    f32 = jnp.float32
    direct = (n_seg, n_ctx) == DIRECT_SHARDS
    limit = (16 if direct else 56) * 1024 * 1024
    shape = jax.ShapeDtypeStruct
    lines = 2 * FINE + shards + 8
    prepared = pl.pallas_call(
        functools.partial(prepare_kernel, query_start_of),
        out_shape=(
            shape((HEAD_DIM, query_rows * heads), jnp.bfloat16),
            shape((lines, HEAD_DIM), f32),
            shape((lines, HEAD_DIM), f32),
            shape((shards * rows, query_rows), jnp.bfloat16),
        ),
        in_specs=[smem, smem, smem, pl.BlockSpec(memory_space=pltpu.HBM), vmem],
        out_specs=[vmem] * 4,
        scratch_shapes=[
            pltpu.VMEM((lines, HEAD_DIM), jnp.int32),
            pltpu.VMEM((shards * rows // BLOCK, query_rows), f32),
            pltpu.VMEM(queries.shape, queries.dtype),
            pltpu.SemaphoreType.DMA(()),
        ],
        compiler_params=pltpu.CompilerParams(vmem_limit_bytes=limit),
        cost_estimate=pl.CostEstimate(flops=4 * 10**9, bytes_accessed=10**6, transcendentals=10**5),
        name="prepare",
    )(key_offsets, vertical_blocks, slash_offsets, queries, jnp.asarray(frequency_row()))

    def attend(prepared, pieces, shards_of, state, last):
        state_shape = (
            shape((8, query_rows * heads), f32),
            shape((HEAD_DIM + SUM_ROWS, query_rows * heads), f32),
        )
        return pl.pallas_call(
            functools.partial(attend_kernel, place_of, shards_of, not state, last),
            out_shape=shape(queries.shape, queries.dtype) if last else state_shape,
            in_specs=[vmem] * (4 + len(state) + len(pieces)),
            out_specs=vmem if last else (vmem, vmem),
            compiler_params=pltpu.CompilerParams(vmem_limit_bytes=limit),
            cost_estimate=pl.CostEstimate(
                flops=4 * 10**9, bytes_accessed=10**6, transcendentals=10**6
            ),
            name="attend",
        )(*prepared, *state, *pieces)

    own = jnp.concatenate([cached_keys, cached_values], axis=0)
    if not direct:
        gathered = lax.all_gather(own, ("seg", "ctx"), axis=0, tiled=True)
        return attend(prepared, [gathered], None, (), True)

    def number(seg, ctx):
        return seg * n_ctx + ctx

    def whole(ref):
        return ref[:rows, :], ref[rows : 2 * rows, :]

    far = exchange(own, lambda s, c, h: (s ^ (3 - h), c, h))
    near = exchange(own, lambda s, c, h: (s ^ (1 - h), c ^ h, h))
    near, prepared = lax.optimization_barrier((near, prepared))
    beside = swap(near)
    across = exchange(far, lambda s, c, h: (s, c ^ 1, h))
    state = attend(
        prepared,
        [own, near, beside, far],
        lambda refs, s, c, h: [
            (*whole(refs[0]), number(s, c)),
            (*whole(refs[1]), number(s ^ (1 - h), c ^ h)),
            (*whole(refs[2]), number(s ^ h, c ^ (1 - h))),
            (*whole(refs[3]), number(s ^ (3 - h), c)),
        ],
        (),
        False,
    )
    far_after, beside = lax.optimization_barrier((far, beside))
    far_beside = swap(far_after)
    half = jnp.where(lax.axis_index("head") == 0, beside[:rows], near[rows:])
    diagonal = exchange(half, lambda s, c, h: (s ^ 1, c, h))
    across, diagonal, state = lax.optimization_barrier((across, diagonal, state))
    last_beside = swap(jnp.concatenate([across, diagonal], axis=0))
    state = attend(
        prepared,
        [far_beside, across],
        lambda refs, s, c, h: [
            (*whole(refs[0]), number(s ^ (2 + h), c)),
            (*whole(refs[1]), number(s ^ (3 - h), c ^ 1)),
        ],
        state,
        False,
    )

    def last_shards(refs, s, c, h):
        diagonal, beside = refs
        mine, other = diagonal[...], beside[2 * rows :, :]
        return [
            (*whole(beside), number(s ^ (2 + h), c ^ 1)),
            (
                jnp.where(h == 0, mine, other),
                jnp.where(h == 0, other, mine),
                number(s ^ 1, c ^ 1),
            ),
        ]

    return attend(prepared, [diagonal, last_beside], last_shards, state, True)


def solution(mesh):
    return jax.shard_map(
        local,
        mesh=mesh,
        in_specs=(
            P(("groups", "ctx"), "head"),
            P(("groups", "seg", "ctx"), None),
            P(("groups", "seg", "ctx"), None),
            P("groups"),
            P("groups", None),
            P("groups", None),
        ),
        out_specs=P(("groups", "ctx"), "head"),
        check_vma=False,
    )
```

```python
import functools
import math

import jax
import jax.numpy as jnp
import numpy as np
from jax import lax
from jax.experimental import pallas as pl
from jax.experimental.pallas import tpu as pltpu
from jax.sharding import PartitionSpec as P

HEAD_DIM = 128
BLOCK = 64
ROPE_THETA = 500000.0
ROPE_FACTOR = 8.0
LOW_FACTOR = 1.0
HIGH_FACTOR = 4.0
TRAINED_CONTEXT = 8192.0
MASKED_SCORE = -1e30
SCORE_SCALE = HEAD_DIM**-0.5 * math.log2(math.e)
TILE = 128
FINE = 16
SUM_ROWS = 16
CHUNK = 256
DIRECT_SHARDS = (4, 2)
AXES = ("seg", "ctx", "head")


def frequency_row():
    exponent = np.arange(0, HEAD_DIM, 2, dtype=np.float64) / HEAD_DIM
    base = ROPE_THETA**-exponent
    wavelength = 2.0 * np.pi / base
    smooth = (TRAINED_CONTEXT / wavelength - LOW_FACTOR) / (HIGH_FACTOR - LOW_FACTOR)
    blended = (1.0 - smooth) * base / ROPE_FACTOR + smooth * base
    frequencies = np.where(
        wavelength < TRAINED_CONTEXT / HIGH_FACTOR,
        base,
        np.where(wavelength > TRAINED_CONTEXT / LOW_FACTOR, base / ROPE_FACTOR, blended),
    )
    return np.tile(frequencies, 2)[None, :].astype(np.float32)


def turned_sine(sine):
    lane = lax.broadcasted_iota(jnp.int32, sine.shape, 1)
    return jnp.where(lane < HEAD_DIM // 2, -sine, sine)


def rotate(vectors, cosine, signed_sine):
    wide = vectors.astype(jnp.float32)
    return (wide * cosine + pltpu.roll(wide, HEAD_DIM // 2, 1) * signed_sine).astype(jnp.bfloat16)


def angle_sum(cos_a, sin_a, cos_b, sin_b):
    return cos_a * cos_b - sin_a * sin_b, sin_a * cos_b + cos_a * sin_b


def shard_tables(cosines, sines, line, rows):
    cos_f, sin_f = cosines[pl.ds(0, FINE), :], turned_sine(sines[pl.ds(0, FINE), :])
    cos_c, sin_c = angle_sum(
        cosines[pl.ds(FINE, FINE), :],
        sines[pl.ds(FINE, FINE), :],
        cosines[pl.ds(line, 1), :],
        sines[pl.ds(line, 1), :],
    )
    signed = turned_sine(sin_c)
    parts = [
        (
            cos_f * cos_c[i : i + 1] - sin_f * signed[i : i + 1],
            sin_f * cos_c[i : i + 1] + cos_f * signed[i : i + 1],
        )
        for i in range(rows // FINE)
    ]
    return tuple(jnp.concatenate(table, axis=0) for table in zip(*parts))


def prepare_kernel(
    query_start_of, offsets, vertical, slash, queries, freq, rotated, cosines, sines, masks,
    angles, bias, held, arrival,
):
    query_rows, columns = held.shape
    heads = columns // HEAD_DIM
    fetch = pltpu.make_async_copy(queries, held, arrival)
    fetch.start()
    query_start, first_list = query_start_of()

    step = lax.broadcasted_iota(jnp.int32, (FINE, HEAD_DIM), 0)
    angles[pl.ds(0, FINE), :] = step
    angles[pl.ds(FINE, FINE), :] = step * FINE
    for shard in range(offsets.shape[0]):
        angles[pl.ds(2 * FINE + shard, 1), :] = jnp.full((1, HEAD_DIM), offsets[shard], jnp.int32)
    angles[pl.ds(angles.shape[0] - 8, 8), :] = jnp.full((8, HEAD_DIM), query_start, jnp.int32)
    angle = angles[...].astype(jnp.float32) * freq[...]
    cosines[...] = jnp.cos(angle)
    sines[...] = jnp.sin(angle)

    key_block = lax.broadcasted_iota(jnp.int32, bias.shape, 0)
    lane_block = lax.broadcasted_iota(jnp.int32, (1, query_rows), 1) // BLOCK
    hit = jnp.zeros(bias.shape, jnp.bool_)
    for entries, distance in ((vertical, False), (slash, True)):
        for entry in range(entries.shape[1]):
            wanted = jnp.zeros((1, query_rows), jnp.int32)
            for block in range(query_rows // BLOCK):
                value = entries[first_list + block, entry]
                if distance:
                    value = query_start // BLOCK + block - value
                wanted = jnp.where(lane_block == block, value, wanted)
            hit = hit | (key_block == wanted)
    bias[...] = jnp.where(hit, 0.0, MASKED_SCORE)

    rows = masks.shape[0] // offsets.shape[0]
    ahead = lax.broadcasted_iota(jnp.int32, (rows, query_rows), 1) - lax.broadcasted_iota(
        jnp.int32, (rows, query_rows), 0
    )

    @pl.loop(0, offsets.shape[0])
    def _(shard):
        offset = offsets[shard]
        lines = [
            jnp.broadcast_to(bias[pl.ds(offset // BLOCK + block, 1), :], (BLOCK, query_rows))
            for block in range(rows // BLOCK)
        ]
        masks[pl.ds(pl.multiple_of(shard * rows, rows), rows), :] = jnp.where(
            ahead >= offset - query_start, jnp.concatenate(lines, axis=0), MASKED_SCORE
        ).astype(masks.dtype)

    cosine, sine = shard_tables(cosines, sines, angles.shape[0] - 8, query_rows)
    fetch.wait()
    for head in range(heads):
        turned = rotate(held[:, pl.ds(head * HEAD_DIM, HEAD_DIM)], cosine, sine).T
        for tile in range(query_rows // TILE):
            lines = pl.ds((tile * heads + head) * TILE, TILE)
            rotated[:, lines] = turned[:, tile * TILE : (tile + 1) * TILE]


def attend_kernel(place_of, shards_of, first, last, *refs):
    rotated, cosines, sines, masks = refs[:4]
    refs = refs[4:]
    if not first:
        old_peak, old_sums = refs[:2]
        refs = refs[2:]
    if last:
        pieces, out = refs[:-1], refs[-1]
    else:
        pieces, new_peak, new_sums = refs[:-2], refs[-2], refs[-1]
    query_rows = masks.shape[1]
    tiles = query_rows // TILE
    width = rotated.shape[1] // tiles
    rows = masks.shape[0] // (cosines.shape[0] - 2 * FINE - 8)
    ones = jnp.ones((SUM_ROWS, rows), jnp.bfloat16)
    unit = (
        lax.broadcasted_iota(jnp.int32, (TILE, width), 0)
        == lax.broadcasted_iota(jnp.int32, (TILE, width), 1) % TILE
    ).astype(jnp.bfloat16)

    def load_keys(keys, shard):
        keys = rotate(keys, *shard_tables(cosines, sines, 2 * FINE + shard, rows))
        return keys, masks[pl.ds(pl.multiple_of(shard * rows, rows), rows), :]

    def load_values(values):
        return jnp.concatenate([values.T, ones], axis=0)

    def score(keys, mask, start, size):
        tile = start // width
        query = jnp.concatenate([rotated[:, pl.ds(start, size)], unit[:, :size]], axis=0)
        return jnp.dot(
            jnp.concatenate([keys, mask[:, tile * TILE : (tile + 1) * TILE]], axis=1),
            query,
            preferred_element_type=jnp.float32,
        )

    def update(scores, values, before):
        peak = scores.max(axis=0, keepdims=True)
        if before is not None:
            peak = jnp.maximum(before[0], peak)
        weights = jnp.exp2((scores - peak) * SCORE_SCALE).astype(jnp.bfloat16)
        sums = jnp.dot(values, weights, preferred_element_type=jnp.float32)
        if before is not None:
            sums = sums + before[1] * jnp.exp2((before[0] - peak) * SCORE_SCALE)
        return peak, sums

    def finish(start, peak, sums):
        size = sums.shape[1]
        if not last:
            span = pl.ds(start, size)
            new_peak[:, span] = jnp.broadcast_to(peak, (new_peak.shape[0], size))
            new_sums[:, span] = sums
            return
        part = sums[:HEAD_DIM] * (1.0 / sums[HEAD_DIM : HEAD_DIM + 1])
        part = part.astype(out.dtype)
        for column in range(0, size, TILE):
            tile, head = divmod((start + column) // TILE, width // TILE)
            out[pl.ds(tile * TILE, TILE), pl.ds(head * HEAD_DIM, HEAD_DIM)] = part[
                :, column : column + TILE
            ].T

    if shards_of is not None:
        shards = shards_of(pieces, *place_of())
        keys, mask = (
            jnp.concatenate(part, axis=0)
            for part in zip(*(load_keys(keys, shard) for keys, _, shard in shards))
        )
        starts = list(range(0, rotated.shape[1], CHUNK))
        ahead = score(keys, mask, starts[0], CHUNK)
        values = jnp.concatenate([load_values(values) for _, values, _ in shards], axis=1)
        for start in starts:
            scores = ahead
            if start != starts[-1]:
                ahead = score(keys, mask, start + CHUNK, CHUNK)
            before = None
            if not first:
                before = (old_peak[:1, pl.ds(start, CHUNK)], old_sums[:, pl.ds(start, CHUNK)])
            finish(start, *update(scores, values, before))
    else:
        (whole,) = pieces
        for tile in range(tiles):

            def step(shard, before, tile=tile):
                start = pl.multiple_of(shard * (2 * rows), 2 * rows)
                keys, mask = load_keys(whole[pl.ds(start, rows), :], shard)
                values = load_values(whole[pl.ds(start + rows, rows), :])
                return update(score(keys, mask, tile * width, width), values, before)

            initial = (
                jnp.full((1, width), MASKED_SCORE, jnp.float32),
                jnp.zeros((HEAD_DIM + SUM_ROWS, width), jnp.float32),
            )
            finish(
                tile * width, *lax.fori_loop(0, whole.shape[0] // (2 * rows), step, initial)
            )


def local(queries, cached_keys, cached_values, key_offsets, vertical_blocks, slash_offsets):
    query_rows = queries.shape[0]
    heads = queries.shape[1] // HEAD_DIM
    rows = cached_keys.shape[0]
    n_seg, n_ctx = lax.axis_size("seg"), lax.axis_size("ctx")
    shards = n_seg * n_ctx
    prefix = rows * shards - query_rows * n_ctx

    def query_start_of():
        ctx = lax.axis_index("ctx")
        return prefix + ctx * query_rows, ctx * (query_rows // BLOCK)

    def place_of():
        return tuple(lax.axis_index(axis) for axis in AXES)

    def exchange(a, partner):
        pairs = []
        for seg in range(n_seg):
            for ctx in range(n_ctx):
                for head in range(2):
                    to_seg, to_ctx, to_head = partner(seg, ctx, head)
                    pairs.append(
                        ((seg * n_ctx + ctx) * 2 + head, (to_seg * n_ctx + to_ctx) * 2 + to_head)
                    )
        return lax.ppermute(a, AXES, pairs)

    def swap(a):
        return exchange(a, lambda s, c, h: (s, c, 1 - h))

    vmem = pl.BlockSpec(memory_space=pltpu.VMEM)
    smem = pl.BlockSpec(memory_space=pltpu.SMEM)
    f32 = jnp.float32
    direct = (n_seg, n_ctx) == DIRECT_SHARDS
    limit = (16 if direct else 56) * 1024 * 1024
    shape = jax.ShapeDtypeStruct
    lines = 2 * FINE + shards + 8
    prepared = pl.pallas_call(
        functools.partial(prepare_kernel, query_start_of),
        out_shape=(
            shape((HEAD_DIM, query_rows * heads), jnp.bfloat16),
            shape((lines, HEAD_DIM), f32),
            shape((lines, HEAD_DIM), f32),
            shape((shards * rows, query_rows), jnp.bfloat16),
        ),
        in_specs=[smem, smem, smem, pl.BlockSpec(memory_space=pltpu.HBM), vmem],
        out_specs=[vmem] * 4,
        scratch_shapes=[
            pltpu.VMEM((lines, HEAD_DIM), jnp.int32),
            pltpu.VMEM((shards * rows // BLOCK, query_rows), f32),
            pltpu.VMEM(queries.shape, queries.dtype),
            pltpu.SemaphoreType.DMA(()),
        ],
        compiler_params=pltpu.CompilerParams(vmem_limit_bytes=limit),
        cost_estimate=pl.CostEstimate(flops=4 * 10**9, bytes_accessed=10**6, transcendentals=10**5),
        name="prepare",
    )(key_offsets, vertical_blocks, slash_offsets, queries, jnp.asarray(frequency_row()))

    def attend(prepared, pieces, shards_of, state, last):
        state_shape = (
            shape((8, query_rows * heads), f32),
            shape((HEAD_DIM + SUM_ROWS, query_rows * heads), f32),
        )
        return pl.pallas_call(
            functools.partial(attend_kernel, place_of, shards_of, not state, last),
            out_shape=shape(queries.shape, queries.dtype) if last else state_shape,
            in_specs=[vmem] * (4 + len(state) + len(pieces)),
            out_specs=vmem if last else (vmem, vmem),
            compiler_params=pltpu.CompilerParams(vmem_limit_bytes=limit),
            cost_estimate=pl.CostEstimate(
                flops=4 * 10**9, bytes_accessed=10**6, transcendentals=10**6
            ),
            name="attend",
        )(*prepared, *state, *pieces)

    own = jnp.concatenate([cached_keys, cached_values], axis=0)
    if not direct:
        gathered = lax.all_gather(own, ("seg", "ctx"), axis=0, tiled=True)
        return attend(prepared, [gathered], None, (), True)

    def number(seg, ctx):
        return seg * n_ctx + ctx

    def whole(ref):
        return ref[:rows, :], ref[rows : 2 * rows, :]

    far = exchange(own, lambda s, c, h: (s ^ (3 - h), c, h))
    near = exchange(own, lambda s, c, h: (s ^ (1 - h), c ^ h, h))
    near, prepared = lax.optimization_barrier((near, prepared))
    beside = swap(near)
    across = exchange(far, lambda s, c, h: (s, c ^ 1, h))
    state = attend(
        prepared,
        [own, near, beside, far],
        lambda refs, s, c, h: [
            (*whole(refs[0]), number(s, c)),
            (*whole(refs[1]), number(s ^ (1 - h), c ^ h)),
            (*whole(refs[2]), number(s ^ h, c ^ (1 - h))),
            (*whole(refs[3]), number(s ^ (3 - h), c)),
        ],
        (),
        False,
    )
    far_after, beside = lax.optimization_barrier((far, beside))
    far_beside = swap(far_after)
    half = jnp.where(lax.axis_index("head") == 0, beside[:rows], near[rows:])
    diagonal = exchange(half, lambda s, c, h: (s ^ 1, c, h))
    across, diagonal, state = lax.optimization_barrier((across, diagonal, state))
    last_beside = swap(jnp.concatenate([across, diagonal], axis=0))
    state = attend(
        prepared,
        [far_beside, across],
        lambda refs, s, c, h: [
            (*whole(refs[0]), number(s ^ (2 + h), c)),
            (*whole(refs[1]), number(s ^ (3 - h), c ^ 1)),
        ],
        state,
        False,
    )

    def last_shards(refs, s, c, h):
        diagonal, beside = refs
        mine, other = diagonal[...], beside[2 * rows :, :]
        return [
            (*whole(beside), number(s ^ (2 + h), c ^ 1)),
            (
                jnp.where(h == 0, mine, other),
                jnp.where(h == 0, other, mine),
                number(s ^ 1, c ^ 1),
            ),
        ]

    return attend(prepared, [diagonal, last_beside], last_shards, state, True)


def solution(mesh):
    return jax.shard_map(
        local,
        mesh=mesh,
        in_specs=(
            P(("groups", "ctx"), "head"),
            P(("groups", "seg", "ctx"), None),
            P(("groups", "seg", "ctx"), None),
            P("groups"),
            P("groups", None),
            P("groups", None),
        ),
        out_specs=P(("groups", "ctx"), "head"),
        check_vma=False,
    )
```

```python
import functools
import math

import jax
import jax.numpy as jnp
import numpy as np
from jax import lax
from jax.experimental import pallas as pl
from jax.experimental.pallas import tpu as pltpu
from jax.sharding import PartitionSpec as P

HEAD_DIM = 128
BLOCK = 64
ROPE_THETA = 500000.0
ROPE_FACTOR = 8.0
LOW_FACTOR = 1.0
HIGH_FACTOR = 4.0
TRAINED_CONTEXT = 8192.0
MASKED_SCORE = -1e30
SCORE_SCALE = HEAD_DIM**-0.5 * math.log2(math.e)
TILE = 128
FINE = 16
SUM_ROWS = 16
CHUNK = 256
DIRECT_SHARDS = (4, 2)
AXES = ("seg", "ctx", "head")


def frequency_row():
    exponent = np.arange(0, HEAD_DIM, 2, dtype=np.float64) / HEAD_DIM
    base = ROPE_THETA**-exponent
    wavelength = 2.0 * np.pi / base
    smooth = (TRAINED_CONTEXT / wavelength - LOW_FACTOR) / (HIGH_FACTOR - LOW_FACTOR)
    blended = (1.0 - smooth) * base / ROPE_FACTOR + smooth * base
    frequencies = np.where(
        wavelength < TRAINED_CONTEXT / HIGH_FACTOR,
        base,
        np.where(wavelength > TRAINED_CONTEXT / LOW_FACTOR, base / ROPE_FACTOR, blended),
    )
    return np.tile(frequencies, 2)[None, :].astype(np.float32)


def turned_sine(sine):
    lane = lax.broadcasted_iota(jnp.int32, sine.shape, 1)
    return jnp.where(lane < HEAD_DIM // 2, -sine, sine)


def rotate(vectors, cosine, signed_sine):
    wide = vectors.astype(jnp.float32)
    return (wide * cosine + pltpu.roll(wide, HEAD_DIM // 2, 1) * signed_sine).astype(jnp.bfloat16)


def angle_sum(cos_a, sin_a, cos_b, sin_b):
    return cos_a * cos_b - sin_a * sin_b, sin_a * cos_b + cos_a * sin_b


def shard_tables(cosines, sines, line, rows):
    cos_f, sin_f = cosines[pl.ds(0, FINE), :], turned_sine(sines[pl.ds(0, FINE), :])
    cos_c, sin_c = angle_sum(
        cosines[pl.ds(FINE, FINE), :],
        sines[pl.ds(FINE, FINE), :],
        cosines[pl.ds(line, 1), :],
        sines[pl.ds(line, 1), :],
    )
    signed = turned_sine(sin_c)
    parts = [
        (
            cos_f * cos_c[i : i + 1] - sin_f * signed[i : i + 1],
            sin_f * cos_c[i : i + 1] + cos_f * signed[i : i + 1],
        )
        for i in range(rows // FINE)
    ]
    return tuple(jnp.concatenate(table, axis=0) for table in zip(*parts))


def prepare_kernel(
    query_start_of, offsets, vertical, slash, queries, freq, rotated, cosines, sines, masks,
    angles, bias, held, arrival,
):
    query_rows, columns = held.shape
    heads = columns // HEAD_DIM
    fetch = pltpu.make_async_copy(queries, held, arrival)
    fetch.start()
    query_start, first_list = query_start_of()

    step = lax.broadcasted_iota(jnp.int32, (FINE, HEAD_DIM), 0)
    angles[pl.ds(0, FINE), :] = step
    angles[pl.ds(FINE, FINE), :] = step * FINE
    for shard in range(offsets.shape[0]):
        angles[pl.ds(2 * FINE + shard, 1), :] = jnp.full((1, HEAD_DIM), offsets[shard], jnp.int32)
    angles[pl.ds(angles.shape[0] - 8, 8), :] = jnp.full((8, HEAD_DIM), query_start, jnp.int32)
    angle = angles[...].astype(jnp.float32) * freq[...]
    cosines[...] = jnp.cos(angle)
    sines[...] = jnp.sin(angle)

    key_block = lax.broadcasted_iota(jnp.int32, bias.shape, 0)
    lane_block = lax.broadcasted_iota(jnp.int32, (1, query_rows), 1) // BLOCK
    hit = jnp.zeros(bias.shape, jnp.bool_)
    for entries, distance in ((vertical, False), (slash, True)):
        for entry in range(entries.shape[1]):
            wanted = jnp.zeros((1, query_rows), jnp.int32)
            for block in range(query_rows // BLOCK):
                value = entries[first_list + block, entry]
                if distance:
                    value = query_start // BLOCK + block - value
                wanted = jnp.where(lane_block == block, value, wanted)
            hit = hit | (key_block == wanted)
    bias[...] = jnp.where(hit, 0.0, MASKED_SCORE)

    rows = masks.shape[0] // offsets.shape[0]
    ahead = lax.broadcasted_iota(jnp.int32, (rows, query_rows), 1) - lax.broadcasted_iota(
        jnp.int32, (rows, query_rows), 0
    )

    @pl.loop(0, offsets.shape[0])
    def _(shard):
        offset = offsets[shard]
        lines = [
            jnp.broadcast_to(bias[pl.ds(offset // BLOCK + block, 1), :], (BLOCK, query_rows))
            for block in range(rows // BLOCK)
        ]
        masks[pl.ds(pl.multiple_of(shard * rows, rows), rows), :] = jnp.where(
            ahead >= offset - query_start, jnp.concatenate(lines, axis=0), MASKED_SCORE
        ).astype(masks.dtype)

    cosine, sine = shard_tables(cosines, sines, angles.shape[0] - 8, query_rows)
    fetch.wait()
    for head in range(heads):
        turned = rotate(held[:, pl.ds(head * HEAD_DIM, HEAD_DIM)], cosine, sine).T
        for tile in range(query_rows // TILE):
            lines = pl.ds((tile * heads + head) * TILE, TILE)
            rotated[:, lines] = turned[:, tile * TILE : (tile + 1) * TILE]


def attend_kernel(place_of, shards_of, first, last, *refs):
    rotated, cosines, sines, masks = refs[:4]
    refs = refs[4:]
    if not first:
        old_peak, old_sums = refs[:2]
        refs = refs[2:]
    if last:
        pieces, out = refs[:-1], refs[-1]
    else:
        pieces, new_peak, new_sums = refs[:-2], refs[-2], refs[-1]
    query_rows = masks.shape[1]
    tiles = query_rows // TILE
    width = rotated.shape[1] // tiles
    rows = masks.shape[0] // (cosines.shape[0] - 2 * FINE - 8)
    ones = jnp.ones((SUM_ROWS, rows), jnp.bfloat16)
    unit = (
        lax.broadcasted_iota(jnp.int32, (TILE, width), 0)
        == lax.broadcasted_iota(jnp.int32, (TILE, width), 1) % TILE
    ).astype(jnp.bfloat16)

    def load_keys(keys, shard):
        keys = rotate(keys, *shard_tables(cosines, sines, 2 * FINE + shard, rows))
        return keys, masks[pl.ds(pl.multiple_of(shard * rows, rows), rows), :]

    def load_values(values):
        return jnp.concatenate([values.T, ones], axis=0)

    def score(keys, mask, start, size):
        tile = start // width
        query = jnp.concatenate([rotated[:, pl.ds(start, size)], unit[:, :size]], axis=0)
        return jnp.dot(
            jnp.concatenate([keys, mask[:, tile * TILE : (tile + 1) * TILE]], axis=1),
            query,
            preferred_element_type=jnp.float32,
        )

    def update(scores, values, before):
        peak = scores.max(axis=0, keepdims=True)
        if before is not None:
            peak = jnp.maximum(before[0], peak)
        weights = jnp.exp2((scores - peak) * SCORE_SCALE).astype(jnp.bfloat16)
        sums = jnp.dot(values, weights, preferred_element_type=jnp.float32)
        if before is not None:
            sums = sums + before[1] * jnp.exp2((before[0] - peak) * SCORE_SCALE)
        return peak, sums

    def finish(start, peak, sums):
        size = sums.shape[1]
        if not last:
            span = pl.ds(start, size)
            new_peak[:, span] = jnp.broadcast_to(peak, (new_peak.shape[0], size))
            new_sums[:, span] = sums
            return
        part = sums[:HEAD_DIM] * (1.0 / sums[HEAD_DIM : HEAD_DIM + 1])
        part = part.astype(out.dtype)
        for column in range(0, size, TILE):
            tile, head = divmod((start + column) // TILE, width // TILE)
            out[pl.ds(tile * TILE, TILE), pl.ds(head * HEAD_DIM, HEAD_DIM)] = part[
                :, column : column + TILE
            ].T

    if shards_of is not None:
        shards = shards_of(pieces, *place_of())
        keys, mask = (
            jnp.concatenate(part, axis=0)
            for part in zip(*(load_keys(keys, shard) for keys, _, shard in shards))
        )
        starts = list(range(0, rotated.shape[1], CHUNK))
        ahead = score(keys, mask, starts[0], CHUNK)
        values = jnp.concatenate([load_values(values) for _, values, _ in shards], axis=1)
        for start in starts:
            scores = ahead
            if start != starts[-1]:
                ahead = score(keys, mask, start + CHUNK, CHUNK)
            before = None
            if not first:
                before = (old_peak[:1, pl.ds(start, CHUNK)], old_sums[:, pl.ds(start, CHUNK)])
            finish(start, *update(scores, values, before))
    else:
        (whole,) = pieces
        for tile in range(tiles):

            def step(shard, before, tile=tile):
                start = pl.multiple_of(shard * (2 * rows), 2 * rows)
                keys, mask = load_keys(whole[pl.ds(start, rows), :], shard)
                values = load_values(whole[pl.ds(start + rows, rows), :])
                return update(score(keys, mask, tile * width, width), values, before)

            initial = (
                jnp.full((1, width), MASKED_SCORE, jnp.float32),
                jnp.zeros((HEAD_DIM + SUM_ROWS, width), jnp.float32),
            )
            finish(
                tile * width, *lax.fori_loop(0, whole.shape[0] // (2 * rows), step, initial)
            )


def local(queries, cached_keys, cached_values, key_offsets, vertical_blocks, slash_offsets):
    query_rows = queries.shape[0]
    heads = queries.shape[1] // HEAD_DIM
    rows = cached_keys.shape[0]
    n_seg, n_ctx = lax.axis_size("seg"), lax.axis_size("ctx")
    shards = n_seg * n_ctx
    prefix = rows * shards - query_rows * n_ctx

    def query_start_of():
        ctx = lax.axis_index("ctx")
        return prefix + ctx * query_rows, ctx * (query_rows // BLOCK)

    def place_of():
        return tuple(lax.axis_index(axis) for axis in AXES)

    def exchange(a, partner):
        pairs = []
        for seg in range(n_seg):
            for ctx in range(n_ctx):
                for head in range(2):
                    to_seg, to_ctx, to_head = partner(seg, ctx, head)
                    pairs.append(
                        ((seg * n_ctx + ctx) * 2 + head, (to_seg * n_ctx + to_ctx) * 2 + to_head)
                    )
        return lax.ppermute(a, AXES, pairs)

    def swap(a):
        return exchange(a, lambda s, c, h: (s, c, 1 - h))

    vmem = pl.BlockSpec(memory_space=pltpu.VMEM)
    smem = pl.BlockSpec(memory_space=pltpu.SMEM)
    f32 = jnp.float32
    direct = (n_seg, n_ctx) == DIRECT_SHARDS
    limit = (16 if direct else 56) * 1024 * 1024
    shape = jax.ShapeDtypeStruct
    lines = 2 * FINE + shards + 8
    prepared = pl.pallas_call(
        functools.partial(prepare_kernel, query_start_of),
        out_shape=(
            shape((HEAD_DIM, query_rows * heads), jnp.bfloat16),
            shape((lines, HEAD_DIM), f32),
            shape((lines, HEAD_DIM), f32),
            shape((shards * rows, query_rows), jnp.bfloat16),
        ),
        in_specs=[smem, smem, smem, pl.BlockSpec(memory_space=pltpu.HBM), vmem],
        out_specs=[vmem] * 4,
        scratch_shapes=[
            pltpu.VMEM((lines, HEAD_DIM), jnp.int32),
            pltpu.VMEM((shards * rows // BLOCK, query_rows), f32),
            pltpu.VMEM(queries.shape, queries.dtype),
            pltpu.SemaphoreType.DMA(()),
        ],
        compiler_params=pltpu.CompilerParams(vmem_limit_bytes=limit),
        name="prepare",
    )(key_offsets, vertical_blocks, slash_offsets, queries, jnp.asarray(frequency_row()))

    def attend(prepared, pieces, shards_of, state, last):
        state_shape = (
            shape((8, query_rows * heads), f32),
            shape((HEAD_DIM + SUM_ROWS, query_rows * heads), f32),
        )
        return pl.pallas_call(
            functools.partial(attend_kernel, place_of, shards_of, not state, last),
            out_shape=shape(queries.shape, queries.dtype) if last else state_shape,
            in_specs=[vmem] * (4 + len(state) + len(pieces)),
            out_specs=vmem if last else (vmem, vmem),
            compiler_params=pltpu.CompilerParams(vmem_limit_bytes=limit),
            cost_estimate=pl.CostEstimate(
                flops=4 * 10**9, bytes_accessed=10**6, transcendentals=10**6
            ),
            name="attend",
        )(*prepared, *state, *pieces)

    own = jnp.concatenate([cached_keys, cached_values], axis=0)
    if not direct:
        gathered = lax.all_gather(own, ("seg", "ctx"), axis=0, tiled=True)
        return attend(prepared, [gathered], None, (), True)

    def number(seg, ctx):
        return seg * n_ctx + ctx

    def whole(ref):
        return ref[:rows, :], ref[rows : 2 * rows, :]

    far = exchange(own, lambda s, c, h: (s ^ (3 - h), c, h))
    near = exchange(own, lambda s, c, h: (s ^ (1 - h), c ^ h, h))
    near, prepared = lax.optimization_barrier((near, prepared))
    beside = swap(near)
    across = exchange(far, lambda s, c, h: (s, c ^ 1, h))
    state = attend(
        prepared,
        [own, near, beside, far],
        lambda refs, s, c, h: [
            (*whole(refs[0]), number(s, c)),
            (*whole(refs[1]), number(s ^ (1 - h), c ^ h)),
            (*whole(refs[2]), number(s ^ h, c ^ (1 - h))),
            (*whole(refs[3]), number(s ^ (3 - h), c)),
        ],
        (),
        False,
    )
    far_after, beside = lax.optimization_barrier((far, beside))
    far_beside = swap(far_after)
    half = jnp.where(lax.axis_index("head") == 0, beside[:rows], near[rows:])
    diagonal = exchange(half, lambda s, c, h: (s ^ 1, c, h))
    across, diagonal, state = lax.optimization_barrier((across, diagonal, state))
    last_beside = swap(jnp.concatenate([across, diagonal], axis=0))
    state = attend(
        prepared,
        [far_beside, across],
        lambda refs, s, c, h: [
            (*whole(refs[0]), number(s ^ (2 + h), c)),
            (*whole(refs[1]), number(s ^ (3 - h), c ^ 1)),
        ],
        state,
        False,
    )

    def last_shards(refs, s, c, h):
        diagonal, beside = refs
        mine, other = diagonal[...], beside[2 * rows :, :]
        return [
            (*whole(beside), number(s ^ (2 + h), c ^ 1)),
            (
                jnp.where(h == 0, mine, other),
                jnp.where(h == 0, other, mine),
                number(s ^ 1, c ^ 1),
            ),
        ]

    return attend(prepared, [diagonal, last_beside], last_shards, state, True)


def solution(mesh):
    return jax.shard_map(
        local,
        mesh=mesh,
        in_specs=(
            P(("groups", "ctx"), "head"),
            P(("groups", "seg", "ctx"), None),
            P(("groups", "seg", "ctx"), None),
            P("groups"),
            P("groups", None),
            P("groups", None),
        ),
        out_specs=P(("groups", "ctx"), "head"),
        check_vma=False,
    )
```

```python
import functools
import math

import jax
import jax.numpy as jnp
import numpy as np
from jax import lax
from jax.experimental import pallas as pl
from jax.experimental.pallas import tpu as pltpu
from jax.sharding import PartitionSpec as P

HEAD_DIM = 128
BLOCK = 64
ROPE_THETA = 500000.0
ROPE_FACTOR = 8.0
LOW_FACTOR = 1.0
HIGH_FACTOR = 4.0
TRAINED_CONTEXT = 8192.0
MASKED_SCORE = -1e30
SCORE_SCALE = HEAD_DIM**-0.5 * math.log2(math.e)
TILE = 128
FINE = 16
SUM_ROWS = 16
CHUNK = 256
DIRECT_SHARDS = (4, 2)
AXES = ("seg", "ctx", "head")


def frequency_row():
    exponent = np.arange(0, HEAD_DIM, 2, dtype=np.float64) / HEAD_DIM
    base = ROPE_THETA**-exponent
    wavelength = 2.0 * np.pi / base
    smooth = (TRAINED_CONTEXT / wavelength - LOW_FACTOR) / (HIGH_FACTOR - LOW_FACTOR)
    blended = (1.0 - smooth) * base / ROPE_FACTOR + smooth * base
    frequencies = np.where(
        wavelength < TRAINED_CONTEXT / HIGH_FACTOR,
        base,
        np.where(wavelength > TRAINED_CONTEXT / LOW_FACTOR, base / ROPE_FACTOR, blended),
    )
    return np.tile(frequencies, 2)[None, :].astype(np.float32)


def turned_sine(sine):
    lane = lax.broadcasted_iota(jnp.int32, sine.shape, 1)
    return jnp.where(lane < HEAD_DIM // 2, -sine, sine)


def rotate(vectors, cosine, signed_sine):
    wide = vectors.astype(jnp.float32)
    return (wide * cosine + pltpu.roll(wide, HEAD_DIM // 2, 1) * signed_sine).astype(jnp.bfloat16)


def angle_sum(cos_a, sin_a, cos_b, sin_b):
    return cos_a * cos_b - sin_a * sin_b, sin_a * cos_b + cos_a * sin_b


def shard_tables(cosines, sines, line, rows):
    cos_f, sin_f = cosines[pl.ds(0, FINE), :], turned_sine(sines[pl.ds(0, FINE), :])
    cos_c, sin_c = angle_sum(
        cosines[pl.ds(FINE, FINE), :],
        sines[pl.ds(FINE, FINE), :],
        cosines[pl.ds(line, 1), :],
        sines[pl.ds(line, 1), :],
    )
    signed = turned_sine(sin_c)
    parts = [
        (
            cos_f * cos_c[i : i + 1] - sin_f * signed[i : i + 1],
            sin_f * cos_c[i : i + 1] + cos_f * signed[i : i + 1],
        )
        for i in range(rows // FINE)
    ]
    return tuple(jnp.concatenate(table, axis=0) for table in zip(*parts))


def prepare_kernel(
    query_start_of, offsets, vertical, slash, queries, freq, rotated, cosines, sines, masks,
    angles, bias, held, arrival,
):
    query_rows, columns = held.shape
    heads = columns // HEAD_DIM
    fetch = pltpu.make_async_copy(queries, held, arrival)
    fetch.start()
    query_start, first_list = query_start_of()

    step = lax.broadcasted_iota(jnp.int32, (FINE, HEAD_DIM), 0)
    angles[pl.ds(0, FINE), :] = step
    angles[pl.ds(FINE, FINE), :] = step * FINE
    for shard in range(offsets.shape[0]):
        angles[pl.ds(2 * FINE + shard, 1), :] = jnp.full((1, HEAD_DIM), offsets[shard], jnp.int32)
    angles[pl.ds(angles.shape[0] - 8, 8), :] = jnp.full((8, HEAD_DIM), query_start, jnp.int32)
    angle = angles[...].astype(jnp.float32) * freq[...]
    cosines[...] = jnp.cos(angle)
    sines[...] = jnp.sin(angle)

    key_block = lax.broadcasted_iota(jnp.int32, bias.shape, 0)
    lane_block = lax.broadcasted_iota(jnp.int32, (1, query_rows), 1) // BLOCK
    hit = jnp.zeros(bias.shape, jnp.bool_)
    for entries, distance in ((vertical, False), (slash, True)):
        for entry in range(entries.shape[1]):
            wanted = jnp.zeros((1, query_rows), jnp.int32)
            for block in range(query_rows // BLOCK):
                value = entries[first_list + block, entry]
                if distance:
                    value = query_start // BLOCK + block - value
                wanted = jnp.where(lane_block == block, value, wanted)
            hit = hit | (key_block == wanted)
    bias[...] = jnp.where(hit, 0.0, MASKED_SCORE)

    rows = masks.shape[0] // offsets.shape[0]
    ahead = lax.broadcasted_iota(jnp.int32, (rows, query_rows), 1) - lax.broadcasted_iota(
        jnp.int32, (rows, query_rows), 0
    )

    @pl.loop(0, offsets.shape[0])
    def _(shard):
        offset = offsets[shard]
        lines = [
            jnp.broadcast_to(bias[pl.ds(offset // BLOCK + block, 1), :], (BLOCK, query_rows))
            for block in range(rows // BLOCK)
        ]
        masks[pl.ds(pl.multiple_of(shard * rows, rows), rows), :] = jnp.where(
            ahead >= offset - query_start, jnp.concatenate(lines, axis=0), MASKED_SCORE
        ).astype(masks.dtype)

    cosine, sine = shard_tables(cosines, sines, angles.shape[0] - 8, query_rows)
    fetch.wait()
    for head in range(heads):
        turned = rotate(held[:, pl.ds(head * HEAD_DIM, HEAD_DIM)], cosine, sine).T
        for tile in range(query_rows // TILE):
            lines = pl.ds((tile * heads + head) * TILE, TILE)
            rotated[:, lines] = turned[:, tile * TILE : (tile + 1) * TILE]


def attend_kernel(place_of, shards_of, first, last, *refs):
    rotated, cosines, sines, masks = refs[:4]
    refs = refs[4:]
    if not first:
        old_peak, old_sums = refs[:2]
        refs = refs[2:]
    if last:
        pieces, out = refs[:-1], refs[-1]
    else:
        pieces, new_peak, new_sums = refs[:-2], refs[-2], refs[-1]
    query_rows = masks.shape[1]
    tiles = query_rows // TILE
    width = rotated.shape[1] // tiles
    rows = masks.shape[0] // (cosines.shape[0] - 2 * FINE - 8)
    ones = jnp.ones((SUM_ROWS, rows), jnp.bfloat16)
    unit = (
        lax.broadcasted_iota(jnp.int32, (TILE, width), 0)
        == lax.broadcasted_iota(jnp.int32, (TILE, width), 1) % TILE
    ).astype(jnp.bfloat16)

    def load_keys(keys, shard):
        keys = rotate(keys, *shard_tables(cosines, sines, 2 * FINE + shard, rows))
        return keys, masks[pl.ds(pl.multiple_of(shard * rows, rows), rows), :]

    def load_values(values):
        return jnp.concatenate([values.T, ones], axis=0)

    def score(keys, mask, start, size):
        tile = start // width
        query = jnp.concatenate([rotated[:, pl.ds(start, size)], unit[:, :size]], axis=0)
        return jnp.dot(
            jnp.concatenate([keys, mask[:, tile * TILE : (tile + 1) * TILE]], axis=1),
            query,
            preferred_element_type=jnp.float32,
        )

    def update(scores, values, before):
        peak = scores.max(axis=0, keepdims=True)
        if before is not None:
            peak = jnp.maximum(before[0], peak)
        weights = jnp.exp2((scores - peak) * SCORE_SCALE).astype(jnp.bfloat16)
        sums = jnp.dot(values, weights, preferred_element_type=jnp.float32)
        if before is not None:
            sums = sums + before[1] * jnp.exp2((before[0] - peak) * SCORE_SCALE)
        return peak, sums

    def finish(start, peak, sums):
        size = sums.shape[1]
        if not last:
            span = pl.ds(start, size)
            new_peak[:, span] = jnp.broadcast_to(peak, (new_peak.shape[0], size))
            new_sums[:, span] = sums
            return
        part = sums[:HEAD_DIM] * (1.0 / sums[HEAD_DIM : HEAD_DIM + 1])
        part = part.astype(out.dtype)
        for column in range(0, size, TILE):
            tile, head = divmod((start + column) // TILE, width // TILE)
            out[pl.ds(tile * TILE, TILE), pl.ds(head * HEAD_DIM, HEAD_DIM)] = part[
                :, column : column + TILE
            ].T

    if shards_of is not None:
        shards = shards_of(pieces, *place_of())
        keys, mask = (
            jnp.concatenate(part, axis=0)
            for part in zip(*(load_keys(keys, shard) for keys, _, shard in shards))
        )
        starts = list(range(0, rotated.shape[1], CHUNK))
        ahead = score(keys, mask, starts[0], CHUNK)
        values = jnp.concatenate([load_values(values) for _, values, _ in shards], axis=1)
        for start in starts:
            scores = ahead
            if start != starts[-1]:
                ahead = score(keys, mask, start + CHUNK, CHUNK)
            before = None
            if not first:
                before = (old_peak[:1, pl.ds(start, CHUNK)], old_sums[:, pl.ds(start, CHUNK)])
            finish(start, *update(scores, values, before))
    else:
        (whole,) = pieces
        for tile in range(tiles):

            def step(shard, before, tile=tile):
                start = pl.multiple_of(shard * (2 * rows), 2 * rows)
                keys, mask = load_keys(whole[pl.ds(start, rows), :], shard)
                values = load_values(whole[pl.ds(start + rows, rows), :])
                return update(score(keys, mask, tile * width, width), values, before)

            initial = (
                jnp.full((1, width), MASKED_SCORE, jnp.float32),
                jnp.zeros((HEAD_DIM + SUM_ROWS, width), jnp.float32),
            )
            finish(
                tile * width, *lax.fori_loop(0, whole.shape[0] // (2 * rows), step, initial)
            )


def local(queries, cached_keys, cached_values, key_offsets, vertical_blocks, slash_offsets):
    query_rows = queries.shape[0]
    heads = queries.shape[1] // HEAD_DIM
    rows = cached_keys.shape[0]
    n_seg, n_ctx = lax.axis_size("seg"), lax.axis_size("ctx")
    shards = n_seg * n_ctx
    prefix = rows * shards - query_rows * n_ctx

    def query_start_of():
        ctx = lax.axis_index("ctx")
        return prefix + ctx * query_rows, ctx * (query_rows // BLOCK)

    def place_of():
        return tuple(lax.axis_index(axis) for axis in AXES)

    def exchange(a, partner):
        pairs = []
        for seg in range(n_seg):
            for ctx in range(n_ctx):
                for head in range(2):
                    to_seg, to_ctx, to_head = partner(seg, ctx, head)
                    pairs.append(
                        ((seg * n_ctx + ctx) * 2 + head, (to_seg * n_ctx + to_ctx) * 2 + to_head)
                    )
        return lax.ppermute(a, AXES, pairs)

    def swap(a):
        return exchange(a, lambda s, c, h: (s, c, 1 - h))

    vmem = pl.BlockSpec(memory_space=pltpu.VMEM)
    smem = pl.BlockSpec(memory_space=pltpu.SMEM)
    f32 = jnp.float32
    direct = (n_seg, n_ctx) == DIRECT_SHARDS
    limit = (16 if direct else 56) * 1024 * 1024
    shape = jax.ShapeDtypeStruct
    lines = 2 * FINE + shards + 8
    prepared = pl.pallas_call(
        functools.partial(prepare_kernel, query_start_of),
        out_shape=(
            shape((HEAD_DIM, query_rows * heads), jnp.bfloat16),
            shape((lines, HEAD_DIM), f32),
            shape((lines, HEAD_DIM), f32),
            shape((shards * rows, query_rows), jnp.bfloat16),
        ),
        in_specs=[smem, smem, smem, pl.BlockSpec(memory_space=pltpu.HBM), vmem],
        out_specs=[vmem] * 4,
        scratch_shapes=[
            pltpu.VMEM((lines, HEAD_DIM), jnp.int32),
            pltpu.VMEM((shards * rows // BLOCK, query_rows), f32),
            pltpu.VMEM(queries.shape, queries.dtype),
            pltpu.SemaphoreType.DMA(()),
        ],
        compiler_params=pltpu.CompilerParams(vmem_limit_bytes=limit),
        cost_estimate=pl.CostEstimate(flops=4 * 10**9, bytes_accessed=10**6, transcendentals=10**5),
        name="prepare",
    )(key_offsets, vertical_blocks, slash_offsets, queries, jnp.asarray(frequency_row()))

    def attend(prepared, pieces, shards_of, state, last):
        state_shape = (
            shape((8, query_rows * heads), f32),
            shape((HEAD_DIM + SUM_ROWS, query_rows * heads), f32),
        )
        return pl.pallas_call(
            functools.partial(attend_kernel, place_of, shards_of, not state, last),
            out_shape=shape(queries.shape, queries.dtype) if last else state_shape,
            in_specs=[vmem] * (4 + len(state) + len(pieces)),
            out_specs=vmem if last else (vmem, vmem),
            compiler_params=pltpu.CompilerParams(vmem_limit_bytes=limit),
            cost_estimate=pl.CostEstimate(
                flops=4 * 10**9, bytes_accessed=10**6, transcendentals=10**6
            ),
            name="attend",
        )(*prepared, *state, *pieces)

    own = jnp.concatenate([cached_keys, cached_values], axis=0)
    if not direct:
        gathered = lax.all_gather(own, ("seg", "ctx"), axis=0, tiled=True)
        return attend(prepared, [gathered], None, (), True)

    def number(seg, ctx):
        return lax.rem(seg, n_seg) * n_ctx + ctx

    def whole(ref):
        return ref[:rows, :], ref[rows : 2 * rows, :]

    far = exchange(own, lambda s, c, h: ((s + 1 + h) % n_seg, c, h))
    near = exchange(own, lambda s, c, h: ((s + 3 - 3 * h) % n_seg, c ^ h, h))
    near, prepared = lax.optimization_barrier((near, prepared))
    beside = swap(near)
    across = exchange(far, lambda s, c, h: (s, c ^ 1, h))
    state = attend(
        prepared,
        [own, near, beside, far],
        lambda refs, s, c, h: [
            (*whole(refs[0]), number(s, c)),
            (*whole(refs[1]), number(s + (1 - h), c ^ h)),
            (*whole(refs[2]), number(s + h, c ^ (1 - h))),
            (*whole(refs[3]), number(s + (3 - h), c)),
        ],
        (),
        False,
    )
    far_after, beside = lax.optimization_barrier((far, beside))
    far_beside = swap(far_after)
    half = jnp.where(lax.axis_index("head") == 0, beside[:rows], near[rows:])
    diagonal = exchange(half, lambda s, c, h: ((s + 3) % n_seg, c, h))
    across, diagonal, state = lax.optimization_barrier((across, diagonal, state))
    last_beside = swap(jnp.concatenate([across, diagonal], axis=0))
    state = attend(
        prepared,
        [far_beside, across],
        lambda refs, s, c, h: [
            (*whole(refs[0]), number(s + (2 + h), c)),
            (*whole(refs[1]), number(s + (3 - h), c ^ 1)),
        ],
        state,
        False,
    )

    def last_shards(refs, s, c, h):
        diagonal, beside = refs
        mine, other = diagonal[...], beside[2 * rows :, :]
        return [
            (*whole(beside), number(s + (2 + h), c ^ 1)),
            (
                jnp.where(h == 0, mine, other),
                jnp.where(h == 0, other, mine),
                number(s + 1, c ^ 1),
            ),
        ]

    return attend(prepared, [diagonal, last_beside], last_shards, state, True)


def solution(mesh):
    return jax.shard_map(
        local,
        mesh=mesh,
        in_specs=(
            P(("groups", "ctx"), "head"),
            P(("groups", "seg", "ctx"), None),
            P(("groups", "seg", "ctx"), None),
            P("groups"),
            P("groups", None),
            P("groups", None),
        ),
        out_specs=P(("groups", "ctx"), "head"),
        check_vma=False,
    )
```

```python
import functools
import math

import jax
import jax.numpy as jnp
import numpy as np
from jax import lax
from jax.experimental import pallas as pl
from jax.experimental.pallas import tpu as pltpu
from jax.sharding import PartitionSpec as P

HEAD_DIM = 128
BLOCK = 64
ROPE_THETA = 500000.0
ROPE_FACTOR = 8.0
LOW_FACTOR = 1.0
HIGH_FACTOR = 4.0
TRAINED_CONTEXT = 8192.0
MASKED_SCORE = -1e30
SCORE_SCALE = HEAD_DIM**-0.5 * math.log2(math.e)
TILE = 128
FINE = 16
SUM_ROWS = 16
CHUNK = 256
DIRECT_SHARDS = (4, 2)
AXES = ("seg", "ctx", "head")


def frequency_row():
    exponent = np.arange(0, HEAD_DIM, 2, dtype=np.float64) / HEAD_DIM
    base = ROPE_THETA**-exponent
    wavelength = 2.0 * np.pi / base
    smooth = (TRAINED_CONTEXT / wavelength - LOW_FACTOR) / (HIGH_FACTOR - LOW_FACTOR)
    blended = (1.0 - smooth) * base / ROPE_FACTOR + smooth * base
    frequencies = np.where(
        wavelength < TRAINED_CONTEXT / HIGH_FACTOR,
        base,
        np.where(wavelength > TRAINED_CONTEXT / LOW_FACTOR, base / ROPE_FACTOR, blended),
    )
    return np.tile(frequencies, 2)[None, :].astype(np.float32)


def turned_sine(sine):
    lane = lax.broadcasted_iota(jnp.int32, sine.shape, 1)
    return jnp.where(lane < HEAD_DIM // 2, -sine, sine)


def rotate(vectors, cosine, signed_sine):
    wide = vectors.astype(jnp.float32)
    return (wide * cosine + pltpu.roll(wide, HEAD_DIM // 2, 1) * signed_sine).astype(jnp.bfloat16)


def angle_sum(cos_a, sin_a, cos_b, sin_b):
    return cos_a * cos_b - sin_a * sin_b, sin_a * cos_b + cos_a * sin_b


def shard_tables(cosines, sines, line, rows):
    cos_f, sin_f = cosines[pl.ds(0, FINE), :], turned_sine(sines[pl.ds(0, FINE), :])
    cos_c, sin_c = angle_sum(
        cosines[pl.ds(FINE, FINE), :],
        sines[pl.ds(FINE, FINE), :],
        cosines[pl.ds(line, 1), :],
        sines[pl.ds(line, 1), :],
    )
    signed = turned_sine(sin_c)
    parts = [
        (
            cos_f * cos_c[i : i + 1] - sin_f * signed[i : i + 1],
            sin_f * cos_c[i : i + 1] + cos_f * signed[i : i + 1],
        )
        for i in range(rows // FINE)
    ]
    return tuple(jnp.concatenate(table, axis=0) for table in zip(*parts))


def prepare_kernel(
    query_start_of, offsets, vertical, slash, queries, freq, rotated, cosines, sines, masks,
    angles, bias, held, arrival,
):
    query_rows, columns = held.shape
    heads = columns // HEAD_DIM
    fetch = pltpu.make_async_copy(queries, held, arrival)
    fetch.start()
    query_start, first_list = query_start_of()

    step = lax.broadcasted_iota(jnp.int32, (FINE, HEAD_DIM), 0)
    angles[pl.ds(0, FINE), :] = step
    angles[pl.ds(FINE, FINE), :] = step * FINE
    for shard in range(offsets.shape[0]):
        angles[pl.ds(2 * FINE + shard, 1), :] = jnp.full((1, HEAD_DIM), offsets[shard], jnp.int32)
    angles[pl.ds(angles.shape[0] - 8, 8), :] = jnp.full((8, HEAD_DIM), query_start, jnp.int32)
    angle = angles[...].astype(jnp.float32) * freq[...]
    cosines[...] = jnp.cos(angle)
    sines[...] = jnp.sin(angle)

    key_block = lax.broadcasted_iota(jnp.int32, bias.shape, 0)
    lane_block = lax.broadcasted_iota(jnp.int32, (1, query_rows), 1) // BLOCK
    hit = jnp.zeros(bias.shape, jnp.bool_)
    for entries, distance in ((vertical, False), (slash, True)):
        for entry in range(entries.shape[1]):
            wanted = jnp.zeros((1, query_rows), jnp.int32)
            for block in range(query_rows // BLOCK):
                value = entries[first_list + block, entry]
                if distance:
                    value = query_start // BLOCK + block - value
                wanted = jnp.where(lane_block == block, value, wanted)
            hit = hit | (key_block == wanted)
    bias[...] = jnp.where(hit, 0.0, MASKED_SCORE)

    rows = masks.shape[0] // offsets.shape[0]
    ahead = lax.broadcasted_iota(jnp.int32, (rows, query_rows), 1) - lax.broadcasted_iota(
        jnp.int32, (rows, query_rows), 0
    )

    @pl.loop(0, offsets.shape[0])
    def _(shard):
        offset = offsets[shard]
        lines = [
            jnp.broadcast_to(bias[pl.ds(offset // BLOCK + block, 1), :], (BLOCK, query_rows))
            for block in range(rows // BLOCK)
        ]
        masks[pl.ds(pl.multiple_of(shard * rows, rows), rows), :] = jnp.where(
            ahead >= offset - query_start, jnp.concatenate(lines, axis=0), MASKED_SCORE
        ).astype(masks.dtype)

    cosine, sine = shard_tables(cosines, sines, angles.shape[0] - 8, query_rows)
    fetch.wait()
    for head in range(heads):
        turned = rotate(held[:, pl.ds(head * HEAD_DIM, HEAD_DIM)], cosine, sine).T
        for tile in range(query_rows // TILE):
            lines = pl.ds((tile * heads + head) * TILE, TILE)
            rotated[:, lines] = turned[:, tile * TILE : (tile + 1) * TILE]


def attend_kernel(place_of, shards_of, first, last, *refs):
    rotated, cosines, sines, masks = refs[:4]
    refs = refs[4:]
    if not first:
        old_peak, old_sums = refs[:2]
        refs = refs[2:]
    if last:
        pieces, out = refs[:-1], refs[-1]
    else:
        pieces, new_peak, new_sums = refs[:-2], refs[-2], refs[-1]
    query_rows = masks.shape[1]
    tiles = query_rows // TILE
    width = rotated.shape[1] // tiles
    rows = masks.shape[0] // (cosines.shape[0] - 2 * FINE - 8)
    ones = jnp.ones((SUM_ROWS, rows), jnp.bfloat16)
    unit = (
        lax.broadcasted_iota(jnp.int32, (TILE, width), 0)
        == lax.broadcasted_iota(jnp.int32, (TILE, width), 1) % TILE
    ).astype(jnp.bfloat16)

    def load_keys(keys, shard):
        keys = rotate(keys, *shard_tables(cosines, sines, 2 * FINE + shard, rows))
        return keys, masks[pl.ds(pl.multiple_of(shard * rows, rows), rows), :]

    def load_values(values):
        return jnp.concatenate([values.T, ones], axis=0)

    def score(keys, mask, start, size):
        tile = start // width
        query = jnp.concatenate([rotated[:, pl.ds(start, size)], unit[:, :size]], axis=0)
        return jnp.dot(
            jnp.concatenate([keys, mask[:, tile * TILE : (tile + 1) * TILE]], axis=1),
            query,
            preferred_element_type=jnp.float32,
        )

    def update(scores, values, before):
        peak = scores.max(axis=0, keepdims=True)
        if before is not None:
            peak = jnp.maximum(before[0], peak)
        weights = jnp.exp2((scores - peak) * SCORE_SCALE).astype(jnp.bfloat16)
        sums = jnp.dot(values, weights, preferred_element_type=jnp.float32)
        if before is not None:
            sums = sums + before[1] * jnp.exp2((before[0] - peak) * SCORE_SCALE)
        return peak, sums

    def finish(start, peak, sums):
        size = sums.shape[1]
        if not last:
            span = pl.ds(start, size)
            new_peak[:, span] = jnp.broadcast_to(peak, (new_peak.shape[0], size))
            new_sums[:, span] = sums
            return
        part = sums[:HEAD_DIM] * (1.0 / sums[HEAD_DIM : HEAD_DIM + 1])
        part = part.astype(out.dtype)
        for column in range(0, size, TILE):
            tile, head = divmod((start + column) // TILE, width // TILE)
            out[pl.ds(tile * TILE, TILE), pl.ds(head * HEAD_DIM, HEAD_DIM)] = part[
                :, column : column + TILE
            ].T

    if shards_of is not None:
        shards = shards_of(pieces, *place_of())
        keys, mask = (
            jnp.concatenate(part, axis=0)
            for part in zip(*(load_keys(keys, shard) for keys, _, shard in shards))
        )
        starts = list(range(0, rotated.shape[1], CHUNK))
        ahead = score(keys, mask, starts[0], CHUNK)
        values = jnp.concatenate([load_values(values) for _, values, _ in shards], axis=1)
        for start in starts:
            scores = ahead
            if start != starts[-1]:
                ahead = score(keys, mask, start + CHUNK, CHUNK)
            before = None
            if not first:
                before = (old_peak[:1, pl.ds(start, CHUNK)], old_sums[:, pl.ds(start, CHUNK)])
            finish(start, *update(scores, values, before))
    else:
        (whole,) = pieces
        for tile in range(tiles):

            def step(shard, before, tile=tile):
                start = pl.multiple_of(shard * (2 * rows), 2 * rows)
                keys, mask = load_keys(whole[pl.ds(start, rows), :], shard)
                values = load_values(whole[pl.ds(start + rows, rows), :])
                return update(score(keys, mask, tile * width, width), values, before)

            initial = (
                jnp.full((1, width), MASKED_SCORE, jnp.float32),
                jnp.zeros((HEAD_DIM + SUM_ROWS, width), jnp.float32),
            )
            finish(
                tile * width, *lax.fori_loop(0, whole.shape[0] // (2 * rows), step, initial)
            )


def local(queries, cached_keys, cached_values, key_offsets, vertical_blocks, slash_offsets):
    query_rows = queries.shape[0]
    heads = queries.shape[1] // HEAD_DIM
    rows = cached_keys.shape[0]
    n_seg, n_ctx = lax.axis_size("seg"), lax.axis_size("ctx")
    shards = n_seg * n_ctx
    prefix = rows * shards - query_rows * n_ctx

    def query_start_of():
        ctx = lax.axis_index("ctx")
        return prefix + ctx * query_rows, ctx * (query_rows // BLOCK)

    def place_of():
        return tuple(lax.axis_index(axis) for axis in AXES)

    def exchange(a, partner):
        pairs = []
        for seg in range(n_seg):
            for ctx in range(n_ctx):
                for head in range(2):
                    to_seg, to_ctx, to_head = partner(seg, ctx, head)
                    pairs.append(
                        ((seg * n_ctx + ctx) * 2 + head, (to_seg * n_ctx + to_ctx) * 2 + to_head)
                    )
        return lax.ppermute(a, AXES, pairs)

    def swap(a):
        return exchange(a, lambda s, c, h: (s, c, 1 - h))

    vmem = pl.BlockSpec(memory_space=pltpu.VMEM)
    smem = pl.BlockSpec(memory_space=pltpu.SMEM)
    f32 = jnp.float32
    direct = (n_seg, n_ctx) == DIRECT_SHARDS
    limit = (16 if direct else 56) * 1024 * 1024
    shape = jax.ShapeDtypeStruct
    lines = 2 * FINE + shards + 8
    prepared = pl.pallas_call(
        functools.partial(prepare_kernel, query_start_of),
        out_shape=(
            shape((HEAD_DIM, query_rows * heads), jnp.bfloat16),
            shape((lines, HEAD_DIM), f32),
            shape((lines, HEAD_DIM), f32),
            shape((shards * rows, query_rows), jnp.bfloat16),
        ),
        in_specs=[smem, smem, smem, pl.BlockSpec(memory_space=pltpu.HBM), vmem],
        out_specs=[vmem] * 4,
        scratch_shapes=[
            pltpu.VMEM((lines, HEAD_DIM), jnp.int32),
            pltpu.VMEM((shards * rows // BLOCK, query_rows), f32),
            pltpu.VMEM(queries.shape, queries.dtype),
            pltpu.SemaphoreType.DMA(()),
        ],
        compiler_params=pltpu.CompilerParams(vmem_limit_bytes=limit),
        cost_estimate=pl.CostEstimate(flops=4 * 10**9, bytes_accessed=10**6, transcendentals=10**5),
        name="prepare",
    )(key_offsets, vertical_blocks, slash_offsets, queries, jnp.asarray(frequency_row()))

    def attend(prepared, pieces, shards_of, state, last):
        state_shape = (
            shape((8, query_rows * heads), f32),
            shape((HEAD_DIM + SUM_ROWS, query_rows * heads), f32),
        )
        return pl.pallas_call(
            functools.partial(attend_kernel, place_of, shards_of, not state, last),
            out_shape=shape(queries.shape, queries.dtype) if last else state_shape,
            in_specs=[vmem] * (4 + len(state) + len(pieces)),
            out_specs=vmem if last else (vmem, vmem),
            compiler_params=pltpu.CompilerParams(vmem_limit_bytes=limit),
            cost_estimate=pl.CostEstimate(
                flops=4 * 10**9, bytes_accessed=10**6, transcendentals=10**6
            ),
            name="attend",
        )(*prepared, *state, *pieces)

    own = jnp.concatenate([cached_keys, cached_values], axis=0)
    if not direct:
        gathered = lax.all_gather(own, ("seg", "ctx"), axis=0, tiled=True)
        return attend(prepared, [gathered], None, (), True)

    def number(seg, ctx):
        return lax.rem(seg, n_seg) * n_ctx + ctx

    def whole(ref):
        return ref[:rows, :], ref[rows : 2 * rows, :]

    far = exchange(own, lambda s, c, h: ((s + 1 + h) % n_seg, c, h))
    near = exchange(own, lambda s, c, h: ((s + 3 - 3 * h) % n_seg, c ^ h, h))
    near, prepared = lax.optimization_barrier((near, prepared))
    beside = swap(near)
    across = exchange(far, lambda s, c, h: (s, c ^ 1, h))
    state = attend(
        prepared,
        [own, near, beside, far],
        lambda refs, s, c, h: [
            (*whole(refs[0]), number(s, c)),
            (*whole(refs[1]), number(s + (1 - h), c ^ h)),
            (*whole(refs[2]), number(s + h, c ^ (1 - h))),
            (*whole(refs[3]), number(s + (3 - h), c)),
        ],
        (),
        False,
    )
    far_after, beside = lax.optimization_barrier((far, beside))
    far_beside = swap(far_after)
    half = jnp.where(lax.axis_index("head") == 0, near[:rows], beside[rows:])
    diagonal = exchange(half, lambda s, c, h: (s, c ^ 1, h))
    across, diagonal, state = lax.optimization_barrier((across, diagonal, state))
    last_beside = swap(jnp.concatenate([across, diagonal], axis=0))
    state = attend(
        prepared,
        [far_beside, across],
        lambda refs, s, c, h: [
            (*whole(refs[0]), number(s + (2 + h), c)),
            (*whole(refs[1]), number(s + (3 - h), c ^ 1)),
        ],
        state,
        False,
    )

    def last_shards(refs, s, c, h):
        diagonal, beside = refs
        mine, other = diagonal[...], beside[2 * rows :, :]
        return [
            (*whole(beside), number(s + (2 + h), c ^ 1)),
            (
                jnp.where(h == 0, mine, other),
                jnp.where(h == 0, other, mine),
                number(s + 1, c ^ 1),
            ),
        ]

    return attend(prepared, [diagonal, last_beside], last_shards, state, True)


def solution(mesh):
    return jax.shard_map(
        local,
        mesh=mesh,
        in_specs=(
            P(("groups", "ctx"), "head"),
            P(("groups", "seg", "ctx"), None),
            P(("groups", "seg", "ctx"), None),
            P("groups"),
            P("groups", None),
            P("groups", None),
        ),
        out_specs=P(("groups", "ctx"), "head"),
        check_vma=False,
    )
```

```python
import functools
import math

import jax
import jax.numpy as jnp
import numpy as np
from jax import lax
from jax.experimental import pallas as pl
from jax.experimental.pallas import tpu as pltpu
from jax.sharding import PartitionSpec as P

HEAD_DIM = 128
BLOCK = 64
ROPE_THETA = 500000.0
ROPE_FACTOR = 8.0
LOW_FACTOR = 1.0
HIGH_FACTOR = 4.0
TRAINED_CONTEXT = 8192.0
MASKED_SCORE = -1e30
SCORE_SCALE = HEAD_DIM**-0.5 * math.log2(math.e)
TILE = 128
FINE = 16
SUM_ROWS = 16
CHUNK = 256
DIRECT_SHARDS = (4, 2)
AXES = ("seg", "ctx", "head")


def frequency_row():
    exponent = np.arange(0, HEAD_DIM, 2, dtype=np.float64) / HEAD_DIM
    base = ROPE_THETA**-exponent
    wavelength = 2.0 * np.pi / base
    smooth = (TRAINED_CONTEXT / wavelength - LOW_FACTOR) / (HIGH_FACTOR - LOW_FACTOR)
    blended = (1.0 - smooth) * base / ROPE_FACTOR + smooth * base
    frequencies = np.where(
        wavelength < TRAINED_CONTEXT / HIGH_FACTOR,
        base,
        np.where(wavelength > TRAINED_CONTEXT / LOW_FACTOR, base / ROPE_FACTOR, blended),
    )
    return np.tile(frequencies, 2)[None, :].astype(np.float32)


def turned_sine(sine):
    lane = lax.broadcasted_iota(jnp.int32, sine.shape, 1)
    return jnp.where(lane < HEAD_DIM // 2, -sine, sine)


def rotate(vectors, cosine, signed_sine):
    wide = vectors.astype(jnp.float32)
    return (wide * cosine + pltpu.roll(wide, HEAD_DIM // 2, 1) * signed_sine).astype(jnp.bfloat16)


def angle_sum(cos_a, sin_a, cos_b, sin_b):
    return cos_a * cos_b - sin_a * sin_b, sin_a * cos_b + cos_a * sin_b


def shard_tables(cosines, sines, line, rows):
    cos_f, sin_f = cosines[pl.ds(0, FINE), :], turned_sine(sines[pl.ds(0, FINE), :])
    cos_c, sin_c = angle_sum(
        cosines[pl.ds(FINE, FINE), :],
        sines[pl.ds(FINE, FINE), :],
        cosines[pl.ds(line, 1), :],
        sines[pl.ds(line, 1), :],
    )
    signed = turned_sine(sin_c)
    parts = [
        (
            cos_f * cos_c[i : i + 1] - sin_f * signed[i : i + 1],
            sin_f * cos_c[i : i + 1] + cos_f * signed[i : i + 1],
        )
        for i in range(rows // FINE)
    ]
    return tuple(jnp.concatenate(table, axis=0) for table in zip(*parts))


def prepare_kernel(
    query_start_of, offsets, vertical, slash, queries, freq, rotated, cosines, sines, masks,
    angles, bias, held, arrival,
):
    query_rows, columns = held.shape
    heads = columns // HEAD_DIM
    fetch = pltpu.make_async_copy(queries, held, arrival)
    fetch.start()
    query_start, first_list = query_start_of()

    step = lax.broadcasted_iota(jnp.int32, (FINE, HEAD_DIM), 0)
    angles[pl.ds(0, FINE), :] = step
    angles[pl.ds(FINE, FINE), :] = step * FINE
    for shard in range(offsets.shape[0]):
        angles[pl.ds(2 * FINE + shard, 1), :] = jnp.full((1, HEAD_DIM), offsets[shard], jnp.int32)
    angles[pl.ds(angles.shape[0] - 8, 8), :] = jnp.full((8, HEAD_DIM), query_start, jnp.int32)
    angle = angles[...].astype(jnp.float32) * freq[...]
    cosines[...] = jnp.cos(angle)
    sines[...] = jnp.sin(angle)

    key_block = lax.broadcasted_iota(jnp.int32, bias.shape, 0)
    lane_block = lax.broadcasted_iota(jnp.int32, (1, query_rows), 1) // BLOCK
    hit = jnp.zeros(bias.shape, jnp.bool_)
    for entries, distance in ((vertical, False), (slash, True)):
        for entry in range(entries.shape[1]):
            wanted = jnp.zeros((1, query_rows), jnp.int32)
            for block in range(query_rows // BLOCK):
                value = entries[first_list + block, entry]
                if distance:
                    value = query_start // BLOCK + block - value
                wanted = jnp.where(lane_block == block, value, wanted)
            hit = hit | (key_block == wanted)
    bias[...] = jnp.where(hit, 0.0, MASKED_SCORE)

    rows = masks.shape[0] // offsets.shape[0]
    ahead = lax.broadcasted_iota(jnp.int32, (rows, query_rows), 1) - lax.broadcasted_iota(
        jnp.int32, (rows, query_rows), 0
    )

    @pl.loop(0, offsets.shape[0])
    def _(shard):
        offset = offsets[shard]
        lines = [
            jnp.broadcast_to(bias[pl.ds(offset // BLOCK + block, 1), :], (BLOCK, query_rows))
            for block in range(rows // BLOCK)
        ]
        masks[pl.ds(pl.multiple_of(shard * rows, rows), rows), :] = jnp.where(
            ahead >= offset - query_start, jnp.concatenate(lines, axis=0), MASKED_SCORE
        ).astype(masks.dtype)

    cosine, sine = shard_tables(cosines, sines, angles.shape[0] - 8, query_rows)
    fetch.wait()
    for head in range(heads):
        turned = rotate(held[:, pl.ds(head * HEAD_DIM, HEAD_DIM)], cosine, sine).T
        for tile in range(query_rows // TILE):
            lines = pl.ds((tile * heads + head) * TILE, TILE)
            rotated[:, lines] = turned[:, tile * TILE : (tile + 1) * TILE]


def attend_kernel(place_of, shards_of, first, last, *refs):
    rotated, cosines, sines, masks = refs[:4]
    refs = refs[4:]
    if not first:
        old_peak, old_sums = refs[:2]
        refs = refs[2:]
    if last:
        pieces, out = refs[:-1], refs[-1]
    else:
        pieces, new_peak, new_sums = refs[:-2], refs[-2], refs[-1]
    query_rows = masks.shape[1]
    tiles = query_rows // TILE
    width = rotated.shape[1] // tiles
    rows = masks.shape[0] // (cosines.shape[0] - 2 * FINE - 8)
    ones = jnp.ones((SUM_ROWS, rows), jnp.bfloat16)
    unit = (
        lax.broadcasted_iota(jnp.int32, (TILE, width), 0)
        == lax.broadcasted_iota(jnp.int32, (TILE, width), 1) % TILE
    ).astype(jnp.bfloat16)

    def load_keys(keys, shard):
        keys = rotate(keys, *shard_tables(cosines, sines, 2 * FINE + shard, rows))
        return keys, masks[pl.ds(pl.multiple_of(shard * rows, rows), rows), :]

    def load_values(values):
        return jnp.concatenate([values.T, ones], axis=0)

    def score(keys, mask, start, size):
        tile = start // width
        query = jnp.concatenate([rotated[:, pl.ds(start, size)], unit[:, :size]], axis=0)
        return jnp.dot(
            jnp.concatenate([keys, mask[:, tile * TILE : (tile + 1) * TILE]], axis=1),
            query,
            preferred_element_type=jnp.float32,
        )

    def update(scores, values, before):
        peak = scores.max(axis=0, keepdims=True)
        if before is not None:
            peak = jnp.maximum(before[0], peak)
        weights = jnp.exp2((scores - peak) * SCORE_SCALE).astype(jnp.bfloat16)
        sums = jnp.dot(values, weights, preferred_element_type=jnp.float32)
        if before is not None:
            sums = sums + before[1] * jnp.exp2((before[0] - peak) * SCORE_SCALE)
        return peak, sums

    def finish(start, peak, sums):
        size = sums.shape[1]
        if not last:
            span = pl.ds(start, size)
            new_peak[:, span] = jnp.broadcast_to(peak, (new_peak.shape[0], size))
            new_sums[:, span] = sums
            return
        part = sums[:HEAD_DIM] * (1.0 / sums[HEAD_DIM : HEAD_DIM + 1])
        part = part.astype(out.dtype)
        for column in range(0, size, TILE):
            tile, head = divmod((start + column) // TILE, width // TILE)
            out[pl.ds(tile * TILE, TILE), pl.ds(head * HEAD_DIM, HEAD_DIM)] = part[
                :, column : column + TILE
            ].T

    if shards_of is not None:
        shards = shards_of(pieces, *place_of())
        keys, mask = (
            jnp.concatenate(part, axis=0)
            for part in zip(*(load_keys(keys, shard) for keys, _, shard in shards))
        )
        starts = list(range(0, rotated.shape[1], CHUNK))
        ahead = score(keys, mask, starts[0], CHUNK)
        values = jnp.concatenate([load_values(values) for _, values, _ in shards], axis=1)
        for start in starts:
            scores = ahead
            if start != starts[-1]:
                ahead = score(keys, mask, start + CHUNK, CHUNK)
            before = None
            if not first:
                before = (old_peak[:1, pl.ds(start, CHUNK)], old_sums[:, pl.ds(start, CHUNK)])
            finish(start, *update(scores, values, before))
    else:
        (whole,) = pieces
        for tile in range(tiles):

            def step(shard, before, tile=tile):
                start = pl.multiple_of(shard * (2 * rows), 2 * rows)
                keys, mask = load_keys(whole[pl.ds(start, rows), :], shard)
                values = load_values(whole[pl.ds(start + rows, rows), :])
                return update(score(keys, mask, tile * width, width), values, before)

            initial = (
                jnp.full((1, width), MASKED_SCORE, jnp.float32),
                jnp.zeros((HEAD_DIM + SUM_ROWS, width), jnp.float32),
            )
            finish(
                tile * width, *lax.fori_loop(0, whole.shape[0] // (2 * rows), step, initial)
            )


def local(queries, cached_keys, cached_values, key_offsets, vertical_blocks, slash_offsets):
    query_rows = queries.shape[0]
    heads = queries.shape[1] // HEAD_DIM
    rows = cached_keys.shape[0]
    n_seg, n_ctx = lax.axis_size("seg"), lax.axis_size("ctx")
    shards = n_seg * n_ctx
    prefix = rows * shards - query_rows * n_ctx

    def query_start_of():
        ctx = lax.axis_index("ctx")
        return prefix + ctx * query_rows, ctx * (query_rows // BLOCK)

    def place_of():
        return tuple(lax.axis_index(axis) for axis in AXES)

    def exchange(a, partner):
        pairs = []
        for seg in range(n_seg):
            for ctx in range(n_ctx):
                for head in range(2):
                    to_seg, to_ctx, to_head = partner(seg, ctx, head)
                    pairs.append(
                        ((seg * n_ctx + ctx) * 2 + head, (to_seg * n_ctx + to_ctx) * 2 + to_head)
                    )
        return lax.ppermute(a, AXES, pairs)

    def swap(a):
        return exchange(a, lambda s, c, h: (s, c, 1 - h))

    vmem = pl.BlockSpec(memory_space=pltpu.VMEM)
    smem = pl.BlockSpec(memory_space=pltpu.SMEM)
    f32 = jnp.float32
    direct = (n_seg, n_ctx) == DIRECT_SHARDS
    limit = (16 if direct else 56) * 1024 * 1024
    shape = jax.ShapeDtypeStruct
    lines = 2 * FINE + shards + 8
    prepared = pl.pallas_call(
        functools.partial(prepare_kernel, query_start_of),
        out_shape=(
            shape((HEAD_DIM, query_rows * heads), jnp.bfloat16),
            shape((lines, HEAD_DIM), f32),
            shape((lines, HEAD_DIM), f32),
            shape((shards * rows, query_rows), jnp.bfloat16),
        ),
        in_specs=[smem, smem, smem, pl.BlockSpec(memory_space=pltpu.HBM), vmem],
        out_specs=[vmem] * 4,
        scratch_shapes=[
            pltpu.VMEM((lines, HEAD_DIM), jnp.int32),
            pltpu.VMEM((shards * rows // BLOCK, query_rows), f32),
            pltpu.VMEM(queries.shape, queries.dtype),
            pltpu.SemaphoreType.DMA(()),
        ],
        compiler_params=pltpu.CompilerParams(vmem_limit_bytes=limit),
        cost_estimate=pl.CostEstimate(flops=4 * 10**9, bytes_accessed=10**6, transcendentals=10**5),
        name="prepare",
    )(key_offsets, vertical_blocks, slash_offsets, queries, jnp.asarray(frequency_row()))

    def attend(prepared, pieces, shards_of, state, last):
        state_shape = (
            shape((8, query_rows * heads), f32),
            shape((HEAD_DIM + SUM_ROWS, query_rows * heads), f32),
        )
        return pl.pallas_call(
            functools.partial(attend_kernel, place_of, shards_of, not state, last),
            out_shape=shape(queries.shape, queries.dtype) if last else state_shape,
            in_specs=[vmem] * (4 + len(state) + len(pieces)),
            out_specs=vmem if last else (vmem, vmem),
            compiler_params=pltpu.CompilerParams(vmem_limit_bytes=limit),
            cost_estimate=pl.CostEstimate(
                flops=4 * 10**9, bytes_accessed=10**6, transcendentals=10**6
            ),
            name="attend",
        )(*prepared, *state, *pieces)

    own = jnp.concatenate([cached_keys, cached_values], axis=0)
    if not direct:
        gathered = lax.all_gather(own, ("seg", "ctx"), axis=0, tiled=True)
        return attend(prepared, [gathered], None, (), True)

    def number(seg, ctx):
        return seg * n_ctx + ctx

    def whole(ref):
        return ref[:rows, :], ref[rows : 2 * rows, :]

    far = exchange(own, lambda s, c, h: (s ^ (3 - h), c, h))
    near = exchange(own, lambda s, c, h: (s ^ (1 - h), c ^ h, h))
    near, prepared = lax.optimization_barrier((near, prepared))
    beside = swap(near)
    across = exchange(far, lambda s, c, h: (s, c ^ 1, h))
    state = attend(
        prepared,
        [own, near, beside, far],
        lambda refs, s, c, h: [
            (*whole(refs[0]), number(s, c)),
            (*whole(refs[1]), number(s ^ (1 - h), c ^ h)),
            (*whole(refs[2]), number(s ^ h, c ^ (1 - h))),
            (*whole(refs[3]), number(s ^ (3 - h), c)),
        ],
        (),
        False,
    )
    far_after, beside = lax.optimization_barrier((far, beside))
    far_beside = swap(far_after)
    half = jnp.where(lax.axis_index("head") == 0, beside[:rows], near[rows:])
    diagonal = exchange(half, lambda s, c, h: (s ^ 1, c, h))
    def middle_shards(refs, s, c, h):
        beside, across, mine, other = refs
        mine, other = mine[...], other[...]
        return [
            (*whole(beside), number(s ^ (2 + h), c)),
            (*whole(across), number(s ^ (3 - h), c ^ 1)),
            (
                jnp.where(h == 0, mine, other),
                jnp.where(h == 0, other, mine),
                number(s ^ 1, c ^ 1),
            ),
        ]

    diagonal, state = lax.optimization_barrier((diagonal, state))
    diagonal_beside = swap(diagonal)
    across, state = lax.optimization_barrier((across, state))
    across_beside = swap(across)
    state = attend(
        prepared,
        [far_beside, across, diagonal, diagonal_beside],
        middle_shards,
        state,
        False,
    )
    return attend(
        prepared,
        [across_beside],
        lambda refs, s, c, h: [(*whole(refs[0]), number(s ^ (2 + h), c ^ 1))],
        state,
        True,
    )


def solution(mesh):
    return jax.shard_map(
        local,
        mesh=mesh,
        in_specs=(
            P(("groups", "ctx"), "head"),
            P(("groups", "seg", "ctx"), None),
            P(("groups", "seg", "ctx"), None),
            P("groups"),
            P("groups", None),
            P("groups", None),
        ),
        out_specs=P(("groups", "ctx"), "head"),
        check_vma=False,
    )
```

```python
import functools
import math

import jax
import jax.numpy as jnp
import numpy as np
from jax import lax
from jax.experimental import pallas as pl
from jax.experimental.pallas import tpu as pltpu
from jax.sharding import PartitionSpec as P

HEAD_DIM = 128
BLOCK = 64
ROPE_THETA = 500000.0
ROPE_FACTOR = 8.0
LOW_FACTOR = 1.0
HIGH_FACTOR = 4.0
TRAINED_CONTEXT = 8192.0
MASKED_SCORE = -1e30
SCORE_SCALE = HEAD_DIM**-0.5 * math.log2(math.e)
TILE = 128
FINE = 16
SUM_ROWS = 16
CHUNK = 256
DIRECT_SHARDS = (4, 2)
AXES = ("seg", "ctx", "head")


def frequency_row():
    exponent = np.arange(0, HEAD_DIM, 2, dtype=np.float64) / HEAD_DIM
    base = ROPE_THETA**-exponent
    wavelength = 2.0 * np.pi / base
    smooth = (TRAINED_CONTEXT / wavelength - LOW_FACTOR) / (HIGH_FACTOR - LOW_FACTOR)
    blended = (1.0 - smooth) * base / ROPE_FACTOR + smooth * base
    frequencies = np.where(
        wavelength < TRAINED_CONTEXT / HIGH_FACTOR,
        base,
        np.where(wavelength > TRAINED_CONTEXT / LOW_FACTOR, base / ROPE_FACTOR, blended),
    )
    return np.tile(frequencies, 2)[None, :].astype(np.float32)


def turned_sine(sine):
    lane = lax.broadcasted_iota(jnp.int32, sine.shape, 1)
    return jnp.where(lane < HEAD_DIM // 2, -sine, sine)


def rotate(vectors, cosine, signed_sine):
    wide = vectors.astype(jnp.float32)
    return (wide * cosine + pltpu.roll(wide, HEAD_DIM // 2, 1) * signed_sine).astype(jnp.bfloat16)


def angle_sum(cos_a, sin_a, cos_b, sin_b):
    return cos_a * cos_b - sin_a * sin_b, sin_a * cos_b + cos_a * sin_b


def shard_tables(cosines, sines, line, rows):
    cos_f, sin_f = cosines[pl.ds(0, FINE), :], turned_sine(sines[pl.ds(0, FINE), :])
    cos_c, sin_c = angle_sum(
        cosines[pl.ds(FINE, FINE), :],
        sines[pl.ds(FINE, FINE), :],
        cosines[pl.ds(line, 1), :],
        sines[pl.ds(line, 1), :],
    )
    signed = turned_sine(sin_c)
    parts = [
        (
            cos_f * cos_c[i : i + 1] - sin_f * signed[i : i + 1],
            sin_f * cos_c[i : i + 1] + cos_f * signed[i : i + 1],
        )
        for i in range(rows // FINE)
    ]
    return tuple(jnp.concatenate(table, axis=0) for table in zip(*parts))


def prepare_kernel(
    query_start_of, offsets, vertical, slash, queries, freq, rotated, cosines, sines, masks,
    angles, bias, held, arrival,
):
    query_rows, columns = held.shape
    heads = columns // HEAD_DIM
    fetch = pltpu.make_async_copy(queries, held, arrival)
    fetch.start()
    query_start, first_list = query_start_of()

    step = lax.broadcasted_iota(jnp.int32, (FINE, HEAD_DIM), 0)
    angles[pl.ds(0, FINE), :] = step
    angles[pl.ds(FINE, FINE), :] = step * FINE
    for shard in range(offsets.shape[0]):
        angles[pl.ds(2 * FINE + shard, 1), :] = jnp.full((1, HEAD_DIM), offsets[shard], jnp.int32)
    angles[pl.ds(angles.shape[0] - 8, 8), :] = jnp.full((8, HEAD_DIM), query_start, jnp.int32)
    angle = angles[...].astype(jnp.float32) * freq[...]
    cosines[...] = jnp.cos(angle)
    sines[...] = jnp.sin(angle)

    key_block = lax.broadcasted_iota(jnp.int32, bias.shape, 0)
    lane_block = lax.broadcasted_iota(jnp.int32, (1, query_rows), 1) // BLOCK
    hit = jnp.zeros(bias.shape, jnp.bool_)
    for entries, distance in ((vertical, False), (slash, True)):
        for entry in range(entries.shape[1]):
            wanted = jnp.zeros((1, query_rows), jnp.int32)
            for block in range(query_rows // BLOCK):
                value = entries[first_list + block, entry]
                if distance:
                    value = query_start // BLOCK + block - value
                wanted = jnp.where(lane_block == block, value, wanted)
            hit = hit | (key_block == wanted)
    bias[...] = jnp.where(hit, 0.0, MASKED_SCORE)

    rows = masks.shape[0] // offsets.shape[0]
    ahead = lax.broadcasted_iota(jnp.int32, (rows, query_rows), 1) - lax.broadcasted_iota(
        jnp.int32, (rows, query_rows), 0
    )

    @pl.loop(0, offsets.shape[0])
    def _(shard):
        offset = offsets[shard]
        lines = [
            jnp.broadcast_to(bias[pl.ds(offset // BLOCK + block, 1), :], (BLOCK, query_rows))
            for block in range(rows // BLOCK)
        ]
        masks[pl.ds(pl.multiple_of(shard * rows, rows), rows), :] = jnp.where(
            ahead >= offset - query_start, jnp.concatenate(lines, axis=0), MASKED_SCORE
        ).astype(masks.dtype)

    cosine, sine = shard_tables(cosines, sines, angles.shape[0] - 8, query_rows)
    fetch.wait()
    for head in range(heads):
        turned = rotate(held[:, pl.ds(head * HEAD_DIM, HEAD_DIM)], cosine, sine).T
        for tile in range(query_rows // TILE):
            lines = pl.ds((tile * heads + head) * TILE, TILE)
            rotated[:, lines] = turned[:, tile * TILE : (tile + 1) * TILE]


def attend_kernel(place_of, shards_of, first, last, *refs):
    rotated, cosines, sines, masks = refs[:4]
    refs = refs[4:]
    if not first:
        old_peak, old_sums = refs[:2]
        refs = refs[2:]
    if last:
        pieces, out = refs[:-1], refs[-1]
    else:
        pieces, new_peak, new_sums = refs[:-2], refs[-2], refs[-1]
    query_rows = masks.shape[1]
    tiles = query_rows // TILE
    width = rotated.shape[1] // tiles
    rows = masks.shape[0] // (cosines.shape[0] - 2 * FINE - 8)
    ones = jnp.ones((SUM_ROWS, rows), jnp.bfloat16)
    unit = (
        lax.broadcasted_iota(jnp.int32, (TILE, width), 0)
        == lax.broadcasted_iota(jnp.int32, (TILE, width), 1) % TILE
    ).astype(jnp.bfloat16)

    def load_keys(keys, shard):
        keys = rotate(keys, *shard_tables(cosines, sines, 2 * FINE + shard, rows))
        return keys, masks[pl.ds(pl.multiple_of(shard * rows, rows), rows), :]

    def load_values(values):
        return jnp.concatenate([values.T, ones], axis=0)

    def score(keys, mask, start, size):
        tile = start // width
        query = jnp.concatenate([rotated[:, pl.ds(start, size)], unit[:, :size]], axis=0)
        return jnp.dot(
            jnp.concatenate([keys, mask[:, tile * TILE : (tile + 1) * TILE]], axis=1),
            query,
            preferred_element_type=jnp.float32,
        )

    def update(scores, values, before):
        peak = scores.max(axis=0, keepdims=True)
        if before is not None:
            peak = jnp.maximum(before[0], peak)
        weights = jnp.exp2((scores - peak) * SCORE_SCALE).astype(jnp.bfloat16)
        sums = jnp.dot(values, weights, preferred_element_type=jnp.float32)
        if before is not None:
            sums = sums + before[1] * jnp.exp2((before[0] - peak) * SCORE_SCALE)
        return peak, sums

    def finish(start, peak, sums):
        size = sums.shape[1]
        if not last:
            span = pl.ds(start, size)
            new_peak[:, span] = jnp.broadcast_to(peak, (new_peak.shape[0], size))
            new_sums[:, span] = sums
            return
        part = sums[:HEAD_DIM] * (1.0 / sums[HEAD_DIM : HEAD_DIM + 1])
        part = part.astype(out.dtype)
        for column in range(0, size, TILE):
            tile, head = divmod((start + column) // TILE, width // TILE)
            out[pl.ds(tile * TILE, TILE), pl.ds(head * HEAD_DIM, HEAD_DIM)] = part[
                :, column : column + TILE
            ].T

    if shards_of is not None:
        shards = shards_of(pieces, *place_of())
        keys, mask = (
            jnp.concatenate(part, axis=0)
            for part in zip(*(load_keys(keys, shard) for keys, _, shard in shards))
        )
        starts = list(range(0, rotated.shape[1], CHUNK))
        ahead = score(keys, mask, starts[0], CHUNK)
        values = jnp.concatenate([load_values(values) for _, values, _ in shards], axis=1)
        for start in starts:
            scores = ahead
            if start != starts[-1]:
                ahead = score(keys, mask, start + CHUNK, CHUNK)
            before = None
            if not first:
                before = (old_peak[:1, pl.ds(start, CHUNK)], old_sums[:, pl.ds(start, CHUNK)])
            finish(start, *update(scores, values, before))
    else:
        (whole,) = pieces
        for tile in range(tiles):

            def step(shard, before, tile=tile):
                start = pl.multiple_of(shard * (2 * rows), 2 * rows)
                keys, mask = load_keys(whole[pl.ds(start, rows), :], shard)
                values = load_values(whole[pl.ds(start + rows, rows), :])
                return update(score(keys, mask, tile * width, width), values, before)

            initial = (
                jnp.full((1, width), MASKED_SCORE, jnp.float32),
                jnp.zeros((HEAD_DIM + SUM_ROWS, width), jnp.float32),
            )
            finish(
                tile * width, *lax.fori_loop(0, whole.shape[0] // (2 * rows), step, initial)
            )


def local(queries, cached_keys, cached_values, key_offsets, vertical_blocks, slash_offsets):
    query_rows = queries.shape[0]
    heads = queries.shape[1] // HEAD_DIM
    rows = cached_keys.shape[0]
    n_seg, n_ctx = lax.axis_size("seg"), lax.axis_size("ctx")
    shards = n_seg * n_ctx
    prefix = rows * shards - query_rows * n_ctx

    def query_start_of():
        ctx = lax.axis_index("ctx")
        return prefix + ctx * query_rows, ctx * (query_rows // BLOCK)

    def place_of():
        return tuple(lax.axis_index(axis) for axis in AXES)

    def exchange(a, partner):
        pairs = []
        for seg in range(n_seg):
            for ctx in range(n_ctx):
                for head in range(2):
                    to_seg, to_ctx, to_head = partner(seg, ctx, head)
                    pairs.append(
                        ((seg * n_ctx + ctx) * 2 + head, (to_seg * n_ctx + to_ctx) * 2 + to_head)
                    )
        return lax.ppermute(a, AXES, pairs)

    def swap(a):
        return exchange(a, lambda s, c, h: (s, c, 1 - h))

    vmem = pl.BlockSpec(memory_space=pltpu.VMEM)
    smem = pl.BlockSpec(memory_space=pltpu.SMEM)
    f32 = jnp.float32
    direct = (n_seg, n_ctx) == DIRECT_SHARDS
    limit = (16 if direct else 56) * 1024 * 1024
    shape = jax.ShapeDtypeStruct
    lines = 2 * FINE + shards + 8
    prepared = pl.pallas_call(
        functools.partial(prepare_kernel, query_start_of),
        out_shape=(
            shape((HEAD_DIM, query_rows * heads), jnp.bfloat16),
            shape((lines, HEAD_DIM), f32),
            shape((lines, HEAD_DIM), f32),
            shape((shards * rows, query_rows), jnp.bfloat16),
        ),
        in_specs=[smem, smem, smem, pl.BlockSpec(memory_space=pltpu.HBM), vmem],
        out_specs=[vmem] * 4,
        scratch_shapes=[
            pltpu.VMEM((lines, HEAD_DIM), jnp.int32),
            pltpu.VMEM((shards * rows // BLOCK, query_rows), f32),
            pltpu.VMEM(queries.shape, queries.dtype),
            pltpu.SemaphoreType.DMA(()),
        ],
        compiler_params=pltpu.CompilerParams(vmem_limit_bytes=limit),
        cost_estimate=pl.CostEstimate(flops=4 * 10**9, bytes_accessed=10**6, transcendentals=10**5),
        name="prepare",
    )(key_offsets, vertical_blocks, slash_offsets, queries, jnp.asarray(frequency_row()))

    def attend(prepared, pieces, shards_of, state, last):
        state_shape = (
            shape((8, query_rows * heads), f32),
            shape((HEAD_DIM + SUM_ROWS, query_rows * heads), f32),
        )
        return pl.pallas_call(
            functools.partial(attend_kernel, place_of, shards_of, not state, last),
            out_shape=shape(queries.shape, queries.dtype) if last else state_shape,
            in_specs=[vmem] * (4 + len(state) + len(pieces)),
            out_specs=vmem if last else (vmem, vmem),
            compiler_params=pltpu.CompilerParams(vmem_limit_bytes=limit),
            cost_estimate=pl.CostEstimate(
                flops=4 * 10**9, bytes_accessed=10**6, transcendentals=10**6
            ),
            name="attend",
        )(*prepared, *state, *pieces)

    own = jnp.concatenate([cached_keys, cached_values], axis=0)
    if not direct:
        gathered = lax.all_gather(own, ("seg", "ctx"), axis=0, tiled=True)
        return attend(prepared, [gathered], None, (), True)

    def number(seg, ctx):
        return seg * n_ctx + ctx

    def whole(ref):
        return ref[:rows, :], ref[rows : 2 * rows, :]

    far = exchange(own, lambda s, c, h: (s ^ (3 - h), c, h))
    near = exchange(own, lambda s, c, h: (s ^ (1 - h), c ^ h, h))
    near, prepared = lax.optimization_barrier((near, prepared))
    beside = swap(near)
    across = exchange(far, lambda s, c, h: (s, c ^ 1, h))
    state = attend(
        prepared,
        [own, near, beside, far],
        lambda refs, s, c, h: [
            (*whole(refs[0]), number(s, c)),
            (*whole(refs[1]), number(s ^ (1 - h), c ^ h)),
            (*whole(refs[2]), number(s ^ h, c ^ (1 - h))),
            (*whole(refs[3]), number(s ^ (3 - h), c)),
        ],
        (),
        False,
    )
    far_after, beside = lax.optimization_barrier((far, beside))
    far_beside = swap(far_after)
    half = jnp.where(lax.axis_index("head") == 0, beside[:rows], near[rows:])
    diagonal = exchange(half, lambda s, c, h: (s ^ 1, c, h))
    across, state = lax.optimization_barrier((across, state))
    across_beside = swap(across)
    state = attend(
        prepared,
        [far_beside, across],
        lambda refs, s, c, h: [
            (*whole(refs[0]), number(s ^ (2 + h), c)),
            (*whole(refs[1]), number(s ^ (3 - h), c ^ 1)),
        ],
        state,
        False,
    )
    diagonal, state = lax.optimization_barrier((diagonal, state))
    diagonal_beside = swap(diagonal)
    state = attend(
        prepared,
        [across_beside],
        lambda refs, s, c, h: [(*whole(refs[0]), number(s ^ (2 + h), c ^ 1))],
        state,
        False,
    )

    def corner(refs, s, c, h):
        mine, other = (ref[...] for ref in refs)
        return [
            (
                jnp.where(h == 0, mine, other),
                jnp.where(h == 0, other, mine),
                number(s ^ 1, c ^ 1),
            )
        ]

    return attend(prepared, [diagonal, diagonal_beside], corner, state, True)


def solution(mesh):
    return jax.shard_map(
        local,
        mesh=mesh,
        in_specs=(
            P(("groups", "ctx"), "head"),
            P(("groups", "seg", "ctx"), None),
            P(("groups", "seg", "ctx"), None),
            P("groups"),
            P("groups", None),
            P("groups", None),
        ),
        out_specs=P(("groups", "ctx"), "head"),
        check_vma=False,
    )
```

```python
import functools
import math

import jax
import jax.numpy as jnp
import numpy as np
from jax import lax
from jax.experimental import pallas as pl
from jax.experimental.pallas import tpu as pltpu
from jax.sharding import PartitionSpec as P

HEAD_DIM = 128
BLOCK = 64
ROPE_THETA = 500000.0
ROPE_FACTOR = 8.0
LOW_FACTOR = 1.0
HIGH_FACTOR = 4.0
TRAINED_CONTEXT = 8192.0
MASKED_SCORE = -1e30
SCORE_SCALE = HEAD_DIM**-0.5 * math.log2(math.e)
TILE = 128
FINE = 16
SUM_ROWS = 16
CHUNK = 256
DIRECT_SHARDS = (4, 2)
AXES = ("seg", "ctx", "head")


def frequency_row():
    exponent = np.arange(0, HEAD_DIM, 2, dtype=np.float64) / HEAD_DIM
    base = ROPE_THETA**-exponent
    wavelength = 2.0 * np.pi / base
    smooth = (TRAINED_CONTEXT / wavelength - LOW_FACTOR) / (HIGH_FACTOR - LOW_FACTOR)
    blended = (1.0 - smooth) * base / ROPE_FACTOR + smooth * base
    frequencies = np.where(
        wavelength < TRAINED_CONTEXT / HIGH_FACTOR,
        base,
        np.where(wavelength > TRAINED_CONTEXT / LOW_FACTOR, base / ROPE_FACTOR, blended),
    )
    return np.tile(frequencies, 2)[None, :].astype(np.float32)


def turned_sine(sine):
    lane = lax.broadcasted_iota(jnp.int32, sine.shape, 1)
    return jnp.where(lane < HEAD_DIM // 2, -sine, sine)


def rotate(vectors, cosine, signed_sine):
    wide = vectors.astype(jnp.float32)
    return (wide * cosine + pltpu.roll(wide, HEAD_DIM // 2, 1) * signed_sine).astype(jnp.bfloat16)


def angle_sum(cos_a, sin_a, cos_b, sin_b):
    return cos_a * cos_b - sin_a * sin_b, sin_a * cos_b + cos_a * sin_b


def shard_tables(cosines, sines, line, rows):
    cos_f, sin_f = cosines[pl.ds(0, FINE), :], turned_sine(sines[pl.ds(0, FINE), :])
    cos_c, sin_c = angle_sum(
        cosines[pl.ds(FINE, FINE), :],
        sines[pl.ds(FINE, FINE), :],
        cosines[pl.ds(line, 1), :],
        sines[pl.ds(line, 1), :],
    )
    signed = turned_sine(sin_c)
    parts = [
        (
            cos_f * cos_c[i : i + 1] - sin_f * signed[i : i + 1],
            sin_f * cos_c[i : i + 1] + cos_f * signed[i : i + 1],
        )
        for i in range(rows // FINE)
    ]
    return tuple(jnp.concatenate(table, axis=0) for table in zip(*parts))


def prepare_kernel(
    query_start_of, offsets, vertical, slash, queries, freq, rotated, cosines, sines, masks,
    angles, bias, held, arrival,
):
    query_rows, columns = held.shape
    heads = columns // HEAD_DIM
    fetch = pltpu.make_async_copy(queries, held, arrival)
    fetch.start()
    query_start, first_list = query_start_of()

    step = lax.broadcasted_iota(jnp.int32, (FINE, HEAD_DIM), 0)
    angles[pl.ds(0, FINE), :] = step
    angles[pl.ds(FINE, FINE), :] = step * FINE
    for shard in range(offsets.shape[0]):
        angles[pl.ds(2 * FINE + shard, 1), :] = jnp.full((1, HEAD_DIM), offsets[shard], jnp.int32)
    angles[pl.ds(angles.shape[0] - 8, 8), :] = jnp.full((8, HEAD_DIM), query_start, jnp.int32)
    angle = angles[...].astype(jnp.float32) * freq[...]
    cosines[...] = jnp.cos(angle)
    sines[...] = jnp.sin(angle)

    key_block = lax.broadcasted_iota(jnp.int32, bias.shape, 0)
    lane_block = lax.broadcasted_iota(jnp.int32, (1, query_rows), 1) // BLOCK
    hit = jnp.zeros(bias.shape, jnp.bool_)
    for entries, distance in ((vertical, False), (slash, True)):
        for entry in range(entries.shape[1]):
            wanted = jnp.zeros((1, query_rows), jnp.int32)
            for block in range(query_rows // BLOCK):
                value = entries[first_list + block, entry]
                if distance:
                    value = query_start // BLOCK + block - value
                wanted = jnp.where(lane_block == block, value, wanted)
            hit = hit | (key_block == wanted)
    bias[...] = jnp.where(hit, 0.0, MASKED_SCORE)

    rows = masks.shape[0] // offsets.shape[0]
    ahead = lax.broadcasted_iota(jnp.int32, (rows, query_rows), 1) - lax.broadcasted_iota(
        jnp.int32, (rows, query_rows), 0
    )

    @pl.loop(0, offsets.shape[0])
    def _(shard):
        offset = offsets[shard]
        lines = [
            jnp.broadcast_to(bias[pl.ds(offset // BLOCK + block, 1), :], (BLOCK, query_rows))
            for block in range(rows // BLOCK)
        ]
        masks[pl.ds(pl.multiple_of(shard * rows, rows), rows), :] = jnp.where(
            ahead >= offset - query_start, jnp.concatenate(lines, axis=0), MASKED_SCORE
        ).astype(masks.dtype)

    cosine, sine = shard_tables(cosines, sines, angles.shape[0] - 8, query_rows)
    fetch.wait()
    for head in range(heads):
        turned = rotate(held[:, pl.ds(head * HEAD_DIM, HEAD_DIM)], cosine, sine).T
        for tile in range(query_rows // TILE):
            lines = pl.ds((tile * heads + head) * TILE, TILE)
            rotated[:, lines] = turned[:, tile * TILE : (tile + 1) * TILE]


def attend_kernel(place_of, shards_of, first, last, *refs):
    rotated, cosines, sines, masks = refs[:4]
    refs = refs[4:]
    if not first:
        old_peak, old_sums = refs[:2]
        refs = refs[2:]
    if last:
        pieces, out = refs[:-1], refs[-1]
    else:
        pieces, new_peak, new_sums = refs[:-2], refs[-2], refs[-1]
    query_rows = masks.shape[1]
    tiles = query_rows // TILE
    width = rotated.shape[1] // tiles
    rows = masks.shape[0] // (cosines.shape[0] - 2 * FINE - 8)
    ones = jnp.ones((SUM_ROWS, rows), jnp.bfloat16)
    unit = (
        lax.broadcasted_iota(jnp.int32, (TILE, width), 0)
        == lax.broadcasted_iota(jnp.int32, (TILE, width), 1) % TILE
    ).astype(jnp.bfloat16)

    def load_keys(keys, shard):
        keys = rotate(keys, *shard_tables(cosines, sines, 2 * FINE + shard, rows))
        return keys, masks[pl.ds(pl.multiple_of(shard * rows, rows), rows), :]

    def load_values(values):
        return jnp.concatenate([values.T, ones], axis=0)

    def score(keys, mask, start, size):
        tile = start // width
        query = jnp.concatenate([rotated[:, pl.ds(start, size)], unit[:, :size]], axis=0)
        return jnp.dot(
            jnp.concatenate([keys, mask[:, tile * TILE : (tile + 1) * TILE]], axis=1),
            query,
            preferred_element_type=jnp.float32,
        )

    def update(scores, values, before):
        peak = scores.max(axis=0, keepdims=True)
        if before is not None:
            peak = jnp.maximum(before[0], peak)
        weights = jnp.exp2(((scores - peak) * SCORE_SCALE).astype(jnp.bfloat16))
        sums = jnp.dot(values, weights, preferred_element_type=jnp.float32)
        if before is not None:
            sums = sums + before[1] * jnp.exp2((before[0] - peak) * SCORE_SCALE)
        return peak, sums

    def finish(start, peak, sums):
        size = sums.shape[1]
        if not last:
            span = pl.ds(start, size)
            new_peak[:, span] = jnp.broadcast_to(peak, (new_peak.shape[0], size))
            new_sums[:, span] = sums
            return
        part = sums[:HEAD_DIM] * (1.0 / sums[HEAD_DIM : HEAD_DIM + 1])
        part = part.astype(out.dtype)
        for column in range(0, size, TILE):
            tile, head = divmod((start + column) // TILE, width // TILE)
            out[pl.ds(tile * TILE, TILE), pl.ds(head * HEAD_DIM, HEAD_DIM)] = part[
                :, column : column + TILE
            ].T

    if shards_of is not None:
        shards = shards_of(pieces, *place_of())
        keys, mask = (
            jnp.concatenate(part, axis=0)
            for part in zip(*(load_keys(keys, shard) for keys, _, shard in shards))
        )
        starts = list(range(0, rotated.shape[1], CHUNK))
        ahead = score(keys, mask, starts[0], CHUNK)
        values = jnp.concatenate([load_values(values) for _, values, _ in shards], axis=1)
        for start in starts:
            scores = ahead
            if start != starts[-1]:
                ahead = score(keys, mask, start + CHUNK, CHUNK)
            before = None
            if not first:
                before = (old_peak[:1, pl.ds(start, CHUNK)], old_sums[:, pl.ds(start, CHUNK)])
            finish(start, *update(scores, values, before))
    else:
        (whole,) = pieces
        for tile in range(tiles):

            def step(shard, before, tile=tile):
                start = pl.multiple_of(shard * (2 * rows), 2 * rows)
                keys, mask = load_keys(whole[pl.ds(start, rows), :], shard)
                values = load_values(whole[pl.ds(start + rows, rows), :])
                return update(score(keys, mask, tile * width, width), values, before)

            initial = (
                jnp.full((1, width), MASKED_SCORE, jnp.float32),
                jnp.zeros((HEAD_DIM + SUM_ROWS, width), jnp.float32),
            )
            finish(
                tile * width, *lax.fori_loop(0, whole.shape[0] // (2 * rows), step, initial)
            )


def local(queries, cached_keys, cached_values, key_offsets, vertical_blocks, slash_offsets):
    query_rows = queries.shape[0]
    heads = queries.shape[1] // HEAD_DIM
    rows = cached_keys.shape[0]
    n_seg, n_ctx = lax.axis_size("seg"), lax.axis_size("ctx")
    shards = n_seg * n_ctx
    prefix = rows * shards - query_rows * n_ctx

    def query_start_of():
        ctx = lax.axis_index("ctx")
        return prefix + ctx * query_rows, ctx * (query_rows // BLOCK)

    def place_of():
        return tuple(lax.axis_index(axis) for axis in AXES)

    def exchange(a, partner):
        pairs = []
        for seg in range(n_seg):
            for ctx in range(n_ctx):
                for head in range(2):
                    to_seg, to_ctx, to_head = partner(seg, ctx, head)
                    pairs.append(
                        ((seg * n_ctx + ctx) * 2 + head, (to_seg * n_ctx + to_ctx) * 2 + to_head)
                    )
        return lax.ppermute(a, AXES, pairs)

    def swap(a):
        return exchange(a, lambda s, c, h: (s, c, 1 - h))

    vmem = pl.BlockSpec(memory_space=pltpu.VMEM)
    smem = pl.BlockSpec(memory_space=pltpu.SMEM)
    f32 = jnp.float32
    direct = (n_seg, n_ctx) == DIRECT_SHARDS
    limit = (16 if direct else 56) * 1024 * 1024
    shape = jax.ShapeDtypeStruct
    lines = 2 * FINE + shards + 8
    prepared = pl.pallas_call(
        functools.partial(prepare_kernel, query_start_of),
        out_shape=(
            shape((HEAD_DIM, query_rows * heads), jnp.bfloat16),
            shape((lines, HEAD_DIM), f32),
            shape((lines, HEAD_DIM), f32),
            shape((shards * rows, query_rows), jnp.bfloat16),
        ),
        in_specs=[smem, smem, smem, pl.BlockSpec(memory_space=pltpu.HBM), vmem],
        out_specs=[vmem] * 4,
        scratch_shapes=[
            pltpu.VMEM((lines, HEAD_DIM), jnp.int32),
            pltpu.VMEM((shards * rows // BLOCK, query_rows), f32),
            pltpu.VMEM(queries.shape, queries.dtype),
            pltpu.SemaphoreType.DMA(()),
        ],
        compiler_params=pltpu.CompilerParams(vmem_limit_bytes=limit),
        cost_estimate=pl.CostEstimate(flops=4 * 10**9, bytes_accessed=10**6, transcendentals=10**5),
        name="prepare",
    )(key_offsets, vertical_blocks, slash_offsets, queries, jnp.asarray(frequency_row()))

    def attend(prepared, pieces, shards_of, state, last):
        state_shape = (
            shape((8, query_rows * heads), f32),
            shape((HEAD_DIM + SUM_ROWS, query_rows * heads), f32),
        )
        return pl.pallas_call(
            functools.partial(attend_kernel, place_of, shards_of, not state, last),
            out_shape=shape(queries.shape, queries.dtype) if last else state_shape,
            in_specs=[vmem] * (4 + len(state) + len(pieces)),
            out_specs=vmem if last else (vmem, vmem),
            compiler_params=pltpu.CompilerParams(vmem_limit_bytes=limit),
            cost_estimate=pl.CostEstimate(
                flops=4 * 10**9, bytes_accessed=10**6, transcendentals=10**6
            ),
            name="attend",
        )(*prepared, *state, *pieces)

    own = jnp.concatenate([cached_keys, cached_values], axis=0)
    if not direct:
        gathered = lax.all_gather(own, ("seg", "ctx"), axis=0, tiled=True)
        return attend(prepared, [gathered], None, (), True)

    def number(seg, ctx):
        return seg * n_ctx + ctx

    def whole(ref):
        return ref[:rows, :], ref[rows : 2 * rows, :]

    far = exchange(own, lambda s, c, h: (s ^ (3 - h), c, h))
    near = exchange(own, lambda s, c, h: (s ^ (1 - h), c ^ h, h))
    near, prepared = lax.optimization_barrier((near, prepared))
    beside = swap(near)
    across = exchange(far, lambda s, c, h: (s, c ^ 1, h))
    state = attend(
        prepared,
        [own, near, beside, far],
        lambda refs, s, c, h: [
            (*whole(refs[0]), number(s, c)),
            (*whole(refs[1]), number(s ^ (1 - h), c ^ h)),
            (*whole(refs[2]), number(s ^ h, c ^ (1 - h))),
            (*whole(refs[3]), number(s ^ (3 - h), c)),
        ],
        (),
        False,
    )
    far_after, beside = lax.optimization_barrier((far, beside))
    far_beside = swap(far_after)
    half = jnp.where(lax.axis_index("head") == 0, beside[:rows], near[rows:])
    diagonal = exchange(half, lambda s, c, h: (s ^ 1, c, h))
    across, diagonal, state = lax.optimization_barrier((across, diagonal, state))
    last_beside = swap(jnp.concatenate([across, diagonal], axis=0))
    state = attend(
        prepared,
        [far_beside, across],
        lambda refs, s, c, h: [
            (*whole(refs[0]), number(s ^ (2 + h), c)),
            (*whole(refs[1]), number(s ^ (3 - h), c ^ 1)),
        ],
        state,
        False,
    )

    def last_shards(refs, s, c, h):
        diagonal, beside = refs
        mine, other = diagonal[...], beside[2 * rows :, :]
        return [
            (*whole(beside), number(s ^ (2 + h), c ^ 1)),
            (
                jnp.where(h == 0, mine, other),
                jnp.where(h == 0, other, mine),
                number(s ^ 1, c ^ 1),
            ),
        ]

    return attend(prepared, [diagonal, last_beside], last_shards, state, True)


def solution(mesh):
    return jax.shard_map(
        local,
        mesh=mesh,
        in_specs=(
            P(("groups", "ctx"), "head"),
            P(("groups", "seg", "ctx"), None),
            P(("groups", "seg", "ctx"), None),
            P("groups"),
            P("groups", None),
            P("groups", None),
        ),
        out_specs=P(("groups", "ctx"), "head"),
        check_vma=False,
    )
```

```python
import functools
import math

import jax
import jax.numpy as jnp
import numpy as np
from jax import lax
from jax.experimental import pallas as pl
from jax.experimental.pallas import tpu as pltpu
from jax.sharding import PartitionSpec as P

HEAD_DIM = 128
BLOCK = 64
ROPE_THETA = 500000.0
ROPE_FACTOR = 8.0
LOW_FACTOR = 1.0
HIGH_FACTOR = 4.0
TRAINED_CONTEXT = 8192.0
MASKED_SCORE = -1e30
SCORE_SCALE = HEAD_DIM**-0.5 * math.log2(math.e)
TILE = 128
FINE = 16
SUM_ROWS = 16
CHUNK = 256
DIRECT_SHARDS = (4, 2)
AXES = ("seg", "ctx", "head")


def frequency_row():
    exponent = np.arange(0, HEAD_DIM, 2, dtype=np.float64) / HEAD_DIM
    base = ROPE_THETA**-exponent
    wavelength = 2.0 * np.pi / base
    smooth = (TRAINED_CONTEXT / wavelength - LOW_FACTOR) / (HIGH_FACTOR - LOW_FACTOR)
    blended = (1.0 - smooth) * base / ROPE_FACTOR + smooth * base
    frequencies = np.where(
        wavelength < TRAINED_CONTEXT / HIGH_FACTOR,
        base,
        np.where(wavelength > TRAINED_CONTEXT / LOW_FACTOR, base / ROPE_FACTOR, blended),
    )
    return np.tile(frequencies, 2)[None, :].astype(np.float32)


def turned_sine(sine):
    lane = lax.broadcasted_iota(jnp.int32, sine.shape, 1)
    return jnp.where(lane < HEAD_DIM // 2, -sine, sine)


def rotate(vectors, cosine, signed_sine):
    wide = vectors.astype(jnp.float32)
    return (wide * cosine + pltpu.roll(wide, HEAD_DIM // 2, 1) * signed_sine).astype(jnp.bfloat16)


def angle_sum(cos_a, sin_a, cos_b, sin_b):
    return cos_a * cos_b - sin_a * sin_b, sin_a * cos_b + cos_a * sin_b


def shard_tables(cosines, sines, line, rows):
    cos_f, sin_f = cosines[pl.ds(0, FINE), :], turned_sine(sines[pl.ds(0, FINE), :])
    cos_c, sin_c = angle_sum(
        cosines[pl.ds(FINE, FINE), :],
        sines[pl.ds(FINE, FINE), :],
        cosines[pl.ds(line, 1), :],
        sines[pl.ds(line, 1), :],
    )
    signed = turned_sine(sin_c)
    parts = [
        (
            cos_f * cos_c[i : i + 1] - sin_f * signed[i : i + 1],
            sin_f * cos_c[i : i + 1] + cos_f * signed[i : i + 1],
        )
        for i in range(rows // FINE)
    ]
    return tuple(jnp.concatenate(table, axis=0) for table in zip(*parts))


def prepare_kernel(
    query_start_of, offsets, vertical, slash, queries, freq, rotated, cosines, sines, masks,
    angles, bias, held, arrival,
):
    query_rows, columns = held.shape
    heads = columns // HEAD_DIM
    fetch = pltpu.make_async_copy(queries, held, arrival)
    fetch.start()
    query_start, first_list = query_start_of()

    step = lax.broadcasted_iota(jnp.int32, (FINE, HEAD_DIM), 0)
    angles[pl.ds(0, FINE), :] = step
    angles[pl.ds(FINE, FINE), :] = step * FINE
    for shard in range(offsets.shape[0]):
        angles[pl.ds(2 * FINE + shard, 1), :] = jnp.full((1, HEAD_DIM), offsets[shard], jnp.int32)
    angles[pl.ds(angles.shape[0] - 8, 8), :] = jnp.full((8, HEAD_DIM), query_start, jnp.int32)
    angle = angles[...].astype(jnp.float32) * freq[...]
    cosines[...] = jnp.cos(angle)
    sines[...] = jnp.sin(angle)

    key_block = lax.broadcasted_iota(jnp.int32, bias.shape, 0)
    lane_block = lax.broadcasted_iota(jnp.int32, (1, query_rows), 1) // BLOCK
    hit = jnp.zeros(bias.shape, jnp.bool_)
    for entries, distance in ((vertical, False), (slash, True)):
        for entry in range(entries.shape[1]):
            wanted = jnp.zeros((1, query_rows), jnp.int32)
            for block in range(query_rows // BLOCK):
                value = entries[first_list + block, entry]
                if distance:
                    value = query_start // BLOCK + block - value
                wanted = jnp.where(lane_block == block, value, wanted)
            hit = hit | (key_block == wanted)
    bias[...] = jnp.where(hit, 0.0, MASKED_SCORE)

    rows = masks.shape[0] // offsets.shape[0]
    ahead = lax.broadcasted_iota(jnp.int32, (rows, query_rows), 1) - lax.broadcasted_iota(
        jnp.int32, (rows, query_rows), 0
    )

    @pl.loop(0, offsets.shape[0])
    def _(shard):
        offset = offsets[shard]
        lines = [
            jnp.broadcast_to(bias[pl.ds(offset // BLOCK + block, 1), :], (BLOCK, query_rows))
            for block in range(rows // BLOCK)
        ]
        masks[pl.ds(pl.multiple_of(shard * rows, rows), rows), :] = jnp.where(
            ahead >= offset - query_start, jnp.concatenate(lines, axis=0), MASKED_SCORE
        ).astype(masks.dtype)

    cosine, sine = shard_tables(cosines, sines, angles.shape[0] - 8, query_rows)
    fetch.wait()
    for head in range(heads):
        turned = rotate(held[:, pl.ds(head * HEAD_DIM, HEAD_DIM)], cosine, sine).T
        for tile in range(query_rows // TILE):
            lines = pl.ds((tile * heads + head) * TILE, TILE)
            rotated[:, lines] = turned[:, tile * TILE : (tile + 1) * TILE]


def attend_kernel(place_of, shards_of, first, last, *refs):
    rotated, cosines, sines, masks = refs[:4]
    refs = refs[4:]
    if not first:
        old_peak, old_sums = refs[:2]
        refs = refs[2:]
    if last:
        pieces, out = refs[:-1], refs[-1]
    else:
        pieces, new_peak, new_sums = refs[:-2], refs[-2], refs[-1]
    query_rows = masks.shape[1]
    tiles = query_rows // TILE
    width = rotated.shape[1] // tiles
    rows = masks.shape[0] // (cosines.shape[0] - 2 * FINE - 8)
    ones = jnp.ones((SUM_ROWS, rows), jnp.bfloat16)
    unit = (
        lax.broadcasted_iota(jnp.int32, (TILE, width), 0)
        == lax.broadcasted_iota(jnp.int32, (TILE, width), 1) % TILE
    ).astype(jnp.bfloat16)

    def load_keys(keys, shard):
        keys = rotate(keys, *shard_tables(cosines, sines, 2 * FINE + shard, rows))
        return keys, masks[pl.ds(pl.multiple_of(shard * rows, rows), rows), :]

    def load_values(values):
        return jnp.concatenate([values.T, ones], axis=0)

    def score(keys, mask, start, size):
        tile = start // width
        query = jnp.concatenate([rotated[:, pl.ds(start, size)], unit[:, :size]], axis=0)
        return jnp.dot(
            jnp.concatenate([keys, mask[:, tile * TILE : (tile + 1) * TILE]], axis=1),
            query,
            preferred_element_type=jnp.float32,
        )

    def weigh(scores, values, before):
        peak = scores.max(axis=0, keepdims=True)
        if before is not None:
            peak = jnp.maximum(before[0], peak)
        weights = jnp.exp2((scores - peak) * SCORE_SCALE).astype(jnp.bfloat16)
        return peak, jnp.dot(values, weights, preferred_element_type=jnp.float32)

    def joined(peak, sums, before):
        if before is not None:
            sums = sums + before[1] * jnp.exp2((before[0] - peak) * SCORE_SCALE)
        return peak, sums

    def update(scores, values, before):
        return joined(*weigh(scores, values, before), before)

    def finish(start, peak, sums):
        size = sums.shape[1]
        if not last:
            span = pl.ds(start, size)
            new_peak[:, span] = jnp.broadcast_to(peak, (new_peak.shape[0], size))
            new_sums[:, span] = sums
            return
        part = sums[:HEAD_DIM] * (1.0 / sums[HEAD_DIM : HEAD_DIM + 1])
        part = part.astype(out.dtype)
        for column in range(0, size, TILE):
            tile, head = divmod((start + column) // TILE, width // TILE)
            out[pl.ds(tile * TILE, TILE), pl.ds(head * HEAD_DIM, HEAD_DIM)] = part[
                :, column : column + TILE
            ].T

    if shards_of is not None:
        shards = shards_of(pieces, *place_of())
        keys, mask = (
            jnp.concatenate(part, axis=0)
            for part in zip(*(load_keys(keys, shard) for keys, _, shard in shards))
        )
        starts = list(range(0, rotated.shape[1], CHUNK))
        ahead = score(keys, mask, starts[0], CHUNK)
        values = jnp.concatenate([load_values(values) for _, values, _ in shards], axis=1)
        waiting = None
        for start in starts:
            scores = ahead
            if start != starts[-1]:
                ahead = score(keys, mask, start + CHUNK, CHUNK)
            before = None
            if not first:
                before = (old_peak[:1, pl.ds(start, CHUNK)], old_sums[:, pl.ds(start, CHUNK)])
            fresh = weigh(scores, values, before)
            if waiting is not None:
                finish(waiting[0], *joined(*waiting[1:]))
            waiting = (start, *fresh, before)
        finish(waiting[0], *joined(*waiting[1:]))
    else:
        (whole,) = pieces
        for tile in range(tiles):

            def step(shard, before, tile=tile):
                start = pl.multiple_of(shard * (2 * rows), 2 * rows)
                keys, mask = load_keys(whole[pl.ds(start, rows), :], shard)
                values = load_values(whole[pl.ds(start + rows, rows), :])
                return update(score(keys, mask, tile * width, width), values, before)

            initial = (
                jnp.full((1, width), MASKED_SCORE, jnp.float32),
                jnp.zeros((HEAD_DIM + SUM_ROWS, width), jnp.float32),
            )
            finish(
                tile * width, *lax.fori_loop(0, whole.shape[0] // (2 * rows), step, initial)
            )


def local(queries, cached_keys, cached_values, key_offsets, vertical_blocks, slash_offsets):
    query_rows = queries.shape[0]
    heads = queries.shape[1] // HEAD_DIM
    rows = cached_keys.shape[0]
    n_seg, n_ctx = lax.axis_size("seg"), lax.axis_size("ctx")
    shards = n_seg * n_ctx
    prefix = rows * shards - query_rows * n_ctx

    def query_start_of():
        ctx = lax.axis_index("ctx")
        return prefix + ctx * query_rows, ctx * (query_rows // BLOCK)

    def place_of():
        return tuple(lax.axis_index(axis) for axis in AXES)

    def exchange(a, partner):
        pairs = []
        for seg in range(n_seg):
            for ctx in range(n_ctx):
                for head in range(2):
                    to_seg, to_ctx, to_head = partner(seg, ctx, head)
                    pairs.append(
                        ((seg * n_ctx + ctx) * 2 + head, (to_seg * n_ctx + to_ctx) * 2 + to_head)
                    )
        return lax.ppermute(a, AXES, pairs)

    def swap(a):
        return exchange(a, lambda s, c, h: (s, c, 1 - h))

    vmem = pl.BlockSpec(memory_space=pltpu.VMEM)
    smem = pl.BlockSpec(memory_space=pltpu.SMEM)
    f32 = jnp.float32
    direct = (n_seg, n_ctx) == DIRECT_SHARDS
    limit = (16 if direct else 56) * 1024 * 1024
    shape = jax.ShapeDtypeStruct
    lines = 2 * FINE + shards + 8
    prepared = pl.pallas_call(
        functools.partial(prepare_kernel, query_start_of),
        out_shape=(
            shape((HEAD_DIM, query_rows * heads), jnp.bfloat16),
            shape((lines, HEAD_DIM), f32),
            shape((lines, HEAD_DIM), f32),
            shape((shards * rows, query_rows), jnp.bfloat16),
        ),
        in_specs=[smem, smem, smem, pl.BlockSpec(memory_space=pltpu.HBM), vmem],
        out_specs=[vmem] * 4,
        scratch_shapes=[
            pltpu.VMEM((lines, HEAD_DIM), jnp.int32),
            pltpu.VMEM((shards * rows // BLOCK, query_rows), f32),
            pltpu.VMEM(queries.shape, queries.dtype),
            pltpu.SemaphoreType.DMA(()),
        ],
        compiler_params=pltpu.CompilerParams(vmem_limit_bytes=limit),
        cost_estimate=pl.CostEstimate(flops=4 * 10**9, bytes_accessed=10**6, transcendentals=10**5),
        name="prepare",
    )(key_offsets, vertical_blocks, slash_offsets, queries, jnp.asarray(frequency_row()))

    def attend(prepared, pieces, shards_of, state, last):
        state_shape = (
            shape((8, query_rows * heads), f32),
            shape((HEAD_DIM + SUM_ROWS, query_rows * heads), f32),
        )
        return pl.pallas_call(
            functools.partial(attend_kernel, place_of, shards_of, not state, last),
            out_shape=shape(queries.shape, queries.dtype) if last else state_shape,
            in_specs=[vmem] * (4 + len(state) + len(pieces)),
            out_specs=vmem if last else (vmem, vmem),
            compiler_params=pltpu.CompilerParams(vmem_limit_bytes=limit),
            cost_estimate=pl.CostEstimate(
                flops=4 * 10**9, bytes_accessed=10**6, transcendentals=10**6
            ),
            name="attend",
        )(*prepared, *state, *pieces)

    own = jnp.concatenate([cached_keys, cached_values], axis=0)
    if not direct:
        gathered = lax.all_gather(own, ("seg", "ctx"), axis=0, tiled=True)
        return attend(prepared, [gathered], None, (), True)

    def number(seg, ctx):
        return seg * n_ctx + ctx

    def whole(ref):
        return ref[:rows, :], ref[rows : 2 * rows, :]

    far = exchange(own, lambda s, c, h: (s ^ (3 - h), c, h))
    near = exchange(own, lambda s, c, h: (s ^ (1 - h), c ^ h, h))
    near, prepared = lax.optimization_barrier((near, prepared))
    beside = swap(near)
    across = exchange(far, lambda s, c, h: (s, c ^ 1, h))
    state = attend(
        prepared,
        [own, near, beside, far],
        lambda refs, s, c, h: [
            (*whole(refs[0]), number(s, c)),
            (*whole(refs[1]), number(s ^ (1 - h), c ^ h)),
            (*whole(refs[2]), number(s ^ h, c ^ (1 - h))),
            (*whole(refs[3]), number(s ^ (3 - h), c)),
        ],
        (),
        False,
    )
    far_after, beside = lax.optimization_barrier((far, beside))
    far_beside = swap(far_after)
    half = jnp.where(lax.axis_index("head") == 0, beside[:rows], near[rows:])
    diagonal = exchange(half, lambda s, c, h: (s ^ 1, c, h))
    across, diagonal, state = lax.optimization_barrier((across, diagonal, state))
    last_beside = swap(jnp.concatenate([across, diagonal], axis=0))
    state = attend(
        prepared,
        [far_beside, across],
        lambda refs, s, c, h: [
            (*whole(refs[0]), number(s ^ (2 + h), c)),
            (*whole(refs[1]), number(s ^ (3 - h), c ^ 1)),
        ],
        state,
        False,
    )

    def last_shards(refs, s, c, h):
        diagonal, beside = refs
        mine, other = diagonal[...], beside[2 * rows :, :]
        return [
            (*whole(beside), number(s ^ (2 + h), c ^ 1)),
            (
                jnp.where(h == 0, mine, other),
                jnp.where(h == 0, other, mine),
                number(s ^ 1, c ^ 1),
            ),
        ]

    return attend(prepared, [diagonal, last_beside], last_shards, state, True)


def solution(mesh):
    return jax.shard_map(
        local,
        mesh=mesh,
        in_specs=(
            P(("groups", "ctx"), "head"),
            P(("groups", "seg", "ctx"), None),
            P(("groups", "seg", "ctx"), None),
            P("groups"),
            P("groups", None),
            P("groups", None),
        ),
        out_specs=P(("groups", "ctx"), "head"),
        check_vma=False,
    )
```

```python
import functools
import math

import jax
import jax.numpy as jnp
import numpy as np
from jax import lax
from jax.experimental import pallas as pl
from jax.experimental.pallas import tpu as pltpu
from jax.sharding import PartitionSpec as P

HEAD_DIM = 128
BLOCK = 64
ROPE_THETA = 500000.0
ROPE_FACTOR = 8.0
LOW_FACTOR = 1.0
HIGH_FACTOR = 4.0
TRAINED_CONTEXT = 8192.0
MASKED_SCORE = -1e30
SCORE_SCALE = HEAD_DIM**-0.5 * math.log2(math.e)
TILE = 128
FINE = 16
SUM_ROWS = 16
CHUNK = 256
DIRECT_SHARDS = (4, 2)
AXES = ("seg", "ctx", "head")


def frequency_row():
    exponent = np.arange(0, HEAD_DIM, 2, dtype=np.float64) / HEAD_DIM
    base = ROPE_THETA**-exponent
    wavelength = 2.0 * np.pi / base
    smooth = (TRAINED_CONTEXT / wavelength - LOW_FACTOR) / (HIGH_FACTOR - LOW_FACTOR)
    blended = (1.0 - smooth) * base / ROPE_FACTOR + smooth * base
    frequencies = np.where(
        wavelength < TRAINED_CONTEXT / HIGH_FACTOR,
        base,
        np.where(wavelength > TRAINED_CONTEXT / LOW_FACTOR, base / ROPE_FACTOR, blended),
    )
    return np.tile(frequencies, 2)[None, :].astype(np.float32)


def turned_sine(sine):
    lane = lax.broadcasted_iota(jnp.int32, sine.shape, 1)
    return jnp.where(lane < HEAD_DIM // 2, -sine, sine)


def rotate(vectors, cosine, signed_sine):
    wide = vectors.astype(jnp.float32)
    return (wide * cosine + pltpu.roll(wide, HEAD_DIM // 2, 1) * signed_sine).astype(jnp.bfloat16)


def angle_sum(cos_a, sin_a, cos_b, sin_b):
    return cos_a * cos_b - sin_a * sin_b, sin_a * cos_b + cos_a * sin_b


def shard_tables(cosines, sines, line, rows):
    cos_f, sin_f = cosines[pl.ds(0, FINE), :], turned_sine(sines[pl.ds(0, FINE), :])
    cos_c, sin_c = angle_sum(
        cosines[pl.ds(FINE, FINE), :],
        sines[pl.ds(FINE, FINE), :],
        cosines[pl.ds(line, 1), :],
        sines[pl.ds(line, 1), :],
    )
    signed = turned_sine(sin_c)
    parts = [
        (
            cos_f * cos_c[i : i + 1] - sin_f * signed[i : i + 1],
            sin_f * cos_c[i : i + 1] + cos_f * signed[i : i + 1],
        )
        for i in range(rows // FINE)
    ]
    return tuple(jnp.concatenate(table, axis=0) for table in zip(*parts))


def prepare_kernel(
    query_start_of, offsets, vertical, slash, queries, freq, rotated, cosines, sines, masks,
    angles, bias, held, arrival,
):
    query_rows, columns = held.shape
    heads = columns // HEAD_DIM
    fetch = pltpu.make_async_copy(queries, held, arrival)
    fetch.start()
    query_start, first_list = query_start_of()

    step = lax.broadcasted_iota(jnp.int32, (FINE, HEAD_DIM), 0)
    angles[pl.ds(0, FINE), :] = step
    angles[pl.ds(FINE, FINE), :] = step * FINE
    for shard in range(offsets.shape[0]):
        angles[pl.ds(2 * FINE + shard, 1), :] = jnp.full((1, HEAD_DIM), offsets[shard], jnp.int32)
    angles[pl.ds(angles.shape[0] - 8, 8), :] = jnp.full((8, HEAD_DIM), query_start, jnp.int32)
    angle = angles[...].astype(jnp.float32) * freq[...]
    cosines[...] = jnp.cos(angle)
    sines[...] = jnp.sin(angle)

    key_block = lax.broadcasted_iota(jnp.int32, bias.shape, 0)
    lane_block = lax.broadcasted_iota(jnp.int32, (1, query_rows), 1) // BLOCK
    hit = jnp.zeros(bias.shape, jnp.bool_)
    for entries, distance in ((vertical, False), (slash, True)):
        for entry in range(entries.shape[1]):
            wanted = jnp.zeros((1, query_rows), jnp.int32)
            for block in range(query_rows // BLOCK):
                value = entries[first_list + block, entry]
                if distance:
                    value = query_start // BLOCK + block - value
                wanted = jnp.where(lane_block == block, value, wanted)
            hit = hit | (key_block == wanted)
    bias[...] = jnp.where(hit, 0.0, MASKED_SCORE)

    rows = masks.shape[0] // offsets.shape[0]
    ahead = lax.broadcasted_iota(jnp.int32, (rows, query_rows), 1) - lax.broadcasted_iota(
        jnp.int32, (rows, query_rows), 0
    )

    @pl.loop(0, offsets.shape[0])
    def _(shard):
        offset = offsets[shard]
        lines = [
            jnp.broadcast_to(bias[pl.ds(offset // BLOCK + block, 1), :], (BLOCK, query_rows))
            for block in range(rows // BLOCK)
        ]
        masks[pl.ds(pl.multiple_of(shard * rows, rows), rows), :] = jnp.where(
            ahead >= offset - query_start, jnp.concatenate(lines, axis=0), MASKED_SCORE
        ).astype(masks.dtype)

    cosine, sine = shard_tables(cosines, sines, angles.shape[0] - 8, query_rows)
    fetch.wait()
    for head in range(heads):
        turned = rotate(held[:, pl.ds(head * HEAD_DIM, HEAD_DIM)], cosine, sine).T
        for tile in range(query_rows // TILE):
            lines = pl.ds((tile * heads + head) * TILE, TILE)
            rotated[:, lines] = turned[:, tile * TILE : (tile + 1) * TILE]


def attend_kernel(place_of, shards_of, first, last, *refs):
    rotated, cosines, sines, masks = refs[:4]
    refs = refs[4:]
    if not first:
        old_peak, old_sums = refs[:2]
        refs = refs[2:]
    if last:
        pieces, out = refs[:-1], refs[-1]
    else:
        pieces, new_peak, new_sums = refs[:-2], refs[-2], refs[-1]
    query_rows = masks.shape[1]
    tiles = query_rows // TILE
    width = rotated.shape[1] // tiles
    rows = masks.shape[0] // (cosines.shape[0] - 2 * FINE - 8)
    ones = jnp.ones((SUM_ROWS, rows), jnp.bfloat16)
    unit = (
        lax.broadcasted_iota(jnp.int32, (TILE, width), 0)
        == lax.broadcasted_iota(jnp.int32, (TILE, width), 1) % TILE
    ).astype(jnp.bfloat16)

    def load_keys(keys, shard):
        keys = rotate(keys, *shard_tables(cosines, sines, 2 * FINE + shard, rows))
        return keys, masks[pl.ds(pl.multiple_of(shard * rows, rows), rows), :]

    def load_values(values):
        return jnp.concatenate([values.T, ones], axis=0)

    def score(keys, mask, start, size):
        tile = start // width
        query = jnp.concatenate([rotated[:, pl.ds(start, size)], unit[:, :size]], axis=0)
        return jnp.dot(
            jnp.concatenate([keys, mask[:, tile * TILE : (tile + 1) * TILE]], axis=1),
            query,
            preferred_element_type=jnp.float32,
        )

    def update(scores, values, before):
        peak = scores.max(axis=0, keepdims=True)
        if before is not None:
            peak = jnp.maximum(before[0], peak)
        weights = jnp.exp2((scores - peak) * SCORE_SCALE).astype(jnp.bfloat16)
        sums = jnp.dot(values, weights, preferred_element_type=jnp.float32)
        if before is not None:
            sums = sums + before[1] * jnp.exp2((before[0] - peak) * SCORE_SCALE)
        return peak, sums

    def finish(start, peak, sums):
        size = sums.shape[1]
        if not last:
            span = pl.ds(start, size)
            new_peak[:, span] = jnp.broadcast_to(peak, (new_peak.shape[0], size))
            new_sums[:, span] = sums
            return
        part = sums[:HEAD_DIM] * (1.0 / sums[HEAD_DIM : HEAD_DIM + 1])
        part = part.astype(out.dtype)
        for column in range(0, size, TILE):
            tile, head = divmod((start + column) // TILE, width // TILE)
            out[pl.ds(tile * TILE, TILE), pl.ds(head * HEAD_DIM, HEAD_DIM)] = part[
                :, column : column + TILE
            ].T

    if shards_of is not None:
        shards = shards_of(pieces, *place_of())
        keys, mask = (
            jnp.concatenate(part, axis=0)
            for part in zip(*(load_keys(keys, shard) for keys, _, shard in shards))
        )
        starts = list(range(0, rotated.shape[1], CHUNK))
        ahead = score(keys, mask, starts[0], CHUNK)
        values = jnp.concatenate([load_values(values) for _, values, _ in shards], axis=1)
        for start in starts:
            scores = ahead
            if start != starts[-1]:
                ahead = score(keys, mask, start + CHUNK, CHUNK)
            before = None
            if not first:
                before = (old_peak[:1, pl.ds(start, CHUNK)], old_sums[:, pl.ds(start, CHUNK)])
            finish(start, *update(scores, values, before))
    else:
        (whole,) = pieces
        for tile in range(tiles):

            def step(shard, before, tile=tile):
                start = pl.multiple_of(shard * (2 * rows), 2 * rows)
                keys, mask = load_keys(whole[pl.ds(start, rows), :], shard)
                values = load_values(whole[pl.ds(start + rows, rows), :])
                return update(score(keys, mask, tile * width, width), values, before)

            initial = (
                jnp.full((1, width), MASKED_SCORE, jnp.float32),
                jnp.zeros((HEAD_DIM + SUM_ROWS, width), jnp.float32),
            )
            finish(
                tile * width, *lax.fori_loop(0, whole.shape[0] // (2 * rows), step, initial)
            )


def local(queries, cached_keys, cached_values, key_offsets, vertical_blocks, slash_offsets):
    query_rows = queries.shape[0]
    heads = queries.shape[1] // HEAD_DIM
    rows = cached_keys.shape[0]
    n_seg, n_ctx = lax.axis_size("seg"), lax.axis_size("ctx")
    shards = n_seg * n_ctx
    prefix = rows * shards - query_rows * n_ctx

    def query_start_of():
        ctx = lax.axis_index("ctx")
        return prefix + ctx * query_rows, ctx * (query_rows // BLOCK)

    def place_of():
        return tuple(lax.axis_index(axis) for axis in AXES)

    def exchange(a, partner):
        pairs = []
        for seg in range(n_seg):
            for ctx in range(n_ctx):
                for head in range(2):
                    to_seg, to_ctx, to_head = partner(seg, ctx, head)
                    pairs.append(
                        ((seg * n_ctx + ctx) * 2 + head, (to_seg * n_ctx + to_ctx) * 2 + to_head)
                    )
        return lax.ppermute(a, AXES, pairs)

    def swap(a):
        return exchange(a, lambda s, c, h: (s, c, 1 - h))

    vmem = pl.BlockSpec(memory_space=pltpu.VMEM)
    smem = pl.BlockSpec(memory_space=pltpu.SMEM)
    f32 = jnp.float32
    direct = (n_seg, n_ctx) == DIRECT_SHARDS
    limit = (16 if direct else 56) * 1024 * 1024
    shape = jax.ShapeDtypeStruct
    lines = 2 * FINE + shards + 8
    prepared = pl.pallas_call(
        functools.partial(prepare_kernel, query_start_of),
        out_shape=(
            shape((HEAD_DIM, query_rows * heads), jnp.bfloat16),
            shape((lines, HEAD_DIM), f32),
            shape((lines, HEAD_DIM), f32),
            shape((shards * rows, query_rows), jnp.bfloat16),
        ),
        in_specs=[smem, smem, smem, pl.BlockSpec(memory_space=pltpu.HBM), vmem],
        out_specs=[vmem] * 4,
        scratch_shapes=[
            pltpu.VMEM((lines, HEAD_DIM), jnp.int32),
            pltpu.VMEM((shards * rows // BLOCK, query_rows), f32),
            pltpu.VMEM(queries.shape, queries.dtype),
            pltpu.SemaphoreType.DMA(()),
        ],
        compiler_params=pltpu.CompilerParams(vmem_limit_bytes=limit),
        cost_estimate=pl.CostEstimate(flops=4 * 10**9, bytes_accessed=10**6, transcendentals=10**5),
        name="prepare",
    )(key_offsets, vertical_blocks, slash_offsets, queries, jnp.asarray(frequency_row()))

    def attend(prepared, pieces, shards_of, state, last):
        state_shape = (
            shape((8, query_rows * heads), f32),
            shape((HEAD_DIM + SUM_ROWS, query_rows * heads), f32),
        )
        return pl.pallas_call(
            functools.partial(attend_kernel, place_of, shards_of, not state, last),
            out_shape=shape(queries.shape, queries.dtype) if last else state_shape,
            in_specs=[vmem] * (4 + len(state) + len(pieces)),
            out_specs=vmem if last else (vmem, vmem),
            compiler_params=pltpu.CompilerParams(vmem_limit_bytes=limit),
            cost_estimate=pl.CostEstimate(
                flops=4 * 10**9, bytes_accessed=10**6, transcendentals=10**6
            ),
            name="attend",
        )(*prepared, *state, *pieces)

    own = jnp.concatenate([cached_keys, cached_values], axis=0)
    if not direct:
        gathered = lax.all_gather(own, ("seg", "ctx"), axis=0, tiled=True)
        return attend(prepared, [gathered], None, (), True)

    def number(seg, ctx):
        return seg * n_ctx + ctx

    def whole(ref):
        return ref[:rows, :], ref[rows : 2 * rows, :]

    far = exchange(own, lambda s, c, h: (s ^ (2 + h), c, h))
    near = exchange(own, lambda s, c, h: (s ^ h, c ^ (1 - h), h))
    near, prepared = lax.optimization_barrier((near, prepared))
    beside = swap(near)
    across = exchange(far, lambda s, c, h: (s, c ^ 1, h))
    state = attend(
        prepared,
        [own, near, beside, far],
        lambda refs, s, c, h: [
            (*whole(refs[0]), number(s, c)),
            (*whole(refs[1]), number(s ^ h, c ^ (1 - h))),
            (*whole(refs[2]), number(s ^ (1 - h), c ^ h)),
            (*whole(refs[3]), number(s ^ (2 + h), c)),
        ],
        (),
        False,
    )
    far_after, beside = lax.optimization_barrier((far, beside))
    far_beside = swap(far_after)
    half = jnp.where(lax.axis_index("head") == 0, near[:rows], beside[rows:])
    diagonal = exchange(half, lambda s, c, h: (s ^ 1, c, h))
    across, diagonal, state = lax.optimization_barrier((across, diagonal, state))
    last_beside = swap(jnp.concatenate([across, diagonal], axis=0))
    state = attend(
        prepared,
        [far_beside, across],
        lambda refs, s, c, h: [
            (*whole(refs[0]), number(s ^ (3 - h), c)),
            (*whole(refs[1]), number(s ^ (2 + h), c ^ 1)),
        ],
        state,
        False,
    )

    def last_shards(refs, s, c, h):
        diagonal, beside = refs
        mine, other = diagonal[...], beside[2 * rows :, :]
        return [
            (*whole(beside), number(s ^ (3 - h), c ^ 1)),
            (
                jnp.where(h == 0, mine, other),
                jnp.where(h == 0, other, mine),
                number(s ^ 1, c ^ 1),
            ),
        ]

    return attend(prepared, [diagonal, last_beside], last_shards, state, True)


def solution(mesh):
    return jax.shard_map(
        local,
        mesh=mesh,
        in_specs=(
            P(("groups", "ctx"), "head"),
            P(("groups", "seg", "ctx"), None),
            P(("groups", "seg", "ctx"), None),
            P("groups"),
            P("groups", None),
            P("groups", None),
        ),
        out_specs=P(("groups", "ctx"), "head"),
        check_vma=False,
    )
```

```python
import functools
import math

import jax
import jax.numpy as jnp
import numpy as np
from jax import lax
from jax.experimental import pallas as pl
from jax.experimental.pallas import tpu as pltpu
from jax.sharding import PartitionSpec as P

HEAD_DIM = 128
BLOCK = 64
ROPE_THETA = 500000.0
ROPE_FACTOR = 8.0
LOW_FACTOR = 1.0
HIGH_FACTOR = 4.0
TRAINED_CONTEXT = 8192.0
MASKED_SCORE = -1e30
SCORE_SCALE = HEAD_DIM**-0.5 * math.log2(math.e)
TILE = 128
FINE = 16
SUM_ROWS = 16
CHUNK = 256
DIRECT_SHARDS = (4, 2)
AXES = ("seg", "ctx", "head")


def frequency_row():
    exponent = np.arange(0, HEAD_DIM, 2, dtype=np.float64) / HEAD_DIM
    base = ROPE_THETA**-exponent
    wavelength = 2.0 * np.pi / base
    smooth = (TRAINED_CONTEXT / wavelength - LOW_FACTOR) / (HIGH_FACTOR - LOW_FACTOR)
    blended = (1.0 - smooth) * base / ROPE_FACTOR + smooth * base
    frequencies = np.where(
        wavelength < TRAINED_CONTEXT / HIGH_FACTOR,
        base,
        np.where(wavelength > TRAINED_CONTEXT / LOW_FACTOR, base / ROPE_FACTOR, blended),
    )
    return np.tile(frequencies, 2)[None, :].astype(np.float32)


def turned_sine(sine):
    lane = lax.broadcasted_iota(jnp.int32, sine.shape, 1)
    return jnp.where(lane < HEAD_DIM // 2, -sine, sine)


def rotate(vectors, cosine, signed_sine):
    wide = vectors.astype(jnp.float32)
    return (wide * cosine + pltpu.roll(wide, HEAD_DIM // 2, 1) * signed_sine).astype(jnp.bfloat16)


def angle_sum(cos_a, sin_a, cos_b, sin_b):
    return cos_a * cos_b - sin_a * sin_b, sin_a * cos_b + cos_a * sin_b


def shard_tables(cosines, sines, line, rows):
    cos_f, sin_f = cosines[pl.ds(0, FINE), :], turned_sine(sines[pl.ds(0, FINE), :])
    cos_c, sin_c = angle_sum(
        cosines[pl.ds(FINE, FINE), :],
        sines[pl.ds(FINE, FINE), :],
        cosines[pl.ds(line, 1), :],
        sines[pl.ds(line, 1), :],
    )
    signed = turned_sine(sin_c)
    parts = [
        (
            cos_f * cos_c[i : i + 1] - sin_f * signed[i : i + 1],
            sin_f * cos_c[i : i + 1] + cos_f * signed[i : i + 1],
        )
        for i in range(rows // FINE)
    ]
    return tuple(jnp.concatenate(table, axis=0) for table in zip(*parts))


def prepare_kernel(
    query_start_of, offsets, vertical, slash, queries, freq, rotated, cosines, sines, masks,
    angles, bias, held, arrival,
):
    query_rows, columns = held.shape
    heads = columns // HEAD_DIM
    fetch = pltpu.make_async_copy(queries, held, arrival)
    fetch.start()
    query_start, first_list = query_start_of()

    step = lax.broadcasted_iota(jnp.int32, (FINE, HEAD_DIM), 0)
    angles[pl.ds(0, FINE), :] = step
    angles[pl.ds(FINE, FINE), :] = step * FINE
    for shard in range(offsets.shape[0]):
        angles[pl.ds(2 * FINE + shard, 1), :] = jnp.full((1, HEAD_DIM), offsets[shard], jnp.int32)
    angles[pl.ds(angles.shape[0] - 8, 8), :] = jnp.full((8, HEAD_DIM), query_start, jnp.int32)
    angle = angles[...].astype(jnp.float32) * freq[...]
    cosines[...] = jnp.cos(angle)
    sines[...] = jnp.sin(angle)

    key_block = lax.broadcasted_iota(jnp.int32, bias.shape, 0)
    lane_block = lax.broadcasted_iota(jnp.int32, (1, query_rows), 1) // BLOCK
    hit = jnp.zeros(bias.shape, jnp.bool_)
    for entries, distance in ((vertical, False), (slash, True)):
        for entry in range(entries.shape[1]):
            wanted = jnp.zeros((1, query_rows), jnp.int32)
            for block in range(query_rows // BLOCK):
                value = entries[first_list + block, entry]
                if distance:
                    value = query_start // BLOCK + block - value
                wanted = jnp.where(lane_block == block, value, wanted)
            hit = hit | (key_block == wanted)
    bias[...] = jnp.where(hit, 0.0, MASKED_SCORE)

    rows = masks.shape[0] // offsets.shape[0]
    ahead = lax.broadcasted_iota(jnp.int32, (rows, query_rows), 1) - lax.broadcasted_iota(
        jnp.int32, (rows, query_rows), 0
    )

    @pl.loop(0, offsets.shape[0])
    def _(shard):
        offset = offsets[shard]
        lines = [
            jnp.broadcast_to(bias[pl.ds(offset // BLOCK + block, 1), :], (BLOCK, query_rows))
            for block in range(rows // BLOCK)
        ]
        masks[pl.ds(pl.multiple_of(shard * rows, rows), rows), :] = jnp.where(
            ahead >= offset - query_start, jnp.concatenate(lines, axis=0), MASKED_SCORE
        ).astype(masks.dtype)

    cosine, sine = shard_tables(cosines, sines, angles.shape[0] - 8, query_rows)
    fetch.wait()
    for head in range(heads):
        turned = rotate(held[:, pl.ds(head * HEAD_DIM, HEAD_DIM)], cosine, sine).T
        for tile in range(query_rows // TILE):
            lines = pl.ds((tile * heads + head) * TILE, TILE)
            rotated[:, lines] = turned[:, tile * TILE : (tile + 1) * TILE]


def attend_kernel(place_of, shards_of, first, last, *refs):
    rotated, cosines, sines, masks = refs[:4]
    refs = refs[4:]
    if not first:
        old_peak, old_sums = refs[:2]
        refs = refs[2:]
    if last:
        pieces, out = refs[:-1], refs[-1]
    else:
        pieces, new_peak, new_sums = refs[:-2], refs[-2], refs[-1]
    query_rows = masks.shape[1]
    tiles = query_rows // TILE
    width = rotated.shape[1] // tiles
    rows = masks.shape[0] // (cosines.shape[0] - 2 * FINE - 8)
    ones = jnp.ones((SUM_ROWS, rows), jnp.bfloat16)
    unit = (
        lax.broadcasted_iota(jnp.int32, (TILE, width), 0)
        == lax.broadcasted_iota(jnp.int32, (TILE, width), 1) % TILE
    ).astype(jnp.bfloat16)

    def load_keys(keys, shard):
        keys = rotate(keys, *shard_tables(cosines, sines, 2 * FINE + shard, rows))
        return keys, masks[pl.ds(pl.multiple_of(shard * rows, rows), rows), :]

    def load_values(values):
        return jnp.concatenate([values.T, ones], axis=0)

    def score(keys, mask, start, size):
        tile = start // width
        query = jnp.concatenate([rotated[:, pl.ds(start, size)], unit[:, :size]], axis=0)
        return jnp.dot(
            jnp.concatenate([keys, mask[:, tile * TILE : (tile + 1) * TILE]], axis=1),
            query,
            preferred_element_type=jnp.float32,
        )

    def update(scores, values, before):
        peak = scores.max(axis=0, keepdims=True)
        if before is not None:
            peak = jnp.maximum(before[0], peak)
        weights = jnp.exp2((scores - peak) * SCORE_SCALE).astype(jnp.bfloat16)
        sums = jnp.dot(values, weights, preferred_element_type=jnp.float32)
        if before is not None:
            sums = sums + before[1] * jnp.exp2((before[0] - peak) * SCORE_SCALE)
        return peak, sums

    def finish(start, peak, sums):
        size = sums.shape[1]
        if not last:
            span = pl.ds(start, size)
            new_peak[:, span] = jnp.broadcast_to(peak, (new_peak.shape[0], size))
            new_sums[:, span] = sums
            return
        part = sums[:HEAD_DIM] * (1.0 / sums[HEAD_DIM : HEAD_DIM + 1])
        part = part.astype(out.dtype)
        for column in range(0, size, TILE):
            tile, head = divmod((start + column) // TILE, width // TILE)
            out[pl.ds(tile * TILE, TILE), pl.ds(head * HEAD_DIM, HEAD_DIM)] = part[
                :, column : column + TILE
            ].T

    if shards_of is not None:
        shards = shards_of(pieces, *place_of())
        keys, mask = (
            jnp.concatenate(part, axis=0)
            for part in zip(*(load_keys(keys, shard) for keys, _, shard in shards))
        )
        starts = list(range(0, rotated.shape[1], CHUNK))
        ahead = score(keys, mask, starts[0], CHUNK)
        values = jnp.concatenate([load_values(values) for _, values, _ in shards], axis=1)
        for start in starts:
            scores = ahead
            if start != starts[-1]:
                ahead = score(keys, mask, start + CHUNK, CHUNK)
            before = None
            if not first:
                before = (old_peak[:1, pl.ds(start, CHUNK)], old_sums[:, pl.ds(start, CHUNK)])
            finish(start, *update(scores, values, before))
    else:
        (whole,) = pieces
        for tile in range(tiles):

            def step(shard, before, tile=tile):
                start = pl.multiple_of(shard * (2 * rows), 2 * rows)
                keys, mask = load_keys(whole[pl.ds(start, rows), :], shard)
                values = load_values(whole[pl.ds(start + rows, rows), :])
                return update(score(keys, mask, tile * width, width), values, before)

            initial = (
                jnp.full((1, width), MASKED_SCORE, jnp.float32),
                jnp.zeros((HEAD_DIM + SUM_ROWS, width), jnp.float32),
            )
            finish(
                tile * width, *lax.fori_loop(0, whole.shape[0] // (2 * rows), step, initial)
            )


def local(queries, cached_keys, cached_values, key_offsets, vertical_blocks, slash_offsets):
    query_rows = queries.shape[0]
    heads = queries.shape[1] // HEAD_DIM
    rows = cached_keys.shape[0]
    n_seg, n_ctx = lax.axis_size("seg"), lax.axis_size("ctx")
    shards = n_seg * n_ctx
    prefix = rows * shards - query_rows * n_ctx

    def query_start_of():
        ctx = lax.axis_index("ctx")
        return prefix + ctx * query_rows, ctx * (query_rows // BLOCK)

    def place_of():
        return tuple(lax.axis_index(axis) for axis in AXES)

    def exchange(a, partner):
        pairs = []
        for seg in range(n_seg):
            for ctx in range(n_ctx):
                for head in range(2):
                    to_seg, to_ctx, to_head = partner(seg, ctx, head)
                    pairs.append(
                        ((seg * n_ctx + ctx) * 2 + head, (to_seg * n_ctx + to_ctx) * 2 + to_head)
                    )
        return lax.ppermute(a, AXES, pairs)

    def swap(a):
        return exchange(a, lambda s, c, h: (s, c, 1 - h))

    vmem = pl.BlockSpec(memory_space=pltpu.VMEM)
    smem = pl.BlockSpec(memory_space=pltpu.SMEM)
    f32 = jnp.float32
    direct = (n_seg, n_ctx) == DIRECT_SHARDS
    limit = (16 if direct else 56) * 1024 * 1024
    shape = jax.ShapeDtypeStruct
    lines = 2 * FINE + shards + 8
    prepared = pl.pallas_call(
        functools.partial(prepare_kernel, query_start_of),
        out_shape=(
            shape((HEAD_DIM, query_rows * heads), jnp.bfloat16),
            shape((lines, HEAD_DIM), f32),
            shape((lines, HEAD_DIM), f32),
            shape((shards * rows, query_rows), jnp.bfloat16),
        ),
        in_specs=[smem, smem, smem, pl.BlockSpec(memory_space=pltpu.HBM), vmem],
        out_specs=[vmem] * 4,
        scratch_shapes=[
            pltpu.VMEM((lines, HEAD_DIM), jnp.int32),
            pltpu.VMEM((shards * rows // BLOCK, query_rows), f32),
            pltpu.VMEM(queries.shape, queries.dtype),
            pltpu.SemaphoreType.DMA(()),
        ],
        compiler_params=pltpu.CompilerParams(vmem_limit_bytes=limit),
        cost_estimate=pl.CostEstimate(flops=4 * 10**9, bytes_accessed=10**6, transcendentals=10**5),
        name="prepare",
    )(key_offsets, vertical_blocks, slash_offsets, queries, jnp.asarray(frequency_row()))

    def attend(prepared, pieces, shards_of, state, last):
        state_shape = (
            shape((8, query_rows * heads), f32),
            shape((HEAD_DIM + SUM_ROWS, query_rows * heads), f32),
        )
        return pl.pallas_call(
            functools.partial(attend_kernel, place_of, shards_of, not state, last),
            out_shape=shape(queries.shape, queries.dtype) if last else state_shape,
            in_specs=[vmem] * (4 + len(state) + len(pieces)),
            out_specs=vmem if last else (vmem, vmem),
            compiler_params=pltpu.CompilerParams(vmem_limit_bytes=limit),
            cost_estimate=pl.CostEstimate(
                flops=4 * 10**9, bytes_accessed=10**6, transcendentals=10**6
            ),
            name="attend",
        )(*prepared, *state, *pieces)

    own = jnp.concatenate([cached_keys, cached_values], axis=0)
    if not direct:
        gathered = lax.all_gather(own, ("seg", "ctx"), axis=0, tiled=True)
        return attend(prepared, [gathered], None, (), True)

    def number(seg, ctx):
        return seg * n_ctx + ctx

    def whole(ref):
        return ref[:rows, :], ref[rows : 2 * rows, :]

    far = exchange(own, lambda s, c, h: (s ^ (2 + h), c, h))
    near = exchange(own, lambda s, c, h: (s ^ (1 - h), c ^ h, h))
    near, prepared = lax.optimization_barrier((near, prepared))
    beside = swap(near)
    across = exchange(far, lambda s, c, h: (s, c ^ 1, h))
    state = attend(
        prepared,
        [own, near, beside, far],
        lambda refs, s, c, h: [
            (*whole(refs[0]), number(s, c)),
            (*whole(refs[1]), number(s ^ (1 - h), c ^ h)),
            (*whole(refs[2]), number(s ^ h, c ^ (1 - h))),
            (*whole(refs[3]), number(s ^ (2 + h), c)),
        ],
        (),
        False,
    )
    far_after, beside = lax.optimization_barrier((far, beside))
    far_beside = swap(far_after)
    half = jnp.where(lax.axis_index("head") == 0, beside[:rows], near[rows:])
    diagonal = exchange(half, lambda s, c, h: (s ^ 1, c, h))
    across, diagonal, state = lax.optimization_barrier((across, diagonal, state))
    last_beside = swap(jnp.concatenate([across, diagonal], axis=0))
    state = attend(
        prepared,
        [far_beside, across],
        lambda refs, s, c, h: [
            (*whole(refs[0]), number(s ^ (3 - h), c)),
            (*whole(refs[1]), number(s ^ (2 + h), c ^ 1)),
        ],
        state,
        False,
    )

    def last_shards(refs, s, c, h):
        diagonal, beside = refs
        mine, other = diagonal[...], beside[2 * rows :, :]
        return [
            (*whole(beside), number(s ^ (3 - h), c ^ 1)),
            (
                jnp.where(h == 0, mine, other),
                jnp.where(h == 0, other, mine),
                number(s ^ 1, c ^ 1),
            ),
        ]

    return attend(prepared, [diagonal, last_beside], last_shards, state, True)


def solution(mesh):
    return jax.shard_map(
        local,
        mesh=mesh,
        in_specs=(
            P(("groups", "ctx"), "head"),
            P(("groups", "seg", "ctx"), None),
            P(("groups", "seg", "ctx"), None),
            P("groups"),
            P("groups", None),
            P("groups", None),
        ),
        out_specs=P(("groups", "ctx"), "head"),
        check_vma=False,
    )
```

```python
import functools
import math

import jax
import jax.numpy as jnp
import numpy as np
from jax import lax
from jax.experimental import pallas as pl
from jax.experimental.pallas import tpu as pltpu
from jax.sharding import PartitionSpec as P

HEAD_DIM = 128
BLOCK = 64
ROPE_THETA = 500000.0
ROPE_FACTOR = 8.0
LOW_FACTOR = 1.0
HIGH_FACTOR = 4.0
TRAINED_CONTEXT = 8192.0
MASKED_SCORE = -1e30
SCORE_SCALE = HEAD_DIM**-0.5 * math.log2(math.e)
TILE = 128
FINE = 16
SUM_ROWS = 16
CHUNK = 512
DIRECT_SHARDS = (4, 2)
AXES = ("seg", "ctx", "head")


def frequency_row():
    exponent = np.arange(0, HEAD_DIM, 2, dtype=np.float64) / HEAD_DIM
    base = ROPE_THETA**-exponent
    wavelength = 2.0 * np.pi / base
    smooth = (TRAINED_CONTEXT / wavelength - LOW_FACTOR) / (HIGH_FACTOR - LOW_FACTOR)
    blended = (1.0 - smooth) * base / ROPE_FACTOR + smooth * base
    frequencies = np.where(
        wavelength < TRAINED_CONTEXT / HIGH_FACTOR,
        base,
        np.where(wavelength > TRAINED_CONTEXT / LOW_FACTOR, base / ROPE_FACTOR, blended),
    )
    return np.tile(frequencies, 2)[None, :].astype(np.float32)


def turned_sine(sine):
    lane = lax.broadcasted_iota(jnp.int32, sine.shape, 1)
    return jnp.where(lane < HEAD_DIM // 2, -sine, sine)


def rotate(vectors, cosine, signed_sine):
    wide = vectors.astype(jnp.float32)
    return (wide * cosine + pltpu.roll(wide, HEAD_DIM // 2, 1) * signed_sine).astype(jnp.bfloat16)


def angle_sum(cos_a, sin_a, cos_b, sin_b):
    return cos_a * cos_b - sin_a * sin_b, sin_a * cos_b + cos_a * sin_b


def shard_tables(cosines, sines, line, rows):
    cos_f, sin_f = cosines[pl.ds(0, FINE), :], turned_sine(sines[pl.ds(0, FINE), :])
    cos_c, sin_c = angle_sum(
        cosines[pl.ds(FINE, FINE), :],
        sines[pl.ds(FINE, FINE), :],
        cosines[pl.ds(line, 1), :],
        sines[pl.ds(line, 1), :],
    )
    signed = turned_sine(sin_c)
    parts = [
        (
            cos_f * cos_c[i : i + 1] - sin_f * signed[i : i + 1],
            sin_f * cos_c[i : i + 1] + cos_f * signed[i : i + 1],
        )
        for i in range(rows // FINE)
    ]
    return tuple(jnp.concatenate(table, axis=0) for table in zip(*parts))


def prepare_kernel(
    query_start_of, offsets, vertical, slash, queries, freq, rotated, cosines, sines, masks,
    angles, bias, held, arrival,
):
    query_rows, columns = held.shape
    heads = columns // HEAD_DIM
    fetch = pltpu.make_async_copy(queries, held, arrival)
    fetch.start()
    query_start, first_list = query_start_of()

    step = lax.broadcasted_iota(jnp.int32, (FINE, HEAD_DIM), 0)
    angles[pl.ds(0, FINE), :] = step
    angles[pl.ds(FINE, FINE), :] = step * FINE
    for shard in range(offsets.shape[0]):
        angles[pl.ds(2 * FINE + shard, 1), :] = jnp.full((1, HEAD_DIM), offsets[shard], jnp.int32)
    angles[pl.ds(angles.shape[0] - 8, 8), :] = jnp.full((8, HEAD_DIM), query_start, jnp.int32)
    angle = angles[...].astype(jnp.float32) * freq[...]
    cosines[...] = jnp.cos(angle)
    sines[...] = jnp.sin(angle)

    key_block = lax.broadcasted_iota(jnp.int32, bias.shape, 0)
    lane_block = lax.broadcasted_iota(jnp.int32, (1, query_rows), 1) // BLOCK
    hit = jnp.zeros(bias.shape, jnp.bool_)
    for entries, distance in ((vertical, False), (slash, True)):
        for entry in range(entries.shape[1]):
            wanted = jnp.zeros((1, query_rows), jnp.int32)
            for block in range(query_rows // BLOCK):
                value = entries[first_list + block, entry]
                if distance:
                    value = query_start // BLOCK + block - value
                wanted = jnp.where(lane_block == block, value, wanted)
            hit = hit | (key_block == wanted)
    bias[...] = jnp.where(hit, 0.0, MASKED_SCORE)

    rows = masks.shape[0] // offsets.shape[0]
    ahead = lax.broadcasted_iota(jnp.int32, (rows, query_rows), 1) - lax.broadcasted_iota(
        jnp.int32, (rows, query_rows), 0
    )

    @pl.loop(0, offsets.shape[0])
    def _(shard):
        offset = offsets[shard]
        lines = [
            jnp.broadcast_to(bias[pl.ds(offset // BLOCK + block, 1), :], (BLOCK, query_rows))
            for block in range(rows // BLOCK)
        ]
        masks[pl.ds(pl.multiple_of(shard * rows, rows), rows), :] = jnp.where(
            ahead >= offset - query_start, jnp.concatenate(lines, axis=0), MASKED_SCORE
        ).astype(masks.dtype)

    cosine, sine = shard_tables(cosines, sines, angles.shape[0] - 8, query_rows)
    fetch.wait()
    for head in range(heads):
        turned = rotate(held[:, pl.ds(head * HEAD_DIM, HEAD_DIM)], cosine, sine).T
        for tile in range(query_rows // TILE):
            lines = pl.ds((tile * heads + head) * TILE, TILE)
            rotated[:, lines] = turned[:, tile * TILE : (tile + 1) * TILE]


def attend_kernel(place_of, shards_of, first, last, *refs):
    rotated, cosines, sines, masks = refs[:4]
    refs = refs[4:]
    if not first:
        old_peak, old_sums = refs[:2]
        refs = refs[2:]
    if last:
        pieces, out = refs[:-1], refs[-1]
    else:
        pieces, new_peak, new_sums = refs[:-2], refs[-2], refs[-1]
    query_rows = masks.shape[1]
    tiles = query_rows // TILE
    width = rotated.shape[1] // tiles
    rows = masks.shape[0] // (cosines.shape[0] - 2 * FINE - 8)
    ones = jnp.ones((SUM_ROWS, rows), jnp.bfloat16)
    unit = (
        lax.broadcasted_iota(jnp.int32, (TILE, width), 0)
        == lax.broadcasted_iota(jnp.int32, (TILE, width), 1) % TILE
    ).astype(jnp.bfloat16)

    def load_keys(keys, shard):
        keys = rotate(keys, *shard_tables(cosines, sines, 2 * FINE + shard, rows))
        return keys, masks[pl.ds(pl.multiple_of(shard * rows, rows), rows), :]

    def load_values(values):
        return jnp.concatenate([values.T, ones], axis=0)

    def score(keys, mask, start, size):
        tile = start // width
        query = jnp.concatenate([rotated[:, pl.ds(start, size)], unit[:, :size]], axis=0)
        return jnp.dot(
            jnp.concatenate([keys, mask[:, tile * TILE : (tile + 1) * TILE]], axis=1),
            query,
            preferred_element_type=jnp.float32,
        )

    def update(scores, values, before):
        peak = scores.max(axis=0, keepdims=True)
        if before is not None:
            peak = jnp.maximum(before[0], peak)
        weights = jnp.exp2((scores - peak) * SCORE_SCALE).astype(jnp.bfloat16)
        sums = jnp.dot(values, weights, preferred_element_type=jnp.float32)
        if before is not None:
            sums = sums + before[1] * jnp.exp2((before[0] - peak) * SCORE_SCALE)
        return peak, sums

    def finish(start, peak, sums):
        size = sums.shape[1]
        if not last:
            span = pl.ds(start, size)
            new_peak[:, span] = jnp.broadcast_to(peak, (new_peak.shape[0], size))
            new_sums[:, span] = sums
            return
        part = sums[:HEAD_DIM] * (1.0 / sums[HEAD_DIM : HEAD_DIM + 1])
        part = part.astype(out.dtype)
        for column in range(0, size, TILE):
            tile, head = divmod((start + column) // TILE, width // TILE)
            out[pl.ds(tile * TILE, TILE), pl.ds(head * HEAD_DIM, HEAD_DIM)] = part[
                :, column : column + TILE
            ].T

    if shards_of is not None:
        shards = shards_of(pieces, *place_of())
        keys, mask = (
            jnp.concatenate(part, axis=0)
            for part in zip(*(load_keys(keys, shard) for keys, _, shard in shards))
        )
        starts = list(range(0, rotated.shape[1], CHUNK))
        ahead = score(keys, mask, starts[0], CHUNK)
        values = jnp.concatenate([load_values(values) for _, values, _ in shards], axis=1)
        for start in starts:
            scores = ahead
            if start != starts[-1]:
                ahead = score(keys, mask, start + CHUNK, CHUNK)
            before = None
            if not first:
                before = (old_peak[:1, pl.ds(start, CHUNK)], old_sums[:, pl.ds(start, CHUNK)])
            finish(start, *update(scores, values, before))
    else:
        (whole,) = pieces
        for tile in range(tiles):

            def step(shard, before, tile=tile):
                start = pl.multiple_of(shard * (2 * rows), 2 * rows)
                keys, mask = load_keys(whole[pl.ds(start, rows), :], shard)
                values = load_values(whole[pl.ds(start + rows, rows), :])
                return update(score(keys, mask, tile * width, width), values, before)

            initial = (
                jnp.full((1, width), MASKED_SCORE, jnp.float32),
                jnp.zeros((HEAD_DIM + SUM_ROWS, width), jnp.float32),
            )
            finish(
                tile * width, *lax.fori_loop(0, whole.shape[0] // (2 * rows), step, initial)
            )


def local(queries, cached_keys, cached_values, key_offsets, vertical_blocks, slash_offsets):
    query_rows = queries.shape[0]
    heads = queries.shape[1] // HEAD_DIM
    rows = cached_keys.shape[0]
    n_seg, n_ctx = lax.axis_size("seg"), lax.axis_size("ctx")
    shards = n_seg * n_ctx
    prefix = rows * shards - query_rows * n_ctx

    def query_start_of():
        ctx = lax.axis_index("ctx")
        return prefix + ctx * query_rows, ctx * (query_rows // BLOCK)

    def place_of():
        return tuple(lax.axis_index(axis) for axis in AXES)

    def exchange(a, partner):
        pairs = []
        for seg in range(n_seg):
            for ctx in range(n_ctx):
                for head in range(2):
                    to_seg, to_ctx, to_head = partner(seg, ctx, head)
                    pairs.append(
                        ((seg * n_ctx + ctx) * 2 + head, (to_seg * n_ctx + to_ctx) * 2 + to_head)
                    )
        return lax.ppermute(a, AXES, pairs)

    def swap(a):
        return exchange(a, lambda s, c, h: (s, c, 1 - h))

    vmem = pl.BlockSpec(memory_space=pltpu.VMEM)
    smem = pl.BlockSpec(memory_space=pltpu.SMEM)
    f32 = jnp.float32
    direct = (n_seg, n_ctx) == DIRECT_SHARDS
    limit = (16 if direct else 56) * 1024 * 1024
    shape = jax.ShapeDtypeStruct
    lines = 2 * FINE + shards + 8
    prepared = pl.pallas_call(
        functools.partial(prepare_kernel, query_start_of),
        out_shape=(
            shape((HEAD_DIM, query_rows * heads), jnp.bfloat16),
            shape((lines, HEAD_DIM), f32),
            shape((lines, HEAD_DIM), f32),
            shape((shards * rows, query_rows), jnp.bfloat16),
        ),
        in_specs=[smem, smem, smem, pl.BlockSpec(memory_space=pltpu.HBM), vmem],
        out_specs=[vmem] * 4,
        scratch_shapes=[
            pltpu.VMEM((lines, HEAD_DIM), jnp.int32),
            pltpu.VMEM((shards * rows // BLOCK, query_rows), f32),
            pltpu.VMEM(queries.shape, queries.dtype),
            pltpu.SemaphoreType.DMA(()),
        ],
        compiler_params=pltpu.CompilerParams(vmem_limit_bytes=limit),
        cost_estimate=pl.CostEstimate(flops=4 * 10**9, bytes_accessed=10**6, transcendentals=10**5),
        name="prepare",
    )(key_offsets, vertical_blocks, slash_offsets, queries, jnp.asarray(frequency_row()))

    def attend(prepared, pieces, shards_of, state, last):
        state_shape = (
            shape((8, query_rows * heads), f32),
            shape((HEAD_DIM + SUM_ROWS, query_rows * heads), f32),
        )
        return pl.pallas_call(
            functools.partial(attend_kernel, place_of, shards_of, not state, last),
            out_shape=shape(queries.shape, queries.dtype) if last else state_shape,
            in_specs=[vmem] * (4 + len(state) + len(pieces)),
            out_specs=vmem if last else (vmem, vmem),
            compiler_params=pltpu.CompilerParams(vmem_limit_bytes=limit),
            cost_estimate=pl.CostEstimate(
                flops=4 * 10**9, bytes_accessed=10**6, transcendentals=10**6
            ),
            name="attend",
        )(*prepared, *state, *pieces)

    own = jnp.concatenate([cached_keys, cached_values], axis=0)
    if not direct:
        gathered = lax.all_gather(own, ("seg", "ctx"), axis=0, tiled=True)
        return attend(prepared, [gathered], None, (), True)

    def number(seg, ctx):
        return seg * n_ctx + ctx

    def whole(ref):
        return ref[:rows, :], ref[rows : 2 * rows, :]

    far = exchange(own, lambda s, c, h: (s ^ (2 + h), c, h))
    near = exchange(own, lambda s, c, h: (s ^ (1 - h), c ^ h, h))
    near, prepared = lax.optimization_barrier((near, prepared))
    beside = swap(near)
    across = exchange(far, lambda s, c, h: (s, c ^ 1, h))
    state = attend(
        prepared,
        [own, near, beside, far],
        lambda refs, s, c, h: [
            (*whole(refs[0]), number(s, c)),
            (*whole(refs[1]), number(s ^ (1 - h), c ^ h)),
            (*whole(refs[2]), number(s ^ h, c ^ (1 - h))),
            (*whole(refs[3]), number(s ^ (2 + h), c)),
        ],
        (),
        False,
    )
    far_after, beside = lax.optimization_barrier((far, beside))
    far_beside = swap(far_after)
    half = jnp.where(lax.axis_index("head") == 0, beside[:rows], near[rows:])
    diagonal = exchange(half, lambda s, c, h: (s ^ 1, c, h))
    across, diagonal, state = lax.optimization_barrier((across, diagonal, state))
    last_beside = swap(jnp.concatenate([across, diagonal], axis=0))
    state = attend(
        prepared,
        [far_beside, across],
        lambda refs, s, c, h: [
            (*whole(refs[0]), number(s ^ (3 - h), c)),
            (*whole(refs[1]), number(s ^ (2 + h), c ^ 1)),
        ],
        state,
        False,
    )

    def last_shards(refs, s, c, h):
        diagonal, beside = refs
        mine, other = diagonal[...], beside[2 * rows :, :]
        return [
            (*whole(beside), number(s ^ (3 - h), c ^ 1)),
            (
                jnp.where(h == 0, mine, other),
                jnp.where(h == 0, other, mine),
                number(s ^ 1, c ^ 1),
            ),
        ]

    return attend(prepared, [diagonal, last_beside], last_shards, state, True)


def solution(mesh):
    return jax.shard_map(
        local,
        mesh=mesh,
        in_specs=(
            P(("groups", "ctx"), "head"),
            P(("groups", "seg", "ctx"), None),
            P(("groups", "seg", "ctx"), None),
            P("groups"),
            P("groups", None),
            P("groups", None),
        ),
        out_specs=P(("groups", "ctx"), "head"),
        check_vma=False,
    )
```

```python
import functools
import math

import jax
import jax.numpy as jnp
import numpy as np
from jax import lax
from jax.experimental import pallas as pl
from jax.experimental.pallas import tpu as pltpu
from jax.sharding import PartitionSpec as P

HEAD_DIM = 128
BLOCK = 64
ROPE_THETA = 500000.0
ROPE_FACTOR = 8.0
LOW_FACTOR = 1.0
HIGH_FACTOR = 4.0
TRAINED_CONTEXT = 8192.0
MASKED_SCORE = -1e30
SCORE_SCALE = HEAD_DIM**-0.5 * math.log2(math.e)
TILE = 128
FINE = 16
SUM_ROWS = 16
CHUNK = 256
DIRECT_SHARDS = (4, 2)
AXES = ("seg", "ctx", "head")


def frequency_row():
    exponent = np.arange(0, HEAD_DIM, 2, dtype=np.float64) / HEAD_DIM
    base = ROPE_THETA**-exponent
    wavelength = 2.0 * np.pi / base
    smooth = (TRAINED_CONTEXT / wavelength - LOW_FACTOR) / (HIGH_FACTOR - LOW_FACTOR)
    blended = (1.0 - smooth) * base / ROPE_FACTOR + smooth * base
    frequencies = np.where(
        wavelength < TRAINED_CONTEXT / HIGH_FACTOR,
        base,
        np.where(wavelength > TRAINED_CONTEXT / LOW_FACTOR, base / ROPE_FACTOR, blended),
    )
    return np.tile(frequencies, 2)[None, :].astype(np.float32)


def turned_sine(sine):
    lane = lax.broadcasted_iota(jnp.int32, sine.shape, 1)
    return jnp.where(lane < HEAD_DIM // 2, -sine, sine)


def rotate(vectors, cosine, signed_sine):
    wide = vectors.astype(jnp.float32)
    return (wide * cosine + pltpu.roll(wide, HEAD_DIM // 2, 1) * signed_sine).astype(jnp.bfloat16)


def angle_sum(cos_a, sin_a, cos_b, sin_b):
    return cos_a * cos_b - sin_a * sin_b, sin_a * cos_b + cos_a * sin_b


def shard_tables(cosines, sines, line, rows):
    cos_f, sin_f = cosines[pl.ds(0, FINE), :], turned_sine(sines[pl.ds(0, FINE), :])
    cos_c, sin_c = angle_sum(
        cosines[pl.ds(FINE, FINE), :],
        sines[pl.ds(FINE, FINE), :],
        cosines[pl.ds(line, 1), :],
        sines[pl.ds(line, 1), :],
    )
    signed = turned_sine(sin_c)
    parts = [
        (
            cos_f * cos_c[i : i + 1] - sin_f * signed[i : i + 1],
            sin_f * cos_c[i : i + 1] + cos_f * signed[i : i + 1],
        )
        for i in range(rows // FINE)
    ]
    return tuple(jnp.concatenate(table, axis=0) for table in zip(*parts))


def prepare_kernel(
    query_start_of, offsets, vertical, slash, queries, freq, rotated, cosines, sines, masks,
    angles, bias, held, arrival,
):
    query_rows, columns = held.shape
    heads = columns // HEAD_DIM
    fetch = pltpu.make_async_copy(queries, held, arrival)
    fetch.start()
    query_start, first_list = query_start_of()

    step = lax.broadcasted_iota(jnp.int32, (FINE, HEAD_DIM), 0)
    angles[pl.ds(0, FINE), :] = step
    angles[pl.ds(FINE, FINE), :] = step * FINE
    for shard in range(offsets.shape[0]):
        angles[pl.ds(2 * FINE + shard, 1), :] = jnp.full((1, HEAD_DIM), offsets[shard], jnp.int32)
    angles[pl.ds(angles.shape[0] - 8, 8), :] = jnp.full((8, HEAD_DIM), query_start, jnp.int32)
    angle = angles[...].astype(jnp.float32) * freq[...]
    cosines[...] = jnp.cos(angle)
    sines[...] = jnp.sin(angle)

    key_block = lax.broadcasted_iota(jnp.int32, bias.shape, 0)
    lane_block = lax.broadcasted_iota(jnp.int32, (1, query_rows), 1) // BLOCK
    hit = jnp.zeros(bias.shape, jnp.bool_)
    for entries, distance in ((vertical, False), (slash, True)):
        for entry in range(entries.shape[1]):
            wanted = jnp.zeros((1, query_rows), jnp.int32)
            for block in range(query_rows // BLOCK):
                value = entries[first_list + block, entry]
                if distance:
                    value = query_start // BLOCK + block - value
                wanted = jnp.where(lane_block == block, value, wanted)
            hit = hit | (key_block == wanted)
    bias[...] = jnp.where(hit, 0.0, MASKED_SCORE)

    rows = masks.shape[0] // offsets.shape[0]
    ahead = lax.broadcasted_iota(jnp.int32, (rows, query_rows), 1) - lax.broadcasted_iota(
        jnp.int32, (rows, query_rows), 0
    )

    @pl.loop(0, offsets.shape[0])
    def _(shard):
        offset = offsets[shard]
        lines = [
            jnp.broadcast_to(bias[pl.ds(offset // BLOCK + block, 1), :], (BLOCK, query_rows))
            for block in range(rows // BLOCK)
        ]
        masks[pl.ds(pl.multiple_of(shard * rows, rows), rows), :] = jnp.where(
            ahead >= offset - query_start, jnp.concatenate(lines, axis=0), MASKED_SCORE
        ).astype(masks.dtype)

    cosine, sine = shard_tables(cosines, sines, angles.shape[0] - 8, query_rows)
    fetch.wait()
    for head in range(heads):
        turned = rotate(held[:, pl.ds(head * HEAD_DIM, HEAD_DIM)], cosine, sine).T
        for tile in range(query_rows // TILE):
            lines = pl.ds((tile * heads + head) * TILE, TILE)
            rotated[:, lines] = turned[:, tile * TILE : (tile + 1) * TILE]


def attend_kernel(place_of, shards_of, first, last, *refs):
    rotated, cosines, sines, masks = refs[:4]
    refs = refs[4:]
    if not first:
        old_peak, old_sums = refs[:2]
        refs = refs[2:]
    if last:
        pieces, out = refs[:-1], refs[-1]
    else:
        pieces, new_peak, new_sums = refs[:-2], refs[-2], refs[-1]
    query_rows = masks.shape[1]
    tiles = query_rows // TILE
    width = rotated.shape[1] // tiles
    rows = masks.shape[0] // (cosines.shape[0] - 2 * FINE - 8)
    ones = jnp.ones((SUM_ROWS, rows), jnp.bfloat16)
    unit = (
        lax.broadcasted_iota(jnp.int32, (TILE, width), 0)
        == lax.broadcasted_iota(jnp.int32, (TILE, width), 1) % TILE
    ).astype(jnp.bfloat16)

    def load_keys(keys, shard):
        keys = rotate(keys, *shard_tables(cosines, sines, 2 * FINE + shard, rows))
        return keys, masks[pl.ds(pl.multiple_of(shard * rows, rows), rows), :]

    def load_values(values):
        return jnp.concatenate([values.T, ones], axis=0)

    def score(keys, mask, start, size):
        tile = start // width
        query = jnp.concatenate([rotated[:, pl.ds(start, size)], unit[:, :size]], axis=0)
        return jnp.dot(
            jnp.concatenate([keys, mask[:, tile * TILE : (tile + 1) * TILE]], axis=1),
            query,
            preferred_element_type=jnp.float32,
        )

    def update(scores, values, before):
        peak = scores.max(axis=0, keepdims=True)
        if before is not None:
            peak = jnp.maximum(before[0], peak)
        weights = jnp.exp2((scores - peak) * SCORE_SCALE).astype(jnp.bfloat16)
        sums = jnp.dot(values, weights, preferred_element_type=jnp.float32)
        if before is not None:
            sums = sums + before[1] * jnp.exp2((before[0] - peak) * SCORE_SCALE)
        return peak, sums

    def finish(start, peak, sums):
        size = sums.shape[1]
        if not last:
            span = pl.ds(start, size)
            new_peak[:, span] = jnp.broadcast_to(peak, (new_peak.shape[0], size))
            new_sums[:, span] = sums
            return
        part = sums[:HEAD_DIM] * (1.0 / sums[HEAD_DIM : HEAD_DIM + 1])
        part = part.astype(out.dtype)
        for column in range(0, size, TILE):
            tile, head = divmod((start + column) // TILE, width // TILE)
            out[pl.ds(tile * TILE, TILE), pl.ds(head * HEAD_DIM, HEAD_DIM)] = part[
                :, column : column + TILE
            ].T

    if shards_of is not None:
        shards = shards_of(pieces, *place_of())
        keys, mask = (
            jnp.concatenate(part, axis=0)
            for part in zip(*(load_keys(keys, shard) for keys, _, shard in shards))
        )
        starts = list(range(0, rotated.shape[1], CHUNK))
        ahead = score(keys, mask, starts[0], CHUNK)
        values = jnp.concatenate([load_values(values) for _, values, _ in shards], axis=1)
        for start in starts:
            scores = ahead
            if start != starts[-1]:
                ahead = score(keys, mask, start + CHUNK, CHUNK)
            before = None
            if not first:
                before = (old_peak[:1, pl.ds(start, CHUNK)], old_sums[:, pl.ds(start, CHUNK)])
            finish(start, *update(scores, values, before))
    else:
        (whole,) = pieces
        for tile in range(tiles):

            def step(shard, before, tile=tile):
                start = pl.multiple_of(shard * (2 * rows), 2 * rows)
                keys, mask = load_keys(whole[pl.ds(start, rows), :], shard)
                values = load_values(whole[pl.ds(start + rows, rows), :])
                return update(score(keys, mask, tile * width, width), values, before)

            initial = (
                jnp.full((1, width), MASKED_SCORE, jnp.float32),
                jnp.zeros((HEAD_DIM + SUM_ROWS, width), jnp.float32),
            )
            finish(
                tile * width, *lax.fori_loop(0, whole.shape[0] // (2 * rows), step, initial)
            )


def local(queries, cached_keys, cached_values, key_offsets, vertical_blocks, slash_offsets):
    query_rows = queries.shape[0]
    heads = queries.shape[1] // HEAD_DIM
    rows = cached_keys.shape[0]
    n_seg, n_ctx = lax.axis_size("seg"), lax.axis_size("ctx")
    shards = n_seg * n_ctx
    prefix = rows * shards - query_rows * n_ctx

    def query_start_of():
        ctx = lax.axis_index("ctx")
        return prefix + ctx * query_rows, ctx * (query_rows // BLOCK)

    def place_of():
        return tuple(lax.axis_index(axis) for axis in AXES)

    def exchange(a, partner):
        pairs = []
        for seg in range(n_seg):
            for ctx in range(n_ctx):
                for head in range(2):
                    to_seg, to_ctx, to_head = partner(seg, ctx, head)
                    pairs.append(
                        ((seg * n_ctx + ctx) * 2 + head, (to_seg * n_ctx + to_ctx) * 2 + to_head)
                    )
        return lax.ppermute(a, AXES, pairs)

    def swap(a):
        return exchange(a, lambda s, c, h: (s, c, 1 - h))

    vmem = pl.BlockSpec(memory_space=pltpu.VMEM)
    smem = pl.BlockSpec(memory_space=pltpu.SMEM)
    f32 = jnp.float32
    direct = (n_seg, n_ctx) == DIRECT_SHARDS
    limit = (16 if direct else 56) * 1024 * 1024
    shape = jax.ShapeDtypeStruct
    lines = 2 * FINE + shards + 8
    prepared = pl.pallas_call(
        functools.partial(prepare_kernel, query_start_of),
        out_shape=(
            shape((HEAD_DIM, query_rows * heads), jnp.bfloat16),
            shape((lines, HEAD_DIM), f32),
            shape((lines, HEAD_DIM), f32),
            shape((shards * rows, query_rows), jnp.bfloat16),
        ),
        in_specs=[smem, smem, smem, pl.BlockSpec(memory_space=pltpu.HBM), vmem],
        out_specs=[vmem] * 4,
        scratch_shapes=[
            pltpu.VMEM((lines, HEAD_DIM), jnp.int32),
            pltpu.VMEM((shards * rows // BLOCK, query_rows), f32),
            pltpu.VMEM(queries.shape, queries.dtype),
            pltpu.SemaphoreType.DMA(()),
        ],
        compiler_params=pltpu.CompilerParams(vmem_limit_bytes=limit),
        cost_estimate=pl.CostEstimate(flops=4 * 10**9, bytes_accessed=10**6, transcendentals=10**5),
        name="prepare",
    )(key_offsets, vertical_blocks, slash_offsets, queries, jnp.asarray(frequency_row()))

    def attend(prepared, pieces, shards_of, state, last):
        state_shape = (
            shape((8, query_rows * heads), f32),
            shape((HEAD_DIM + SUM_ROWS, query_rows * heads), f32),
        )
        return pl.pallas_call(
            functools.partial(attend_kernel, place_of, shards_of, not state, last),
            out_shape=shape(queries.shape, queries.dtype) if last else state_shape,
            in_specs=[vmem] * (4 + len(state) + len(pieces)),
            out_specs=vmem if last else (vmem, vmem),
            compiler_params=pltpu.CompilerParams(vmem_limit_bytes=limit),
            cost_estimate=pl.CostEstimate(
                flops=4 * 10**9, bytes_accessed=10**6, transcendentals=10**6
            ),
            name="attend",
        )(*prepared, *state, *pieces)

    own = jnp.concatenate([cached_keys, cached_values], axis=0)
    if not direct:
        gathered = lax.all_gather(own, ("seg", "ctx"), axis=0, tiled=True)
        return attend(prepared, [gathered], None, (), True)

    def number(seg, ctx):
        return seg * n_ctx + ctx

    def whole(ref):
        return ref[:rows, :], ref[rows : 2 * rows, :]

    far = exchange(own, lambda s, c, h: (s ^ (2 + h), c, h))
    near = exchange(own, lambda s, c, h: (s ^ (1 - h), c ^ h, h))
    near, prepared = lax.optimization_barrier((near, prepared))
    beside = swap(near)
    across = exchange(far, lambda s, c, h: (s, c ^ 1, h))
    state = attend(
        prepared,
        [own, near, beside, far],
        lambda refs, s, c, h: [
            (*whole(refs[0]), number(s, c)),
            (*whole(refs[1]), number(s ^ (1 - h), c ^ h)),
            (*whole(refs[2]), number(s ^ h, c ^ (1 - h))),
            (*whole(refs[3]), number(s ^ (2 + h), c)),
        ],
        (),
        False,
    )
    far_after, beside = lax.optimization_barrier((far, beside))
    far_beside = swap(far_after)
    half = jnp.where(lax.axis_index("head") == 0, beside[:rows], near[rows:])
    diagonal = exchange(half, lambda s, c, h: (s ^ 1, c, h))
    across, state = lax.optimization_barrier((across, state))
    across_beside = swap(across)
    diagonal, state = lax.optimization_barrier((diagonal, state))
    diagonal_beside = swap(diagonal)
    state = attend(
        prepared,
        [far_beside, across],
        lambda refs, s, c, h: [
            (*whole(refs[0]), number(s ^ (3 - h), c)),
            (*whole(refs[1]), number(s ^ (2 + h), c ^ 1)),
        ],
        state,
        False,
    )

    def last_shards(refs, s, c, h):
        diagonal, diagonal_beside, beside = refs
        mine, other = diagonal[...], diagonal_beside[...]
        return [
            (*whole(beside), number(s ^ (3 - h), c ^ 1)),
            (
                jnp.where(h == 0, mine, other),
                jnp.where(h == 0, other, mine),
                number(s ^ 1, c ^ 1),
            ),
        ]

    return attend(prepared, [diagonal, diagonal_beside, across_beside], last_shards, state, True)


def solution(mesh):
    return jax.shard_map(
        local,
        mesh=mesh,
        in_specs=(
            P(("groups", "ctx"), "head"),
            P(("groups", "seg", "ctx"), None),
            P(("groups", "seg", "ctx"), None),
            P("groups"),
            P("groups", None),
            P("groups", None),
        ),
        out_specs=P(("groups", "ctx"), "head"),
        check_vma=False,
    )
```
